32 devices in a mesh: seq: 8 (over y, x, core), head: 4 (over z).
Axes of the slice: x: 2, y: 2, z: 4, core: 2. Of those that a mesh axis runs over, the one named last changes fastest.
Arguments:
- tokens: bfloat16 [4096, 2048], P(('seq', 'head')), may hold values from -6 to 6
- cotangent: bfloat16 [4096, 2048], P(('seq', 'head')), may hold values from -6 to 6
- doc_lengths: int32 [3], replicated, may hold values from 1 to 3840, as said below
- q_weight: bfloat16 [2048, 2048], P('seq', 'head'), may hold values from -0.125 to 0.125
- k_weight: bfloat16 [2048, 2048], P('seq', 'head'), may hold values from -0.125 to 0.125
- v_weight: bfloat16 [2048, 2048], P('seq', 'head'), may hold values from -0.125 to 0.125
- o_weight: bfloat16 [2048, 2048], P('head', 'seq'), may hold values from -0.125 to 0.125
- gate_weight: bfloat16 [2048, 8192], P('seq', 'head'), may hold values from -0.125 to 0.125
- up_weight: bfloat16 [2048, 8192], P('seq', 'head'), may hold values from -0.125 to 0.125
- down_weight: bfloat16 [8192, 2048], P('head', 'seq'), may hold values from -0.0625 to 0.0625
- q_gain: float32 [2048], replicated, may hold values from 0.25 to 1.75
- k_gain: float32 [2048], replicated, may hold values from 0.25 to 1.75
- attn_gain: float32 [2048], replicated, may hold values from 0.25 to 1.75
- mlp_gain: float32 [2048], replicated, may hold values from 0.25 to 1.75
Outputs:
- output: bfloat16 [4096, 2048], P(('seq', 'head'))
- input_grad: float32 [4096, 2048], P(('seq', 'head'))
- q_weight_grad: float32 [2048, 2048], P('seq', 'head')
- k_weight_grad: float32 [2048, 2048], P('seq', 'head')
- v_weight_grad: float32 [2048, 2048], P('seq', 'head')
- o_weight_grad: float32 [2048, 2048], P('head', 'seq')
- gate_weight_grad: float32 [2048, 8192], P('seq', 'head')
- up_weight_grad: float32 [2048, 8192], P('seq', 'head')
- down_weight_grad: float32 [8192, 2048], P('head', 'seq')
- q_gain_grad: float32 [2048], P('seq')
- k_gain_grad: float32 [2048], P('seq')
- attn_gain_grad: float32 [2048], P('seq')
- mlp_gain_grad: float32 [2048], P('seq')
The draws below stay inside these ranges and needn't reach their ends.
Inputs may be any that keep to these rules, and one draw needn't show every extreme that they name: `doc_lengths`: three documents packed in order fill the row; the longest has exactly 3840 tokens.
All inputs are finite; a program needn't handle non-finite values.
Results may differ from the reference program's by a relative error of at most 0.025.
Values may be sent and summed in bfloat16 or wider, within the bound.
A program may use at most 192 MiB of HBM per device.

```python
import jax
import jax.numpy as jnp
from jax import lax

D = 2048
HEADS = 16
HEAD_DIM = 128
FF = 8192
TOK_DEV = 512
KEY_BLOCK = 1024
TOKENS = 4096


def draw_doc_lengths(key, part):
    key = jax.random.fold_in(key, 11)
    split_key, place_key = jax.random.split(key)
    longest = TOKENS - TOK_DEV // 2
    remaining = TOK_DEV // 2
    first_short = jax.random.randint(split_key, (), 1, remaining, dtype=jnp.int32)
    place = jax.random.randint(place_key, (), 0, 3, dtype=jnp.int32)
    slots = jnp.arange(3, dtype=jnp.int32)
    other_rank = slots - (slots > place).astype(jnp.int32)
    shorts = jnp.where(other_rank == 0, first_short, remaining - first_short)
    return jnp.where(slots == place, longest, shorts).astype(jnp.int32)


def block_scale(stream_key, dims, cuts, low, top_value):
    level, own = 1.0, jax.random.fold_in(stream_key, 6)
    for axis_at, shards_of in cuts:
        draws = jnp.exp(jax.random.uniform(jax.random.fold_in(own, axis_at), (shards_of,), jnp.float32, low / len(cuts), top_value / len(cuts)))
        level = level * jnp.repeat(draws, dims[axis_at] // shards_of).reshape([-1 if axis == axis_at else 1 for axis in range(len(dims))])
    return level


def scatter_about(stream_key, dims, width, bound, cuts=(), held_as=jnp.bfloat16):
    loudness = block_scale(stream_key, dims, cuts, -0.22, 0.18) if cuts else 1.0
    array = jax.random.normal(stream_key, dims, jnp.float32) * width * loudness
    return jnp.minimum(jnp.maximum(array, -bound), bound).astype(held_as)


def setup_inputs(seed: int = 0) -> dict:
    seeds = jax.random.split(jax.random.key(seed), 15)
    tokens = scatter_about(seeds[0], (TOKENS, D), 1.0, 6.0, ((0, 32),))
    cotangent = scatter_about(seeds[1], (TOKENS, D), 1.0, 6.0, ((0, 32),))
    doc_lengths = draw_doc_lengths(jax.random.fold_in(seeds[14], 71), 0)
    q_weight = scatter_about(seeds[3], (D, D), D ** -0.5, 0.125, ((0, 8), (1, 4)))
    k_weight = scatter_about(seeds[4], (D, D), D ** -0.5, 0.125, ((0, 8), (1, 4)))
    v_weight = scatter_about(seeds[5], (D, D), D ** -0.5, 0.125, ((0, 8), (1, 4)))
    o_weight = scatter_about(seeds[6], (D, D), D ** -0.5, 0.125, ((0, 4), (1, 8)))
    gate_weight = scatter_about(seeds[7], (D, FF), D ** -0.5, 0.125, ((0, 8), (1, 4)))
    up_weight = scatter_about(seeds[8], (D, FF), D ** -0.5, 0.125, ((0, 8), (1, 4)))
    down_weight = scatter_about(seeds[9], (FF, D), FF ** -0.5, 0.0625, ((0, 4), (1, 8)))
    q_gain = jnp.clip(1.0 + 0.15 * jax.random.normal(seeds[10], (D,), jnp.float32), 0.25, 1.75)
    k_gain = jnp.clip(1.0 + 0.15 * jax.random.normal(seeds[11], (D,), jnp.float32), 0.25, 1.75)
    attn_gain = jnp.clip(1.0 + 0.15 * jax.random.normal(seeds[12], (D,), jnp.float32), 0.25, 1.75)
    mlp_gain = jnp.clip(1.0 + 0.15 * jax.random.normal(seeds[13], (D,), jnp.float32), 0.25, 1.75)
    return {"tokens": tokens, "cotangent": cotangent, "doc_lengths": doc_lengths, "q_weight": q_weight, "k_weight": k_weight, "v_weight": v_weight, "o_weight": o_weight, "gate_weight": gate_weight, "up_weight": up_weight, "down_weight": down_weight, "q_gain": q_gain, "k_gain": k_gain, "attn_gain": attn_gain, "mlp_gain": mlp_gain}


epsilon = 1e-06
rope_base = 500000.0
highest = lax.Precision.HIGHEST

@jax.custom_vjp
def low(v):
    return lax.optimization_barrier(v.astype(jnp.bfloat16)).astype(jnp.float32)

@jax.custom_vjp
def low_back(v):
    return v

def low_keep(v):
    return (low(v), None)

def low_pass(kept, grad):
    return (grad,)

def back_keep(v):
    return (v, None)

def back_low(kept, grad):
    return (low(grad),)
low.defvjp(low_keep, low_pass)
low_back.defvjp(back_keep, back_low)

def rms_norm(vector):
    return vector * lax.rsqrt(lax.optimization_barrier(jnp.mean(vector * vector, axis=-1, keepdims=True)) + epsilon)

def rope_tables(positions):
    frequency = jnp.power(rope_base, -jnp.arange(HEAD_DIM // 2, dtype=jnp.float32) * (2.0 / HEAD_DIM))
    angles = positions.astype(jnp.float32)[:, None] * frequency[None, :]
    return (jnp.cos(angles), jnp.sin(angles))

def rotate(head_rows, cosine_table, sine_table):
    half_dim = HEAD_DIM // 2
    first_half = head_rows[..., :half_dim]
    second_half = head_rows[..., half_dim:]
    cosine_rows = cosine_table[:, None, :]
    sine_rows = sine_table[:, None, :]
    return jnp.concatenate([first_half * cosine_rows - second_half * sine_rows, second_half * cosine_rows + first_half * sine_rows], axis=-1)

def doc_layout(doc_lengths, first_row, row_count):
    token_index = (first_row + jnp.arange(row_count, dtype=jnp.int32)).astype(jnp.int32)
    doc_ends = jnp.cumsum(doc_lengths).astype(jnp.int32)
    doc_starts = (doc_ends - doc_lengths).astype(jnp.int32)
    segment = lax.optimization_barrier(jnp.sum((token_index[:, None] >= doc_ends[None, :]).astype(jnp.int32), axis=1)).astype(jnp.int32)
    inside = (token_index[:, None] >= doc_starts[None, :]) & (token_index[:, None] < doc_ends[None, :])
    positions = (token_index - lax.optimization_barrier(jnp.sum(jnp.where(inside, doc_starts[None, :], 0), axis=1))).astype(jnp.int32)
    return (token_index, segment, positions)

def attend(queries, key_rows, value_rows, token_index, segment):
    score_scale = HEAD_DIM ** (-0.5)
    block_rows = KEY_BLOCK // 4
    block_total = TOKENS // block_rows

    def one_block(block_args):
        block_query, block_index, block_segment = block_args
        scores = jnp.einsum('qhd,khd->hqk', block_query, key_rows, precision=highest)
        scores = low_back(scores * score_scale)
        allowed_mask = (token_index[None, :] <= block_index[:, None]) & (segment[None, :] == block_segment[:, None])
        scores = jnp.where(allowed_mask[None], scores, -1e+30)
        attn_weights = low(jax.nn.softmax(scores, axis=-1))
        return jnp.einsum('hqk,khd->qhd', attn_weights, value_rows, precision=highest)
    outputs = lax.map(jax.checkpoint(one_block), (queries.reshape(block_total, block_rows, HEADS, HEAD_DIM), token_index.reshape(block_total, block_rows), segment.reshape(block_total, block_rows)))
    return outputs.reshape(TOKENS, D)

def matmul(left, right):
    return jnp.dot(left, right, precision=highest, preferred_element_type=jnp.float32)

def reference(tokens, cotangent, doc_lengths, q_weight, k_weight, v_weight, o_weight, gate_weight, up_weight, down_weight, q_gain, k_gain, attn_gain, mlp_gain):
    token_index, segment, positions = doc_layout(doc_lengths, 0, TOKENS)
    cosine_table, sine_table = rope_tables(positions)

    def layer(inputs, w_query, w_key, w_value, w_out, w_gate, w_up, w_down, gain_query, gain_key, gain_attn, gain_mlp):
        queries = low_back(matmul(inputs, w_query))
        key_pre = low_back(matmul(inputs, w_key))
        value_pre = low_back(matmul(inputs, w_value))
        query_rot = low(rotate((rms_norm(queries) * gain_query).reshape(TOKENS, HEADS, HEAD_DIM), cosine_table, sine_table))
        key_rot = low(rotate((rms_norm(key_pre) * gain_key).reshape(TOKENS, HEADS, HEAD_DIM), cosine_table, sine_table))
        value_rows = low(value_pre).reshape(TOKENS, HEADS, HEAD_DIM)
        attended = attend(query_rot, key_rot, value_rows, token_index, segment)
        attended = low(low_back(attended))
        branch = low_back(matmul(attended, w_out))
        hidden_in = inputs + rms_norm(branch) * gain_attn
        mlp_in = low(hidden_in)
        gate_pre = low_back(matmul(mlp_in, w_gate))
        up_pre = low_back(matmul(mlp_in, w_up))
        hidden = low(jax.nn.silu(gate_pre) * up_pre)
        second = low_back(matmul(hidden, w_down))
        return hidden_in + rms_norm(second) * gain_mlp
    primal = (tokens.astype(jnp.float32), q_weight.astype(jnp.float32), k_weight.astype(jnp.float32), v_weight.astype(jnp.float32), o_weight.astype(jnp.float32), gate_weight.astype(jnp.float32), up_weight.astype(jnp.float32), down_weight.astype(jnp.float32), q_gain.astype(jnp.float32), k_gain.astype(jnp.float32), attn_gain.astype(jnp.float32), mlp_gain.astype(jnp.float32))
    output, layer_vjp = jax.vjp(layer, *primal)
    grads = layer_vjp(cotangent.astype(jnp.float32))
    return (output.astype(jnp.bfloat16), grads[0], grads[1], grads[2], grads[3], grads[4], grads[5], grads[6], grads[7], grads[8], grads[9], grads[10], grads[11])
```

```python
import functools

import jax
import jax.numpy as jnp
from jax import lax
from jax.experimental import pallas as pl
from jax.experimental.pallas import tpu as pltpu
from jax.sharding import PartitionSpec as P

D = 2048
HEAD_DIM = 128
KEY_BLOCK = 1024


epsilon = 1e-06
rope_base = 500000.0


def rms_norm(vector):
    return vector * lax.rsqrt(jnp.mean(vector * vector, axis=-1, keepdims=True) + epsilon)


def norm_grad(normed_rows, raw_rows, upstream, gain):
    row_scale = lax.rsqrt(jnp.mean(raw_rows * raw_rows, axis=-1, keepdims=True) + epsilon)
    grad_normed = upstream * gain
    inner_sum = jnp.mean(grad_normed * normed_rows, axis=-1, keepdims=True)
    return (
        row_scale * (grad_normed - normed_rows * inner_sum),
        jnp.sum(upstream * normed_rows, axis=0),
    )


def rope_tables(positions):
    frequency = jnp.power(
        rope_base, -jnp.arange(HEAD_DIM // 2, dtype=jnp.float32) * (2.0 / HEAD_DIM)
    )
    angles = positions.astype(jnp.float32)[:, None] * frequency[None, :]
    return (jnp.cos(angles), jnp.sin(angles))


def rotate(head_rows, cosine_table, sine_table):
    half_dim = HEAD_DIM // 2
    first_half = head_rows[..., :half_dim]
    second_half = head_rows[..., half_dim:]
    cosine_rows = cosine_table[:, None, :]
    sine_rows = sine_table[:, None, :]
    return jnp.concatenate(
        [
            first_half * cosine_rows - second_half * sine_rows,
            second_half * cosine_rows + first_half * sine_rows,
        ],
        axis=-1,
    )


def unrotate(head_rows, cosine_table, sine_table):
    half_dim = HEAD_DIM // 2
    first_half = head_rows[..., :half_dim]
    second_half = head_rows[..., half_dim:]
    cosine_rows = cosine_table[:, None, :]
    sine_rows = sine_table[:, None, :]
    return jnp.concatenate(
        [
            first_half * cosine_rows + second_half * sine_rows,
            second_half * cosine_rows - first_half * sine_rows,
        ],
        axis=-1,
    )


def segments_of(doc_lengths, token_index):
    doc_ends = jnp.cumsum(doc_lengths)
    return jnp.sum((token_index[:, None] >= doc_ends[None, :]).astype(jnp.int32), axis=1)


def doc_layout(doc_lengths, first_row, row_count):
    token_index = first_row + jnp.arange(row_count, dtype=jnp.int32)
    doc_ends = jnp.cumsum(doc_lengths)
    doc_starts = doc_ends - doc_lengths
    segment = segments_of(doc_lengths, token_index)
    inside = (token_index[:, None] >= doc_starts[None, :]) & (
        token_index[:, None] < doc_ends[None, :]
    )
    positions = token_index - jnp.sum(jnp.where(inside, doc_starts[None, :], 0), axis=1)
    return (token_index, segment, positions)


MESH = pl.DeviceIdType.MESH
F32 = jnp.float32
BF16 = jnp.bfloat16
STEPS = 4
AG_CHUNKS = 2
VMEM_BYTES = 60 * 1024 * 1024
ANY = pl.BlockSpec(memory_space=pl.ANY)
VMEM = pl.BlockSpec(memory_space=pltpu.VMEM)
NN = (((1,), (0,)), ((), ()))
NT = (((1,), (1,)), ((), ()))
TN = (((0,), (0,)), ((), ()))


def mm(left, right, dims=NN):
    return lax.dot_general(left, right, dims, preferred_element_type=F32)


def rows_at(index, count):
    return pl.ds(pl.multiple_of(index * count, count), count)


def line_barrier(z, n):
    bar = pltpu.get_barrier_semaphore()
    for other, there in ((z - 1, z > 0), (z + 1, z < n - 1)):

        @pl.when(there)
        def _():
            pl.semaphore_signal(bar, inc=1, device_id={"head": other}, device_id_type=MESH)

    pl.semaphore_wait(bar, (z > 0).astype(jnp.int32) + (z < n - 1).astype(jnp.int32))


def line_gather(z, n, buf, rows, send_sem, recv_sem, use):
    part = rows // AG_CHUNKS

    def copy(src, c, up):
        at = pl.ds(pl.multiple_of(src * rows + c * part, part), part)
        return pltpu.make_async_remote_copy(
            src_ref=buf.at[at],
            dst_ref=buf.at[at],
            send_sem=send_sem.at[up, src, c],
            recv_sem=recv_sem.at[src, c],
            device_id={"head": z + 1 if up else z - 1},
            device_id_type=MESH,
        )

    more = (z > 0, z < n - 1)
    for c in range(AG_CHUNKS):
        for up in (0, 1):

            @pl.when(more[up])
            def _():
                copy(z, c, up).start()

    use(z)

    @pl.loop(1, n)
    def _(k):
        sides = ((z + k, z + k < n, 0), (z - k, z - k >= 0, 1))
        for c in range(AG_CHUNKS):
            for src, there, up in sides:

                @pl.when(there)
                def _():
                    copy(src, c, up).wait_recv()

                    @pl.when(more[up])
                    def _():
                        copy(src, c, up).start()

        for src, there, up in sides:

            @pl.when(there)
            def _():
                use(src)

    @pl.loop(0, n)
    def _(src):
        for c in range(AG_CHUNKS):

            @pl.when((src >= z) & (z > 0))
            def _():
                copy(src, c, 0).wait_send()

            @pl.when((src <= z) & (z < n - 1))
            def _():
                copy(src, c, 1).wait_send()


def line_scatter(z, n, partial, land, send_sem, recv_sem, total):
    width = total.shape[1] // STEPS

    def copy(d, c, up):
        return pltpu.make_async_remote_copy(
            src_ref=land.at[up, d, c],
            dst_ref=land.at[up, d, c],
            send_sem=send_sem.at[up, d, c],
            recv_sem=recv_sem.at[up, d, c],
            device_id={"head": z + 1 if up else z - 1},
            device_id_type=MESH,
        )

    @pl.loop(0, (n - 1) * STEPS)
    def _(t):
        j, c = t // STEPS, t % STEPS
        for d, there, first, up in ((n - 1 - j, n - 1 - j > z, z == 0, 1), (j, j < z, z == n - 1, 0)):

            @pl.when(there)
            def _():
                mine = partial(d, c)

                @pl.when(first)
                def _():
                    land[up, d, c] = mine.astype(land.dtype)

                @pl.when(jnp.logical_not(first))
                def _():
                    copy(d, c, up).wait_recv()
                    land[up, d, c] = (land[up, d, c].astype(F32) + mine).astype(land.dtype)

                copy(d, c, up).start()

    @pl.loop(0, STEPS)
    def _(c):
        at = rows_at(c, width)
        total[:, at] = partial(z, c)
        for there, up in ((z > 0, 1), (z < n - 1, 0)):

            @pl.when(there)
            def _():
                copy(z, c, up).wait_recv()
                total[:, at] += land[up, z, c].astype(F32)

    @pl.loop(0, n * STEPS)
    def _(t):
        d, c = t // STEPS, t % STEPS
        for there, up in ((d > z, 1), (d < z, 0)):

            @pl.when(there)
            def _():
                copy(d, c, up).wait_send()


def line_sems(n):
    dma = pltpu.SemaphoreType.DMA
    return {
        "gather": [dma((2, n, AG_CHUNKS)), dma((n, AG_CHUNKS))],
        "scatter": [dma((2, n, STEPS)), dma((2, n, STEPS))],
    }


BLOCK = 16


def row_scale(block):
    return lax.rsqrt(jnp.mean(block * block, axis=-1, keepdims=True) + epsilon)


def norm_back(e, normed, scale, gain):
    g = e * gain
    return scale * (g - normed * jnp.mean(g * normed, axis=-1, keepdims=True))


def sigmoid(x):
    return 1.0 / (1.0 + jnp.exp(-x))


def forward_kernel(
    n, ns,
    att, tok, cot, wod, wgu, attn_gain, mlp_gain,
    out, h1r, branch_out, hidden, dy2, dg, du, gain_part,
    wo, wd, wg, wu, land, branch, h1, second, g_pre, u_pre,
    wsem, osem, g1s, g1r, s1s, s1r, g2s, g2r, s2s, s2r,
):
    z = lax.axis_index("head")
    rows, depth = tok.shape
    lw, ff = att.shape[1], hidden.shape[1]
    col = depth // ns
    width = depth // STEPS
    line_barrier(z, n)
    loads = []
    for s in range(ns):
        loads.append(pltpu.make_async_copy(wod.at[s, pl.ds(0, lw)], wo.at[:, pl.ds(s * col, col)], wsem.at[0]))
    l_g = pltpu.make_async_copy(wgu.at[:, pl.ds(0, ff)], wg, wsem.at[1])
    l_u = pltpu.make_async_copy(wgu.at[:, pl.ds(ff, ff)], wu, wsem.at[2])
    d_loads = [
        pltpu.make_async_copy(wod.at[s, pl.ds(lw, ff)], wd.at[:, pl.ds(s * col, col)], wsem.at[3]) for s in range(ns)
    ]
    for copy in loads + [l_g, l_u] + d_loads:
        copy.start()
    for copy in loads:
        copy.wait()

    def out_part(d, c):
        return mm(att[rows_at(d, rows), :], wo[:, rows_at(c, width)])

    line_scatter(z, n, out_part, land, s1s, s1r, branch)
    o_branch = pltpu.make_async_copy(branch, branch_out, osem)
    o_branch.start()
    gain_part[...] = jnp.zeros_like(gain_part)

    @pl.loop(0, rows // BLOCK)
    def _(i):
        at = rows_at(i, BLOCK)
        y = branch[at, :]
        h = tok[at, :].astype(F32) + y * row_scale(y) * attn_gain[...]
        h1[at, :] = h
        h1r[pl.ds(pl.multiple_of(z * rows + i * BLOCK, BLOCK), BLOCK), :] = h.astype(BF16)

    l_g.wait()
    l_u.wait()
    fw = ff // STEPS

    def up_block(src):
        at = rows_at(src, rows)

        @pl.loop(0, STEPS)
        def _(c):
            cols = rows_at(c, fw)
            x = h1r[at, :]
            g = mm(x, wg[:, cols])
            u = mm(x, wu[:, cols])
            g_pre[at, cols] = g
            u_pre[at, cols] = u
            hidden[at, cols] = (g * sigmoid(g) * u).astype(BF16)

    line_gather(z, n, h1r, rows, g1s, g1r, up_block)
    for copy in d_loads:
        copy.wait()

    def down_part(d, c):
        return mm(hidden[rows_at(d, rows), :], wd[:, rows_at(c, width)])

    line_scatter(z, n, down_part, land, s2s, s2r, second)

    @pl.loop(0, rows // BLOCK)
    def _(i):
        at = rows_at(i, BLOCK)
        y = second[at, :]
        scale = row_scale(y)
        normed = y * scale
        e = cot[at, :].astype(F32)
        out[at, :] = (h1[at, :] + normed * mlp_gain[...]).astype(BF16)
        gain_part[...] += jnp.sum(e * normed, axis=0, keepdims=True)
        dy2[pl.ds(pl.multiple_of(z * rows + i * BLOCK, BLOCK), BLOCK), :] = norm_back(
            e, normed, scale, mlp_gain[...]
        ).astype(BF16)

    def back_block(src):
        at = rows_at(src, rows)

        @pl.loop(0, STEPS)
        def _(c):
            cols = rows_at(c, fw)
            dh = mm(dy2[at, :], wd[cols, :], NT)
            g = g_pre[at, cols]
            u = u_pre[at, cols]
            sig = sigmoid(g)
            du[at, cols] = (dh * g * sig).astype(BF16)
            dg[at, cols] = (dh * u * sig * (1.0 + g * (1.0 - sig))).astype(BF16)

    line_gather(z, n, dy2, rows, g2s, g2r, back_block)
    o_branch.wait()


def run_forward(n, ns, att, tok, cot, wod, wgu, attn_gain, mlp_gain):
    rows, depth = tok.shape
    tl, lw = att.shape
    ff = wgu.shape[1] // 2
    dma = pltpu.SemaphoreType.DMA
    sems = line_sems(n)
    shape = jax.ShapeDtypeStruct
    return pl.pallas_call(
        functools.partial(forward_kernel, n, ns),
        out_shape=(
            shape((rows, depth), BF16),
            shape((tl, depth), BF16),
            shape((rows, depth), F32),
            shape((tl, ff), BF16),
            shape((tl, depth), BF16),
            shape((tl, ff), BF16),
            shape((tl, ff), BF16),
            shape((1, depth), F32),
        ),
        in_specs=[VMEM, VMEM, VMEM, ANY, ANY, VMEM, VMEM],
        out_specs=(VMEM, VMEM, ANY, VMEM, VMEM, VMEM, VMEM, VMEM),
        scratch_shapes=[
            pltpu.VMEM((lw, depth), BF16),
            pltpu.VMEM((ff, depth), BF16),
            pltpu.VMEM((depth, ff), BF16),
            pltpu.VMEM((depth, ff), BF16),
            pltpu.VMEM((2, n, STEPS, rows, depth // STEPS), BF16),
            pltpu.VMEM((rows, depth), F32),
            pltpu.VMEM((rows, depth), F32),
            pltpu.VMEM((rows, depth), F32),
            pltpu.VMEM((tl, ff), F32),
            pltpu.VMEM((tl, ff), F32),
            dma((4,)),
            dma,
            *sems["gather"], *sems["scatter"], *sems["gather"], *sems["scatter"],
        ],
        compiler_params=pltpu.CompilerParams(
            collective_id=1, has_side_effects=True, vmem_limit_bytes=VMEM_BYTES
        ),
        cost_estimate=pl.CostEstimate(flops=18 * 10**9, bytes_accessed=40 * 10**6, transcendentals=2 * 10**6),
        name="feed_forward",
    )(att, tok, cot, wod, wgu, attn_gain, mlp_gain)


def backward_kernel(
    n, ns,
    dg, du, cot, branch, wod, wgu, attn_gain,
    middle, dy1, datt, gain_part,
    wo, wg, wu, land, total,
    wsem, s1s, s1r, g1s, g1r,
):
    z = lax.axis_index("head")
    rows, depth = cot.shape
    lw, ff = datt.shape[1], dg.shape[1]
    col = depth // ns
    width = depth // STEPS
    line_barrier(z, n)
    l_g = pltpu.make_async_copy(wgu.at[:, pl.ds(0, ff)], wg, wsem.at[0])
    l_u = pltpu.make_async_copy(wgu.at[:, pl.ds(ff, ff)], wu, wsem.at[1])
    loads = [
        pltpu.make_async_copy(wod.at[s, pl.ds(0, lw)], wo.at[:, pl.ds(s * col, col)], wsem.at[2]) for s in range(ns)
    ]
    for copy in [l_g, l_u] + loads:
        copy.start()
    l_g.wait()
    l_u.wait()

    def in_part(d, c):
        at, cols = rows_at(d, rows), rows_at(c, width)
        return mm(dg[at, :], wg[cols, :], NT) + mm(du[at, :], wu[cols, :], NT)

    line_scatter(z, n, in_part, land, s1s, s1r, total)
    gain_part[...] = jnp.zeros_like(gain_part)

    @pl.loop(0, rows // BLOCK)
    def _(i):
        at = rows_at(i, BLOCK)
        y = branch[at, :]
        scale = row_scale(y)
        normed = y * scale
        e = cot[at, :].astype(F32) + total[at, :]
        middle[at, :] = e
        gain_part[...] += jnp.sum(e * normed, axis=0, keepdims=True)
        dy1[pl.ds(pl.multiple_of(z * rows + i * BLOCK, BLOCK), BLOCK), :] = norm_back(
            e, normed, scale, attn_gain[...]
        ).astype(BF16)

    for copy in loads:
        copy.wait()

    def att_block(src):
        at = rows_at(src, rows)
        datt[at, :] = mm(dy1[at, :], wo[...], NT).astype(BF16)

    line_gather(z, n, dy1, rows, g1s, g1r, att_block)


def run_backward(n, ns, dg, du, cot, branch, wod, wgu, attn_gain):
    rows, depth = cot.shape
    tl, ff = dg.shape
    lw = wod.shape[1] - ff
    dma = pltpu.SemaphoreType.DMA
    sems = line_sems(n)
    shape = jax.ShapeDtypeStruct
    return pl.pallas_call(
        functools.partial(backward_kernel, n, ns),
        out_shape=(
            shape((rows, depth), F32),
            shape((tl, depth), BF16),
            shape((tl, lw), BF16),
            shape((1, depth), F32),
        ),
        in_specs=[VMEM, VMEM, VMEM, VMEM, ANY, ANY, VMEM],
        out_specs=(VMEM, VMEM, VMEM, VMEM),
        scratch_shapes=[
            pltpu.VMEM((lw, depth), BF16),
            pltpu.VMEM((depth, ff), BF16),
            pltpu.VMEM((depth, ff), BF16),
            pltpu.VMEM((2, n, STEPS, rows, depth // STEPS), BF16),
            pltpu.VMEM((rows, depth), F32),
            dma((3,)),
            *sems["scatter"], *sems["gather"],
        ],
        compiler_params=pltpu.CompilerParams(
            collective_id=2, has_side_effects=True, vmem_limit_bytes=VMEM_BYTES
        ),
        cost_estimate=pl.CostEstimate(flops=10 * 10**9, bytes_accessed=30 * 10**6, transcendentals=0),
        name="into_attention",
    )(dg, du, cot, branch, wod, wgu, attn_gain)


def place_gain(vector, head_index, total_width):
    return lax.dynamic_update_slice_in_dim(
        jnp.zeros((total_width,), jnp.float32), vector, head_index * vector.shape[0], 0
    )


def on_device(
    tokens,
    cotangent,
    doc_lengths,
    q_weight,
    k_weight,
    v_weight,
    o_weight,
    gate_weight,
    up_weight,
    down_weight,
    q_gain,
    k_gain,
    attn_gain,
    mlp_gain,
):
    local_width = q_weight.shape[1]
    local_heads = local_width // HEAD_DIM
    seq_index = lax.axis_index("seq")
    head_index = lax.axis_index("head")
    f32 = jnp.float32
    bf16 = jnp.bfloat16
    gathered = lax.all_gather(tokens, "head", axis=0, tiled=True)
    tok_local = gathered.shape[0]
    total_tokens = tok_local * lax.axis_size("seq")
    token_index, segment, positions = doc_layout(doc_lengths, seq_index * tok_local, tok_local)
    cosine_table, sine_table = rope_tables(positions)
    gain_query = lax.dynamic_slice_in_dim(q_gain, head_index * local_width, local_width)
    gain_key = lax.dynamic_slice_in_dim(k_gain, head_index * local_width, local_width)
    ns, nz = lax.axis_size("seq"), lax.axis_size("head")
    w_qkv = lax.all_gather(
        jnp.concatenate([q_weight, k_weight, v_weight], axis=1), "seq", axis=0, tiled=True
    )
    w_query, w_key, w_value = (w_qkv[:, i * local_width : (i + 1) * local_width] for i in range(3))
    w_od = lax.all_gather(jnp.concatenate([o_weight, down_weight], axis=0), "seq", axis=0)
    w_gu = lax.all_gather(jnp.concatenate([gate_weight, up_weight], axis=1), "seq", axis=0, tiled=True)
    queries = jnp.dot(gathered, w_query, preferred_element_type=f32)
    key_pre = jnp.dot(gathered, w_key, preferred_element_type=f32)
    value_pre = jnp.dot(gathered, w_value, preferred_element_type=f32)
    q_total, k_total = lax.psum(
        (jnp.sum(queries * queries, axis=1), jnp.sum(key_pre * key_pre, axis=1)), "head"
    )
    q_scale = lax.rsqrt(q_total / D + epsilon)
    k_scale = lax.rsqrt(k_total / D + epsilon)
    q_hat = queries * q_scale[:, None]
    k_hat = key_pre * k_scale[:, None]
    q_rot = rotate(
        (q_hat * gain_query).reshape(tok_local, local_heads, HEAD_DIM), cosine_table, sine_table
    ).astype(bf16)
    k_rot = rotate(
        (k_hat * gain_key).reshape(tok_local, local_heads, HEAD_DIM), cosine_table, sine_table
    ).astype(bf16)
    key_all, value_all = (
        lax.all_gather(k_rot.reshape(tok_local, local_width), "seq", axis=0, tiled=True),
        lax.all_gather(value_pre.astype(bf16), "seq", axis=0, tiled=True),
    )
    score_scale = HEAD_DIM ** (-0.5)
    block_count = ((seq_index + 1) * tok_local + KEY_BLOCK - 1) // KEY_BLOCK

    def block_scores(block_id):
        begin_row = block_id * KEY_BLOCK
        key_slab = lax.dynamic_slice_in_dim(key_all, begin_row, KEY_BLOCK, 0).reshape(
            KEY_BLOCK, local_heads, HEAD_DIM
        )
        value_slab = lax.dynamic_slice_in_dim(value_all, begin_row, KEY_BLOCK, 0).reshape(
            KEY_BLOCK, local_heads, HEAD_DIM
        )
        scores = (
            jnp.einsum("qhd,khd->hqk", q_rot, key_slab, preferred_element_type=f32) * score_scale
        )
        key_index = begin_row + jnp.arange(KEY_BLOCK, dtype=jnp.int32)
        key_segment = segments_of(doc_lengths, key_index)
        allowed_mask = (key_index[None, :] <= token_index[:, None]) & (
            key_segment[None, :] == segment[:, None]
        )
        return (scores, allowed_mask, key_slab, value_slab)

    def stats_step(block_id, carry):
        row_top, row_total = carry
        scores, allowed_mask, key_slab, value_slab = block_scores(block_id)
        masked = jnp.where(allowed_mask[None], scores, -1e30)
        new_top = jnp.maximum(row_top, jnp.max(masked, axis=-1))
        terms = jnp.where(allowed_mask[None], jnp.exp(masked - new_top[:, :, None]), 0.0)
        return (new_top, row_total * jnp.exp(row_top - new_top) + jnp.sum(terms, axis=-1))

    row_top, row_total = lax.fori_loop(
        0,
        block_count,
        stats_step,
        (jnp.full((local_heads, tok_local), -1e30, f32), jnp.zeros((local_heads, tok_local), f32)),
    )
    log_total = row_top + jnp.log(row_total)

    def apply_step(block_id, summed):
        scores, allowed_mask, key_slab, value_slab = block_scores(block_id)
        attn_weights = jnp.where(
            allowed_mask[None], jnp.exp(scores - log_total[:, :, None]), 0.0
        ).astype(bf16)
        return summed + jnp.einsum(
            "hqk,khd->qhd", attn_weights, value_slab, preferred_element_type=f32
        )

    summed = lax.fori_loop(
        0, block_count, apply_step, jnp.zeros((tok_local, local_heads, HEAD_DIM), f32)
    )
    attended = summed.reshape(tok_local, local_width).astype(bf16)
    output, mlp_gathered, branch, hidden, second_grads, d_gate, d_up, mlp_gain_part = run_forward(
        nz, ns, attended, tokens, cotangent, w_od, w_gu, attn_gain[None], mlp_gain[None]
    )
    mlp_gain_part = mlp_gain_part[0]
    grad_down = jnp.einsum("tf,td->fd", hidden, second_grads, preferred_element_type=f32)
    grad_gate = jnp.einsum("td,tf->df", mlp_gathered, d_gate, preferred_element_type=f32)
    grad_up = jnp.einsum("td,tf->df", mlp_gathered, d_up, preferred_element_type=f32)
    d_middle, branch_grads, d_attended, attn_gain_part = run_backward(
        nz, ns, d_gate, d_up, cotangent, branch, w_od, w_gu, attn_gain[None]
    )
    attn_gain_part = attn_gain_part[0]
    grad_out = jnp.einsum("tc,td->cd", attended, branch_grads, preferred_element_type=f32)
    d_heads = d_attended.reshape(tok_local, local_heads, HEAD_DIM)
    delta_rows = jnp.transpose(jnp.sum(d_heads.astype(f32) * summed, axis=-1))

    def grad_step(block_id, carry):
        d_query, d_keys, d_values = carry
        scores, allowed_mask, key_slab, value_slab = block_scores(block_id)
        attn_weights = jnp.where(allowed_mask[None], jnp.exp(scores - log_total[:, :, None]), 0.0)
        weights_low = attn_weights.astype(bf16)
        d_weights = jnp.einsum("qhd,khd->hqk", d_heads, value_slab, preferred_element_type=f32)
        d_scores = (attn_weights * (d_weights - delta_rows[:, :, None])).astype(bf16)
        d_query = (
            d_query
            + jnp.einsum("hqk,khd->qhd", d_scores, key_slab, preferred_element_type=f32)
            * score_scale
        )
        key_part = (
            jnp.einsum("hqk,qhd->khd", d_scores, q_rot, preferred_element_type=f32) * score_scale
        ).reshape(KEY_BLOCK, local_width)
        value_part = jnp.einsum(
            "hqk,qhd->khd", weights_low, d_heads, preferred_element_type=f32
        ).reshape(KEY_BLOCK, local_width)
        begin_row = block_id * KEY_BLOCK
        d_keys = lax.dynamic_update_slice_in_dim(d_keys, key_part, begin_row, 0)
        d_values = lax.dynamic_update_slice_in_dim(d_values, value_part, begin_row, 0)
        return (d_query, d_keys, d_values)

    d_query, d_keys, d_values = lax.fori_loop(
        0,
        block_count,
        grad_step,
        (
            jnp.zeros((tok_local, local_heads, HEAD_DIM), f32),
            jnp.zeros((total_tokens, local_width), f32),
            jnp.zeros((total_tokens, local_width), f32),
        ),
    )
    key_grads, value_grads = (
        lax.psum_scatter(
            d_keys.astype(jnp.bfloat16), "seq", scatter_dimension=0, tiled=True
        ).astype(jnp.float32),
        lax.psum_scatter(
            d_values.astype(jnp.bfloat16), "seq", scatter_dimension=0, tiled=True
        ).astype(jnp.float32),
    )
    d_qnorm = unrotate(d_query, cosine_table, sine_table).reshape(tok_local, local_width)
    d_knorm = unrotate(
        key_grads.reshape(tok_local, local_heads, HEAD_DIM), cosine_table, sine_table
    ).reshape(tok_local, local_width)
    q_gain_part = jnp.sum(d_qnorm * q_hat, axis=0)
    k_gain_part = jnp.sum(d_knorm * k_hat, axis=0)
    d_qhat = d_qnorm * gain_query
    d_khat = d_knorm * gain_key
    q_inner, k_inner, q_gain_full, k_gain_full, attn_gain_full, mlp_gain_full = (
        lax.psum(jnp.sum(d_qhat * q_hat, axis=1).astype(jnp.bfloat16), "head").astype(jnp.float32),
        lax.psum(jnp.sum(d_khat * k_hat, axis=1).astype(jnp.bfloat16), "head").astype(jnp.float32),
        lax.psum(place_gain(q_gain_part, head_index, D).astype(jnp.bfloat16), "head").astype(
            jnp.float32
        ),
        lax.psum(place_gain(k_gain_part, head_index, D).astype(jnp.bfloat16), "head").astype(
            jnp.float32
        ),
        lax.psum(attn_gain_part.astype(jnp.bfloat16), "head").astype(jnp.float32),
        lax.psum(mlp_gain_part.astype(jnp.bfloat16), "head").astype(jnp.float32),
    )
    d_q = (q_scale[:, None] * (d_qhat - q_hat * (q_inner / D)[:, None])).astype(bf16)
    d_k = (k_scale[:, None] * (d_khat - k_hat * (k_inner / D)[:, None])).astype(bf16)
    d_v = value_grads.astype(bf16)
    grad_query = jnp.einsum("td,tc->dc", gathered, d_q, preferred_element_type=f32)
    grad_key = jnp.einsum("td,tc->dc", gathered, d_k, preferred_element_type=f32)
    grad_value = jnp.einsum("td,tc->dc", gathered, d_v, preferred_element_type=f32)
    input_grad = d_middle + lax.psum_scatter(
        (
            jnp.einsum("tc,dc->td", d_q, w_query, preferred_element_type=f32)
            + jnp.einsum("tc,dc->td", d_k, w_key, preferred_element_type=f32)
            + jnp.einsum("tc,dc->td", d_v, w_value, preferred_element_type=f32)
        ).astype(jnp.bfloat16),
        "head",
        scatter_dimension=0,
        tiled=True,
    ).astype(jnp.float32)
    reduced = (
        lax.psum_scatter(
            grad_query.astype(jnp.bfloat16), "seq", scatter_dimension=0, tiled=True
        ).astype(jnp.float32),
        lax.psum_scatter(
            grad_key.astype(jnp.bfloat16), "seq", scatter_dimension=0, tiled=True
        ).astype(jnp.float32),
        lax.psum_scatter(
            grad_value.astype(jnp.bfloat16), "seq", scatter_dimension=0, tiled=True
        ).astype(jnp.float32),
        lax.psum_scatter(
            grad_out.astype(jnp.bfloat16), "seq", scatter_dimension=1, tiled=True
        ).astype(jnp.float32),
        lax.psum_scatter(
            grad_gate.astype(jnp.bfloat16), "seq", scatter_dimension=0, tiled=True
        ).astype(jnp.float32),
        lax.psum_scatter(
            grad_up.astype(jnp.bfloat16), "seq", scatter_dimension=0, tiled=True
        ).astype(jnp.float32),
        lax.psum_scatter(
            grad_down.astype(jnp.bfloat16), "seq", scatter_dimension=1, tiled=True
        ).astype(jnp.float32),
        lax.psum_scatter(
            q_gain_full.astype(jnp.bfloat16), "seq", scatter_dimension=0, tiled=True
        ).astype(jnp.float32),
        lax.psum_scatter(
            k_gain_full.astype(jnp.bfloat16), "seq", scatter_dimension=0, tiled=True
        ).astype(jnp.float32),
        lax.psum_scatter(
            attn_gain_full.astype(jnp.bfloat16), "seq", scatter_dimension=0, tiled=True
        ).astype(jnp.float32),
        lax.psum_scatter(
            mlp_gain_full.astype(jnp.bfloat16), "seq", scatter_dimension=0, tiled=True
        ).astype(jnp.float32),
    )
    return (
        output,
        input_grad,
        reduced[0],
        reduced[1],
        reduced[2],
        reduced[3],
        reduced[4],
        reduced[5],
        reduced[6],
        reduced[7],
        reduced[8],
        reduced[9],
        reduced[10],
    )


def solution(mesh):
    in_specs = (
        P(("seq", "head"), None),
        P(("seq", "head"), None),
        P(),
        P("seq", "head"),
        P("seq", "head"),
        P("seq", "head"),
        P("head", "seq"),
        P("seq", "head"),
        P("seq", "head"),
        P("head", "seq"),
        P(),
        P(),
        P(),
        P(),
    )
    out_specs = (
        P(("seq", "head"), None),
        P(("seq", "head"), None),
        P("seq", "head"),
        P("seq", "head"),
        P("seq", "head"),
        P("head", "seq"),
        P("seq", "head"),
        P("seq", "head"),
        P("head", "seq"),
        P("seq"),
        P("seq"),
        P("seq"),
        P("seq"),
    )
    return jax.shard_map(
        on_device, mesh=mesh, in_specs=in_specs, out_specs=out_specs, check_vma=False
    )
```

```python
import functools

import jax
import jax.numpy as jnp
from jax import lax
from jax.experimental import pallas as pl
from jax.experimental.pallas import tpu as pltpu
from jax.sharding import PartitionSpec as P

D = 2048
HEAD_DIM = 128
KEY_BLOCK = 1024


epsilon = 1e-06
rope_base = 500000.0


def rms_norm(vector):
    return vector * lax.rsqrt(jnp.mean(vector * vector, axis=-1, keepdims=True) + epsilon)


def norm_grad(normed_rows, raw_rows, upstream, gain):
    row_scale = lax.rsqrt(jnp.mean(raw_rows * raw_rows, axis=-1, keepdims=True) + epsilon)
    grad_normed = upstream * gain
    inner_sum = jnp.mean(grad_normed * normed_rows, axis=-1, keepdims=True)
    return (
        row_scale * (grad_normed - normed_rows * inner_sum),
        jnp.sum(upstream * normed_rows, axis=0),
    )


def rope_tables(positions):
    frequency = jnp.power(
        rope_base, -jnp.arange(HEAD_DIM // 2, dtype=jnp.float32) * (2.0 / HEAD_DIM)
    )
    angles = positions.astype(jnp.float32)[:, None] * frequency[None, :]
    return (jnp.cos(angles), jnp.sin(angles))


def rotate(head_rows, cosine_table, sine_table):
    half_dim = HEAD_DIM // 2
    first_half = head_rows[..., :half_dim]
    second_half = head_rows[..., half_dim:]
    cosine_rows = cosine_table[:, None, :]
    sine_rows = sine_table[:, None, :]
    return jnp.concatenate(
        [
            first_half * cosine_rows - second_half * sine_rows,
            second_half * cosine_rows + first_half * sine_rows,
        ],
        axis=-1,
    )


def unrotate(head_rows, cosine_table, sine_table):
    half_dim = HEAD_DIM // 2
    first_half = head_rows[..., :half_dim]
    second_half = head_rows[..., half_dim:]
    cosine_rows = cosine_table[:, None, :]
    sine_rows = sine_table[:, None, :]
    return jnp.concatenate(
        [
            first_half * cosine_rows + second_half * sine_rows,
            second_half * cosine_rows - first_half * sine_rows,
        ],
        axis=-1,
    )


def segments_of(doc_lengths, token_index):
    doc_ends = jnp.cumsum(doc_lengths)
    return jnp.sum((token_index[:, None] >= doc_ends[None, :]).astype(jnp.int32), axis=1)


def doc_layout(doc_lengths, first_row, row_count):
    token_index = first_row + jnp.arange(row_count, dtype=jnp.int32)
    doc_ends = jnp.cumsum(doc_lengths)
    doc_starts = doc_ends - doc_lengths
    segment = segments_of(doc_lengths, token_index)
    inside = (token_index[:, None] >= doc_starts[None, :]) & (
        token_index[:, None] < doc_ends[None, :]
    )
    positions = token_index - jnp.sum(jnp.where(inside, doc_starts[None, :], 0), axis=1)
    return (token_index, segment, positions)


MESH = pl.DeviceIdType.MESH
F32 = jnp.float32
BF16 = jnp.bfloat16
STEPS = 4
AG_CHUNKS = 2
VMEM_BYTES = 60 * 1024 * 1024
ANY = pl.BlockSpec(memory_space=pl.ANY)
VMEM = pl.BlockSpec(memory_space=pltpu.VMEM)
NN = (((1,), (0,)), ((), ()))
NT = (((1,), (1,)), ((), ()))
TN = (((0,), (0,)), ((), ()))


def mm(left, right, dims=NN):
    return lax.dot_general(left, right, dims, preferred_element_type=F32)


def rows_at(index, count):
    return pl.ds(pl.multiple_of(index * count, count), count)


def line_barrier(z, n):
    bar = pltpu.get_barrier_semaphore()
    for other, there in ((z - 1, z > 0), (z + 1, z < n - 1)):

        @pl.when(there)
        def _():
            pl.semaphore_signal(bar, inc=1, device_id={"head": other}, device_id_type=MESH)

    pl.semaphore_wait(bar, (z > 0).astype(jnp.int32) + (z < n - 1).astype(jnp.int32))


def line_gather(z, n, buf, rows, send_sem, recv_sem, use):
    part = rows // AG_CHUNKS

    def copy(src, c, up):
        at = pl.ds(pl.multiple_of(src * rows + c * part, part), part)
        return pltpu.make_async_remote_copy(
            src_ref=buf.at[at],
            dst_ref=buf.at[at],
            send_sem=send_sem.at[up, src, c],
            recv_sem=recv_sem.at[src, c],
            device_id={"head": z + 1 if up else z - 1},
            device_id_type=MESH,
        )

    more = (z > 0, z < n - 1)
    for c in range(AG_CHUNKS):
        for up in (0, 1):

            @pl.when(more[up])
            def _():
                copy(z, c, up).start()

    use(z)

    @pl.loop(1, n)
    def _(k):
        sides = ((z + k, z + k < n, 0), (z - k, z - k >= 0, 1))
        for c in range(AG_CHUNKS):
            for src, there, up in sides:

                @pl.when(there)
                def _():
                    copy(src, c, up).wait_recv()

                    @pl.when(more[up])
                    def _():
                        copy(src, c, up).start()

        for src, there, up in sides:

            @pl.when(there)
            def _():
                use(src)

    @pl.loop(0, n)
    def _(src):
        for c in range(AG_CHUNKS):

            @pl.when((src >= z) & (z > 0))
            def _():
                copy(src, c, 0).wait_send()

            @pl.when((src <= z) & (z < n - 1))
            def _():
                copy(src, c, 1).wait_send()


def line_scatter(z, n, partial, land, send_sem, recv_sem, total):
    width = total.shape[1] // STEPS

    def copy(d, c, up):
        return pltpu.make_async_remote_copy(
            src_ref=land.at[up, d, c],
            dst_ref=land.at[up, d, c],
            send_sem=send_sem.at[up, d, c],
            recv_sem=recv_sem.at[up, d, c],
            device_id={"head": z + 1 if up else z - 1},
            device_id_type=MESH,
        )

    @pl.loop(0, (n - 1) * STEPS)
    def _(t):
        j, c = t // STEPS, t % STEPS
        for d, there, first, up in ((n - 1 - j, n - 1 - j > z, z == 0, 1), (j, j < z, z == n - 1, 0)):

            @pl.when(there)
            def _():
                mine = partial(d, c)

                @pl.when(first)
                def _():
                    land[up, d, c] = mine.astype(land.dtype)

                @pl.when(jnp.logical_not(first))
                def _():
                    copy(d, c, up).wait_recv()
                    land[up, d, c] = (land[up, d, c].astype(F32) + mine).astype(land.dtype)

                copy(d, c, up).start()

    @pl.loop(0, STEPS)
    def _(c):
        at = rows_at(c, width)
        total[:, at] = partial(z, c)
        for there, up in ((z > 0, 1), (z < n - 1, 0)):

            @pl.when(there)
            def _():
                copy(z, c, up).wait_recv()
                total[:, at] += land[up, z, c].astype(F32)

    @pl.loop(0, n * STEPS)
    def _(t):
        d, c = t // STEPS, t % STEPS
        for there, up in ((d > z, 1), (d < z, 0)):

            @pl.when(there)
            def _():
                copy(d, c, up).wait_send()


def line_sems(n):
    dma = pltpu.SemaphoreType.DMA
    return {
        "gather": [dma((2, n, AG_CHUNKS)), dma((n, AG_CHUNKS))],
        "scatter": [dma((2, n, STEPS)), dma((2, n, STEPS))],
    }


BLOCK = 16


def row_scale(block):
    return lax.rsqrt(jnp.mean(block * block, axis=-1, keepdims=True) + epsilon)


def norm_back(e, normed, scale, gain):
    g = e * gain
    return scale * (g - normed * jnp.mean(g * normed, axis=-1, keepdims=True))


def sigmoid(x):
    return 1.0 / (1.0 + jnp.exp(-x))


def forward_kernel(
    n, ns,
    att, tok, cot, wod, wgu, attn_gain, mlp_gain,
    out, h1r, branch_out, hidden, dy2, dg, du, gain_part,
    wo, wd, wg, wu, land, branch, h1, second, g_pre, u_pre,
    wsem, osem, g1s, g1r, s1s, s1r, g2s, g2r, s2s, s2r,
):
    z = lax.axis_index("head")
    rows, depth = tok.shape
    lw, ff = att.shape[1], hidden.shape[1]
    col = depth // ns
    width = depth // STEPS
    line_barrier(z, n)
    loads = []
    for s in range(ns):
        loads.append(pltpu.make_async_copy(wod.at[s, pl.ds(0, lw)], wo.at[:, pl.ds(s * col, col)], wsem.at[0]))
    l_g = pltpu.make_async_copy(wgu.at[:, pl.ds(0, ff)], wg, wsem.at[1])
    l_u = pltpu.make_async_copy(wgu.at[:, pl.ds(ff, ff)], wu, wsem.at[2])
    d_loads = [
        pltpu.make_async_copy(wod.at[s, pl.ds(lw, ff)], wd.at[:, pl.ds(s * col, col)], wsem.at[3]) for s in range(ns)
    ]
    for copy in loads + [l_g, l_u] + d_loads:
        copy.start()
    for copy in loads:
        copy.wait()

    def out_part(d, c):
        return mm(att[rows_at(d, rows), :], wo[:, rows_at(c, width)])

    line_scatter(z, n, out_part, land, s1s, s1r, branch)
    o_branch = pltpu.make_async_copy(branch, branch_out, osem)
    o_branch.start()
    gain_part[...] = jnp.zeros_like(gain_part)

    @pl.loop(0, rows // BLOCK)
    def _(i):
        at = rows_at(i, BLOCK)
        y = branch[at, :]
        h = tok[at, :].astype(F32) + y * row_scale(y) * attn_gain[...]
        h1[at, :] = h
        h1r[pl.ds(pl.multiple_of(z * rows + i * BLOCK, BLOCK), BLOCK), :] = h.astype(BF16)

    l_g.wait()
    l_u.wait()
    fw = ff // STEPS

    def up_block(src):
        at = rows_at(src, rows)

        @pl.loop(0, STEPS)
        def _(c):
            cols = rows_at(c, fw)
            x = h1r[at, :]
            g = mm(x, wg[:, cols])
            u = mm(x, wu[:, cols])
            g_pre[at, cols] = g
            u_pre[at, cols] = u
            hidden[at, cols] = (g * sigmoid(g) * u).astype(BF16)

    line_gather(z, n, h1r, rows, g1s, g1r, up_block)
    for copy in d_loads:
        copy.wait()

    def down_part(d, c):
        return mm(hidden[rows_at(d, rows), :], wd[:, rows_at(c, width)])

    line_scatter(z, n, down_part, land, s2s, s2r, second)

    @pl.loop(0, rows // BLOCK)
    def _(i):
        at = rows_at(i, BLOCK)
        y = second[at, :]
        scale = row_scale(y)
        normed = y * scale
        e = cot[at, :].astype(F32)
        out[at, :] = (h1[at, :] + normed * mlp_gain[...]).astype(BF16)
        gain_part[...] += jnp.sum(e * normed, axis=0, keepdims=True)
        dy2[pl.ds(pl.multiple_of(z * rows + i * BLOCK, BLOCK), BLOCK), :] = norm_back(
            e, normed, scale, mlp_gain[...]
        ).astype(BF16)

    def back_block(src):
        at = rows_at(src, rows)

        @pl.loop(0, STEPS)
        def _(c):
            cols = rows_at(c, fw)
            dh = mm(dy2[at, :], wd[cols, :], NT)
            g = g_pre[at, cols]
            u = u_pre[at, cols]
            sig = sigmoid(g)
            du[at, cols] = (dh * g * sig).astype(BF16)
            dg[at, cols] = (dh * u * sig * (1.0 + g * (1.0 - sig))).astype(BF16)

    line_gather(z, n, dy2, rows, g2s, g2r, back_block)
    o_branch.wait()


def run_forward(n, ns, att, tok, cot, wod, wgu, attn_gain, mlp_gain):
    rows, depth = tok.shape
    tl, lw = att.shape
    ff = wgu.shape[1] // 2
    dma = pltpu.SemaphoreType.DMA
    sems = line_sems(n)
    shape = jax.ShapeDtypeStruct
    return pl.pallas_call(
        functools.partial(forward_kernel, n, ns),
        out_shape=(
            shape((rows, depth), BF16),
            shape((tl, depth), BF16),
            shape((rows, depth), F32),
            shape((tl, ff), BF16),
            shape((tl, depth), BF16),
            shape((tl, ff), BF16),
            shape((tl, ff), BF16),
            shape((1, depth), F32),
        ),
        in_specs=[VMEM, VMEM, VMEM, ANY, ANY, VMEM, VMEM],
        out_specs=(VMEM, VMEM, ANY, VMEM, VMEM, VMEM, VMEM, VMEM),
        scratch_shapes=[
            pltpu.VMEM((lw, depth), BF16),
            pltpu.VMEM((ff, depth), BF16),
            pltpu.VMEM((depth, ff), BF16),
            pltpu.VMEM((depth, ff), BF16),
            pltpu.VMEM((2, n, STEPS, rows, depth // STEPS), BF16),
            pltpu.VMEM((rows, depth), F32),
            pltpu.VMEM((rows, depth), F32),
            pltpu.VMEM((rows, depth), F32),
            pltpu.VMEM((tl, ff), F32),
            pltpu.VMEM((tl, ff), F32),
            dma((4,)),
            dma,
            *sems["gather"], *sems["scatter"], *sems["gather"], *sems["scatter"],
        ],
        compiler_params=pltpu.CompilerParams(
            collective_id=1, has_side_effects=True, vmem_limit_bytes=VMEM_BYTES
        ),
        cost_estimate=pl.CostEstimate(flops=18 * 10**9, bytes_accessed=40 * 10**6, transcendentals=2 * 10**6),
        name="feed_forward",
    )(att, tok, cot, wod, wgu, attn_gain, mlp_gain)


def backward_kernel(
    n, ns,
    dg, du, cot, branch, wod, wgu, attn_gain,
    middle, dy1, datt, gain_part,
    wo, wg, wu, land, total,
    wsem, s1s, s1r, g1s, g1r,
):
    z = lax.axis_index("head")
    rows, depth = cot.shape
    lw, ff = datt.shape[1], dg.shape[1]
    col = depth // ns
    width = depth // STEPS
    line_barrier(z, n)
    l_g = pltpu.make_async_copy(wgu.at[:, pl.ds(0, ff)], wg, wsem.at[0])
    l_u = pltpu.make_async_copy(wgu.at[:, pl.ds(ff, ff)], wu, wsem.at[1])
    loads = [
        pltpu.make_async_copy(wod.at[s, pl.ds(0, lw)], wo.at[:, pl.ds(s * col, col)], wsem.at[2]) for s in range(ns)
    ]
    for copy in [l_g, l_u] + loads:
        copy.start()
    l_g.wait()
    l_u.wait()

    def in_part(d, c):
        at, cols = rows_at(d, rows), rows_at(c, width)
        return mm(dg[at, :], wg[cols, :], NT) + mm(du[at, :], wu[cols, :], NT)

    line_scatter(z, n, in_part, land, s1s, s1r, total)
    gain_part[...] = jnp.zeros_like(gain_part)

    @pl.loop(0, rows // BLOCK)
    def _(i):
        at = rows_at(i, BLOCK)
        y = branch[at, :]
        scale = row_scale(y)
        normed = y * scale
        e = cot[at, :].astype(F32) + total[at, :]
        middle[at, :] = e
        gain_part[...] += jnp.sum(e * normed, axis=0, keepdims=True)
        dy1[pl.ds(pl.multiple_of(z * rows + i * BLOCK, BLOCK), BLOCK), :] = norm_back(
            e, normed, scale, attn_gain[...]
        ).astype(BF16)

    for copy in loads:
        copy.wait()

    def att_block(src):
        at = rows_at(src, rows)
        datt[at, :] = mm(dy1[at, :], wo[...], NT).astype(BF16)

    line_gather(z, n, dy1, rows, g1s, g1r, att_block)


def run_backward(n, ns, dg, du, cot, branch, wod, wgu, attn_gain):
    rows, depth = cot.shape
    tl, ff = dg.shape
    lw = wod.shape[1] - ff
    dma = pltpu.SemaphoreType.DMA
    sems = line_sems(n)
    shape = jax.ShapeDtypeStruct
    return pl.pallas_call(
        functools.partial(backward_kernel, n, ns),
        out_shape=(
            shape((rows, depth), F32),
            shape((tl, depth), BF16),
            shape((tl, lw), BF16),
            shape((1, depth), F32),
        ),
        in_specs=[VMEM, VMEM, VMEM, VMEM, ANY, ANY, VMEM],
        out_specs=(VMEM, VMEM, VMEM, VMEM),
        scratch_shapes=[
            pltpu.VMEM((lw, depth), BF16),
            pltpu.VMEM((depth, ff), BF16),
            pltpu.VMEM((depth, ff), BF16),
            pltpu.VMEM((2, n, STEPS, rows, depth // STEPS), BF16),
            pltpu.VMEM((rows, depth), F32),
            dma((3,)),
            *sems["scatter"], *sems["gather"],
        ],
        compiler_params=pltpu.CompilerParams(
            collective_id=2, has_side_effects=True, vmem_limit_bytes=VMEM_BYTES
        ),
        cost_estimate=pl.CostEstimate(flops=10 * 10**9, bytes_accessed=30 * 10**6, transcendentals=0),
        name="into_attention",
    )(dg, du, cot, branch, wod, wgu, attn_gain)


LOG2E = 1.4426950408889634
NEG = -1e30


def seq_barrier(s, ns):
    bar = pltpu.get_barrier_semaphore()
    for other in range(ns):

        @pl.when(other != s)
        def _():
            pl.semaphore_signal(bar, inc=1, device_id={"seq": other}, device_id_type=MESH)

    pl.semaphore_wait(bar, ns - 1)


def share_of(s, ns, r):
    per = ns // (2 * r)
    chunk = s // per
    low = chunk < r
    sub = jnp.where(low, chunk, 2 * r - 1 - chunk)
    return sub, jnp.where(low, s - chunk * per, per + s - chunk * per)


def source_of(sub, i, ns, r):
    per = ns // (2 * r)
    return jnp.where(i < per, sub * per + i, (2 * r - 1 - sub) * per + i - per)


def head_cols(h):
    return pl.ds(pl.multiple_of(h * HEAD_DIM, HEAD_DIM), HEAD_DIM)


def attend_kernel(
    ns, heads, q_in, k_in, v_in, starts,
    att, q_buf, k_buf, v_buf, o_buf, lse,
    o_low, qs, qr, ks, kr, vs, vr, osend, orecv, local,
):
    s = lax.axis_index("seq")
    r = ns // heads
    blocks = ns // r
    tl = q_in.shape[0]
    mine, sub = s // r, s % r
    parity = s % 2
    seq_barrier(s, ns)
    to_sub, to_row = share_of(s, ns, r)

    def q_copy(h):
        return pltpu.make_async_remote_copy(
            src_ref=q_in.at[:, head_cols(h)],
            dst_ref=q_buf.at[rows_at(to_row, tl)],
            send_sem=qs.at[h],
            recv_sem=qr.at[to_row],
            device_id={"seq": h * r + to_sub},
            device_id_type=MESH,
        )

    def q_recv(i):
        return pltpu.make_async_remote_copy(
            src_ref=q_buf.at[rows_at(i, tl)],
            dst_ref=q_buf.at[rows_at(i, tl)],
            send_sem=qs.at[0],
            recv_sem=qr.at[i],
            device_id={"seq": s ^ 1},
            device_id_type=MESH,
        )

    def kv_copy(src, buf, send, recv, t, at):
        return pltpu.make_async_remote_copy(
            src_ref=src,
            dst_ref=buf.at[rows_at(at, tl)],
            send_sem=send,
            recv_sem=recv.at[at],
            device_id={"seq": t},
            device_id_type=MESH,
        )

    kv = ((k_in, k_buf, ks, kr), (v_in, v_buf, vs, vr))
    own = [pltpu.make_async_copy(x.at[:, head_cols(mine)], buf.at[rows_at(s, tl)], local.at[i])
           for i, (x, buf, _, _) in enumerate(kv)]
    own_q = pltpu.make_async_copy(q_in.at[:, head_cols(mine)], q_buf.at[rows_at(to_row, tl)], local.at[2])
    for copy in own:
        copy.start()

    @pl.when(to_sub == sub)
    def _():
        own_q.start()

    def far(t):
        return (t != s) & (t % 2 == parity)

    @pl.loop(1, ns)
    def _(step):
        t = s ^ step

        @pl.when(far(t))
        def _():
            for x, buf, ss, rs in kv:
                kv_copy(x.at[:, head_cols(t // r)], buf, ss.at[0, t], rs, t, s).start()

    @pl.loop(0, heads)
    def _(h):
        @pl.when(h * r + to_sub != s)
        def _():
            q_copy(h).start()

    for copy in own:
        copy.wait()

    def pass_on(src, start):
        for _, buf, ss, rs in kv:
            copy = kv_copy(buf.at[rows_at(src, tl)], buf, ss.at[1, src], rs, s ^ 1, src)
            if start:
                copy.start()
            else:
                copy.wait_send()

    pass_on(s, True)

    @pl.loop(1, ns)
    def _(step):
        src = s ^ step

        @pl.when(far(src))
        def _():
            for x, buf, ss, rs in kv:
                kv_copy(buf.at[rows_at(src, tl)], buf, ss.at[0, 0], rs, s ^ 1, src).wait_recv()
            pass_on(src, True)

    @pl.loop(0, ns)
    def _(src):
        @pl.when(src % 2 != parity)
        def _():
            for x, buf, ss, rs in kv:
                kv_copy(buf.at[rows_at(src, tl)], buf, ss.at[0, 0], rs, s ^ 1, src).wait_recv()

    @pl.when(to_sub == sub)
    def _():
        own_q.wait()

    unit = HEAD_DIM ** (-0.5) * LOG2E

    def o_copy(i, t):
        return pltpu.make_async_remote_copy(
            src_ref=o_low.at[rows_at(i, tl)],
            dst_ref=att.at[:, head_cols(mine)],
            send_sem=osend.at[i],
            recv_sem=orecv.at[mine],
            device_id={"seq": t},
            device_id_type=MESH,
        )

    own_o = pltpu.make_async_copy(o_low.at[rows_at(to_row, tl)], att.at[:, head_cols(mine)], local.at[3])

    @pl.loop(0, blocks)
    def _(i):
        src = source_of(sub, i, ns, r)

        @pl.when(src != s)
        def _():
            q_recv(i).wait_recv()

        q = q_buf[rows_at(i, tl), :]
        start = starts[pl.ds(i, 1), :]
        key_at = lax.broadcasted_iota(jnp.int32, (tl, tl), 0)

        def step(j, carry, diagonal):
            top, total, acc = carry
            at = rows_at(j, tl)
            scores = mm(k_buf[at, :], q, NT) * unit
            allowed = key_at >= start - j * tl
            if diagonal:
                allowed = allowed & (key_at <= lax.broadcasted_iota(jnp.int32, (tl, tl), 1))
            scores = jnp.where(allowed, scores, NEG)
            new = jnp.maximum(top, jnp.max(scores, axis=0, keepdims=True))
            terms = jnp.exp2(scores - new)
            fade = jnp.exp2(top - new)
            return (
                new,
                total * fade + jnp.sum(terms, axis=0, keepdims=True),
                acc * fade + mm(v_buf[at, :], terms.astype(BF16), TN),
            )

        carry = (
            jnp.full((1, tl), NEG, F32),
            jnp.zeros((1, tl), F32),
            jnp.zeros((HEAD_DIM, tl), F32),
        )
        carry = lax.fori_loop(0, src, lambda j, c: step(j, c, False), carry)
        top, total, acc = step(src, carry, True)
        lse[pl.ds(i, 1), :] = top + jnp.log(total) * LOG2E
        o = jnp.transpose(acc / total)
        o_buf[rows_at(i, tl), :] = o
        o_low[rows_at(i, tl), :] = o.astype(BF16)

        @pl.when(src != s)
        def _():
            o_copy(i, src).start()

        @pl.when(src == s)
        def _():
            own_o.start()

    @pl.when(to_sub == sub)
    def _():
        own_o.wait()

    @pl.loop(0, heads)
    def _(h):
        @pl.when(h * r + to_sub != s)
        def _():
            q_copy(h).wait_send()
            pltpu.make_async_remote_copy(
                src_ref=o_low.at[rows_at(0, tl)],
                dst_ref=att.at[:, head_cols(h)],
                send_sem=osend.at[0],
                recv_sem=orecv.at[h],
                device_id={"seq": s ^ 1},
                device_id_type=MESH,
            ).wait_recv()

    @pl.loop(0, blocks)
    def _(i):
        src = source_of(sub, i, ns, r)

        @pl.when(src != s)
        def _():
            o_copy(i, src).wait_send()

    pass_on(s, False)

    @pl.loop(1, ns)
    def _(step):
        t = s ^ step

        @pl.when(far(t))
        def _():
            for x, buf, ss, rs in kv:
                kv_copy(x.at[:, head_cols(t // r)], buf, ss.at[0, t], rs, t, s).wait_send()
            pass_on(t, False)


def run_attend(ns, heads, q, k, v, starts):
    tl, lw = q.shape
    r = ns // heads
    nq = ns // r * tl
    nk = ns * tl
    dma = pltpu.SemaphoreType.DMA
    shape = jax.ShapeDtypeStruct
    return pl.pallas_call(
        functools.partial(attend_kernel, ns, heads),
        out_shape=(
            shape((tl, lw), BF16),
            shape((nq, HEAD_DIM), BF16),
            shape((nk, HEAD_DIM), BF16),
            shape((nk, HEAD_DIM), BF16),
            shape((nq, HEAD_DIM), F32),
            shape((ns // r, tl), F32),
        ),
        in_specs=[VMEM] * 4,
        out_specs=(VMEM,) * 6,
        scratch_shapes=[
            pltpu.VMEM((nq, HEAD_DIM), BF16),
            dma((heads,)), dma((ns // r,)),
            dma((2, ns)), dma((ns,)),
            dma((2, ns)), dma((ns,)),
            dma((ns // r,)), dma((heads,)),
            dma((4,)),
        ],
        compiler_params=pltpu.CompilerParams(
            collective_id=3, has_side_effects=True, vmem_limit_bytes=VMEM_BYTES
        ),
        cost_estimate=pl.CostEstimate(flops=3 * 10**9, bytes_accessed=8 * 10**6, transcendentals=5 * 10**6),
        name="attend",
    )(q, k, v, starts)


def attend_back_kernel(
    ns, heads, do_in, starts, q_buf, k_buf, v_buf, o_buf, lse,
    dq, dk, dv,
    do_buf, dq_low, dk_acc, dv_acc, low, pair, land,
    ds_, dr_, ps, pr, gs, gr, qs, qr, local,
):
    s = lax.axis_index("seq")
    r = ns // heads
    blocks = ns // r
    tl = do_in.shape[0]
    mine, sub = s // r, s % r
    parity = s % 2
    seq_barrier(s, ns)
    to_sub, to_row = share_of(s, ns, r)

    def copy(src, dst, send, recv, t):
        return pltpu.make_async_remote_copy(
            src_ref=src, dst_ref=dst, send_sem=send, recv_sem=recv, device_id={"seq": t}, device_id_type=MESH
        )

    def do_copy(h):
        return copy(
            do_in.at[:, head_cols(h)], do_buf.at[rows_at(to_row, tl)], ds_.at[h], dr_.at[to_row], h * r + to_sub
        )

    own_do = pltpu.make_async_copy(do_in.at[:, head_cols(mine)], do_buf.at[rows_at(to_row, tl)], local.at[0])

    @pl.when(to_sub == sub)
    def _():
        own_do.start()

    @pl.loop(0, heads)
    def _(h):
        @pl.when(h * r + to_sub != s)
        def _():
            do_copy(h).start()

    dk_acc[...] = jnp.zeros_like(dk_acc)
    dv_acc[...] = jnp.zeros_like(dv_acc)

    @pl.when(to_sub == sub)
    def _():
        own_do.wait()

    scale = HEAD_DIM ** (-0.5)
    unit = scale * LOG2E

    def dq_copy(i, t):
        return copy(dq_low.at[rows_at(i, tl)], dq.at[:, head_cols(mine)], qs.at[i], qr.at[mine], t)

    own_dq = pltpu.make_async_copy(dq_low.at[rows_at(to_row, tl)], dq.at[:, head_cols(mine)], local.at[1])
    ones = jnp.ones((8, HEAD_DIM), F32)

    @pl.loop(0, blocks)
    def _(i):
        src = source_of(sub, i, ns, r)
        rows = rows_at(i, tl)

        @pl.when(src != s)
        def _():
            copy(do_buf.at[rows], do_buf.at[rows], ds_.at[0], dr_.at[i], s ^ 1).wait_recv()

        q = q_buf[rows, :]
        do = do_buf[rows, :]
        start = starts[pl.ds(i, 1), :]
        norm = lse[pl.ds(i, 1), :]
        delta = lax.dot_general(
            ones, do.astype(F32) * o_buf[rows, :], NT,
            precision=lax.Precision.HIGHEST, preferred_element_type=F32,
        )[:1]
        key_at = lax.broadcasted_iota(jnp.int32, (tl, tl), 0)

        def step(j, dq_sum, diagonal):
            at = rows_at(j, tl)
            keys = k_buf[at, :]
            scores = mm(keys, q, NT) * unit
            allowed = key_at >= start - j * tl
            if diagonal:
                allowed = allowed & (key_at <= lax.broadcasted_iota(jnp.int32, (tl, tl), 1))
            p = jnp.where(allowed, jnp.exp2(scores - norm), 0.0)
            dp = mm(v_buf[at, :], do, NT)
            dscore = (p * (dp - delta)).astype(BF16)
            dv_acc[at, :] += mm(p.astype(BF16), do)
            dk_acc[at, :] += mm(dscore, q)
            return dq_sum + mm(dscore, keys, TN)

        dq_sum = lax.fori_loop(0, src, lambda j, c: step(j, c, False), jnp.zeros((tl, HEAD_DIM), F32))
        dq_sum = step(src, dq_sum, True)
        dq_low[rows, :] = (dq_sum * scale).astype(BF16)

        @pl.when(src != s)
        def _():
            dq_copy(i, src).start()

        @pl.when(src == s)
        def _():
            own_dq.start()

    half = ns // 2

    def pair_copy(w, i):
        src = 2 * i + 1 - parity
        return copy(low.at[w, rows_at(src, tl)], pair.at[w, rows_at(i, tl)], ps.at[w, i], pr.at[w, i], s ^ 1)

    @pl.loop(0, half)
    def _(i):
        at = rows_at(2 * i + 1 - parity, tl)
        low[0, at, :] = (dk_acc[at, :] * scale).astype(BF16)
        pair_copy(0, i).start()
        low[1, at, :] = dv_acc[at, :].astype(BF16)
        pair_copy(1, i).start()

    slot = sub // 2
    outs = (dk, dv)

    def back_copy(w, i):
        dest = 2 * i + parity
        return copy(
            low.at[w, rows_at(dest, tl)], land.at[w, slot, :, head_cols(mine)], gs.at[w, i], gr.at[w, mine, slot], dest
        )

    @pl.loop(0, half)
    def _(i):
        dest = 2 * i + parity
        at = rows_at(dest, tl)
        for w, acc, factor in ((0, dk_acc, scale), (1, dv_acc, 1.0)):
            copy(low.at[w, at], pair.at[w, rows_at(i, tl)], ps.at[w, i], pr.at[w, i], s ^ 1).wait_recv()
            low[w, at, :] = (acc[at, :] * factor + pair[w, rows_at(i, tl), :].astype(F32)).astype(BF16)

            @pl.when(dest != s)
            def _():
                back_copy(w, i).start()

            @pl.when(dest == s)
            def _():
                land[w, slot, :, head_cols(mine)] = low[w, at, :]

    @pl.loop(0, heads)
    def _(h):
        for w in range(2):
            for k in range(r // 2):

                @pl.when(h * r + 2 * k + parity != s)
                def _():
                    copy(
                        low.at[w, rows_at(0, tl)], land.at[w, k, :, head_cols(h)], gs.at[w, 0], gr.at[w, h, k], s ^ 1
                    ).wait_recv()

    for w in range(2):
        outs[w][...] = functools.reduce(
            lambda a, b: a + b, [land[w, k].astype(F32) for k in range(r // 2)]
        ).astype(BF16)

    @pl.when(to_sub == sub)
    def _():
        own_dq.wait()

    @pl.loop(0, heads)
    def _(h):
        @pl.when(h * r + to_sub != s)
        def _():
            do_copy(h).wait_send()
            copy(dq_low.at[rows_at(0, tl)], dq.at[:, head_cols(h)], qs.at[0], qr.at[h], s ^ 1).wait_recv()

    @pl.loop(0, blocks)
    def _(i):
        src = source_of(sub, i, ns, r)

        @pl.when(src != s)
        def _():
            dq_copy(i, src).wait_send()

    @pl.loop(0, half)
    def _(i):
        for w in range(2):
            pair_copy(w, i).wait_send()

            @pl.when(2 * i + parity != s)
            def _():
                back_copy(w, i).wait_send()


def run_attend_back(ns, heads, do, starts, q, k, v, o, lse):
    tl, lw = do.shape
    r = ns // heads
    nq = ns // r * tl
    nk = ns * tl
    dma = pltpu.SemaphoreType.DMA
    shape = jax.ShapeDtypeStruct
    return pl.pallas_call(
        functools.partial(attend_back_kernel, ns, heads),
        out_shape=(shape((tl, lw), BF16),) * 3,
        in_specs=[VMEM] * 7,
        out_specs=(VMEM,) * 3,
        scratch_shapes=[
            pltpu.VMEM((nq, HEAD_DIM), BF16),
            pltpu.VMEM((nq, HEAD_DIM), BF16),
            pltpu.VMEM((nk, HEAD_DIM), F32),
            pltpu.VMEM((nk, HEAD_DIM), F32),
            pltpu.VMEM((2, nk, HEAD_DIM), BF16),
            pltpu.VMEM((2, nk // 2, HEAD_DIM), BF16),
            pltpu.VMEM((2, r // 2, tl, lw), BF16),
            dma((heads,)), dma((ns // r,)),
            dma((2, ns // 2)), dma((2, ns // 2)),
            dma((2, ns // 2)), dma((2, heads, r // 2)),
            dma((ns // r,)), dma((heads,)),
            dma((2,)),
        ],
        compiler_params=pltpu.CompilerParams(
            collective_id=4, has_side_effects=True, vmem_limit_bytes=VMEM_BYTES
        ),
        cost_estimate=pl.CostEstimate(flops=8 * 10**9, bytes_accessed=10 * 10**6, transcendentals=5 * 10**6),
        name="attend_back",
    )(do, starts, q, k, v, o, lse)


def place_gain(vector, head_index, total_width):
    return lax.dynamic_update_slice_in_dim(
        jnp.zeros((total_width,), jnp.float32), vector, head_index * vector.shape[0], 0
    )


def on_device(
    tokens,
    cotangent,
    doc_lengths,
    q_weight,
    k_weight,
    v_weight,
    o_weight,
    gate_weight,
    up_weight,
    down_weight,
    q_gain,
    k_gain,
    attn_gain,
    mlp_gain,
):
    local_width = q_weight.shape[1]
    local_heads = local_width // HEAD_DIM
    seq_index = lax.axis_index("seq")
    head_index = lax.axis_index("head")
    f32 = jnp.float32
    bf16 = jnp.bfloat16
    gathered = lax.all_gather(tokens, "head", axis=0, tiled=True)
    tok_local = gathered.shape[0]
    total_tokens = tok_local * lax.axis_size("seq")
    token_index, segment, positions = doc_layout(doc_lengths, seq_index * tok_local, tok_local)
    cosine_table, sine_table = rope_tables(positions)
    gain_query = lax.dynamic_slice_in_dim(q_gain, head_index * local_width, local_width)
    gain_key = lax.dynamic_slice_in_dim(k_gain, head_index * local_width, local_width)
    ns, nz = lax.axis_size("seq"), lax.axis_size("head")
    w_qkv = lax.all_gather(
        jnp.concatenate([q_weight, k_weight, v_weight], axis=1), "seq", axis=0, tiled=True
    )
    w_query, w_key, w_value = (w_qkv[:, i * local_width : (i + 1) * local_width] for i in range(3))
    w_od = lax.all_gather(jnp.concatenate([o_weight, down_weight], axis=0), "seq", axis=0)
    w_gu = lax.all_gather(jnp.concatenate([gate_weight, up_weight], axis=1), "seq", axis=0, tiled=True)
    queries = jnp.dot(gathered, w_query, preferred_element_type=f32)
    key_pre = jnp.dot(gathered, w_key, preferred_element_type=f32)
    value_pre = jnp.dot(gathered, w_value, preferred_element_type=f32)
    q_total, k_total = lax.psum(
        (jnp.sum(queries * queries, axis=1), jnp.sum(key_pre * key_pre, axis=1)), "head"
    )
    q_scale = lax.rsqrt(q_total / D + epsilon)
    k_scale = lax.rsqrt(k_total / D + epsilon)
    q_hat = queries * q_scale[:, None]
    k_hat = key_pre * k_scale[:, None]
    q_rot = rotate(
        (q_hat * gain_query).reshape(tok_local, local_heads, HEAD_DIM), cosine_table, sine_table
    ).astype(bf16)
    k_rot = rotate(
        (k_hat * gain_key).reshape(tok_local, local_heads, HEAD_DIM), cosine_table, sine_table
    ).astype(bf16)
    share = ns // local_heads
    sub = seq_index % share
    sources = jnp.stack([source_of(sub, i, ns, share) for i in range(ns // share)])
    query_index = sources[:, None] * tok_local + jnp.arange(tok_local, dtype=jnp.int32)[None, :]
    doc_ends = jnp.cumsum(doc_lengths)
    starts = jnp.sum(
        jnp.where(query_index[:, :, None] >= doc_ends, doc_lengths, 0), axis=-1
    ).astype(jnp.int32)
    attended, q_held, k_held, v_held, o_held, lse = run_attend(
        ns, local_heads, q_rot.reshape(tok_local, local_width), k_rot.reshape(tok_local, local_width),
        value_pre.astype(bf16), starts,
    )
    output, mlp_gathered, branch, hidden, second_grads, d_gate, d_up, mlp_gain_part = run_forward(
        nz, ns, attended, tokens, cotangent, w_od, w_gu, attn_gain[None], mlp_gain[None]
    )
    mlp_gain_part = mlp_gain_part[0]
    grad_down = jnp.einsum("tf,td->fd", hidden, second_grads, preferred_element_type=f32)
    grad_gate = jnp.einsum("td,tf->df", mlp_gathered, d_gate, preferred_element_type=f32)
    grad_up = jnp.einsum("td,tf->df", mlp_gathered, d_up, preferred_element_type=f32)
    d_middle, branch_grads, d_attended, attn_gain_part = run_backward(
        nz, ns, d_gate, d_up, cotangent, branch, w_od, w_gu, attn_gain[None]
    )
    attn_gain_part = attn_gain_part[0]
    grad_out = jnp.einsum("tc,td->cd", attended, branch_grads, preferred_element_type=f32)
    d_query, key_grads, value_grads = run_attend_back(
        ns, local_heads, d_attended, starts, q_held, k_held, v_held, o_held, lse
    )
    d_query = d_query.astype(f32).reshape(tok_local, local_heads, HEAD_DIM)
    key_grads = key_grads.astype(f32)
    d_qnorm = unrotate(d_query, cosine_table, sine_table).reshape(tok_local, local_width)
    d_knorm = unrotate(
        key_grads.reshape(tok_local, local_heads, HEAD_DIM), cosine_table, sine_table
    ).reshape(tok_local, local_width)
    q_gain_part = jnp.sum(d_qnorm * q_hat, axis=0)
    k_gain_part = jnp.sum(d_knorm * k_hat, axis=0)
    d_qhat = d_qnorm * gain_query
    d_khat = d_knorm * gain_key
    q_inner, k_inner, q_gain_full, k_gain_full, attn_gain_full, mlp_gain_full = (
        lax.psum(jnp.sum(d_qhat * q_hat, axis=1).astype(jnp.bfloat16), "head").astype(jnp.float32),
        lax.psum(jnp.sum(d_khat * k_hat, axis=1).astype(jnp.bfloat16), "head").astype(jnp.float32),
        lax.psum(place_gain(q_gain_part, head_index, D).astype(jnp.bfloat16), "head").astype(
            jnp.float32
        ),
        lax.psum(place_gain(k_gain_part, head_index, D).astype(jnp.bfloat16), "head").astype(
            jnp.float32
        ),
        lax.psum(attn_gain_part.astype(jnp.bfloat16), "head").astype(jnp.float32),
        lax.psum(mlp_gain_part.astype(jnp.bfloat16), "head").astype(jnp.float32),
    )
    d_q = (q_scale[:, None] * (d_qhat - q_hat * (q_inner / D)[:, None])).astype(bf16)
    d_k = (k_scale[:, None] * (d_khat - k_hat * (k_inner / D)[:, None])).astype(bf16)
    d_v = value_grads.astype(bf16)
    grad_query = jnp.einsum("td,tc->dc", gathered, d_q, preferred_element_type=f32)
    grad_key = jnp.einsum("td,tc->dc", gathered, d_k, preferred_element_type=f32)
    grad_value = jnp.einsum("td,tc->dc", gathered, d_v, preferred_element_type=f32)
    input_grad = d_middle + lax.psum_scatter(
        (
            jnp.einsum("tc,dc->td", d_q, w_query, preferred_element_type=f32)
            + jnp.einsum("tc,dc->td", d_k, w_key, preferred_element_type=f32)
            + jnp.einsum("tc,dc->td", d_v, w_value, preferred_element_type=f32)
        ).astype(jnp.bfloat16),
        "head",
        scatter_dimension=0,
        tiled=True,
    ).astype(jnp.float32)
    reduced = (
        lax.psum_scatter(
            grad_query.astype(jnp.bfloat16), "seq", scatter_dimension=0, tiled=True
        ).astype(jnp.float32),
        lax.psum_scatter(
            grad_key.astype(jnp.bfloat16), "seq", scatter_dimension=0, tiled=True
        ).astype(jnp.float32),
        lax.psum_scatter(
            grad_value.astype(jnp.bfloat16), "seq", scatter_dimension=0, tiled=True
        ).astype(jnp.float32),
        lax.psum_scatter(
            grad_out.astype(jnp.bfloat16), "seq", scatter_dimension=1, tiled=True
        ).astype(jnp.float32),
        lax.psum_scatter(
            grad_gate.astype(jnp.bfloat16), "seq", scatter_dimension=0, tiled=True
        ).astype(jnp.float32),
        lax.psum_scatter(
            grad_up.astype(jnp.bfloat16), "seq", scatter_dimension=0, tiled=True
        ).astype(jnp.float32),
        lax.psum_scatter(
            grad_down.astype(jnp.bfloat16), "seq", scatter_dimension=1, tiled=True
        ).astype(jnp.float32),
        lax.psum_scatter(
            q_gain_full.astype(jnp.bfloat16), "seq", scatter_dimension=0, tiled=True
        ).astype(jnp.float32),
        lax.psum_scatter(
            k_gain_full.astype(jnp.bfloat16), "seq", scatter_dimension=0, tiled=True
        ).astype(jnp.float32),
        lax.psum_scatter(
            attn_gain_full.astype(jnp.bfloat16), "seq", scatter_dimension=0, tiled=True
        ).astype(jnp.float32),
        lax.psum_scatter(
            mlp_gain_full.astype(jnp.bfloat16), "seq", scatter_dimension=0, tiled=True
        ).astype(jnp.float32),
    )
    return (
        output,
        input_grad,
        reduced[0],
        reduced[1],
        reduced[2],
        reduced[3],
        reduced[4],
        reduced[5],
        reduced[6],
        reduced[7],
        reduced[8],
        reduced[9],
        reduced[10],
    )


def solution(mesh):
    in_specs = (
        P(("seq", "head"), None),
        P(("seq", "head"), None),
        P(),
        P("seq", "head"),
        P("seq", "head"),
        P("seq", "head"),
        P("head", "seq"),
        P("seq", "head"),
        P("seq", "head"),
        P("head", "seq"),
        P(),
        P(),
        P(),
        P(),
    )
    out_specs = (
        P(("seq", "head"), None),
        P(("seq", "head"), None),
        P("seq", "head"),
        P("seq", "head"),
        P("seq", "head"),
        P("head", "seq"),
        P("seq", "head"),
        P("seq", "head"),
        P("head", "seq"),
        P("seq"),
        P("seq"),
        P("seq"),
        P("seq"),
    )
    return jax.shard_map(
        on_device, mesh=mesh, in_specs=in_specs, out_specs=out_specs, check_vma=False
    )
```

```python
import functools

import jax
import jax.numpy as jnp
from jax import lax
from jax.experimental import pallas as pl
from jax.experimental.pallas import tpu as pltpu
from jax.sharding import PartitionSpec as P

HEAD_DIM = 128
epsilon = 1e-06
rope_base = 500000.0

MESH = pl.DeviceIdType.MESH
F32 = jnp.float32
BF16 = jnp.bfloat16
STEPS = 4
AG_CHUNKS = 2
VMEM_BYTES = 60 * 1024 * 1024
ANY = pl.BlockSpec(memory_space=pl.ANY)
VMEM = pl.BlockSpec(memory_space=pltpu.VMEM)
NN = (((1,), (0,)), ((), ()))
NT = (((1,), (1,)), ((), ()))
TN = (((0,), (0,)), ((), ()))


def mm(left, right, dims=NN):
    return lax.dot_general(left, right, dims, preferred_element_type=F32)


def rows_at(index, count):
    return pl.ds(pl.multiple_of(index * count, count), count)


def line_barrier(z, n):
    bar = pltpu.get_barrier_semaphore()
    for other, there in ((z - 1, z > 0), (z + 1, z < n - 1)):

        @pl.when(there)
        def _():
            pl.semaphore_signal(bar, inc=1, device_id={"head": other}, device_id_type=MESH)

    pl.semaphore_wait(bar, (z > 0).astype(jnp.int32) + (z < n - 1).astype(jnp.int32))


def line_gather(z, n, buf, rows, send_sem, recv_sem, use):
    part = rows // AG_CHUNKS

    def copy(src, c, up):
        at = pl.ds(pl.multiple_of(src * rows + c * part, part), part)
        return pltpu.make_async_remote_copy(
            src_ref=buf.at[at],
            dst_ref=buf.at[at],
            send_sem=send_sem.at[up, src, c],
            recv_sem=recv_sem.at[src, c],
            device_id={"head": z + 1 if up else z - 1},
            device_id_type=MESH,
        )

    more = (z > 0, z < n - 1)
    for c in range(AG_CHUNKS):
        for up in (0, 1):

            @pl.when(more[up])
            def _():
                copy(z, c, up).start()

    use(z)

    @pl.loop(1, n)
    def _(k):
        sides = ((z + k, z + k < n, 0), (z - k, z - k >= 0, 1))
        for c in range(AG_CHUNKS):
            for src, there, up in sides:

                @pl.when(there)
                def _():
                    copy(src, c, up).wait_recv()

                    @pl.when(more[up])
                    def _():
                        copy(src, c, up).start()

        for src, there, up in sides:

            @pl.when(there)
            def _():
                use(src)

    @pl.loop(0, n)
    def _(src):
        for c in range(AG_CHUNKS):

            @pl.when((src >= z) & (z > 0))
            def _():
                copy(src, c, 0).wait_send()

            @pl.when((src <= z) & (z < n - 1))
            def _():
                copy(src, c, 1).wait_send()


class LineScatter:
    def __init__(self, z, n, partial, land, send_sem, recv_sem, total):
        self.z, self.n, self.partial, self.land, self.total = z, n, partial, land, total
        self.send_sem, self.recv_sem = send_sem, recv_sem

    def copy(self, d, c, up):
        return pltpu.make_async_remote_copy(
            src_ref=self.land.at[up, d, c],
            dst_ref=self.land.at[up, d, c],
            send_sem=self.send_sem.at[up, d, c],
            recv_sem=self.recv_sem.at[up, d, c],
            device_id={"head": self.z + 1 if up else self.z - 1},
            device_id_type=MESH,
        )

    def run(self, low, high):
        z, n, land = self.z, self.n, self.land

        @pl.loop(low * STEPS, high * STEPS)
        def _(t):
            j, c = t // STEPS, t % STEPS
            for d, there, first, up in ((n - 1 - j, n - 1 - j > z, z == 0, 1), (j, j < z, z == n - 1, 0)):

                @pl.when(there)
                def _():
                    mine = self.partial(d, c)

                    @pl.when(first)
                    def _():
                        land[up, d, c] = mine.astype(land.dtype)

                    @pl.when(jnp.logical_not(first))
                    def _():
                        self.copy(d, c, up).wait_recv()
                        land[up, d, c] = (land[up, d, c].astype(F32) + mine).astype(land.dtype)

                    self.copy(d, c, up).start()

    def own(self):
        z, n, total = self.z, self.n, self.total
        width = total.shape[1] // STEPS

        @pl.loop(0, STEPS)
        def _(c):
            at = rows_at(c, width)
            total[:, at] = self.partial(z, c)
            for there, up in ((z > 0, 1), (z < n - 1, 0)):

                @pl.when(there)
                def _():
                    self.copy(z, c, up).wait_recv()
                    total[:, at] += self.land[up, z, c].astype(F32)

    def finish(self):
        @pl.loop(0, self.n * STEPS)
        def _(t):
            d, c = t // STEPS, t % STEPS
            for there, up in ((d > self.z, 1), (d < self.z, 0)):

                @pl.when(there)
                def _():
                    self.copy(d, c, up).wait_send()


def line_scatter(z, n, partial, land, send_sem, recv_sem, total):
    line = LineScatter(z, n, partial, land, send_sem, recv_sem, total)
    line.run(0, n - 1)
    line.own()
    line.finish()


def line_sems(n):
    dma = pltpu.SemaphoreType.DMA
    return {
        "gather": [dma((2, n, AG_CHUNKS)), dma((n, AG_CHUNKS))],
        "scatter": [dma((2, n, STEPS)), dma((2, n, STEPS))],
    }


BLOCK = 16


def row_scale(block):
    return lax.rsqrt(jnp.mean(block * block, axis=-1, keepdims=True) + epsilon)


def norm_back(e, normed, scale, gain):
    g = e * gain
    return scale * (g - normed * jnp.mean(g * normed, axis=-1, keepdims=True))


def sigmoid(x):
    return 1.0 / (1.0 + jnp.exp(-x))


def forward_kernel(
    n, ns,
    att, tok, cot, wod, wgu, attn_gain, mlp_gain,
    out, h1r, branch_out, hidden, dy2, dg, du, gain_part,
    wo, wd, wg, wu, land, branch, h1, second, g_pre, u_pre,
    wsem, osem, g1s, g1r, s1s, s1r, g2s, g2r, s2s, s2r,
):
    z = lax.axis_index("head")
    rows, depth = tok.shape
    lw, ff = att.shape[1], hidden.shape[1]
    col = depth // ns
    width = depth // STEPS
    line_barrier(z, n)
    loads = []
    for s in range(ns):
        loads.append(pltpu.make_async_copy(wod.at[s, pl.ds(0, lw)], wo.at[:, pl.ds(s * col, col)], wsem.at[0]))
    l_g = pltpu.make_async_copy(wgu.at[:, pl.ds(0, ff)], wg, wsem.at[1])
    l_u = pltpu.make_async_copy(wgu.at[:, pl.ds(ff, ff)], wu, wsem.at[2])
    d_loads = [
        pltpu.make_async_copy(wod.at[s, pl.ds(lw, ff)], wd.at[:, pl.ds(s * col, col)], wsem.at[3]) for s in range(ns)
    ]
    for copy in loads + [l_g, l_u] + d_loads:
        copy.start()
    for copy in loads:
        copy.wait()

    def out_part(d, c):
        return mm(att[rows_at(d, rows), :], wo[:, rows_at(c, width)])

    line_scatter(z, n, out_part, land, s1s, s1r, branch)
    o_branch = pltpu.make_async_copy(branch, branch_out, osem)
    o_branch.start()
    gain_part[...] = jnp.zeros_like(gain_part)

    @pl.loop(0, rows // BLOCK)
    def _(i):
        at = rows_at(i, BLOCK)
        y = branch[at, :]
        h = tok[at, :].astype(F32) + y * row_scale(y) * attn_gain[...]
        h1[at, :] = h
        h1r[pl.ds(pl.multiple_of(z * rows + i * BLOCK, BLOCK), BLOCK), :] = h.astype(BF16)

    l_g.wait()
    l_u.wait()
    fw = ff // STEPS

    def up_block(src):
        at = rows_at(src, rows)

        @pl.loop(0, STEPS)
        def _(c):
            cols = rows_at(c, fw)
            x = h1r[at, :]
            g = mm(x, wg[:, cols])
            u = mm(x, wu[:, cols])
            g_pre[at, cols] = g
            u_pre[at, cols] = u
            hidden[at, cols] = (g * sigmoid(g) * u).astype(BF16)

    line_gather(z, n, h1r, rows, g1s, g1r, up_block)
    for copy in d_loads:
        copy.wait()

    def down_part(d, c):
        return mm(hidden[rows_at(d, rows), :], wd[:, rows_at(c, width)])

    line_scatter(z, n, down_part, land, s2s, s2r, second)

    @pl.loop(0, rows // BLOCK)
    def _(i):
        at = rows_at(i, BLOCK)
        y = second[at, :]
        scale = row_scale(y)
        normed = y * scale
        e = cot[at, :].astype(F32)
        out[at, :] = (h1[at, :] + normed * mlp_gain[...]).astype(BF16)
        gain_part[...] += jnp.sum(e * normed, axis=0, keepdims=True)
        dy2[pl.ds(pl.multiple_of(z * rows + i * BLOCK, BLOCK), BLOCK), :] = norm_back(
            e, normed, scale, mlp_gain[...]
        ).astype(BF16)

    def back_block(src):
        at = rows_at(src, rows)

        @pl.loop(0, STEPS)
        def _(c):
            cols = rows_at(c, fw)
            dh = mm(dy2[at, :], wd[cols, :], NT)
            g = g_pre[at, cols]
            u = u_pre[at, cols]
            sig = sigmoid(g)
            du[at, cols] = (dh * g * sig).astype(BF16)
            dg[at, cols] = (dh * u * sig * (1.0 + g * (1.0 - sig))).astype(BF16)

    line_gather(z, n, dy2, rows, g2s, g2r, back_block)
    o_branch.wait()


def run_forward(n, ns, att, tok, cot, wod, wgu, attn_gain, mlp_gain):
    rows, depth = tok.shape
    tl, lw = att.shape
    ff = wgu.shape[1] // 2
    dma = pltpu.SemaphoreType.DMA
    sems = line_sems(n)
    shape = jax.ShapeDtypeStruct
    return pl.pallas_call(
        functools.partial(forward_kernel, n, ns),
        out_shape=(
            shape((rows, depth), BF16),
            shape((tl, depth), BF16),
            shape((rows, depth), F32),
            shape((tl, ff), BF16),
            shape((tl, depth), BF16),
            shape((tl, ff), BF16),
            shape((tl, ff), BF16),
            shape((1, depth), F32),
        ),
        in_specs=[VMEM, VMEM, VMEM, ANY, ANY, VMEM, VMEM],
        out_specs=(VMEM, VMEM, ANY, VMEM, VMEM, VMEM, VMEM, VMEM),
        scratch_shapes=[
            pltpu.VMEM((lw, depth), BF16),
            pltpu.VMEM((ff, depth), BF16),
            pltpu.VMEM((depth, ff), BF16),
            pltpu.VMEM((depth, ff), BF16),
            pltpu.VMEM((2, n, STEPS, rows, depth // STEPS), BF16),
            pltpu.VMEM((rows, depth), F32),
            pltpu.VMEM((rows, depth), F32),
            pltpu.VMEM((rows, depth), F32),
            pltpu.VMEM((tl, ff), F32),
            pltpu.VMEM((tl, ff), F32),
            dma((4,)),
            dma,
            *sems["gather"], *sems["scatter"], *sems["gather"], *sems["scatter"],
        ],
        compiler_params=pltpu.CompilerParams(
            collective_id=1, has_side_effects=True, vmem_limit_bytes=VMEM_BYTES
        ),
        cost_estimate=pl.CostEstimate(flops=18 * 10**9, bytes_accessed=40 * 10**6, transcendentals=2 * 10**6),
        name="feed_forward",
    )(att, tok, cot, wod, wgu, attn_gain, mlp_gain)


def backward_kernel(
    n, ns,
    dg, du, cot, branch, wod, wgu, attn_gain,
    middle, dy1, datt, gain_part,
    wo, wg, wu, land, total,
    wsem, s1s, s1r, g1s, g1r,
):
    z = lax.axis_index("head")
    rows, depth = cot.shape
    lw, ff = datt.shape[1], dg.shape[1]
    col = depth // ns
    width = depth // STEPS
    line_barrier(z, n)
    l_g = pltpu.make_async_copy(wgu.at[:, pl.ds(0, ff)], wg, wsem.at[0])
    l_u = pltpu.make_async_copy(wgu.at[:, pl.ds(ff, ff)], wu, wsem.at[1])
    loads = [
        pltpu.make_async_copy(wod.at[s, pl.ds(0, lw)], wo.at[:, pl.ds(s * col, col)], wsem.at[2]) for s in range(ns)
    ]
    for copy in [l_g, l_u] + loads:
        copy.start()
    l_g.wait()
    l_u.wait()

    def in_part(d, c):
        at, cols = rows_at(d, rows), rows_at(c, width)
        return mm(dg[at, :], wg[cols, :], NT) + mm(du[at, :], wu[cols, :], NT)

    line_scatter(z, n, in_part, land, s1s, s1r, total)
    gain_part[...] = jnp.zeros_like(gain_part)

    @pl.loop(0, rows // BLOCK)
    def _(i):
        at = rows_at(i, BLOCK)
        y = branch[at, :]
        scale = row_scale(y)
        normed = y * scale
        e = cot[at, :].astype(F32) + total[at, :]
        middle[at, :] = e
        gain_part[...] += jnp.sum(e * normed, axis=0, keepdims=True)
        dy1[pl.ds(pl.multiple_of(z * rows + i * BLOCK, BLOCK), BLOCK), :] = norm_back(
            e, normed, scale, attn_gain[...]
        ).astype(BF16)

    for copy in loads:
        copy.wait()

    def att_block(src):
        at = rows_at(src, rows)
        datt[at, :] = mm(dy1[at, :], wo[...], NT).astype(BF16)

    line_gather(z, n, dy1, rows, g1s, g1r, att_block)


def run_backward(n, ns, dg, du, cot, branch, wod, wgu, attn_gain):
    rows, depth = cot.shape
    tl, ff = dg.shape
    lw = wod.shape[1] - ff
    dma = pltpu.SemaphoreType.DMA
    sems = line_sems(n)
    shape = jax.ShapeDtypeStruct
    return pl.pallas_call(
        functools.partial(backward_kernel, n, ns),
        out_shape=(
            shape((rows, depth), F32),
            shape((tl, depth), BF16),
            shape((tl, lw), BF16),
            shape((1, depth), F32),
        ),
        in_specs=[VMEM, VMEM, VMEM, VMEM, ANY, ANY, VMEM],
        out_specs=(VMEM, VMEM, VMEM, VMEM),
        scratch_shapes=[
            pltpu.VMEM((lw, depth), BF16),
            pltpu.VMEM((depth, ff), BF16),
            pltpu.VMEM((depth, ff), BF16),
            pltpu.VMEM((2, n, STEPS, rows, depth // STEPS), BF16),
            pltpu.VMEM((rows, depth), F32),
            dma((3,)),
            *sems["scatter"], *sems["gather"],
        ],
        compiler_params=pltpu.CompilerParams(
            collective_id=2, has_side_effects=True, vmem_limit_bytes=VMEM_BYTES
        ),
        cost_estimate=pl.CostEstimate(flops=10 * 10**9, bytes_accessed=30 * 10**6, transcendentals=0),
        name="into_attention",
    )(dg, du, cot, branch, wod, wgu, attn_gain)


LOG2E = 1.4426950408889634
NEG = -1e30


def seq_barrier(s, ns):
    bar = pltpu.get_barrier_semaphore()
    for other in range(ns):

        @pl.when(other != s)
        def _():
            pl.semaphore_signal(bar, inc=1, device_id={"seq": other}, device_id_type=MESH)

    pl.semaphore_wait(bar, ns - 1)


def share_of(s, ns, r):
    per = ns // (2 * r)
    chunk = s // per
    low = chunk < r
    sub = jnp.where(low, chunk, 2 * r - 1 - chunk)
    return sub, jnp.where(low, s - chunk * per, per + s - chunk * per)


def source_of(sub, i, ns, r):
    per = ns // (2 * r)
    return jnp.where(i < per, sub * per + i, (2 * r - 1 - sub) * per + i - per)


def head_cols(h):
    return pl.ds(pl.multiple_of(h * HEAD_DIM, HEAD_DIM), HEAD_DIM)


def attend_kernel(
    ns, heads, q_in, k_in, v_in, starts,
    att, q_buf, k_buf, v_buf, o_buf, lse,
    o_low, qs, qr, ks, kr, vs, vr, osend, orecv, local,
):
    s = lax.axis_index("seq")
    r = ns // heads
    blocks = ns // r
    tl = q_in.shape[0]
    mine, sub = s // r, s % r
    parity = s % 2
    seq_barrier(s, ns)
    to_sub, to_row = share_of(s, ns, r)

    def q_copy(h):
        return pltpu.make_async_remote_copy(
            src_ref=q_in.at[:, head_cols(h)],
            dst_ref=q_buf.at[rows_at(to_row, tl)],
            send_sem=qs.at[h],
            recv_sem=qr.at[to_row],
            device_id={"seq": h * r + to_sub},
            device_id_type=MESH,
        )

    def q_recv(i):
        return pltpu.make_async_remote_copy(
            src_ref=q_buf.at[rows_at(i, tl)],
            dst_ref=q_buf.at[rows_at(i, tl)],
            send_sem=qs.at[0],
            recv_sem=qr.at[i],
            device_id={"seq": s ^ 1},
            device_id_type=MESH,
        )

    def kv_copy(src, buf, send, recv, t, at):
        return pltpu.make_async_remote_copy(
            src_ref=src,
            dst_ref=buf.at[rows_at(at, tl)],
            send_sem=send,
            recv_sem=recv.at[at],
            device_id={"seq": t},
            device_id_type=MESH,
        )

    kv = ((k_in, k_buf, ks, kr), (v_in, v_buf, vs, vr))
    own = [pltpu.make_async_copy(x.at[:, head_cols(mine)], buf.at[rows_at(s, tl)], local.at[i])
           for i, (x, buf, _, _) in enumerate(kv)]
    own_q = pltpu.make_async_copy(q_in.at[:, head_cols(mine)], q_buf.at[rows_at(to_row, tl)], local.at[2])
    for copy in own:
        copy.start()

    @pl.when(to_sub == sub)
    def _():
        own_q.start()

    def far(t):
        return (t != s) & (t % 2 == parity)

    @pl.loop(1, ns)
    def _(step):
        t = s ^ step

        @pl.when(far(t))
        def _():
            for x, buf, ss, rs in kv:
                kv_copy(x.at[:, head_cols(t // r)], buf, ss.at[0, t], rs, t, s).start()

    @pl.loop(0, heads)
    def _(h):
        @pl.when(h * r + to_sub != s)
        def _():
            q_copy(h).start()

    for copy in own:
        copy.wait()

    def pass_on(src, start):
        for _, buf, ss, rs in kv:
            copy = kv_copy(buf.at[rows_at(src, tl)], buf, ss.at[1, src], rs, s ^ 1, src)
            if start:
                copy.start()
            else:
                copy.wait_send()

    pass_on(s, True)

    @pl.loop(1, ns)
    def _(step):
        src = s ^ step

        @pl.when(far(src))
        def _():
            for x, buf, ss, rs in kv:
                kv_copy(buf.at[rows_at(src, tl)], buf, ss.at[0, 0], rs, s ^ 1, src).wait_recv()
            pass_on(src, True)

    @pl.loop(0, ns)
    def _(src):
        @pl.when(src % 2 != parity)
        def _():
            for x, buf, ss, rs in kv:
                kv_copy(buf.at[rows_at(src, tl)], buf, ss.at[0, 0], rs, s ^ 1, src).wait_recv()

    @pl.when(to_sub == sub)
    def _():
        own_q.wait()

    unit = HEAD_DIM ** (-0.5) * LOG2E

    def o_copy(i, t):
        return pltpu.make_async_remote_copy(
            src_ref=o_low.at[rows_at(i, tl)],
            dst_ref=att.at[:, head_cols(mine)],
            send_sem=osend.at[i],
            recv_sem=orecv.at[mine],
            device_id={"seq": t},
            device_id_type=MESH,
        )

    own_o = pltpu.make_async_copy(o_low.at[rows_at(to_row, tl)], att.at[:, head_cols(mine)], local.at[3])

    @pl.loop(0, blocks)
    def _(i):
        src = source_of(sub, i, ns, r)

        @pl.when(src != s)
        def _():
            q_recv(i).wait_recv()

        q = q_buf[rows_at(i, tl), :]
        start = starts[pl.ds(i, 1), :]
        key_at = lax.broadcasted_iota(jnp.int32, (tl, tl), 0)

        def step(j, carry, diagonal):
            top, total, acc = carry
            at = rows_at(j, tl)
            scores = mm(k_buf[at, :], q, NT) * unit
            allowed = key_at >= start - j * tl
            if diagonal:
                allowed = allowed & (key_at <= lax.broadcasted_iota(jnp.int32, (tl, tl), 1))
            scores = jnp.where(allowed, scores, NEG)
            new = jnp.maximum(top, jnp.max(scores, axis=0, keepdims=True))
            terms = jnp.exp2(scores - new)
            fade = jnp.exp2(top - new)
            return (
                new,
                total * fade + jnp.sum(terms, axis=0, keepdims=True),
                acc * fade + mm(v_buf[at, :], terms.astype(BF16), TN),
            )

        carry = (
            jnp.full((1, tl), NEG, F32),
            jnp.zeros((1, tl), F32),
            jnp.zeros((HEAD_DIM, tl), F32),
        )
        carry = lax.fori_loop(0, src, lambda j, c: step(j, c, False), carry)
        top, total, acc = step(src, carry, True)
        lse[pl.ds(i, 1), :] = top + jnp.log(total) * LOG2E
        o = jnp.transpose(acc / total)
        o_buf[rows_at(i, tl), :] = o
        o_low[rows_at(i, tl), :] = o.astype(BF16)

        @pl.when(src != s)
        def _():
            o_copy(i, src).start()

        @pl.when(src == s)
        def _():
            own_o.start()

    @pl.when(to_sub == sub)
    def _():
        own_o.wait()

    @pl.loop(0, heads)
    def _(h):
        @pl.when(h * r + to_sub != s)
        def _():
            q_copy(h).wait_send()
            pltpu.make_async_remote_copy(
                src_ref=o_low.at[rows_at(0, tl)],
                dst_ref=att.at[:, head_cols(h)],
                send_sem=osend.at[0],
                recv_sem=orecv.at[h],
                device_id={"seq": s ^ 1},
                device_id_type=MESH,
            ).wait_recv()

    @pl.loop(0, blocks)
    def _(i):
        src = source_of(sub, i, ns, r)

        @pl.when(src != s)
        def _():
            o_copy(i, src).wait_send()

    pass_on(s, False)

    @pl.loop(1, ns)
    def _(step):
        t = s ^ step

        @pl.when(far(t))
        def _():
            for x, buf, ss, rs in kv:
                kv_copy(x.at[:, head_cols(t // r)], buf, ss.at[0, t], rs, t, s).wait_send()
            pass_on(t, False)


def run_attend(ns, heads, q, k, v, starts):
    tl, lw = q.shape
    r = ns // heads
    nq = ns // r * tl
    nk = ns * tl
    dma = pltpu.SemaphoreType.DMA
    shape = jax.ShapeDtypeStruct
    return pl.pallas_call(
        functools.partial(attend_kernel, ns, heads),
        out_shape=(
            shape((tl, lw), BF16),
            shape((nq, HEAD_DIM), BF16),
            shape((nk, HEAD_DIM), BF16),
            shape((nk, HEAD_DIM), BF16),
            shape((nq, HEAD_DIM), F32),
            shape((ns // r, tl), F32),
        ),
        in_specs=[VMEM] * 4,
        out_specs=(VMEM,) * 6,
        scratch_shapes=[
            pltpu.VMEM((nq, HEAD_DIM), BF16),
            dma((heads,)), dma((ns // r,)),
            dma((2, ns)), dma((ns,)),
            dma((2, ns)), dma((ns,)),
            dma((ns // r,)), dma((heads,)),
            dma((4,)),
        ],
        compiler_params=pltpu.CompilerParams(
            collective_id=3, has_side_effects=True, vmem_limit_bytes=VMEM_BYTES
        ),
        cost_estimate=pl.CostEstimate(flops=3 * 10**9, bytes_accessed=8 * 10**6, transcendentals=5 * 10**6),
        name="attend",
    )(q, k, v, starts)


def attend_back_kernel(
    ns, heads, do_in, starts, q_buf, k_buf, v_buf, o_buf, lse,
    dq, dk, dv,
    do_buf, dq_low, dk_acc, dv_acc, low, pair, land,
    ds_, dr_, ps, pr, gs, gr, qs, qr, local,
):
    s = lax.axis_index("seq")
    r = ns // heads
    blocks = ns // r
    tl = do_in.shape[0]
    mine, sub = s // r, s % r
    parity = s % 2
    seq_barrier(s, ns)
    to_sub, to_row = share_of(s, ns, r)

    def copy(src, dst, send, recv, t):
        return pltpu.make_async_remote_copy(
            src_ref=src, dst_ref=dst, send_sem=send, recv_sem=recv, device_id={"seq": t}, device_id_type=MESH
        )

    def do_copy(h):
        return copy(
            do_in.at[:, head_cols(h)], do_buf.at[rows_at(to_row, tl)], ds_.at[h], dr_.at[to_row], h * r + to_sub
        )

    own_do = pltpu.make_async_copy(do_in.at[:, head_cols(mine)], do_buf.at[rows_at(to_row, tl)], local.at[0])

    @pl.when(to_sub == sub)
    def _():
        own_do.start()

    @pl.loop(0, heads)
    def _(h):
        @pl.when(h * r + to_sub != s)
        def _():
            do_copy(h).start()

    dk_acc[...] = jnp.zeros_like(dk_acc)
    dv_acc[...] = jnp.zeros_like(dv_acc)

    @pl.when(to_sub == sub)
    def _():
        own_do.wait()

    scale = HEAD_DIM ** (-0.5)
    unit = scale * LOG2E

    def dq_copy(i, t):
        return copy(dq_low.at[rows_at(i, tl)], dq.at[:, head_cols(mine)], qs.at[i], qr.at[mine], t)

    own_dq = pltpu.make_async_copy(dq_low.at[rows_at(to_row, tl)], dq.at[:, head_cols(mine)], local.at[1])
    ones = jnp.ones((8, HEAD_DIM), F32)

    @pl.loop(0, blocks)
    def _(i):
        src = source_of(sub, i, ns, r)
        rows = rows_at(i, tl)

        @pl.when(src != s)
        def _():
            copy(do_buf.at[rows], do_buf.at[rows], ds_.at[0], dr_.at[i], s ^ 1).wait_recv()

        q = q_buf[rows, :]
        do = do_buf[rows, :]
        start = starts[pl.ds(i, 1), :]
        norm = lse[pl.ds(i, 1), :]
        delta = lax.dot_general(
            ones, do.astype(F32) * o_buf[rows, :], NT,
            precision=lax.Precision.HIGHEST, preferred_element_type=F32,
        )[:1]
        key_at = lax.broadcasted_iota(jnp.int32, (tl, tl), 0)

        def step(j, dq_sum, diagonal):
            at = rows_at(j, tl)
            keys = k_buf[at, :]
            scores = mm(keys, q, NT) * unit
            allowed = key_at >= start - j * tl
            if diagonal:
                allowed = allowed & (key_at <= lax.broadcasted_iota(jnp.int32, (tl, tl), 1))
            p = jnp.where(allowed, jnp.exp2(scores - norm), 0.0)
            dp = mm(v_buf[at, :], do, NT)
            dscore = (p * (dp - delta)).astype(BF16)
            dv_acc[at, :] += mm(p.astype(BF16), do)
            dk_acc[at, :] += mm(dscore, q)
            return dq_sum + mm(dscore, keys, TN)

        dq_sum = lax.fori_loop(0, src, lambda j, c: step(j, c, False), jnp.zeros((tl, HEAD_DIM), F32))
        dq_sum = step(src, dq_sum, True)
        dq_low[rows, :] = (dq_sum * scale).astype(BF16)

        @pl.when(src != s)
        def _():
            dq_copy(i, src).start()

        @pl.when(src == s)
        def _():
            own_dq.start()

    half = ns // 2

    def pair_copy(w, i):
        src = 2 * i + 1 - parity
        return copy(low.at[w, rows_at(src, tl)], pair.at[w, rows_at(i, tl)], ps.at[w, i], pr.at[w, i], s ^ 1)

    @pl.loop(0, half)
    def _(i):
        at = rows_at(2 * i + 1 - parity, tl)
        low[0, at, :] = (dk_acc[at, :] * scale).astype(BF16)
        pair_copy(0, i).start()
        low[1, at, :] = dv_acc[at, :].astype(BF16)
        pair_copy(1, i).start()

    slot = sub // 2
    outs = (dk, dv)

    def back_copy(w, i):
        dest = 2 * i + parity
        return copy(
            low.at[w, rows_at(dest, tl)], land.at[w, slot, :, head_cols(mine)], gs.at[w, i], gr.at[w, mine, slot], dest
        )

    @pl.loop(0, half)
    def _(i):
        dest = 2 * i + parity
        at = rows_at(dest, tl)
        for w, acc, factor in ((0, dk_acc, scale), (1, dv_acc, 1.0)):
            copy(low.at[w, at], pair.at[w, rows_at(i, tl)], ps.at[w, i], pr.at[w, i], s ^ 1).wait_recv()
            low[w, at, :] = (acc[at, :] * factor + pair[w, rows_at(i, tl), :].astype(F32)).astype(BF16)

            @pl.when(dest != s)
            def _():
                back_copy(w, i).start()

            @pl.when(dest == s)
            def _():
                land[w, slot, :, head_cols(mine)] = low[w, at, :]

    @pl.loop(0, heads)
    def _(h):
        for w in range(2):
            for k in range(r // 2):

                @pl.when(h * r + 2 * k + parity != s)
                def _():
                    copy(
                        low.at[w, rows_at(0, tl)], land.at[w, k, :, head_cols(h)], gs.at[w, 0], gr.at[w, h, k], s ^ 1
                    ).wait_recv()

    for w in range(2):
        outs[w][...] = functools.reduce(
            lambda a, b: a + b, [land[w, k].astype(F32) for k in range(r // 2)]
        ).astype(BF16)

    @pl.when(to_sub == sub)
    def _():
        own_dq.wait()

    @pl.loop(0, heads)
    def _(h):
        @pl.when(h * r + to_sub != s)
        def _():
            do_copy(h).wait_send()
            copy(dq_low.at[rows_at(0, tl)], dq.at[:, head_cols(h)], qs.at[0], qr.at[h], s ^ 1).wait_recv()

    @pl.loop(0, blocks)
    def _(i):
        src = source_of(sub, i, ns, r)

        @pl.when(src != s)
        def _():
            dq_copy(i, src).wait_send()

    @pl.loop(0, half)
    def _(i):
        for w in range(2):
            pair_copy(w, i).wait_send()

            @pl.when(2 * i + parity != s)
            def _():
                back_copy(w, i).wait_send()


def run_attend_back(ns, heads, do, starts, q, k, v, o, lse):
    tl, lw = do.shape
    r = ns // heads
    nq = ns // r * tl
    nk = ns * tl
    dma = pltpu.SemaphoreType.DMA
    shape = jax.ShapeDtypeStruct
    return pl.pallas_call(
        functools.partial(attend_back_kernel, ns, heads),
        out_shape=(shape((tl, lw), BF16),) * 3,
        in_specs=[VMEM] * 7,
        out_specs=(VMEM,) * 3,
        scratch_shapes=[
            pltpu.VMEM((nq, HEAD_DIM), BF16),
            pltpu.VMEM((nq, HEAD_DIM), BF16),
            pltpu.VMEM((nk, HEAD_DIM), F32),
            pltpu.VMEM((nk, HEAD_DIM), F32),
            pltpu.VMEM((2, nk, HEAD_DIM), BF16),
            pltpu.VMEM((2, nk // 2, HEAD_DIM), BF16),
            pltpu.VMEM((2, r // 2, tl, lw), BF16),
            dma((heads,)), dma((ns // r,)),
            dma((2, ns // 2)), dma((2, ns // 2)),
            dma((2, ns // 2)), dma((2, heads, r // 2)),
            dma((ns // r,)), dma((heads,)),
            dma((2,)),
        ],
        compiler_params=pltpu.CompilerParams(
            collective_id=4, has_side_effects=True, vmem_limit_bytes=VMEM_BYTES
        ),
        cost_estimate=pl.CostEstimate(flops=8 * 10**9, bytes_accessed=10 * 10**6, transcendentals=5 * 10**6),
        name="attend_back",
    )(do, starts, q, k, v, o, lse)


def cross_barrier(s, z, ns, n):
    bar = pltpu.get_barrier_semaphore()
    for axis, me, count in (("seq", s, ns), ("head", z, n)):
        for other in range(count):

            @pl.when(other != me)
            def _():
                pl.semaphore_signal(bar, inc=1, device_id={axis: other}, device_id_type=MESH)

    pl.semaphore_wait(bar, ns - 1 + n - 1)


def subsets(bits):
    found = [0]
    for bit in bits:
        found += [bit | other for other in found]
    return found


def orders_of(ns):
    chips = [1 << i for i in range(1, ns.bit_length() - 1)]
    return (chips, chips[::-1])


def remote(src, dst, send, recv, axis, to):
    return pltpu.make_async_remote_copy(
        src_ref=src, dst_ref=dst, send_sem=send, recv_sem=recv, device_id={axis: to}, device_id_type=MESH
    )


class CubeGather:
    def __init__(self, s, ns, buf, rows, send_sem, recv_sem):
        self.s, self.buf, self.rows, self.send_sem, self.recv_sem = s, buf, rows, send_sem, recv_sem
        self.orders = [order + [1] for order in orders_of(ns)]

    def copy(self, half, bit, block):
        part = self.rows // 2
        at = pl.ds(pl.multiple_of(block * self.rows + half * part, part), part)
        return remote(
            self.buf.at[at], self.buf.at[at],
            self.send_sem.at[bit.bit_length() - 1, block, half], self.recv_sem.at[block, half],
            "seq", self.s ^ bit,
        )

    def start(self):
        for i in range(len(self.orders[0])):
            for half, order in enumerate(self.orders):
                self.copy(half, order[i], self.s).start()

    def level(self, i):
        for j in range(2**i):
            for half, order in enumerate(self.orders):
                block = self.s ^ order[i] ^ subsets(order[:i])[j]
                self.copy(half, order[i], block).wait_recv()
                for bit in order[i + 1 :]:
                    self.copy(half, bit, block).start()

    def finish(self):
        for half, order in enumerate(self.orders):
            for i, bit in enumerate(order):
                for other in subsets(order[:i]):
                    self.copy(half, bit, self.s ^ other).wait_send()

    @staticmethod
    def sems(ns):
        dma = pltpu.SemaphoreType.DMA
        return [dma((ns.bit_length() - 1, ns, 2)), dma((ns, 2))]


class CubeScatter:
    def __init__(self, s, ns, block, rows, first, held, later, sems):
        self.s, self.block, self.rows = s, block, rows
        self.first, self.held, self.later = first, held, later
        self.send0, self.recv0, self.send1, self.recv1 = sems
        self.orders = orders_of(ns)
        self.evens = range(0, ns, 2)

    def core_copy(self, j):
        return remote(self.first.at[j], self.held.at[j], self.send0.at[j], self.recv0.at[j], "seq", self.s ^ 1)

    def send_core(self):
        @pl.loop(0, len(self.evens))
        def _(j):
            self.first[j] = self.block(self.s ^ (2 * j + 1)).astype(BF16)
            self.core_copy(j).start()

    def moves(self, i):
        part = self.rows // 2
        base = sum(2 ** (len(self.orders[0]) - 1 - k) for k in range(i))
        for half, order in enumerate(self.orders):
            for j, other in enumerate(subsets(order[i + 1 :])):
                slot = base + j
                at = pl.ds(half * part, part)
                yield other >> 1, at, half, slot, remote(
                    self.held.at[(order[i] | other) >> 1, at], self.later.at[half, slot],
                    self.send1.at[half, slot], self.recv1.at[half, slot], "seq", self.s ^ order[i],
                )

    def add_core(self):
        @pl.loop(0, len(self.evens))
        def _(j):
            mine = self.block(self.s ^ (2 * j))
            self.core_copy(j).wait_recv()
            self.held[j] = (self.held[j].astype(F32) + mine).astype(BF16)

        self.send(0)

    def send(self, i):
        for *_, copy in self.moves(i):
            copy.start()

    def take(self, i):
        for j, at, half, slot, copy in self.moves(i):
            copy.wait_recv()
            self.held[j, at] = (self.held[j, at].astype(F32) + self.later[half, slot].astype(F32)).astype(BF16)

    @property
    def stages(self):
        return len(self.orders[0])

    def finish(self):
        @pl.loop(0, len(self.evens))
        def _(j):
            self.core_copy(j).wait_send()

        for i in range(self.stages):
            for *_, copy in self.moves(i):
                copy.wait_send()

    @staticmethod
    def scratch(ns, rows, width):
        dma = pltpu.SemaphoreType.DMA
        half = ns // 2
        return [
            pltpu.VMEM((half, rows, width), BF16),
            pltpu.VMEM((half, rows, width), BF16),
            pltpu.VMEM((2, half - 1, rows // 2, width), BF16),
            dma((half,)), dma((half,)), dma((2, half - 1)), dma((2, half - 1)),
        ]


def row_sums(left, right):
    ones = jnp.ones((8, left.shape[1]), F32)
    both = [
        lax.dot_general(ones, x, NT, precision=lax.Precision.HIGHEST, preferred_element_type=F32) for x in (left, right)
    ]
    return jnp.where(lax.broadcasted_iota(jnp.int32, both[0].shape, 0) < 4, both[0], both[1])


def as_column(sums, row):
    pick = (lax.broadcasted_iota(jnp.int32, (8, HEAD_DIM), 0) == row).astype(F32)
    return lax.dot_general(sums, pick, TN, precision=lax.Precision.HIGHEST, preferred_element_type=F32)


class SmallExchange:
    def __init__(self, axis, me, count, land, send_sem, recv_sem):
        self.axis, self.me, self.count, self.land = axis, me, count, land
        self.send_sem, self.recv_sem = send_sem, recv_sem

    def copy(self, slot, to):
        return remote(self.land.at[slot], self.land.at[slot], self.send_sem.at[to], self.recv_sem.at[slot], self.axis, to)

    def each(self, act):
        @pl.loop(0, self.count)
        def _(other):
            @pl.when(other != self.me)
            def _():
                act(other)

    def start(self):
        self.each(lambda other: self.copy(self.me, other).start())

    def receive(self):
        self.each(lambda other: self.copy(other, other).wait_recv())

    def finish(self):
        self.each(lambda other: self.copy(self.me, other).wait_send())


def turn(x, cos, sin):
    return x * cos + pltpu.roll(x, HEAD_DIM // 2, 1) * sin


def turn_back(x, cos, sin):
    return x * cos - pltpu.roll(x, HEAD_DIM // 2, 1) * sin


def project_kernel(
    n, ns, depth_full,
    tok, wq, wk, wv, gq, gk, cos, sin,
    x, w, q_raw, k_raw, totals, q_rot, k_rot, v_low,
    land, lsem, ags, agr, cgs, cgr, ss, sr,
):
    s, z = lax.axis_index("seq"), lax.axis_index("head")
    rows, depth = tok.shape
    block, lw = wq.shape
    heads = lw // HEAD_DIM
    cross_barrier(s, z, ns, n)
    mine = rows_at(s, block)
    loads = [pltpu.make_async_copy(tok, x.at[rows_at(z, rows)], lsem.at[0])] + [
        pltpu.make_async_copy(m, w.at[mine, pl.ds(i * lw, lw)], lsem.at[i + 1]) for i, m in enumerate((wq, wk, wv))
    ]
    for copy in loads:
        copy.start()
    loads[0].wait()
    cube = CubeGather(s, ns, w, block, cgs, cgr)
    levels = len(cube.orders[0])
    done = []

    def weights(k):
        todo = [0] if k == 0 and n > 2 else [i for i in range(levels) if i not in done]
        for i in todo:
            cube.level(i)
            done.append(i)

    def start_weights():
        for copy in loads[1:]:
            copy.wait()
        cube.start()

    def multiply(src):
        at = rows_at(src, rows)
        for i, to in enumerate((q_raw, k_raw)):
            to[at, :] = mm(x[at, :], w[:, i * lw : (i + 1) * lw])
        v_low[at, :] = mm(x[at, :], w[:, 2 * lw :]).astype(BF16)

    part = rows // AG_CHUNKS

    def copy(src, c, up):
        at = pl.ds(pl.multiple_of(src * rows + c * part, part), part)
        return remote(x.at[at], x.at[at], ags.at[up, src, c], agr.at[src, c], "head", z + 1 if up else z - 1)

    more = (z > 0, z < n - 1)
    for c in range(AG_CHUNKS):
        for up in (0, 1):

            @pl.when(more[up])
            def _():
                copy(z, c, up).start()

    start_weights()

    def sides(k):
        return ((z + k, z + k < n, 0), (z - k, z - k >= 0, 1))

    for k in range(1, n):
        for c in range(AG_CHUNKS):
            for src, there, up in sides(k):

                @pl.when(there)
                def _():
                    copy(src, c, up).wait_recv()

                    @pl.when(more[up])
                    def _():
                        copy(src, c, up).start()

        if k <= 2:
            weights(k - 1)
        if k == min(2, n - 1):
            multiply(z)
            for src, there, _ in sides(1):
                pl.when(there)(functools.partial(multiply, src))
        if k > 1:
            for src, there, _ in sides(k):
                pl.when(there)(functools.partial(multiply, src))

    totals[...] = row_sums(q_raw[...] * q_raw[...], k_raw[...] * k_raw[...])
    land[z] = totals[...]
    small = SmallExchange("head", z, n, land, ss, sr)
    small.start()
    small.receive()
    total = land[0]
    for k in range(1, n):
        total = total + land[k]
    totals[...] = total
    for row, raw, gain, to in ((0, q_raw, gq, q_rot), (4, k_raw, gk, k_rot)):
        scale = lax.rsqrt(as_column(total, row) / depth_full + epsilon)
        for h in range(heads):
            cols = slice(h * HEAD_DIM, (h + 1) * HEAD_DIM)
            to[:, cols] = turn(raw[:, cols] * scale * gain[:, cols], cos[...], sin[...]).astype(BF16)
    small.finish()
    cube.finish()

    @pl.loop(0, n)
    def _(src):
        for c in range(AG_CHUNKS):

            @pl.when((src >= z) & (z > 0))
            def _():
                copy(src, c, 0).wait_send()

            @pl.when((src <= z) & (z < n - 1))
            def _():
                copy(src, c, 1).wait_send()


def run_project(n, ns, tok, wq, wk, wv, gq, gk, cos, sin):
    rows, depth = tok.shape
    tl = rows * n
    lw = wq.shape[1]
    dma = pltpu.SemaphoreType.DMA
    shape = jax.ShapeDtypeStruct
    return pl.pallas_call(
        functools.partial(project_kernel, n, ns, depth),
        out_shape=(
            shape((tl, depth), BF16),
            shape((depth, 3 * lw), BF16),
            shape((tl, lw), F32),
            shape((tl, lw), F32),
            shape((8, tl), F32),
            shape((tl, lw), BF16),
            shape((tl, lw), BF16),
            shape((tl, lw), BF16),
        ),
        in_specs=[ANY] * 4 + [VMEM] * 4,
        out_specs=(VMEM,) * 8,
        scratch_shapes=[
            pltpu.VMEM((n, 8, tl), F32),
            dma((4,)),
            dma((2, n, AG_CHUNKS)), dma((n, AG_CHUNKS)),
            *CubeGather.sems(ns),
            dma((n,)), dma((n,)),
        ],
        compiler_params=pltpu.CompilerParams(
            collective_id=5, has_side_effects=True, vmem_limit_bytes=VMEM_BYTES
        ),
        cost_estimate=pl.CostEstimate(flops=3 * 10**9, bytes_accessed=20 * 10**6, transcendentals=0),
        name="project",
    )(tok, wq, wk, wv, gq, gk, cos, sin)


def input_kernel(
    n, ns, depth_full,
    dq, dk, dv, q_raw, k_raw, totals, gq, gk, cos, sin, x, w, middle, att, dy1, attn_part, mlp_part,
    grad_in, grad_q, grad_k, grad_v, grad_o, gains,
    dqkv, q_back, k_back, inner, land, total, message, message_z, gain_land,
    first, held, later, c0s, c0r, c1s, c1r,
    ss, sr, ms, mr, zs, zr, s1s, s1r,
):
    s, z = lax.axis_index("seq"), lax.axis_index("head")
    rows, depth = grad_in.shape
    tl, lw = dq.shape
    block = depth // ns
    heads = lw // HEAD_DIM
    cross_barrier(s, z, ns, n)
    sums = totals[...]
    scales = [lax.rsqrt(as_column(sums, row) / depth_full + epsilon) for row in (0, 4)]
    todo = ((dq, q_raw, gq, q_back), (dk, k_raw, gk, k_back))
    message[...] = jnp.zeros_like(message)
    products = []
    for i, (grad, raw, gain, back) in enumerate(todo):
        product = jnp.zeros((tl, HEAD_DIM), F32)
        for h in range(heads):
            cols = slice(h * HEAD_DIM, (h + 1) * HEAD_DIM)
            hat = raw[:, cols] * scales[i]
            turned = turn_back(grad[:, cols].astype(F32), cos[...], sin[...])
            message[0, pl.ds(i, 1), cols] = jnp.sum(turned * hat, axis=0, keepdims=True)
            turned = turned * gain[:, cols]
            back[:, cols] = turned
            product = product + turned * hat
        products.append(product)
    inner[z] = row_sums(*products)
    small = SmallExchange("head", z, n, inner, ss, sr)
    small.start()
    for t in range(1, ns):
        message[t, pl.ds(0, 2), pl.ds(0, lw)] = message[0, pl.ds(0, 2), pl.ds(0, lw)]
    for t in range(ns):
        for i, part in enumerate((attn_part, mlp_part)):
            message[t, pl.ds(i, 1), pl.ds(lw, block)] = part[:, t * block : (t + 1) * block]

    def message_copy(t, frm):
        return remote(message.at[t], message_z.at[frm], ms.at[t], mr.at[frm], "seq", t)

    def each_seq(act):
        @pl.loop(0, ns)
        def _(t):
            @pl.when(t != s)
            def _():
                act(t)

    message_z[s] = message[s]
    each_seq(lambda t: message_copy(t, s).start())
    dqkv[:, 2 * lw :] = dv[...]
    small.receive()
    sums = inner[0]
    for k in range(1, n):
        sums = sums + inner[k]
    for i, (grad, raw, gain, back) in enumerate(todo):
        mean = as_column(sums, 4 * i) / depth_full
        for h in range(heads):
            cols = slice(h * HEAD_DIM, (h + 1) * HEAD_DIM)
            to = slice(i * lw + h * HEAD_DIM, i * lw + (h + 1) * HEAD_DIM)
            dqkv[:, to] = (scales[i] * (back[:, cols] - raw[:, cols] * scales[i] * mean)).astype(BF16)

    width = depth // STEPS

    def weight_block(b):
        cols = rows_at(b, block)
        return jnp.concatenate([mm(x[:, cols], dqkv[...], TN), mm(dy1[:, cols], att[...], TN)], axis=1)

    def in_part(d, c):
        return mm(dqkv[rows_at(d, rows), :], w[rows_at(c, width), :], NT)

    cube = CubeScatter(s, ns, weight_block, block, first, held, later, (c0s, c0r, c1s, c1r))
    line = LineScatter(z, n, in_part, land, s1s, s1r, total)
    cube.send_core()
    line.run(0, 1)
    cube.add_core()
    for j in range(1, n - 1):
        line.run(j, j + 1)
        if j - 1 < cube.stages - 1:
            cube.take(j - 1)
            cube.send(j)
    for i in range(max(n - 2, 0), cube.stages - 1):
        cube.take(i)
        cube.send(i + 1)

    each_seq(lambda t: message_copy(t, t).wait_recv())
    received = message_z[0]
    for t in range(1, ns):
        received = received + message_z[t]
    each_seq(lambda t: message_copy(t, s).wait_send())
    gain_land[z] = received
    rounds = SmallExchange("head", z, n, gain_land, zs, zr)
    rounds.start()
    line.own()
    grad_in[...] = middle[...] + total[...]
    cube.take(cube.stages - 1)
    for i, to in enumerate((grad_q, grad_k, grad_v)):
        to[...] = held[0, :, i * lw : (i + 1) * lw].astype(F32)
    grad_o[...] = jnp.transpose(held[0, :, 3 * lw :].astype(F32))
    rounds.receive()
    at = s * block
    gains[...] = jnp.zeros_like(gains)
    gains[0:2, :] = gain_land[at // lw, pl.ds(0, 2), pl.ds(pl.multiple_of(at % lw, block), block)]
    both = gain_land[0, pl.ds(0, 2), pl.ds(lw, block)]
    for k in range(1, n):
        both = both + gain_land[k, pl.ds(0, 2), pl.ds(lw, block)]
    gains[2:4, :] = both
    cube.finish()
    line.finish()
    small.finish()
    rounds.finish()


def run_input(n, ns, dq, dk, dv, q_raw, k_raw, totals, gq, gk, cos, sin, x, w, middle, att, dy1, attn_part, mlp_part):
    rows, depth = middle.shape
    tl, lw = dq.shape
    block = depth // ns
    dma = pltpu.SemaphoreType.DMA
    shape = jax.ShapeDtypeStruct
    return pl.pallas_call(
        functools.partial(input_kernel, n, ns, depth),
        out_shape=(shape((rows, depth), F32),)
        + (shape((block, lw), F32),) * 3
        + (shape((lw, block), F32), shape((8, block), F32)),
        in_specs=[VMEM] * 17,
        out_specs=(VMEM,) * 6,
        scratch_shapes=[
            pltpu.VMEM((tl, 3 * lw), BF16),
            pltpu.VMEM((tl, lw), F32),
            pltpu.VMEM((tl, lw), F32),
            pltpu.VMEM((n, 8, tl), F32),
            pltpu.VMEM((2, n, STEPS, rows, depth // STEPS), BF16),
            pltpu.VMEM((rows, depth), F32),
            pltpu.VMEM((ns, 8, lw + block), F32),
            pltpu.VMEM((ns, 8, lw + block), F32),
            pltpu.VMEM((n, 8, lw + block), F32),
            *CubeScatter.scratch(ns, block, 4 * lw),
            dma((n,)), dma((n,)),
            dma((ns,)), dma((ns,)),
            dma((n,)), dma((n,)),
            *line_sems(n)["scatter"],
        ],
        compiler_params=pltpu.CompilerParams(
            collective_id=6, has_side_effects=True, vmem_limit_bytes=VMEM_BYTES
        ),
        cost_estimate=pl.CostEstimate(flops=8 * 10**9, bytes_accessed=30 * 10**6, transcendentals=0),
        name="into_input",
    )(dq, dk, dv, q_raw, k_raw, totals, gq, gk, cos, sin, x, w, middle, att, dy1, attn_part, mlp_part)


def doc_starts(doc_lengths, token_index):
    ends = jnp.cumsum(doc_lengths)
    return jnp.sum(jnp.where(token_index[..., None] >= ends, doc_lengths, 0), axis=-1).astype(jnp.int32)


def turn_tables(positions):
    frequency = jnp.power(rope_base, -jnp.arange(HEAD_DIM // 2, dtype=F32) * (2.0 / HEAD_DIM))
    angles = positions.astype(F32)[:, None] * frequency[None, :]
    cos, sin = jnp.cos(angles), jnp.sin(angles)
    return jnp.concatenate([cos, cos], axis=1), jnp.concatenate([-sin, sin], axis=1)


def scatter_grad(grad):
    return lax.psum_scatter(grad.astype(BF16), "seq", scatter_dimension=0, tiled=True)


def on_device(
    tokens,
    cotangent,
    doc_lengths,
    q_weight,
    k_weight,
    v_weight,
    o_weight,
    gate_weight,
    up_weight,
    down_weight,
    q_gain,
    k_gain,
    attn_gain,
    mlp_gain,
):
    ns, nz = lax.axis_size("seq"), lax.axis_size("head")
    seq_index, head_index = lax.axis_index("seq"), lax.axis_index("head")
    lw = q_weight.shape[1]
    heads = lw // HEAD_DIM
    tl = tokens.shape[0] * nz
    ff = gate_weight.shape[1]
    token_index = seq_index * tl + jnp.arange(tl, dtype=jnp.int32)
    cos, sin = turn_tables(token_index - doc_starts(doc_lengths, token_index))
    share = ns // heads
    sources = jnp.stack([source_of(seq_index % share, i, ns, share) for i in range(ns // share)])
    starts = doc_starts(doc_lengths, sources[:, None] * tl + jnp.arange(tl, dtype=jnp.int32)[None, :])
    gq = lax.dynamic_slice_in_dim(q_gain, head_index * lw, lw)[None]
    gk = lax.dynamic_slice_in_dim(k_gain, head_index * lw, lw)[None]

    w_od = lax.all_gather(jnp.concatenate([o_weight, down_weight], axis=0), "seq", axis=0)
    w_gu = lax.all_gather(jnp.concatenate([gate_weight, up_weight], axis=1), "seq", axis=0, tiled=True)
    x, w_qkv, q_raw, k_raw, totals, q_rot, k_rot, v_low = run_project(
        nz, ns, tokens, q_weight, k_weight, v_weight, gq, gk, cos, sin
    )
    attended, q_held, k_held, v_held, o_held, lse = run_attend(ns, heads, q_rot, k_rot, v_low, starts)
    output, h1r, branch, hidden, dy2, dg, du, mlp_part = run_forward(
        nz, ns, attended, tokens, cotangent, w_od, w_gu, attn_gain[None], mlp_gain[None]
    )
    grad_gate = scatter_grad(mm(h1r, dg, TN))
    grad_up = scatter_grad(mm(h1r, du, TN))
    grad_down = scatter_grad(mm(dy2, hidden, TN))
    middle, dy1, datt, attn_part = run_backward(nz, ns, dg, du, cotangent, branch, w_od, w_gu, attn_gain[None])
    dq, dk, dv = run_attend_back(ns, heads, datt, starts, q_held, k_held, v_held, o_held, lse)
    input_grad, grad_q, grad_k, grad_v, grad_o, gains = run_input(
        nz, ns, dq, dk, dv, q_raw, k_raw, totals, gq, gk, cos, sin, x, w_qkv, middle, attended, dy1, attn_part, mlp_part
    )
    return (
        output,
        input_grad,
        grad_q,
        grad_k,
        grad_v,
        grad_o,
        grad_gate.astype(F32),
        grad_up.astype(F32),
        grad_down.astype(F32).T,
        gains[0],
        gains[1],
        gains[2],
        gains[3],
    )


def solution(mesh):
    in_specs = (
        P(("seq", "head"), None),
        P(("seq", "head"), None),
        P(),
        P("seq", "head"),
        P("seq", "head"),
        P("seq", "head"),
        P("head", "seq"),
        P("seq", "head"),
        P("seq", "head"),
        P("head", "seq"),
        P(),
        P(),
        P(),
        P(),
    )
    out_specs = (
        P(("seq", "head"), None),
        P(("seq", "head"), None),
        P("seq", "head"),
        P("seq", "head"),
        P("seq", "head"),
        P("head", "seq"),
        P("seq", "head"),
        P("seq", "head"),
        P("head", "seq"),
        P("seq"),
        P("seq"),
        P("seq"),
        P("seq"),
    )
    return jax.shard_map(
        on_device, mesh=mesh, in_specs=in_specs, out_specs=out_specs, check_vma=False
    )
```

```python
import functools

import jax
import jax.numpy as jnp
from jax import lax
from jax.experimental import pallas as pl
from jax.experimental.pallas import tpu as pltpu
from jax.sharding import PartitionSpec as P

HEAD_DIM = 128
epsilon = 1e-06
rope_base = 500000.0

MESH = pl.DeviceIdType.MESH
F32 = jnp.float32
BF16 = jnp.bfloat16
STEPS = 4
LAG = 1
AG_CHUNKS = 2
VMEM_BYTES = 62 * 1024 * 1024
ANY = pl.BlockSpec(memory_space=pl.ANY)
VMEM = pl.BlockSpec(memory_space=pltpu.VMEM)
NN = (((1,), (0,)), ((), ()))
NT = (((1,), (1,)), ((), ()))
TN = (((0,), (0,)), ((), ()))


def mm(left, right, dims=NN):
    return lax.dot_general(left, right, dims, preferred_element_type=F32)


def rows_at(index, count):
    return pl.ds(pl.multiple_of(index * count, count), count)


def cube_barrier(s, z, ns, n):
    bar = pltpu.get_barrier_semaphore()
    bits = [1 << i for i in range(ns.bit_length() - 1)]
    for bit in bits:
        pl.semaphore_signal(bar, inc=1, device_id={"seq": s ^ bit}, device_id_type=MESH)
    for other, there in ((z - 1, z > 0), (z + 1, z < n - 1)):

        @pl.when(there)
        def _():
            pl.semaphore_signal(bar, inc=1, device_id={"head": other}, device_id_type=MESH)

    pl.semaphore_wait(bar, len(bits) + (z > 0).astype(jnp.int32) + (z < n - 1).astype(jnp.int32))


def line_gather(z, n, buf, rows, send_sem, recv_sem, use, hooks=(), ready=None):
    part = rows // AG_CHUNKS

    def copy(src, c, up):
        at = pl.ds(pl.multiple_of(src * rows + c * part, part), part)
        return pltpu.make_async_remote_copy(
            src_ref=buf.at[at],
            dst_ref=buf.at[at],
            send_sem=send_sem.at[up, src, c],
            recv_sem=recv_sem.at[src, c],
            device_id={"head": z + 1 if up else z - 1},
            device_id_type=MESH,
        )

    more = (z > 0, z < n - 1)
    for c in range(AG_CHUNKS):
        for up in (0, 1):

            @pl.when(more[up])
            def _():
                copy(z, c, up).start()

    if ready is not None:
        ready()
    use(z)

    @pl.loop(1, n)
    def _(k):
        sides = ((z + k, z + k < n, 0), (z - k, z - k >= 0, 1))
        for c in range(AG_CHUNKS):
            for src, there, up in sides:

                @pl.when(there)
                def _():
                    copy(src, c, up).wait_recv()

                    @pl.when(more[up])
                    def _():
                        copy(src, c, up).start()

        for src, there, up in sides:

            @pl.when(there)
            def _():
                use(src)

        for i, hook in enumerate(hooks):
            pl.when(k == i + 1)(hook)

    @pl.loop(0, n)
    def _(src):
        for c in range(AG_CHUNKS):

            @pl.when((src >= z) & (z > 0))
            def _():
                copy(src, c, 0).wait_send()

            @pl.when((src <= z) & (z < n - 1))
            def _():
                copy(src, c, 1).wait_send()


class LineScatter:
    def __init__(self, z, n, partial, land, send_sem, recv_sem, total):
        self.z, self.n, self.partial, self.land, self.total = z, n, partial, land, total
        self.send_sem, self.recv_sem = send_sem, recv_sem

    def copy(self, d, c, up):
        return pltpu.make_async_remote_copy(
            src_ref=self.land.at[up, d, c],
            dst_ref=self.land.at[up, d, c],
            send_sem=self.send_sem.at[up, d, c],
            recv_sem=self.recv_sem.at[up, d, c],
            device_id={"head": self.z + 1 if up else self.z - 1},
            device_id_type=MESH,
        )

    @property
    def slots(self):
        return (self.n - 1) * (STEPS + LAG)

    def run(self, low, high, before=None, after=None):
        z, n, land = self.z, self.n, self.land

        @pl.loop(low, high)
        def _(slot):
            if before is not None:
                before(slot)
            for up in (1, 0):
                t = slot - (z if up else n - 1 - z) * LAG
                j = t // STEPS
                c = t - j * STEPS
                d = n - 1 - j if up else j
                first = z == 0 if up else z == n - 1
                there = (t >= 0) & (j < n - 1) & ((d > z) if up else (d < z))

                @pl.when(there)
                def _():
                    mine = self.partial(d, c)

                    @pl.when(first)
                    def _():
                        land[up, d, c] = mine.astype(land.dtype)

                    @pl.when(jnp.logical_not(first))
                    def _():
                        self.copy(d, c, up).wait_recv()
                        land[up, d, c] = (land[up, d, c].astype(F32) + mine).astype(land.dtype)

                    self.copy(d, c, up).start()

            if after is not None:
                after(slot)

    def start_own(self):
        width = self.total.shape[1] // STEPS

        @pl.loop(0, STEPS)
        def _(c):
            self.total[:, rows_at(c, width)] = self.partial(self.z, c)

    def own(self):
        z, n, total = self.z, self.n, self.total
        width = total.shape[1] // STEPS

        @pl.loop(0, STEPS)
        def _(c):
            at = rows_at(c, width)
            for there, up in ((z > 0, 1), (z < n - 1, 0)):

                @pl.when(there)
                def _():
                    self.copy(z, c, up).wait_recv()
                    total[:, at] += self.land[up, z, c].astype(F32)

    def finish(self):
        @pl.loop(0, self.n * STEPS)
        def _(t):
            d, c = t // STEPS, t % STEPS
            for there, up in ((d > self.z, 1), (d < self.z, 0)):

                @pl.when(there)
                def _():
                    self.copy(d, c, up).wait_send()


def line_sems(n):
    dma = pltpu.SemaphoreType.DMA
    return {
        "gather": [dma((2, n, AG_CHUNKS)), dma((n, AG_CHUNKS))],
        "scatter": [dma((2, n, STEPS)), dma((2, n, STEPS))],
    }


BLOCK = 16


def row_scale(block):
    return lax.rsqrt(jnp.mean(block * block, axis=-1, keepdims=True) + epsilon)


def norm_back(e, normed, scale, gain):
    g = e * gain
    return scale * (g - normed * jnp.mean(g * normed, axis=-1, keepdims=True))


def sigmoid(x):
    return 1.0 / (1.0 + jnp.exp(-x))


def subsets(bits):
    found = [0]
    for bit in bits:
        found += [bit | other for other in found]
    return found


def orders_of(ns):
    chips = [1 << i for i in range(1, ns.bit_length() - 1)]
    return (chips, chips[::-1])


def remote(src, dst, send, recv, axis, to):
    return pltpu.make_async_remote_copy(
        src_ref=src, dst_ref=dst, send_sem=send, recv_sem=recv, device_id={axis: to}, device_id_type=MESH
    )


class CubeGather:
    def __init__(self, s, ns, buf, rows, send_sem, recv_sem):
        self.s, self.buf, self.rows, self.send_sem, self.recv_sem = s, buf, rows, send_sem, recv_sem
        self.orders = [order + [1] for order in orders_of(ns)]

    def copy(self, half, bit, block):
        part = self.rows // 2
        at = pl.ds(pl.multiple_of(block * self.rows + half * part, part), part)
        return remote(
            self.buf.at[at], self.buf.at[at],
            self.send_sem.at[bit.bit_length() - 1, block, half], self.recv_sem.at[block, half],
            "seq", self.s ^ bit,
        )

    @property
    def levels(self):
        return len(self.orders[0])

    def start(self):
        for i in range(self.levels):
            for half, order in enumerate(self.orders):
                self.copy(half, order[i], self.s).start()

    def level(self, i):
        for j in range(2**i):
            for half, order in enumerate(self.orders):
                block = self.s ^ order[i] ^ subsets(order[:i])[j]
                self.copy(half, order[i], block).wait_recv()
                for bit in order[i + 1 :]:
                    self.copy(half, bit, block).start()

    def finish(self):
        for half, order in enumerate(self.orders):
            for i, bit in enumerate(order):
                for other in subsets(order[:i]):
                    self.copy(half, bit, self.s ^ other).wait_send()

    @staticmethod
    def sems(ns):
        dma = pltpu.SemaphoreType.DMA
        return [dma((ns.bit_length() - 1, ns, 2)), dma((ns, 2))]


class CubeScatter:
    def __init__(self, s, ns, block, rows, first, held, later, sems):
        self.s, self.block, self.rows = s, block, rows
        self.first, self.held, self.later = first, held, later
        self.send0, self.recv0, self.send1, self.recv1 = sems
        self.orders = orders_of(ns)
        self.half = ns // 2

    def core_copy(self, j):
        return remote(self.first.at[j], self.held.at[j], self.send0.at[j], self.recv0.at[j], "seq", self.s ^ 1)

    def send_core(self, j=None):
        if j is None:
            pl.loop(0, self.half)(self.send_core)
            return
        j = self.half - 1 - j
        self.first[j] = self.block(self.s ^ (2 * j + 1)).astype(BF16)
        self.core_copy(j).start()

    def base(self, i):
        return sum(2 ** (self.stages - 1 - k) for k in range(i))

    def move(self, i, half, slot, other):
        part = self.rows // 2
        return remote(
            self.held.at[(self.orders[half][i] | other) >> 1, pl.ds(half * part, part)],
            self.later.at[half, slot], self.send1.at[half, slot], self.recv1.at[half, slot],
            "seq", self.s ^ self.orders[half][i],
        )

    def moves(self, i):
        part = self.rows // 2
        for half, order in enumerate(self.orders):
            for j, other in enumerate(subsets(order[i + 1 :])):
                slot = self.base(i) + j
                yield other >> 1, pl.ds(half * part, part), half, slot, self.move(i, half, slot, other)

    def add_core(self, j=None):
        if j is None:
            pl.loop(0, self.half)(self.add_core)
            return
        j = self.half - 1 - j
        mine = self.block(self.s ^ (2 * j))
        self.core_copy(j).wait_recv()
        self.held[j] = (self.held[j].astype(F32) + mine).astype(BF16)
        for half, order in enumerate(self.orders):
            for slot, other in enumerate(subsets(order[1:])):

                @pl.when(j == (order[0] | other) >> 1)
                def _():
                    self.move(0, half, slot, other).start()

    def send(self, i):
        for *_, copy in self.moves(i):
            copy.start()

    def take(self, i):
        for j, at, half, slot, copy in self.moves(i):
            copy.wait_recv()
            self.held[j, at] = (self.held[j, at].astype(F32) + self.later[half, slot].astype(F32)).astype(BF16)

    def step(self, i):
        self.take(i)
        if i + 1 < self.stages:
            self.send(i + 1)

    @property
    def stages(self):
        return len(self.orders[0])

    def core_sent(self):
        @pl.loop(0, self.half)
        def _(j):
            self.core_copy(j).wait_send()

    def finish(self):
        for i in range(self.stages):
            for *_, copy in self.moves(i):
                copy.wait_send()

    @staticmethod
    def scratch(ns, rows, width):
        dma = pltpu.SemaphoreType.DMA
        half = ns // 2
        return [
            pltpu.VMEM((half, rows, width), BF16),
            pltpu.VMEM((half, rows, width), BF16),
            pltpu.VMEM((2, half - 1, rows // 2, width), BF16),
            dma((half,)), dma((half,)), dma((2, half - 1)), dma((2, half - 1)),
        ]


def forward_kernel(
    n, ns,
    att, tok, cot, w_in, gate, up, down, attn_gain, mlp_gain,
    out, h1r_out, branch_out, hidden_out, dy2_out, dg_out, du_out, gain_part, up_out,
    h1r, hidden, dy2, dg, du,
    wo, wd, wg, wu, land, branch, h1, second, g_pre, u_pre,
    wsem, osem, bsem, g1s, g1r, s1s, s1r, g2s, g2r, s2s, s2r, us, ur, ds, dr,
):
    s, z = lax.axis_index("seq"), lax.axis_index("head")
    rows, depth = tok.shape
    lw, ff = att.shape[1], up.shape[1]
    block = depth // ns
    width = depth // STEPS
    mine = rows_at(s, block)
    l_o = pltpu.make_async_copy(w_in.at[:, pl.ds(3 * lw, lw)], wo, wsem.at[0])
    l_u = pltpu.make_async_copy(up, wu.at[mine], wsem.at[1])
    l_g = pltpu.make_async_copy(gate, wg, wsem.at[2])
    for copy in (l_o, l_u, l_g):
        copy.start()
    cube_barrier(s, z, ns, n)
    cube_u = CubeGather(s, ns, wu, block, us, ur)
    cube_d = CubeGather(s, ns, wd, block, ds, dr)
    levels = cube_u.levels
    l_u.wait()
    cube_u.start()
    l_o.wait()

    def out_part(d, c):
        return mm(att[rows_at(d, rows), :], wo[rows_at(c, width), :], NT)

    line = LineScatter(z, n, out_part, land, s1s, s1r, branch)
    line.run(0, STEPS)
    line.start_own()
    wd[mine, :] = jnp.transpose(down[...].astype(F32)).astype(BF16)
    cube_u.level(0)
    line.run(STEPS, 2 * STEPS)
    for i in range(1, levels - 1):
        cube_u.level(i)
    cube_d.start()
    line.run(2 * STEPS, line.slots)
    line.own()
    line.finish()
    o_branch = pltpu.make_async_copy(branch, branch_out, osem.at[0])
    o_branch.start()
    gain_part[...] = jnp.zeros_like(gain_part)

    @pl.loop(0, rows // BLOCK)
    def _(i):
        at = rows_at(i, BLOCK)
        y = branch[at, :]
        h = tok[at, :].astype(F32) + y * row_scale(y) * attn_gain[...]
        h1[at, :] = h
        h1r[pl.ds(pl.multiple_of(z * rows + i * BLOCK, BLOCK), BLOCK), :] = h.astype(BF16)

    fw = ff // STEPS
    o_up = pltpu.make_async_copy(wu, up_out, osem.at[1])
    o_h1r = pltpu.make_async_copy(h1r, h1r_out, osem.at[2])
    o_hidden = pltpu.make_async_copy(hidden, hidden_out, osem.at[3])
    o_dy2 = pltpu.make_async_copy(dy2, dy2_out, osem.at[4])

    def up_block(src):
        at = rows_at(src, rows)

        @pl.loop(0, STEPS)
        def _(c):
            cols = rows_at(c, fw)
            x = h1r[at, :]
            g = mm(x, wg[:, cols])
            u = mm(x, wu[:, cols])
            g_pre[at, cols] = g
            u_pre[at, cols] = u
            hidden[at, cols] = (g * sigmoid(g) * u).astype(BF16)

    def weights_there():
        l_g.wait()
        cube_u.level(levels - 1)
        o_up.start()

    hooks = [functools.partial(cube_d.level, i) for i in range(levels)]
    line_gather(z, n, h1r, rows, g1s, g1r, up_block, hooks[: n - 1], weights_there)
    for hook in hooks[n - 1 :]:
        hook()
    o_h1r.start()
    o_hidden.start()

    def down_part(d, c):
        return mm(hidden[rows_at(d, rows), :], wd[rows_at(c, width), :], NT)

    line = LineScatter(z, n, down_part, land, s2s, s2r, second)
    line.run(0, STEPS)
    line.start_own()
    line.run(STEPS, line.slots)
    line.own()
    line.finish()

    @pl.loop(0, rows // BLOCK)
    def _(i):
        at = rows_at(i, BLOCK)
        y = second[at, :]
        scale = row_scale(y)
        normed = y * scale
        e = cot[at, :].astype(F32)
        out[at, :] = (h1[at, :] + normed * mlp_gain[...]).astype(BF16)
        gain_part[...] += jnp.sum(e * normed, axis=0, keepdims=True)
        dy2[pl.ds(pl.multiple_of(z * rows + i * BLOCK, BLOCK), BLOCK), :] = norm_back(
            e, normed, scale, mlp_gain[...]
        ).astype(BF16)

    def back_block(src):
        at = rows_at(src, rows)

        @pl.loop(0, STEPS)
        def _(c):
            cols = rows_at(c, fw)
            dh = mm(dy2[at, :], wd[:, cols])
            g = g_pre[at, cols]
            u = u_pre[at, cols]
            sig = sigmoid(g)
            du[at, cols] = (dh * g * sig).astype(BF16)
            dg[at, cols] = (dh * u * sig * (1.0 + g * (1.0 - sig))).astype(BF16)

        for copy in grads_out(src):
            copy.start()

    def grads_out(src):
        at = rows_at(src, rows)
        return [
            pltpu.make_async_copy(held.at[at], to.at[at], bsem.at[i, src])
            for i, (held, to) in enumerate(((dg, dg_out), (du, du_out)))
        ]

    line_gather(z, n, dy2, rows, g2s, g2r, back_block)
    o_dy2.start()
    for copy in (o_branch, o_up, o_h1r, o_hidden, o_dy2):
        copy.wait()

    @pl.loop(0, n)
    def _(src):
        for copy in grads_out(src):
            copy.wait()

    cube_u.finish()
    cube_d.finish()


def run_forward(n, ns, att, tok, cot, w, gate, up, down, attn_gain, mlp_gain):
    rows, depth = tok.shape
    tl, lw = att.shape
    ff = up.shape[1]
    dma = pltpu.SemaphoreType.DMA
    sems = line_sems(n)
    shape = jax.ShapeDtypeStruct
    return pl.pallas_call(
        functools.partial(forward_kernel, n, ns),
        out_shape=(
            shape((rows, depth), BF16),
            shape((tl, depth), BF16),
            shape((rows, depth), F32),
            shape((tl, ff), BF16),
            shape((tl, depth), BF16),
            shape((tl, ff), BF16),
            shape((tl, ff), BF16),
            shape((1, depth), F32),
            shape((depth, ff), BF16),
        ),
        in_specs=[VMEM, VMEM, VMEM, ANY, ANY, ANY, VMEM, VMEM, VMEM],
        out_specs=(VMEM, ANY, ANY, ANY, ANY, ANY, ANY, VMEM, ANY),
        scratch_shapes=[
            pltpu.VMEM((tl, depth), BF16),
            pltpu.VMEM((tl, ff), BF16),
            pltpu.VMEM((tl, depth), BF16),
            pltpu.VMEM((tl, ff), BF16),
            pltpu.VMEM((tl, ff), BF16),
            pltpu.VMEM((depth, lw), BF16),
            pltpu.VMEM((depth, ff), BF16),
            pltpu.VMEM((depth, ff), BF16),
            pltpu.VMEM((depth, ff), BF16),
            pltpu.VMEM((2, n, STEPS, rows, depth // STEPS), BF16),
            pltpu.VMEM((rows, depth), F32),
            pltpu.VMEM((rows, depth), F32),
            pltpu.VMEM((rows, depth), F32),
            pltpu.VMEM((tl, ff), F32),
            pltpu.VMEM((tl, ff), F32),
            dma((3,)),
            dma((5,)),
            dma((2, n)),
            *sems["gather"], *sems["scatter"], *sems["gather"], *sems["scatter"],
            *CubeGather.sems(ns), *CubeGather.sems(ns),
        ],
        compiler_params=pltpu.CompilerParams(
            collective_id=1, has_side_effects=True, vmem_limit_bytes=VMEM_BYTES
        ),
        cost_estimate=pl.CostEstimate(flops=18 * 10**9, bytes_accessed=40 * 10**6, transcendentals=2 * 10**6),
        name="feed_forward",
    )(att, tok, cot, w, gate, up, down, attn_gain, mlp_gain)


def backward_kernel(
    n, ns,
    dg, du, h1r_in, cot, branch, w_in, gate, up, attn_gain,
    middle, dy1, datt, gain_part, grad_gate, grad_up,
    h1r, wo, wg, wu, land, total,
    first, held_g, later_g, held_u, later_u,
    wsem, osem, s1s, s1r, g1s, g1r,
    ga, gb, gc, gd, ua, ub, uc, ud,
):
    s, z = lax.axis_index("seq"), lax.axis_index("head")
    rows, depth = cot.shape
    lw, ff = datt.shape[1], dg.shape[1]
    block = depth // ns
    width = depth // STEPS

    def weights_in(c):
        at = rows_at(c, width)
        return [
            pltpu.make_async_copy(m.at[at], to.at[at], wsem.at[i, c]) for i, (m, to) in enumerate(((gate, wg), (up, wu)))
        ]

    for c in range(STEPS):
        for copy in weights_in(c):
            copy.start()
    l_h = pltpu.make_async_copy(h1r_in, h1r, osem.at[0])
    l_o = pltpu.make_async_copy(w_in.at[:, pl.ds(3 * lw, lw)], wo, osem.at[1])
    l_h.start()
    l_o.start()
    cube_barrier(s, z, ns, n)

    def weight_block(grad):
        return lambda b: mm(h1r[:, rows_at(b, block)], grad[...], TN)

    cube_g = CubeScatter(s, ns, weight_block(dg), block, first, held_g, later_g, (ga, gb, gc, gd))
    cube_u = CubeScatter(s, ns, weight_block(du), block, first, held_u, later_u, (ua, ub, uc, ud))

    def in_part(d, c):
        at, cols = rows_at(d, rows), rows_at(c, width)
        return mm(dg[at, :], wg[cols, :], NT) + mm(du[at, :], wu[cols, :], NT)

    line = LineScatter(z, n, in_part, land, s1s, s1r, total)
    half = ns // 2

    def there(slot):
        @pl.when(slot < STEPS)
        def _():
            for copy in weights_in(slot):
                copy.wait()

    tasks = (cube_g.send_core, cube_g.add_core, cube_u.send_core)
    begin = STEPS - 1

    def task(slot):
        @pl.when(slot == begin)
        def _():
            l_h.wait()

        for i, act in enumerate(tasks):
            low = begin + i * half
            pl.when((slot >= low) & (slot < low + half))(functools.partial(task_of, act, slot - low, i))

    def task_of(act, j, i):
        if i == 2:
            cube_g.core_copy(half - 1 - j).wait_send()
        act(j)

    line.run(0, 2 * STEPS, there, task)
    line.start_own()
    line.run(2 * STEPS, line.slots, None, task)

    @pl.loop(line.slots, begin + 3 * half)
    def _(slot):
        task(slot)

    line.own()
    line.finish()
    gain_part[...] = jnp.zeros_like(gain_part)

    @pl.loop(0, rows // BLOCK)
    def _(i):
        at = rows_at(i, BLOCK)
        y = branch[at, :]
        scale = row_scale(y)
        normed = y * scale
        e = cot[at, :].astype(F32) + total[at, :]
        middle[at, :] = e
        gain_part[...] += jnp.sum(e * normed, axis=0, keepdims=True)
        dy1[pl.ds(pl.multiple_of(z * rows + i * BLOCK, BLOCK), BLOCK), :] = norm_back(
            e, normed, scale, attn_gain[...]
        ).astype(BF16)

    l_o.wait()

    def att_block(src):
        at = rows_at(src, rows)
        datt[at, :] = mm(dy1[at, :], wo[...]).astype(BF16)

    def second_cube():
        cube_u.add_core()
        cube_g.step(0)

    todo = [functools.partial(cube_g.step, i) for i in range(1, cube_g.stages)]
    todo += [functools.partial(cube_u.step, i) for i in range(cube_u.stages)]
    line_gather(z, n, dy1, rows, g1s, g1r, att_block, todo[: n - 1], second_cube)
    for step in todo[n - 1 :]:
        step()
    grad_gate[...] = held_g[0].astype(F32)
    grad_up[...] = held_u[0].astype(F32)
    cube_g.finish()
    cube_u.core_sent()
    cube_u.finish()


def run_backward(n, ns, dg, du, h1r, cot, branch, w, gate, up, attn_gain):
    rows, depth = cot.shape
    tl, ff = dg.shape
    lw = w.shape[1] // 4
    block = depth // ns
    dma = pltpu.SemaphoreType.DMA
    sems = line_sems(n)
    shape = jax.ShapeDtypeStruct
    first, held, later, *cube_sems = CubeScatter.scratch(ns, block, ff)
    return pl.pallas_call(
        functools.partial(backward_kernel, n, ns),
        out_shape=(
            shape((rows, depth), F32),
            shape((tl, depth), BF16),
            shape((tl, lw), BF16),
            shape((1, depth), F32),
            shape((block, ff), F32),
            shape((block, ff), F32),
        ),
        in_specs=[VMEM, VMEM, ANY, VMEM, VMEM, ANY, ANY, ANY, VMEM],
        out_specs=(VMEM,) * 6,
        scratch_shapes=[
            pltpu.VMEM((tl, depth), BF16),
            pltpu.VMEM((depth, lw), BF16),
            pltpu.VMEM((depth, ff), BF16),
            pltpu.VMEM((depth, ff), BF16),
            pltpu.VMEM((2, n, STEPS, rows, depth // STEPS), BF16),
            pltpu.VMEM((rows, depth), F32),
            first, held, later, held, later,
            dma((2, STEPS)),
            dma((2,)),
            *sems["scatter"], *sems["gather"],
            *cube_sems, *cube_sems,
        ],
        compiler_params=pltpu.CompilerParams(
            collective_id=2, has_side_effects=True, vmem_limit_bytes=VMEM_BYTES
        ),
        cost_estimate=pl.CostEstimate(flops=18 * 10**9, bytes_accessed=30 * 10**6, transcendentals=0),
        name="into_attention",
    )(dg, du, h1r, cot, branch, w, gate, up, attn_gain)


LOG2E = 1.4426950408889634
NEG = -1e30


def seq_barrier(s, ns):
    bar = pltpu.get_barrier_semaphore()
    for other in range(ns):

        @pl.when(other != s)
        def _():
            pl.semaphore_signal(bar, inc=1, device_id={"seq": other}, device_id_type=MESH)

    pl.semaphore_wait(bar, ns - 1)


def share_of(s, ns, r):
    per = ns // (2 * r)
    chunk = s // per
    low = chunk < r
    sub = jnp.where(low, chunk, 2 * r - 1 - chunk)
    return sub, jnp.where(low, s - chunk * per, per + s - chunk * per)


def source_of(sub, i, ns, r):
    per = ns // (2 * r)
    return jnp.where(i < per, sub * per + i, (2 * r - 1 - sub) * per + i - per)


def head_cols(h):
    return pl.ds(pl.multiple_of(h * HEAD_DIM, HEAD_DIM), HEAD_DIM)


def attend_kernel(
    ns, heads, q_in, k_in, v_in, starts, gate,
    att, q_buf, k_buf, v_buf, o_buf, lse, gate_out,
    o_low, qs, qr, ks, kr, vs, vr, osend, orecv, local, cs, cr,
):
    s = lax.axis_index("seq")
    r = ns // heads
    blocks = ns // r
    tl = q_in.shape[0]
    mine, sub = s // r, s % r
    parity = s % 2
    seq_barrier(s, ns)
    to_sub, to_row = share_of(s, ns, r)

    def q_copy(h):
        return pltpu.make_async_remote_copy(
            src_ref=q_in.at[:, head_cols(h)],
            dst_ref=q_buf.at[rows_at(to_row, tl)],
            send_sem=qs.at[h],
            recv_sem=qr.at[to_row],
            device_id={"seq": h * r + to_sub},
            device_id_type=MESH,
        )

    def q_recv(i):
        return pltpu.make_async_remote_copy(
            src_ref=q_buf.at[rows_at(i, tl)],
            dst_ref=q_buf.at[rows_at(i, tl)],
            send_sem=qs.at[0],
            recv_sem=qr.at[i],
            device_id={"seq": s ^ 1},
            device_id_type=MESH,
        )

    def kv_copy(src, buf, send, recv, t, at):
        return pltpu.make_async_remote_copy(
            src_ref=src,
            dst_ref=buf.at[rows_at(at, tl)],
            send_sem=send,
            recv_sem=recv.at[at],
            device_id={"seq": t},
            device_id_type=MESH,
        )

    kv = ((k_in, k_buf, ks, kr), (v_in, v_buf, vs, vr))
    own = [pltpu.make_async_copy(x.at[:, head_cols(mine)], buf.at[rows_at(s, tl)], local.at[i])
           for i, (x, buf, _, _) in enumerate(kv)]
    own_q = pltpu.make_async_copy(q_in.at[:, head_cols(mine)], q_buf.at[rows_at(to_row, tl)], local.at[2])
    block = gate.shape[0]
    own_gate = pltpu.make_async_copy(gate, gate_out.at[rows_at(s, block)], local.at[4])
    cube = CubeGather(s, ns, gate_out, block, cs, cr)
    for copy in own + [own_gate]:
        copy.start()

    @pl.when(to_sub == sub)
    def _():
        own_q.start()

    def far(t):
        return (t != s) & (t % 2 == parity)

    @pl.loop(1, ns)
    def _(step):
        t = s ^ step

        @pl.when(far(t))
        def _():
            for x, buf, ss, rs in kv:
                kv_copy(x.at[:, head_cols(t // r)], buf, ss.at[0, t], rs, t, s).start()

    @pl.loop(0, heads)
    def _(h):
        @pl.when(h * r + to_sub != s)
        def _():
            q_copy(h).start()

    for copy in own:
        copy.wait()

    def pass_on(src, start):
        for _, buf, ss, rs in kv:
            copy = kv_copy(buf.at[rows_at(src, tl)], buf, ss.at[1, src], rs, s ^ 1, src)
            if start:
                copy.start()
            else:
                copy.wait_send()

    pass_on(s, True)

    @pl.loop(1, ns)
    def _(step):
        src = s ^ step

        @pl.when(far(src))
        def _():
            for x, buf, ss, rs in kv:
                kv_copy(buf.at[rows_at(src, tl)], buf, ss.at[0, 0], rs, s ^ 1, src).wait_recv()
            pass_on(src, True)

    @pl.loop(0, ns)
    def _(src):
        @pl.when(src % 2 != parity)
        def _():
            for x, buf, ss, rs in kv:
                kv_copy(buf.at[rows_at(src, tl)], buf, ss.at[0, 0], rs, s ^ 1, src).wait_recv()

    @pl.when(to_sub == sub)
    def _():
        own_q.wait()

    unit = HEAD_DIM ** (-0.5) * LOG2E

    def o_copy(i, t):
        return pltpu.make_async_remote_copy(
            src_ref=o_low.at[rows_at(i, tl)],
            dst_ref=att.at[:, head_cols(mine)],
            send_sem=osend.at[i],
            recv_sem=orecv.at[mine],
            device_id={"seq": t},
            device_id_type=MESH,
        )

    own_o = pltpu.make_async_copy(o_low.at[rows_at(to_row, tl)], att.at[:, head_cols(mine)], local.at[3])

    def attend_block(i):
        src = source_of(sub, i, ns, r)

        @pl.when(src != s)
        def _():
            q_recv(i).wait_recv()

        q = q_buf[rows_at(i, tl), :]
        start = starts[pl.ds(i, 1), :]
        key_at = lax.broadcasted_iota(jnp.int32, (tl, tl), 0)

        def step(j, carry, diagonal):
            top, total, acc = carry
            at = rows_at(j, tl)
            scores = mm(k_buf[at, :], q, NT) * unit
            allowed = key_at >= start - j * tl
            if diagonal:
                allowed = allowed & (key_at <= lax.broadcasted_iota(jnp.int32, (tl, tl), 1))
            scores = jnp.where(allowed, scores, NEG)
            new = jnp.maximum(top, jnp.max(scores, axis=0, keepdims=True))
            terms = jnp.exp2(scores - new)
            fade = jnp.exp2(top - new)
            return (
                new,
                total * fade + jnp.sum(terms, axis=0, keepdims=True),
                acc * fade + mm(v_buf[at, :], terms.astype(BF16), TN),
            )

        carry = (
            jnp.full((1, tl), NEG, F32),
            jnp.zeros((1, tl), F32),
            jnp.zeros((HEAD_DIM, tl), F32),
        )
        carry = lax.fori_loop(0, src, lambda j, c: step(j, c, False), carry)
        top, total, acc = step(src, carry, True)
        lse[pl.ds(i, 1), :] = top + jnp.log(total) * LOG2E
        o = jnp.transpose(acc / total)
        o_buf[rows_at(i, tl), :] = o
        o_low[rows_at(i, tl), :] = o.astype(BF16)

        @pl.when(src != s)
        def _():
            o_copy(i, src).start()

        @pl.when(src == s)
        def _():
            own_o.start()

    own_gate.wait()
    cube.start()
    cuts = [0, blocks - 1, blocks, blocks]
    for i in range(3):
        pl.loop(cuts[i], cuts[i + 1])(attend_block)
        if i < 2:
            cube.level(i)
    for i in range(2, cube.levels):
        cube.level(i)

    @pl.when(to_sub == sub)
    def _():
        own_o.wait()

    @pl.loop(0, heads)
    def _(h):
        @pl.when(h * r + to_sub != s)
        def _():
            q_copy(h).wait_send()
            pltpu.make_async_remote_copy(
                src_ref=o_low.at[rows_at(0, tl)],
                dst_ref=att.at[:, head_cols(h)],
                send_sem=osend.at[0],
                recv_sem=orecv.at[h],
                device_id={"seq": s ^ 1},
                device_id_type=MESH,
            ).wait_recv()

    @pl.loop(0, blocks)
    def _(i):
        src = source_of(sub, i, ns, r)

        @pl.when(src != s)
        def _():
            o_copy(i, src).wait_send()

    pass_on(s, False)

    @pl.loop(1, ns)
    def _(step):
        t = s ^ step

        @pl.when(far(t))
        def _():
            for x, buf, ss, rs in kv:
                kv_copy(x.at[:, head_cols(t // r)], buf, ss.at[0, t], rs, t, s).wait_send()
            pass_on(t, False)

    cube.finish()


def run_attend(ns, heads, q, k, v, starts, gate):
    tl, lw = q.shape
    r = ns // heads
    nq = ns // r * tl
    nk = ns * tl
    dma = pltpu.SemaphoreType.DMA
    shape = jax.ShapeDtypeStruct
    return pl.pallas_call(
        functools.partial(attend_kernel, ns, heads),
        out_shape=(
            shape((tl, lw), BF16),
            shape((nq, HEAD_DIM), BF16),
            shape((nk, HEAD_DIM), BF16),
            shape((nk, HEAD_DIM), BF16),
            shape((nq, HEAD_DIM), F32),
            shape((ns // r, tl), F32),
            shape((gate.shape[0] * ns, gate.shape[1]), BF16),
        ),
        in_specs=[VMEM] * 4 + [ANY],
        out_specs=(VMEM,) * 6 + (ANY,),
        scratch_shapes=[
            pltpu.VMEM((nq, HEAD_DIM), BF16),
            dma((heads,)), dma((ns // r,)),
            dma((2, ns)), dma((ns,)),
            dma((2, ns)), dma((ns,)),
            dma((ns // r,)), dma((heads,)),
            dma((5,)),
            *CubeGather.sems(ns),
        ],
        compiler_params=pltpu.CompilerParams(
            collective_id=3, has_side_effects=True, vmem_limit_bytes=VMEM_BYTES
        ),
        cost_estimate=pl.CostEstimate(flops=3 * 10**9, bytes_accessed=8 * 10**6, transcendentals=5 * 10**6),
        name="attend",
    )(q, k, v, starts, gate)


def attend_back_kernel(
    ns, heads, do_in, starts, q_buf, k_buf, v_buf, o_buf, lse, dy2, hidden,
    dq, dk, dv, grad_down,
    do_buf, dq_low, dk_acc, dv_acc, low, pair, land,
    first, held, later, ca, cb, cc, cd,
    ds_, dr_, ps, pr, gs, gr, qs, qr, local,
):
    s = lax.axis_index("seq")
    r = ns // heads
    blocks = ns // r
    tl = do_in.shape[0]
    mine, sub = s // r, s % r
    parity = s % 2
    seq_barrier(s, ns)
    to_sub, to_row = share_of(s, ns, r)

    def copy(src, dst, send, recv, t):
        return pltpu.make_async_remote_copy(
            src_ref=src, dst_ref=dst, send_sem=send, recv_sem=recv, device_id={"seq": t}, device_id_type=MESH
        )

    def do_copy(h):
        return copy(
            do_in.at[:, head_cols(h)], do_buf.at[rows_at(to_row, tl)], ds_.at[h], dr_.at[to_row], h * r + to_sub
        )

    own_do = pltpu.make_async_copy(do_in.at[:, head_cols(mine)], do_buf.at[rows_at(to_row, tl)], local.at[0])

    @pl.when(to_sub == sub)
    def _():
        own_do.start()

    @pl.loop(0, heads)
    def _(h):
        @pl.when(h * r + to_sub != s)
        def _():
            do_copy(h).start()

    block = dy2.shape[1] // ns
    cube = CubeScatter(
        s, ns, lambda b: mm(dy2[:, rows_at(b, block)], hidden[...], TN), block, first, held, later, (ca, cb, cc, cd)
    )
    cube.send_core()
    dk_acc[...] = jnp.zeros_like(dk_acc)
    dv_acc[...] = jnp.zeros_like(dv_acc)
    cube.add_core()

    @pl.when(to_sub == sub)
    def _():
        own_do.wait()

    scale = HEAD_DIM ** (-0.5)
    unit = scale * LOG2E

    def dq_copy(i, t):
        return copy(dq_low.at[rows_at(i, tl)], dq.at[:, head_cols(mine)], qs.at[i], qr.at[mine], t)

    own_dq = pltpu.make_async_copy(dq_low.at[rows_at(to_row, tl)], dq.at[:, head_cols(mine)], local.at[1])
    ones = jnp.ones((8, HEAD_DIM), F32)

    def back_block(i):
        src = source_of(sub, i, ns, r)
        rows = rows_at(i, tl)

        @pl.when(src != s)
        def _():
            copy(do_buf.at[rows], do_buf.at[rows], ds_.at[0], dr_.at[i], s ^ 1).wait_recv()

        q = q_buf[rows, :]
        do = do_buf[rows, :]
        start = starts[pl.ds(i, 1), :]
        norm = lse[pl.ds(i, 1), :]
        delta = lax.dot_general(
            ones, do.astype(F32) * o_buf[rows, :], NT,
            precision=lax.Precision.HIGHEST, preferred_element_type=F32,
        )[:1]
        key_at = lax.broadcasted_iota(jnp.int32, (tl, tl), 0)

        def step(j, dq_sum, diagonal):
            at = rows_at(j, tl)
            keys = k_buf[at, :]
            scores = mm(keys, q, NT) * unit
            allowed = key_at >= start - j * tl
            if diagonal:
                allowed = allowed & (key_at <= lax.broadcasted_iota(jnp.int32, (tl, tl), 1))
            p = jnp.where(allowed, jnp.exp2(scores - norm), 0.0)
            dp = mm(v_buf[at, :], do, NT)
            dscore = (p * (dp - delta)).astype(BF16)
            dv_acc[at, :] += mm(p.astype(BF16), do)
            dk_acc[at, :] += mm(dscore, q)
            return dq_sum + mm(dscore, keys, TN)

        dq_sum = lax.fori_loop(0, src, lambda j, c: step(j, c, False), jnp.zeros((tl, HEAD_DIM), F32))
        dq_sum = step(src, dq_sum, True)
        dq_low[rows, :] = (dq_sum * scale).astype(BF16)

        @pl.when(src != s)
        def _():
            dq_copy(i, src).start()

        @pl.when(src == s)
        def _():
            own_dq.start()

    pl.loop(0, blocks - 1)(back_block)
    cube.step(0)
    pl.loop(blocks - 1, blocks)(back_block)
    half = ns // 2

    def pair_copy(w, i):
        src = 2 * i + 1 - parity
        return copy(low.at[w, rows_at(src, tl)], pair.at[w, rows_at(i, tl)], ps.at[w, i], pr.at[w, i], s ^ 1)

    @pl.loop(0, half)
    def _(i):
        at = rows_at(2 * i + 1 - parity, tl)
        low[0, at, :] = (dk_acc[at, :] * scale).astype(BF16)
        pair_copy(0, i).start()
        low[1, at, :] = dv_acc[at, :].astype(BF16)
        pair_copy(1, i).start()

    slot = sub // 2
    outs = (dk, dv)

    def back_copy(w, i):
        dest = 2 * i + parity
        return copy(
            low.at[w, rows_at(dest, tl)], land.at[w, slot, :, head_cols(mine)], gs.at[w, i], gr.at[w, mine, slot], dest
        )

    @pl.loop(0, half)
    def _(i):
        dest = 2 * i + parity
        at = rows_at(dest, tl)
        for w, acc, factor in ((0, dk_acc, scale), (1, dv_acc, 1.0)):
            copy(low.at[w, at], pair.at[w, rows_at(i, tl)], ps.at[w, i], pr.at[w, i], s ^ 1).wait_recv()
            low[w, at, :] = (acc[at, :] * factor + pair[w, rows_at(i, tl), :].astype(F32)).astype(BF16)

            @pl.when(dest != s)
            def _():
                back_copy(w, i).start()

            @pl.when(dest == s)
            def _():
                land[w, slot, :, head_cols(mine)] = low[w, at, :]

    @pl.loop(0, heads)
    def _(h):
        for w in range(2):
            for k in range(r // 2):

                @pl.when(h * r + 2 * k + parity != s)
                def _():
                    copy(
                        low.at[w, rows_at(0, tl)], land.at[w, k, :, head_cols(h)], gs.at[w, 0], gr.at[w, h, k], s ^ 1
                    ).wait_recv()

    for w in range(2):
        outs[w][...] = functools.reduce(
            lambda a, b: a + b, [land[w, k].astype(F32) for k in range(r // 2)]
        ).astype(BF16)

    @pl.when(to_sub == sub)
    def _():
        own_dq.wait()

    @pl.loop(0, heads)
    def _(h):
        @pl.when(h * r + to_sub != s)
        def _():
            do_copy(h).wait_send()
            copy(dq_low.at[rows_at(0, tl)], dq.at[:, head_cols(h)], qs.at[0], qr.at[h], s ^ 1).wait_recv()

    @pl.loop(0, blocks)
    def _(i):
        src = source_of(sub, i, ns, r)

        @pl.when(src != s)
        def _():
            dq_copy(i, src).wait_send()

    @pl.loop(0, half)
    def _(i):
        for w in range(2):
            pair_copy(w, i).wait_send()

            @pl.when(2 * i + parity != s)
            def _():
                back_copy(w, i).wait_send()

    for i in range(1, cube.stages):
        cube.step(i)
    grad_down[...] = jnp.transpose(held[0].astype(F32))
    cube.core_sent()
    cube.finish()


def run_attend_back(ns, heads, do, starts, q, k, v, o, lse, dy2, hidden):
    tl, lw = do.shape
    r = ns // heads
    nq = ns // r * tl
    nk = ns * tl
    dma = pltpu.SemaphoreType.DMA
    shape = jax.ShapeDtypeStruct
    return pl.pallas_call(
        functools.partial(attend_back_kernel, ns, heads),
        out_shape=(shape((tl, lw), BF16),) * 3 + (shape((hidden.shape[1], dy2.shape[1] // ns), F32),),
        in_specs=[VMEM] * 9,
        out_specs=(VMEM,) * 4,
        scratch_shapes=[
            pltpu.VMEM((nq, HEAD_DIM), BF16),
            pltpu.VMEM((nq, HEAD_DIM), BF16),
            pltpu.VMEM((nk, HEAD_DIM), F32),
            pltpu.VMEM((nk, HEAD_DIM), F32),
            pltpu.VMEM((2, nk, HEAD_DIM), BF16),
            pltpu.VMEM((2, nk // 2, HEAD_DIM), BF16),
            pltpu.VMEM((2, r // 2, tl, lw), BF16),
            *CubeScatter.scratch(ns, dy2.shape[1] // ns, hidden.shape[1]),
            dma((heads,)), dma((ns // r,)),
            dma((2, ns // 2)), dma((2, ns // 2)),
            dma((2, ns // 2)), dma((2, heads, r // 2)),
            dma((ns // r,)), dma((heads,)),
            dma((2,)),
        ],
        compiler_params=pltpu.CompilerParams(
            collective_id=4, has_side_effects=True, vmem_limit_bytes=VMEM_BYTES
        ),
        cost_estimate=pl.CostEstimate(flops=8 * 10**9, bytes_accessed=10 * 10**6, transcendentals=5 * 10**6),
        name="attend_back",
    )(do, starts, q, k, v, o, lse, dy2, hidden)


def cross_barrier(s, z, ns, n):
    bar = pltpu.get_barrier_semaphore()
    for axis, me, count in (("seq", s, ns), ("head", z, n)):
        for other in range(count):

            @pl.when(other != me)
            def _():
                pl.semaphore_signal(bar, inc=1, device_id={axis: other}, device_id_type=MESH)

    pl.semaphore_wait(bar, ns - 1 + n - 1)


def row_sums(left, right):
    ones = jnp.ones((8, left.shape[1]), F32)
    both = [
        lax.dot_general(ones, x, NT, precision=lax.Precision.HIGHEST, preferred_element_type=F32) for x in (left, right)
    ]
    return jnp.where(lax.broadcasted_iota(jnp.int32, both[0].shape, 0) < 4, both[0], both[1])


def as_column(sums, row):
    pick = (lax.broadcasted_iota(jnp.int32, (8, HEAD_DIM), 0) == row).astype(F32)
    return lax.dot_general(sums, pick, TN, precision=lax.Precision.HIGHEST, preferred_element_type=F32)


class SmallExchange:
    def __init__(self, axis, me, count, land, send_sem, recv_sem):
        self.axis, self.me, self.count, self.land = axis, me, count, land
        self.send_sem, self.recv_sem = send_sem, recv_sem

    def copy(self, slot, to):
        return remote(self.land.at[slot], self.land.at[slot], self.send_sem.at[to], self.recv_sem.at[slot], self.axis, to)

    def each(self, act):
        @pl.loop(0, self.count)
        def _(other):
            @pl.when(other != self.me)
            def _():
                act(other)

    def start(self):
        self.each(lambda other: self.copy(self.me, other).start())

    def receive(self):
        self.each(lambda other: self.copy(other, other).wait_recv())

    def finish(self):
        self.each(lambda other: self.copy(self.me, other).wait_send())


def turn(x, cos, sin):
    return x * cos + pltpu.roll(x, HEAD_DIM // 2, 1) * sin


def turn_back(x, cos, sin):
    return x * cos - pltpu.roll(x, HEAD_DIM // 2, 1) * sin


def project_kernel(
    n, ns, depth_full,
    tok, wq, wk, wv, wo, gq, gk, cos, sin,
    x_out, w_out, q_raw, k_raw, totals, q_rot, k_rot, v_low,
    x, w, land, lsem, ags, agr, cgs, cgr, ss, sr,
):
    s, z = lax.axis_index("seq"), lax.axis_index("head")
    rows, depth = tok.shape
    block, lw = wq.shape
    heads = lw // HEAD_DIM
    cross_barrier(s, z, ns, n)
    mine = rows_at(s, block)
    loads = [pltpu.make_async_copy(tok, x.at[rows_at(z, rows)], lsem.at[0])] + [
        pltpu.make_async_copy(m, w.at[mine, pl.ds(i * lw, lw)], lsem.at[i + 1]) for i, m in enumerate((wq, wk, wv))
    ]
    for copy in loads:
        copy.start()
    loads[0].wait()
    cube = CubeGather(s, ns, w, block, cgs, cgr)
    levels = len(cube.orders[0])
    done = []

    def weights(k):
        todo = [0] if k == 0 and n > 2 else [i for i in range(levels) if i not in done]
        for i in todo:
            cube.level(i)
            done.append(i)

    def start_weights():
        w[mine, 3 * lw :] = jnp.transpose(wo[...].astype(F32)).astype(BF16)
        for copy in loads[1:]:
            copy.wait()
        cube.start()

    def multiply(src):
        at = rows_at(src, rows)
        for i, to in enumerate((q_raw, k_raw)):
            to[at, :] = mm(x[at, :], w[:, i * lw : (i + 1) * lw])
        v_low[at, :] = mm(x[at, :], w[:, 2 * lw : 3 * lw]).astype(BF16)

    part = rows // AG_CHUNKS

    def copy(src, c, up):
        at = pl.ds(pl.multiple_of(src * rows + c * part, part), part)
        return remote(x.at[at], x.at[at], ags.at[up, src, c], agr.at[src, c], "head", z + 1 if up else z - 1)

    more = (z > 0, z < n - 1)
    for c in range(AG_CHUNKS):
        for up in (0, 1):

            @pl.when(more[up])
            def _():
                copy(z, c, up).start()

    start_weights()

    def sides(k):
        return ((z + k, z + k < n, 0), (z - k, z - k >= 0, 1))

    for k in range(1, n):
        for c in range(AG_CHUNKS):
            for src, there, up in sides(k):

                @pl.when(there)
                def _():
                    copy(src, c, up).wait_recv()

                    @pl.when(more[up])
                    def _():
                        copy(src, c, up).start()

        if k <= 2:
            weights(k - 1)
        if k == min(2, n - 1):
            multiply(z)
            for src, there, _ in sides(1):
                pl.when(there)(functools.partial(multiply, src))
        if k > 1:
            for src, there, _ in sides(k):
                pl.when(there)(functools.partial(multiply, src))

    outs = [pltpu.make_async_copy(x, x_out, lsem.at[4]), pltpu.make_async_copy(w, w_out, lsem.at[5])]
    for out in outs:
        out.start()
    totals[...] = row_sums(q_raw[...] * q_raw[...], k_raw[...] * k_raw[...])
    land[z] = totals[...]
    small = SmallExchange("head", z, n, land, ss, sr)
    small.start()
    small.receive()
    total = land[0]
    for k in range(1, n):
        total = total + land[k]
    totals[...] = total
    for row, raw, gain, to in ((0, q_raw, gq, q_rot), (4, k_raw, gk, k_rot)):
        scale = lax.rsqrt(as_column(total, row) / depth_full + epsilon)
        for h in range(heads):
            cols = slice(h * HEAD_DIM, (h + 1) * HEAD_DIM)
            to[:, cols] = turn(raw[:, cols] * scale * gain[:, cols], cos[...], sin[...]).astype(BF16)
    small.finish()
    cube.finish()
    for out in outs:
        out.wait()

    @pl.loop(0, n)
    def _(src):
        for c in range(AG_CHUNKS):

            @pl.when((src >= z) & (z > 0))
            def _():
                copy(src, c, 0).wait_send()

            @pl.when((src <= z) & (z < n - 1))
            def _():
                copy(src, c, 1).wait_send()


def run_project(n, ns, tok, wq, wk, wv, wo, gq, gk, cos, sin):
    rows, depth = tok.shape
    tl = rows * n
    lw = wq.shape[1]
    dma = pltpu.SemaphoreType.DMA
    shape = jax.ShapeDtypeStruct
    return pl.pallas_call(
        functools.partial(project_kernel, n, ns, depth),
        out_shape=(
            shape((tl, depth), BF16),
            shape((depth, 4 * lw), BF16),
            shape((tl, lw), F32),
            shape((tl, lw), F32),
            shape((8, tl), F32),
            shape((tl, lw), BF16),
            shape((tl, lw), BF16),
            shape((tl, lw), BF16),
        ),
        in_specs=[ANY] * 4 + [VMEM] * 5,
        out_specs=(ANY,) * 2 + (VMEM,) * 6,
        scratch_shapes=[
            pltpu.VMEM((tl, depth), BF16),
            pltpu.VMEM((depth, 4 * lw), BF16),
            pltpu.VMEM((n, 8, tl), F32),
            dma((6,)),
            dma((2, n, AG_CHUNKS)), dma((n, AG_CHUNKS)),
            *CubeGather.sems(ns),
            dma((n,)), dma((n,)),
        ],
        compiler_params=pltpu.CompilerParams(
            collective_id=5, has_side_effects=True, vmem_limit_bytes=VMEM_BYTES
        ),
        cost_estimate=pl.CostEstimate(flops=3 * 10**9, bytes_accessed=20 * 10**6, transcendentals=0),
        name="project",
    )(tok, wq, wk, wv, wo, gq, gk, cos, sin)


def input_kernel(
    n, ns, depth_full,
    dq, dk, dv, q_raw, k_raw, totals, gq, gk, cos, sin, x, w, middle, att, dy1, attn_part, mlp_part,
    grad_in, grad_q, grad_k, grad_v, grad_o, gains,
    dqkv, q_back, k_back, inner, land, total, message, message_z, gain_land,
    first, held, later, c0s, c0r, c1s, c1r,
    ss, sr, ms, mr, zs, zr, s1s, s1r,
):
    s, z = lax.axis_index("seq"), lax.axis_index("head")
    rows, depth = grad_in.shape
    tl, lw = dq.shape
    block = depth // ns
    heads = lw // HEAD_DIM
    cross_barrier(s, z, ns, n)
    sums = totals[...]
    scales = [lax.rsqrt(as_column(sums, row) / depth_full + epsilon) for row in (0, 4)]
    todo = ((dq, q_raw, gq, q_back), (dk, k_raw, gk, k_back))
    message[...] = jnp.zeros_like(message)
    products = []
    for i, (grad, raw, gain, back) in enumerate(todo):
        product = jnp.zeros((tl, HEAD_DIM), F32)
        for h in range(heads):
            cols = slice(h * HEAD_DIM, (h + 1) * HEAD_DIM)
            hat = raw[:, cols] * scales[i]
            turned = turn_back(grad[:, cols].astype(F32), cos[...], sin[...])
            message[0, pl.ds(i, 1), cols] = jnp.sum(turned * hat, axis=0, keepdims=True)
            turned = turned * gain[:, cols]
            back[:, cols] = turned
            product = product + turned * hat
        products.append(product)
    inner[z] = row_sums(*products)
    small = SmallExchange("head", z, n, inner, ss, sr)
    small.start()
    for t in range(1, ns):
        message[t, pl.ds(0, 2), pl.ds(0, lw)] = message[0, pl.ds(0, 2), pl.ds(0, lw)]
    for t in range(ns):
        for i, part in enumerate((attn_part, mlp_part)):
            message[t, pl.ds(i, 1), pl.ds(lw, block)] = part[:, t * block : (t + 1) * block]

    def message_copy(t, frm):
        return remote(message.at[t], message_z.at[frm], ms.at[t], mr.at[frm], "seq", t)

    def each_seq(act):
        @pl.loop(0, ns)
        def _(t):
            @pl.when(t != s)
            def _():
                act(t)

    message_z[s] = message[s]
    each_seq(lambda t: message_copy(t, s).start())
    dqkv[:, 2 * lw :] = dv[...]
    small.receive()
    sums = inner[0]
    for k in range(1, n):
        sums = sums + inner[k]
    for i, (grad, raw, gain, back) in enumerate(todo):
        mean = as_column(sums, 4 * i) / depth_full
        for h in range(heads):
            cols = slice(h * HEAD_DIM, (h + 1) * HEAD_DIM)
            to = slice(i * lw + h * HEAD_DIM, i * lw + (h + 1) * HEAD_DIM)
            dqkv[:, to] = (scales[i] * (back[:, cols] - raw[:, cols] * scales[i] * mean)).astype(BF16)

    width = depth // STEPS

    def weight_block(b):
        cols = rows_at(b, block)
        return jnp.concatenate([mm(x[:, cols], dqkv[...], TN), mm(dy1[:, cols], att[...], TN)], axis=1)

    def in_part(d, c):
        return mm(dqkv[rows_at(d, rows), :], w[rows_at(c, width), : 3 * lw], NT)

    cube = CubeScatter(s, ns, weight_block, block, first, held, later, (c0s, c0r, c1s, c1r))
    line = LineScatter(z, n, in_part, land, s1s, s1r, total)
    half = ns // 2

    def task(slot):
        for i, act in enumerate((cube.send_core, cube.add_core)):
            low = 1 + i * half
            pl.when((slot >= low) & (slot < low + half))(functools.partial(act, slot - low))

    done = 1 + 2 * half
    line.run(0, done, None, task)
    line.start_own()
    line.run(done, line.slots)
    for i in range(cube.stages - 1):
        cube.step(i)

    each_seq(lambda t: message_copy(t, t).wait_recv())
    received = message_z[0]
    for t in range(1, ns):
        received = received + message_z[t]
    each_seq(lambda t: message_copy(t, s).wait_send())
    gain_land[z] = received
    rounds = SmallExchange("head", z, n, gain_land, zs, zr)
    rounds.start()
    line.own()
    grad_in[...] = middle[...] + total[...]
    cube.step(cube.stages - 1)
    for i, to in enumerate((grad_q, grad_k, grad_v)):
        to[...] = held[0, :, i * lw : (i + 1) * lw].astype(F32)
    grad_o[...] = jnp.transpose(held[0, :, 3 * lw :].astype(F32))
    rounds.receive()
    at = s * block
    gains[...] = jnp.zeros_like(gains)
    gains[0:2, :] = gain_land[at // lw, pl.ds(0, 2), pl.ds(pl.multiple_of(at % lw, block), block)]
    both = gain_land[0, pl.ds(0, 2), pl.ds(lw, block)]
    for k in range(1, n):
        both = both + gain_land[k, pl.ds(0, 2), pl.ds(lw, block)]
    gains[2:4, :] = both
    cube.core_sent()
    cube.finish()
    line.finish()
    small.finish()
    rounds.finish()


def run_input(n, ns, dq, dk, dv, q_raw, k_raw, totals, gq, gk, cos, sin, x, w, middle, att, dy1, attn_part, mlp_part):
    rows, depth = middle.shape
    tl, lw = dq.shape
    block = depth // ns
    dma = pltpu.SemaphoreType.DMA
    shape = jax.ShapeDtypeStruct
    return pl.pallas_call(
        functools.partial(input_kernel, n, ns, depth),
        out_shape=(shape((rows, depth), F32),)
        + (shape((block, lw), F32),) * 3
        + (shape((lw, block), F32), shape((8, block), F32)),
        in_specs=[VMEM] * 17,
        out_specs=(VMEM,) * 6,
        scratch_shapes=[
            pltpu.VMEM((tl, 3 * lw), BF16),
            pltpu.VMEM((tl, lw), F32),
            pltpu.VMEM((tl, lw), F32),
            pltpu.VMEM((n, 8, tl), F32),
            pltpu.VMEM((2, n, STEPS, rows, depth // STEPS), BF16),
            pltpu.VMEM((rows, depth), F32),
            pltpu.VMEM((ns, 8, lw + block), F32),
            pltpu.VMEM((ns, 8, lw + block), F32),
            pltpu.VMEM((n, 8, lw + block), F32),
            *CubeScatter.scratch(ns, block, 4 * lw),
            dma((n,)), dma((n,)),
            dma((ns,)), dma((ns,)),
            dma((n,)), dma((n,)),
            *line_sems(n)["scatter"],
        ],
        compiler_params=pltpu.CompilerParams(
            collective_id=6, has_side_effects=True, vmem_limit_bytes=VMEM_BYTES
        ),
        cost_estimate=pl.CostEstimate(flops=8 * 10**9, bytes_accessed=30 * 10**6, transcendentals=0),
        name="into_input",
    )(dq, dk, dv, q_raw, k_raw, totals, gq, gk, cos, sin, x, w, middle, att, dy1, attn_part, mlp_part)


def doc_starts(doc_lengths, token_index):
    ends = jnp.cumsum(doc_lengths)
    return jnp.sum(jnp.where(token_index[..., None] >= ends, doc_lengths, 0), axis=-1).astype(jnp.int32)


def turn_tables(positions):
    frequency = jnp.power(rope_base, -jnp.arange(HEAD_DIM // 2, dtype=F32) * (2.0 / HEAD_DIM))
    angles = positions.astype(F32)[:, None] * frequency[None, :]
    cos, sin = jnp.cos(angles), jnp.sin(angles)
    return jnp.concatenate([cos, cos], axis=1), jnp.concatenate([-sin, sin], axis=1)


def on_device(
    tokens,
    cotangent,
    doc_lengths,
    q_weight,
    k_weight,
    v_weight,
    o_weight,
    gate_weight,
    up_weight,
    down_weight,
    q_gain,
    k_gain,
    attn_gain,
    mlp_gain,
):
    ns, nz = lax.axis_size("seq"), lax.axis_size("head")
    seq_index, head_index = lax.axis_index("seq"), lax.axis_index("head")
    lw = q_weight.shape[1]
    heads = lw // HEAD_DIM
    tl = tokens.shape[0] * nz
    ff = gate_weight.shape[1]
    token_index = seq_index * tl + jnp.arange(tl, dtype=jnp.int32)
    cos, sin = turn_tables(token_index - doc_starts(doc_lengths, token_index))
    share = ns // heads
    sources = jnp.stack([source_of(seq_index % share, i, ns, share) for i in range(ns // share)])
    starts = doc_starts(doc_lengths, sources[:, None] * tl + jnp.arange(tl, dtype=jnp.int32)[None, :])
    gq = lax.dynamic_slice_in_dim(q_gain, head_index * lw, lw)[None]
    gk = lax.dynamic_slice_in_dim(k_gain, head_index * lw, lw)[None]

    x, w, q_raw, k_raw, totals, q_rot, k_rot, v_low = run_project(
        nz, ns, tokens, q_weight, k_weight, v_weight, o_weight, gq, gk, cos, sin
    )
    attended, q_held, k_held, v_held, o_held, lse, gate = run_attend(
        ns, heads, q_rot, k_rot, v_low, starts, gate_weight
    )
    output, h1r, branch, hidden, dy2, dg, du, mlp_part, up = run_forward(
        nz, ns, attended, tokens, cotangent, w, gate, up_weight, down_weight, attn_gain[None], mlp_gain[None]
    )
    middle, dy1, datt, attn_part, grad_gate, grad_up = run_backward(
        nz, ns, dg, du, h1r, cotangent, branch, w, gate, up, attn_gain[None]
    )
    dq, dk, dv, grad_down = run_attend_back(
        ns, heads, datt, starts, q_held, k_held, v_held, o_held, lse, dy2, hidden
    )
    input_grad, grad_q, grad_k, grad_v, grad_o, gains = run_input(
        nz, ns, dq, dk, dv, q_raw, k_raw, totals, gq, gk, cos, sin, x, w, middle, attended, dy1, attn_part, mlp_part
    )
    return (
        output,
        input_grad,
        grad_q,
        grad_k,
        grad_v,
        grad_o,
        grad_gate,
        grad_up,
        grad_down,
        gains[0],
        gains[1],
        gains[2],
        gains[3],
    )


def solution(mesh):
    in_specs = (
        P(("seq", "head"), None),
        P(("seq", "head"), None),
        P(),
        P("seq", "head"),
        P("seq", "head"),
        P("seq", "head"),
        P("head", "seq"),
        P("seq", "head"),
        P("seq", "head"),
        P("head", "seq"),
        P(),
        P(),
        P(),
        P(),
    )
    out_specs = (
        P(("seq", "head"), None),
        P(("seq", "head"), None),
        P("seq", "head"),
        P("seq", "head"),
        P("seq", "head"),
        P("head", "seq"),
        P("seq", "head"),
        P("seq", "head"),
        P("head", "seq"),
        P("seq"),
        P("seq"),
        P("seq"),
        P("seq"),
    )
    return jax.shard_map(
        on_device, mesh=mesh, in_specs=in_specs, out_specs=out_specs, check_vma=False
    )
```

```python
import functools

import jax
import jax.numpy as jnp
from jax import lax
from jax.experimental import pallas as pl
from jax.experimental.pallas import tpu as pltpu
from jax.sharding import PartitionSpec as P

HEAD_DIM = 128
epsilon = 1e-06
rope_base = 500000.0

MESH = pl.DeviceIdType.MESH
F32 = jnp.float32
BF16 = jnp.bfloat16
STEPS = 4
LAG = 1
AG_CHUNKS = 2
VMEM_BYTES = 62 * 1024 * 1024
ANY = pl.BlockSpec(memory_space=pl.ANY)
VMEM = pl.BlockSpec(memory_space=pltpu.VMEM)
NN = (((1,), (0,)), ((), ()))
NT = (((1,), (1,)), ((), ()))
TN = (((0,), (0,)), ((), ()))


def mm(left, right, dims=NN):
    return lax.dot_general(left, right, dims, preferred_element_type=F32)


def rows_at(index, count):
    return pl.ds(pl.multiple_of(index * count, count), count)


def cube_barrier(s, z, ns, n, between=None):
    bar = pltpu.get_barrier_semaphore()
    bits = [1 << i for i in range(ns.bit_length() - 1)]
    for bit in bits:
        pl.semaphore_signal(bar, inc=1, device_id={"seq": s ^ bit}, device_id_type=MESH)
    for other, there in ((z - 1, z > 0), (z + 1, z < n - 1)):

        @pl.when(there)
        def _():
            pl.semaphore_signal(bar, inc=1, device_id={"head": other}, device_id_type=MESH)

    if between is not None:
        between()
    pl.semaphore_wait(bar, len(bits) + (z > 0).astype(jnp.int32) + (z < n - 1).astype(jnp.int32))


def line_gather(z, n, buf, rows, send_sem, recv_sem, use, hooks=(), ready=None):
    part = rows // AG_CHUNKS

    def copy(src, c, up):
        at = pl.ds(pl.multiple_of(src * rows + c * part, part), part)
        return pltpu.make_async_remote_copy(
            src_ref=buf.at[at],
            dst_ref=buf.at[at],
            send_sem=send_sem.at[up, src, c],
            recv_sem=recv_sem.at[src, c],
            device_id={"head": z + 1 if up else z - 1},
            device_id_type=MESH,
        )

    more = (z > 0, z < n - 1)
    for c in range(AG_CHUNKS):
        for up in (0, 1):

            @pl.when(more[up])
            def _():
                copy(z, c, up).start()

    if ready is not None:
        ready()
    use(z)

    @pl.loop(1, n)
    def _(k):
        sides = ((z + k, z + k < n, 0), (z - k, z - k >= 0, 1))
        for c in range(AG_CHUNKS):
            for src, there, up in sides:

                @pl.when(there)
                def _():
                    copy(src, c, up).wait_recv()

                    @pl.when(more[up])
                    def _():
                        copy(src, c, up).start()

        for src, there, up in sides:

            @pl.when(there)
            def _():
                use(src)

        for i, hook in enumerate(hooks):
            pl.when(k == i + 1)(hook)

    @pl.loop(0, n)
    def _(src):
        for c in range(AG_CHUNKS):

            @pl.when((src >= z) & (z > 0))
            def _():
                copy(src, c, 0).wait_send()

            @pl.when((src <= z) & (z < n - 1))
            def _():
                copy(src, c, 1).wait_send()


class LineScatter:
    def __init__(self, z, n, partial, land, send_sem, recv_sem, total):
        self.z, self.n, self.partial, self.land, self.total = z, n, partial, land, total
        self.send_sem, self.recv_sem = send_sem, recv_sem

    def copy(self, d, c, up):
        return pltpu.make_async_remote_copy(
            src_ref=self.land.at[up, d, c],
            dst_ref=self.land.at[up, d, c],
            send_sem=self.send_sem.at[up, d, c],
            recv_sem=self.recv_sem.at[up, d, c],
            device_id={"head": self.z + 1 if up else self.z - 1},
            device_id_type=MESH,
        )

    @property
    def slots(self):
        return (self.n - 1) * (STEPS + LAG)

    def run(self, low, high, before=None, after=None):
        z, n, land = self.z, self.n, self.land

        @pl.loop(low, high)
        def _(slot):
            if before is not None:
                before(slot)
            for up in (1, 0):
                t = slot - (z if up else n - 1 - z) * LAG
                j = t // STEPS
                c = t - j * STEPS
                d = n - 1 - j if up else j
                first = z == 0 if up else z == n - 1
                there = (t >= 0) & (j < n - 1) & ((d > z) if up else (d < z))

                @pl.when(there)
                def _():
                    mine = self.partial(d, c)

                    @pl.when(first)
                    def _():
                        land[up, d, c] = mine.astype(land.dtype)

                    @pl.when(jnp.logical_not(first))
                    def _():
                        self.copy(d, c, up).wait_recv()
                        land[up, d, c] = (land[up, d, c].astype(F32) + mine).astype(land.dtype)

                    self.copy(d, c, up).start()

            if after is not None:
                after(slot)

    def start_own(self):
        width = self.total.shape[1] // STEPS

        @pl.loop(0, STEPS)
        def _(c):
            self.total[:, rows_at(c, width)] = self.partial(self.z, c)

    def own(self):
        z, n, total = self.z, self.n, self.total
        width = total.shape[1] // STEPS

        @pl.loop(0, STEPS)
        def _(c):
            at = rows_at(c, width)
            for there, up in ((z > 0, 1), (z < n - 1, 0)):

                @pl.when(there)
                def _():
                    self.copy(z, c, up).wait_recv()
                    total[:, at] += self.land[up, z, c].astype(F32)

    def finish(self):
        @pl.loop(0, self.n * STEPS)
        def _(t):
            d, c = t // STEPS, t % STEPS
            for there, up in ((d > self.z, 1), (d < self.z, 0)):

                @pl.when(there)
                def _():
                    self.copy(d, c, up).wait_send()


def line_sems(n):
    dma = pltpu.SemaphoreType.DMA
    return {
        "gather": [dma((2, n, AG_CHUNKS)), dma((n, AG_CHUNKS))],
        "scatter": [dma((2, n, STEPS)), dma((2, n, STEPS))],
    }


BLOCK = 16


def row_scale(block):
    return lax.rsqrt(jnp.mean(block * block, axis=-1, keepdims=True) + epsilon)


def norm_back(e, normed, scale, gain):
    g = e * gain
    return scale * (g - normed * jnp.mean(g * normed, axis=-1, keepdims=True))


def sigmoid(x):
    return 1.0 / (1.0 + jnp.exp(-x))


def subsets(bits):
    found = [0]
    for bit in bits:
        found += [bit | other for other in found]
    return found


def orders_of(ns):
    chips = [1 << i for i in range(1, ns.bit_length() - 1)]
    return (chips, chips[::-1])


def remote(src, dst, send, recv, axis, to):
    return pltpu.make_async_remote_copy(
        src_ref=src, dst_ref=dst, send_sem=send, recv_sem=recv, device_id={axis: to}, device_id_type=MESH
    )


class CubeGather:
    def __init__(self, s, ns, buf, rows, send_sem, recv_sem, own=None):
        self.own = own
        self.s, self.buf, self.rows, self.send_sem, self.recv_sem = s, buf, rows, send_sem, recv_sem
        self.orders = [order + [1] for order in orders_of(ns)]

    def copy(self, half, bit, block):
        part = self.rows // 2
        at = pl.ds(pl.multiple_of(block * self.rows + half * part, part), part)
        source = self.buf.at[at]
        if block is self.s and self.own is not None:
            source = self.own.at[pl.ds(half * part, part)]
        return remote(
            source, self.buf.at[at],
            self.send_sem.at[bit.bit_length() - 1, block, half], self.recv_sem.at[block, half],
            "seq", self.s ^ bit,
        )

    @property
    def levels(self):
        return len(self.orders[0])

    def start(self):
        for i in range(self.levels):
            for half, order in enumerate(self.orders):
                self.copy(half, order[i], self.s).start()

    def level(self, i):
        for j in range(2**i):
            for half, order in enumerate(self.orders):
                block = self.s ^ order[i] ^ subsets(order[:i])[j]
                self.copy(half, order[i], block).wait_recv()
                for bit in order[i + 1 :]:
                    self.copy(half, bit, block).start()

    def finish(self):
        for half, order in enumerate(self.orders):
            for i, bit in enumerate(order):
                for other in subsets(order[:i]):
                    self.copy(half, bit, self.s ^ other if other else self.s).wait_send()

    @staticmethod
    def sems(ns):
        dma = pltpu.SemaphoreType.DMA
        return [dma((ns.bit_length() - 1, ns, 2)), dma((ns, 2))]


class CubeScatter:
    def __init__(self, s, ns, block, rows, first, held, later, sems):
        self.s, self.block, self.rows = s, block, rows
        self.first, self.held, self.later = first, held, later
        self.send0, self.recv0, self.send1, self.recv1 = sems
        self.orders = orders_of(ns)
        self.half = ns // 2

    def core_copy(self, j):
        return remote(self.first.at[j], self.held.at[j], self.send0.at[j], self.recv0.at[j], "seq", self.s ^ 1)

    def send_core(self, j=None):
        if j is None:
            pl.loop(0, self.half)(self.send_core)
            return
        j = self.half - 1 - j
        self.first[j] = self.block(self.s ^ (2 * j + 1)).astype(BF16)
        self.core_copy(j).start()

    def base(self, i):
        return sum(2 ** (self.stages - 1 - k) for k in range(i))

    def move(self, i, half, slot, other):
        part = self.rows // 2
        return remote(
            self.held.at[(self.orders[half][i] | other) >> 1, pl.ds(half * part, part)],
            self.later.at[half, slot], self.send1.at[half, slot], self.recv1.at[half, slot],
            "seq", self.s ^ self.orders[half][i],
        )

    def moves(self, i):
        part = self.rows // 2
        for half, order in enumerate(self.orders):
            for j, other in enumerate(subsets(order[i + 1 :])):
                slot = self.base(i) + j
                yield other >> 1, pl.ds(half * part, part), half, slot, self.move(i, half, slot, other)

    def add_core(self, j=None):
        if j is None:
            pl.loop(0, self.half)(self.add_core)
            return
        j = self.half - 1 - j
        mine = self.block(self.s ^ (2 * j))
        self.core_copy(j).wait_recv()
        self.held[j] = (self.held[j].astype(F32) + mine).astype(BF16)
        for half, order in enumerate(self.orders):
            for slot, other in enumerate(subsets(order[1:])):

                @pl.when(j == (order[0] | other) >> 1)
                def _():
                    self.move(0, half, slot, other).start()

    def send(self, i):
        for *_, copy in self.moves(i):
            copy.start()

    def take(self, i):
        for j, at, half, slot, copy in self.moves(i):
            copy.wait_recv()
            self.held[j, at] = (self.held[j, at].astype(F32) + self.later[half, slot].astype(F32)).astype(BF16)

    def step(self, i):
        self.take(i)
        if i + 1 < self.stages:
            self.send(i + 1)

    @property
    def stages(self):
        return len(self.orders[0])

    def core_sent(self):
        @pl.loop(0, self.half)
        def _(j):
            self.core_copy(j).wait_send()

    def finish(self):
        for i in range(self.stages):
            for *_, copy in self.moves(i):
                copy.wait_send()

    @staticmethod
    def scratch(ns, rows, width):
        dma = pltpu.SemaphoreType.DMA
        half = ns // 2
        return [
            pltpu.VMEM((half, rows, width), BF16),
            pltpu.VMEM((half, rows, width), BF16),
            pltpu.VMEM((2, half - 1, rows // 2, width), BF16),
            dma((half,)), dma((half,)), dma((2, half - 1)), dma((2, half - 1)),
        ]


def forward_kernel(
    n, ns,
    att, tok, cot, w_in, gate, up, down, attn_gain, mlp_gain,
    out, h1r_out, branch_out, hidden_out, dy2_out, dg_out, du_out, gain_part, up_out,
    h1r, hidden, dy2, dg, du,
    wo, wd, wg, wu, land, branch, h1, second, g_pre, u_pre,
    wsem, osem, bsem, g1s, g1r, s1s, s1r, g2s, g2r, s2s, s2r, us, ur, ds, dr,
):
    s, z = lax.axis_index("seq"), lax.axis_index("head")
    rows, depth = tok.shape
    lw, ff = att.shape[1], up.shape[1]
    block = depth // ns
    width = depth // STEPS
    mine = rows_at(s, block)
    l_o = pltpu.make_async_copy(w_in.at[:, pl.ds(3 * lw, lw)], wo, wsem.at[0])
    l_u = pltpu.make_async_copy(up, wu.at[mine], wsem.at[1])
    l_g = pltpu.make_async_copy(gate, wg, wsem.at[2])
    for copy in (l_o, l_u, l_g):
        copy.start()
    cube_barrier(s, z, ns, n)
    cube_u = CubeGather(s, ns, wu, block, us, ur)
    cube_d = CubeGather(s, ns, wd, block, ds, dr)
    levels = cube_u.levels
    l_u.wait()
    cube_u.start()
    l_o.wait()

    def out_part(d, c):
        return mm(att[rows_at(d, rows), :], wo[rows_at(c, width), :], NT)

    line = LineScatter(z, n, out_part, land, s1s, s1r, branch)
    line.run(0, STEPS)
    line.start_own()
    wd[mine, :] = jnp.transpose(down[...].astype(F32)).astype(BF16)
    cube_u.level(0)
    line.run(STEPS, 2 * STEPS)
    for i in range(1, levels - 1):
        cube_u.level(i)
    cube_d.start()
    line.run(2 * STEPS, line.slots)
    line.own()
    line.finish()
    o_branch = pltpu.make_async_copy(branch, branch_out, osem.at[0])
    o_branch.start()
    gain_part[...] = jnp.zeros_like(gain_part)

    @pl.loop(0, rows // BLOCK)
    def _(i):
        at = rows_at(i, BLOCK)
        y = branch[at, :]
        h = tok[at, :].astype(F32) + y * row_scale(y) * attn_gain[...]
        h1[at, :] = h
        h1r[pl.ds(pl.multiple_of(z * rows + i * BLOCK, BLOCK), BLOCK), :] = h.astype(BF16)

    fw = ff // STEPS
    o_up = pltpu.make_async_copy(wu, up_out, osem.at[1])
    o_h1r = pltpu.make_async_copy(h1r, h1r_out, osem.at[2])
    o_hidden = pltpu.make_async_copy(hidden, hidden_out, osem.at[3])
    o_dy2 = pltpu.make_async_copy(dy2, dy2_out, osem.at[4])

    def up_block(src):
        at = rows_at(src, rows)

        @pl.loop(0, STEPS)
        def _(c):
            cols = rows_at(c, fw)
            x = h1r[at, :]
            g = mm(x, wg[:, cols])
            u = mm(x, wu[:, cols])
            g_pre[at, cols] = g
            u_pre[at, cols] = u
            hidden[at, cols] = (g * sigmoid(g) * u).astype(BF16)

    def weights_there():
        l_g.wait()
        cube_u.level(levels - 1)
        o_up.start()

    hooks = [functools.partial(cube_d.level, i) for i in range(levels)]
    line_gather(z, n, h1r, rows, g1s, g1r, up_block, hooks[: n - 1], weights_there)
    for hook in hooks[n - 1 :]:
        hook()
    o_h1r.start()
    o_hidden.start()

    def down_part(d, c):
        return mm(hidden[rows_at(d, rows), :], wd[rows_at(c, width), :], NT)

    line = LineScatter(z, n, down_part, land, s2s, s2r, second)
    line.run(0, STEPS)
    line.start_own()
    line.run(STEPS, line.slots)
    line.own()
    line.finish()

    @pl.loop(0, rows // BLOCK)
    def _(i):
        at = rows_at(i, BLOCK)
        y = second[at, :]
        scale = row_scale(y)
        normed = y * scale
        e = cot[at, :].astype(F32)
        out[at, :] = (h1[at, :] + normed * mlp_gain[...]).astype(BF16)
        gain_part[...] += jnp.sum(e * normed, axis=0, keepdims=True)
        dy2[pl.ds(pl.multiple_of(z * rows + i * BLOCK, BLOCK), BLOCK), :] = norm_back(
            e, normed, scale, mlp_gain[...]
        ).astype(BF16)

    def back_block(src):
        at = rows_at(src, rows)

        @pl.loop(0, STEPS)
        def _(c):
            cols = rows_at(c, fw)
            dh = mm(dy2[at, :], wd[:, cols])
            g = g_pre[at, cols]
            u = u_pre[at, cols]
            sig = sigmoid(g)
            du[at, cols] = (dh * g * sig).astype(BF16)
            dg[at, cols] = (dh * u * sig * (1.0 + g * (1.0 - sig))).astype(BF16)

        for copy in grads_out(src):
            copy.start()

    def grads_out(src):
        at = rows_at(src, rows)
        return [
            pltpu.make_async_copy(held.at[at], to.at[at], bsem.at[i, src])
            for i, (held, to) in enumerate(((dg, dg_out), (du, du_out)))
        ]

    line_gather(z, n, dy2, rows, g2s, g2r, back_block)
    o_dy2.start()
    for copy in (o_branch, o_up, o_h1r, o_hidden, o_dy2):
        copy.wait()

    @pl.loop(0, n)
    def _(src):
        for copy in grads_out(src):
            copy.wait()

    cube_u.finish()
    cube_d.finish()


def run_forward(n, ns, att, tok, cot, w, gate, up, down, attn_gain, mlp_gain):
    rows, depth = tok.shape
    tl, lw = att.shape
    ff = up.shape[1]
    dma = pltpu.SemaphoreType.DMA
    sems = line_sems(n)
    shape = jax.ShapeDtypeStruct
    return pl.pallas_call(
        functools.partial(forward_kernel, n, ns),
        out_shape=(
            shape((rows, depth), BF16),
            shape((tl, depth), BF16),
            shape((rows, depth), F32),
            shape((tl, ff), BF16),
            shape((tl, depth), BF16),
            shape((tl, ff), BF16),
            shape((tl, ff), BF16),
            shape((1, depth), F32),
            shape((depth, ff), BF16),
        ),
        in_specs=[VMEM, VMEM, VMEM, ANY, ANY, ANY, VMEM, VMEM, VMEM],
        out_specs=(VMEM, ANY, ANY, ANY, ANY, ANY, ANY, VMEM, ANY),
        scratch_shapes=[
            pltpu.VMEM((tl, depth), BF16),
            pltpu.VMEM((tl, ff), BF16),
            pltpu.VMEM((tl, depth), BF16),
            pltpu.VMEM((tl, ff), BF16),
            pltpu.VMEM((tl, ff), BF16),
            pltpu.VMEM((depth, lw), BF16),
            pltpu.VMEM((depth, ff), BF16),
            pltpu.VMEM((depth, ff), BF16),
            pltpu.VMEM((depth, ff), BF16),
            pltpu.VMEM((2, n, STEPS, rows, depth // STEPS), BF16),
            pltpu.VMEM((rows, depth), F32),
            pltpu.VMEM((rows, depth), F32),
            pltpu.VMEM((rows, depth), F32),
            pltpu.VMEM((tl, ff), F32),
            pltpu.VMEM((tl, ff), F32),
            dma((3,)),
            dma((5,)),
            dma((2, n)),
            *sems["gather"], *sems["scatter"], *sems["gather"], *sems["scatter"],
            *CubeGather.sems(ns), *CubeGather.sems(ns),
        ],
        compiler_params=pltpu.CompilerParams(
            collective_id=1, has_side_effects=True, vmem_limit_bytes=VMEM_BYTES
        ),
        cost_estimate=pl.CostEstimate(flops=18 * 10**9, bytes_accessed=40 * 10**6, transcendentals=2 * 10**6),
        name="feed_forward",
    )(att, tok, cot, w, gate, up, down, attn_gain, mlp_gain)


def backward_kernel(
    n, ns,
    dg, du, h1r_in, cot, branch, w_in, gate, up, attn_gain,
    middle, dy1, datt, gain_part, grad_gate, grad_up,
    h1r, wo, wg, wu, land, total,
    first, held_g, later_g, held_u, later_u,
    wsem, osem, s1s, s1r, g1s, g1r,
    ga, gb, gc, gd, ua, ub, uc, ud,
):
    s, z = lax.axis_index("seq"), lax.axis_index("head")
    rows, depth = cot.shape
    lw, ff = datt.shape[1], dg.shape[1]
    block = depth // ns
    width = depth // STEPS

    def weights_in(c):
        at = rows_at(c, width)
        return [
            pltpu.make_async_copy(m.at[at], to.at[at], wsem.at[i, c]) for i, (m, to) in enumerate(((gate, wg), (up, wu)))
        ]

    for c in range(STEPS):
        for copy in weights_in(c):
            copy.start()
    l_h = pltpu.make_async_copy(h1r_in, h1r, osem.at[0])
    l_o = pltpu.make_async_copy(w_in.at[:, pl.ds(3 * lw, lw)], wo, osem.at[1])
    l_h.start()
    l_o.start()
    cube_barrier(s, z, ns, n)

    def weight_block(grad):
        return lambda b: mm(h1r[:, rows_at(b, block)], grad[...], TN)

    cube_g = CubeScatter(s, ns, weight_block(dg), block, first, held_g, later_g, (ga, gb, gc, gd))
    cube_u = CubeScatter(s, ns, weight_block(du), block, first, held_u, later_u, (ua, ub, uc, ud))

    def in_part(d, c):
        at, cols = rows_at(d, rows), rows_at(c, width)
        return mm(dg[at, :], wg[cols, :], NT) + mm(du[at, :], wu[cols, :], NT)

    line = LineScatter(z, n, in_part, land, s1s, s1r, total)
    half = ns // 2

    def there(slot):
        @pl.when(slot < STEPS)
        def _():
            for copy in weights_in(slot):
                copy.wait()

    def task(slot):
        @pl.when(slot == 1)
        def _():
            l_h.wait()

        def during(phase, act):
            low = 1 + phase * half
            pl.when((slot >= low) & (slot < low + half))(lambda: act(slot - low))

        def send_second(j):
            cube_g.core_copy(half - 1 - j).wait_send()
            cube_u.send_core(j)

        during(0, cube_g.send_core)
        during(1, cube_g.add_core)
        during(1, send_second)
        during(2, cube_u.add_core)

    line.run(0, 2 * STEPS, there, task)
    line.start_own()
    line.run(2 * STEPS, line.slots, None, task)

    @pl.loop(line.slots, max(line.slots, 1 + 3 * half))
    def _(slot):
        task(slot)

    cube_g.step(0)
    line.own()
    line.finish()
    gain_part[...] = jnp.zeros_like(gain_part)

    @pl.loop(0, rows // BLOCK)
    def _(i):
        at = rows_at(i, BLOCK)
        y = branch[at, :]
        scale = row_scale(y)
        normed = y * scale
        e = cot[at, :].astype(F32) + total[at, :]
        middle[at, :] = e
        gain_part[...] += jnp.sum(e * normed, axis=0, keepdims=True)
        dy1[pl.ds(pl.multiple_of(z * rows + i * BLOCK, BLOCK), BLOCK), :] = norm_back(
            e, normed, scale, attn_gain[...]
        ).astype(BF16)

    l_o.wait()

    def att_block(src):
        at = rows_at(src, rows)
        datt[at, :] = mm(dy1[at, :], wo[...]).astype(BF16)

    todo = [functools.partial(cube.step, i) for i in range(1, cube_g.stages) for cube in (cube_g, cube_u)]
    line_gather(z, n, dy1, rows, g1s, g1r, att_block, todo[: n - 1], functools.partial(cube_u.step, 0))
    for step in todo[n - 1 :]:
        step()
    grad_gate[...] = held_g[0]
    grad_up[...] = held_u[0]
    cube_g.finish()
    cube_u.core_sent()
    cube_u.finish()


def run_backward(n, ns, dg, du, h1r, cot, branch, w, gate, up, attn_gain):
    rows, depth = cot.shape
    tl, ff = dg.shape
    lw = w.shape[1] // 4
    block = depth // ns
    dma = pltpu.SemaphoreType.DMA
    sems = line_sems(n)
    shape = jax.ShapeDtypeStruct
    first, held, later, *cube_sems = CubeScatter.scratch(ns, block, ff)
    return pl.pallas_call(
        functools.partial(backward_kernel, n, ns),
        out_shape=(
            shape((rows, depth), F32),
            shape((tl, depth), BF16),
            shape((tl, lw), BF16),
            shape((1, depth), F32),
            shape((block, ff), BF16),
            shape((block, ff), BF16),
        ),
        in_specs=[VMEM, VMEM, ANY, VMEM, VMEM, ANY, ANY, ANY, VMEM],
        out_specs=(VMEM,) * 6,
        scratch_shapes=[
            pltpu.VMEM((tl, depth), BF16),
            pltpu.VMEM((depth, lw), BF16),
            pltpu.VMEM((depth, ff), BF16),
            pltpu.VMEM((depth, ff), BF16),
            pltpu.VMEM((2, n, STEPS, rows, depth // STEPS), BF16),
            pltpu.VMEM((rows, depth), F32),
            first, held, later, held, later,
            dma((2, STEPS)),
            dma((2,)),
            *sems["scatter"], *sems["gather"],
            *cube_sems, *cube_sems,
        ],
        compiler_params=pltpu.CompilerParams(
            collective_id=2, has_side_effects=True, vmem_limit_bytes=VMEM_BYTES
        ),
        cost_estimate=pl.CostEstimate(flops=18 * 10**9, bytes_accessed=30 * 10**6, transcendentals=0),
        name="into_attention",
    )(dg, du, h1r, cot, branch, w, gate, up, attn_gain)


LOG2E = 1.4426950408889634
NEG = -1e30


def seq_barrier(s, ns, between=None):
    bar = pltpu.get_barrier_semaphore()
    for other in range(ns):

        @pl.when(other != s)
        def _():
            pl.semaphore_signal(bar, inc=1, device_id={"seq": other}, device_id_type=MESH)

    if between is not None:
        between()
    pl.semaphore_wait(bar, ns - 1)


def share_of(s, ns, r):
    per = ns // (2 * r)
    chunk = s // per
    low = chunk < r
    sub = jnp.where(low, chunk, 2 * r - 1 - chunk)
    return sub, jnp.where(low, s - chunk * per, per + s - chunk * per)


def source_of(sub, i, ns, r):
    per = ns // (2 * r)
    return jnp.where(i < per, sub * per + i, (2 * r - 1 - sub) * per + i - per)


def head_cols(h):
    return pl.ds(pl.multiple_of(h * HEAD_DIM, HEAD_DIM), HEAD_DIM)


def attend_kernel(
    ns, heads, q_in, k_in, v_in, starts, gate,
    att, q_buf, k_buf, v_buf, o_buf, lse, gate_out,
    o_low, qs, qr, ks, kr, vs, vr, osend, orecv, local, cs, cr,
):
    s = lax.axis_index("seq")
    r = ns // heads
    blocks = ns // r
    tl = q_in.shape[0]
    mine, sub = s // r, s % r
    parity = s % 2
    to_sub, to_row = share_of(s, ns, r)

    def own_rows():
        for x, buf in ((k_in, k_buf), (v_in, v_buf)):
            buf[rows_at(s, tl), :] = x[:, head_cols(mine)]

        @pl.when(to_sub == sub)
        def _():
            q_buf[rows_at(to_row, tl), :] = q_in[:, head_cols(mine)]

    seq_barrier(s, ns, own_rows)

    def q_copy(h):
        return pltpu.make_async_remote_copy(
            src_ref=q_in.at[:, head_cols(h)],
            dst_ref=q_buf.at[rows_at(to_row, tl)],
            send_sem=qs.at[h],
            recv_sem=qr.at[to_row],
            device_id={"seq": h * r + to_sub},
            device_id_type=MESH,
        )

    def q_recv(i):
        return pltpu.make_async_remote_copy(
            src_ref=q_buf.at[rows_at(i, tl)],
            dst_ref=q_buf.at[rows_at(i, tl)],
            send_sem=qs.at[0],
            recv_sem=qr.at[i],
            device_id={"seq": s ^ 1},
            device_id_type=MESH,
        )

    def kv_copy(src, buf, send, recv, t, at):
        return pltpu.make_async_remote_copy(
            src_ref=src,
            dst_ref=buf.at[rows_at(at, tl)],
            send_sem=send,
            recv_sem=recv.at[at],
            device_id={"seq": t},
            device_id_type=MESH,
        )

    kv = ((k_in, k_buf, ks, kr), (v_in, v_buf, vs, vr))
    block = gate.shape[0]
    own_gate = pltpu.make_async_copy(gate, gate_out.at[rows_at(s, block)], local.at[0])
    cube = CubeGather(s, ns, gate_out, block, cs, cr, gate)
    own_gate.start()

    def far(t):
        return (t != s) & (t % 2 == parity)

    @pl.loop(1, ns)
    def _(step):
        t = s ^ step

        @pl.when(far(t))
        def _():
            for x, buf, ss, rs in kv:
                kv_copy(x.at[:, head_cols(t // r)], buf, ss.at[0, t], rs, t, s).start()

    @pl.loop(0, heads)
    def _(h):
        @pl.when(h * r + to_sub != s)
        def _():
            q_copy(h).start()

    def pass_on(src, start):
        for _, buf, ss, rs in kv:
            copy = kv_copy(buf.at[rows_at(src, tl)], buf, ss.at[1, src], rs, s ^ 1, src)
            if start:
                copy.start()
            else:
                copy.wait_send()

    pass_on(s, True)

    @pl.loop(1, ns)
    def _(step):
        src = s ^ step

        @pl.when(far(src))
        def _():
            for x, buf, ss, rs in kv:
                kv_copy(buf.at[rows_at(src, tl)], buf, ss.at[0, 0], rs, s ^ 1, src).wait_recv()
            pass_on(src, True)

    @pl.loop(0, ns)
    def _(src):
        @pl.when(src % 2 != parity)
        def _():
            for x, buf, ss, rs in kv:
                kv_copy(buf.at[rows_at(src, tl)], buf, ss.at[0, 0], rs, s ^ 1, src).wait_recv()

    unit = HEAD_DIM ** (-0.5) * LOG2E

    def o_copy(i, t):
        return pltpu.make_async_remote_copy(
            src_ref=o_low.at[rows_at(i, tl)],
            dst_ref=att.at[:, head_cols(mine)],
            send_sem=osend.at[i],
            recv_sem=orecv.at[mine],
            device_id={"seq": t},
            device_id_type=MESH,
        )

    def attend_block(i):
        src = source_of(sub, i, ns, r)

        @pl.when(src != s)
        def _():
            q_recv(i).wait_recv()

        q = q_buf[rows_at(i, tl), :]
        start = starts[pl.ds(i, 1), :]
        key_at = lax.broadcasted_iota(jnp.int32, (tl, tl), 0)

        def step(j, carry, diagonal):
            top, total, acc = carry
            at = rows_at(j, tl)
            scores = mm(k_buf[at, :], q, NT) * unit
            allowed = key_at >= start - j * tl
            if diagonal:
                allowed = allowed & (key_at <= lax.broadcasted_iota(jnp.int32, (tl, tl), 1))
            scores = jnp.where(allowed, scores, NEG)
            new = jnp.maximum(top, jnp.max(scores, axis=0, keepdims=True))
            terms = jnp.exp2(scores - new)
            fade = jnp.exp2(top - new)
            return (
                new,
                total * fade + jnp.sum(terms, axis=0, keepdims=True),
                acc * fade + mm(v_buf[at, :], terms.astype(BF16), TN),
            )

        carry = (
            jnp.full((1, tl), NEG, F32),
            jnp.zeros((1, tl), F32),
            jnp.zeros((HEAD_DIM, tl), F32),
        )
        carry = lax.fori_loop(0, src, lambda j, c: step(j, c, False), carry)
        top, total, acc = step(src, carry, True)
        lse[pl.ds(i, 1), :] = top + jnp.log(total) * LOG2E
        o = jnp.transpose(acc / total)
        o_buf[rows_at(i, tl), :] = o
        o_low[rows_at(i, tl), :] = o.astype(BF16)

        @pl.when(src != s)
        def _():
            o_copy(i, src).start()

        @pl.when(src == s)
        def _():
            att[:, head_cols(mine)] = o.astype(BF16)

    cube.start()
    cuts = [0, blocks - 1, blocks, blocks]
    for i in range(3):
        pl.loop(cuts[i], cuts[i + 1])(attend_block)
        if i < 2:
            cube.level(i)
    for i in range(2, cube.levels):
        cube.level(i)

    own_gate.wait()

    @pl.loop(0, heads)
    def _(h):
        @pl.when(h * r + to_sub != s)
        def _():
            q_copy(h).wait_send()
            pltpu.make_async_remote_copy(
                src_ref=o_low.at[rows_at(0, tl)],
                dst_ref=att.at[:, head_cols(h)],
                send_sem=osend.at[0],
                recv_sem=orecv.at[h],
                device_id={"seq": s ^ 1},
                device_id_type=MESH,
            ).wait_recv()

    @pl.loop(0, blocks)
    def _(i):
        src = source_of(sub, i, ns, r)

        @pl.when(src != s)
        def _():
            o_copy(i, src).wait_send()

    pass_on(s, False)

    @pl.loop(1, ns)
    def _(step):
        t = s ^ step

        @pl.when(far(t))
        def _():
            for x, buf, ss, rs in kv:
                kv_copy(x.at[:, head_cols(t // r)], buf, ss.at[0, t], rs, t, s).wait_send()
            pass_on(t, False)

    cube.finish()


def run_attend(ns, heads, q, k, v, starts, gate):
    tl, lw = q.shape
    r = ns // heads
    nq = ns // r * tl
    nk = ns * tl
    dma = pltpu.SemaphoreType.DMA
    shape = jax.ShapeDtypeStruct
    return pl.pallas_call(
        functools.partial(attend_kernel, ns, heads),
        out_shape=(
            shape((tl, lw), BF16),
            shape((nq, HEAD_DIM), BF16),
            shape((nk, HEAD_DIM), BF16),
            shape((nk, HEAD_DIM), BF16),
            shape((nq, HEAD_DIM), F32),
            shape((ns // r, tl), F32),
            shape((gate.shape[0] * ns, gate.shape[1]), BF16),
        ),
        in_specs=[VMEM] * 5,
        out_specs=(VMEM,) * 6 + (ANY,),
        scratch_shapes=[
            pltpu.VMEM((nq, HEAD_DIM), BF16),
            dma((heads,)), dma((ns // r,)),
            dma((2, ns)), dma((ns,)),
            dma((2, ns)), dma((ns,)),
            dma((ns // r,)), dma((heads,)),
            dma((1,)),
            *CubeGather.sems(ns),
        ],
        compiler_params=pltpu.CompilerParams(
            collective_id=3, has_side_effects=True, vmem_limit_bytes=VMEM_BYTES
        ),
        cost_estimate=pl.CostEstimate(flops=3 * 10**9, bytes_accessed=8 * 10**6, transcendentals=5 * 10**6),
        name="attend",
    )(q, k, v, starts, gate)


def attend_back_kernel(
    ns, heads, do_in, starts, q_buf, k_buf, v_buf, o_buf, lse, dy2, hidden,
    dq, dk, dv, grad_down,
    do_buf, dq_low, dk_acc, dv_acc, low, pair, land,
    first, held, later, ca, cb, cc, cd,
    ds_, dr_, ps, pr, gs, gr, qs, qr,
):
    s = lax.axis_index("seq")
    r = ns // heads
    blocks = ns // r
    tl = do_in.shape[0]
    mine, sub = s // r, s % r
    parity = s % 2

    def clear():
        dk_acc[...] = jnp.zeros_like(dk_acc)
        dv_acc[...] = jnp.zeros_like(dv_acc)

    seq_barrier(s, ns, clear)
    to_sub, to_row = share_of(s, ns, r)

    def copy(src, dst, send, recv, t):
        return pltpu.make_async_remote_copy(
            src_ref=src, dst_ref=dst, send_sem=send, recv_sem=recv, device_id={"seq": t}, device_id_type=MESH
        )

    def do_copy(h):
        return copy(
            do_in.at[:, head_cols(h)], do_buf.at[rows_at(to_row, tl)], ds_.at[h], dr_.at[to_row], h * r + to_sub
        )

    @pl.loop(0, heads)
    def _(h):
        @pl.when(h * r + to_sub != s)
        def _():
            do_copy(h).start()

    block = dy2.shape[1] // ns
    cube = CubeScatter(
        s, ns, lambda b: mm(dy2[:, rows_at(b, block)], hidden[...], TN), block, first, held, later, (ca, cb, cc, cd)
    )
    cube.send_core()
    cube.add_core()

    @pl.when(to_sub == sub)
    def _():
        do_buf[rows_at(to_row, tl), :] = do_in[:, head_cols(mine)]

    scale = HEAD_DIM ** (-0.5)
    unit = scale * LOG2E

    def dq_copy(i, t):
        return copy(dq_low.at[rows_at(i, tl)], dq.at[:, head_cols(mine)], qs.at[i], qr.at[mine], t)

    ones = jnp.ones((8, HEAD_DIM), F32)

    def back_block(i):
        src = source_of(sub, i, ns, r)
        rows = rows_at(i, tl)

        @pl.when(src != s)
        def _():
            copy(do_buf.at[rows], do_buf.at[rows], ds_.at[0], dr_.at[i], s ^ 1).wait_recv()

        q = q_buf[rows, :]
        do = do_buf[rows, :]
        start = starts[pl.ds(i, 1), :]
        norm = lse[pl.ds(i, 1), :]
        delta = lax.dot_general(
            ones, do.astype(F32) * o_buf[rows, :], NT,
            precision=lax.Precision.HIGHEST, preferred_element_type=F32,
        )[:1]
        key_at = lax.broadcasted_iota(jnp.int32, (tl, tl), 0)

        def step(j, dq_sum, diagonal):
            at = rows_at(j, tl)
            keys = k_buf[at, :]
            scores = mm(keys, q, NT) * unit
            allowed = key_at >= start - j * tl
            if diagonal:
                allowed = allowed & (key_at <= lax.broadcasted_iota(jnp.int32, (tl, tl), 1))
            p = jnp.where(allowed, jnp.exp2(scores - norm), 0.0)
            dp = mm(v_buf[at, :], do, NT)
            dscore = (p * (dp - delta)).astype(BF16)
            dv_acc[at, :] += mm(p.astype(BF16), do)
            dk_acc[at, :] += mm(dscore, q)
            return dq_sum + mm(dscore, keys, TN)

        dq_sum = lax.fori_loop(0, src, lambda j, c: step(j, c, False), jnp.zeros((tl, HEAD_DIM), F32))
        dq_sum = step(src, dq_sum, True)
        dq_low[rows, :] = (dq_sum * scale).astype(BF16)

        @pl.when(src != s)
        def _():
            dq_copy(i, src).start()

        @pl.when(src == s)
        def _():
            dq[:, head_cols(mine)] = dq_low[rows, :]

    pl.loop(0, blocks - 1)(back_block)
    cube.step(0)
    pl.loop(blocks - 1, blocks)(back_block)
    half = ns // 2

    def pair_copy(w, i):
        src = 2 * i + 1 - parity
        return copy(low.at[w, rows_at(src, tl)], pair.at[w, rows_at(i, tl)], ps.at[w, i], pr.at[w, i], s ^ 1)

    @pl.loop(0, half)
    def _(i):
        at = rows_at(2 * i + 1 - parity, tl)
        low[0, at, :] = (dk_acc[at, :] * scale).astype(BF16)
        pair_copy(0, i).start()
        low[1, at, :] = dv_acc[at, :].astype(BF16)
        pair_copy(1, i).start()

    slot = sub // 2
    outs = (dk, dv)

    def back_copy(w, i):
        dest = 2 * i + parity
        return copy(
            low.at[w, rows_at(dest, tl)], land.at[w, slot, :, head_cols(mine)], gs.at[w, i], gr.at[w, mine, slot], dest
        )

    @pl.loop(0, half)
    def _(i):
        dest = 2 * i + parity
        at = rows_at(dest, tl)
        for w, acc, factor in ((0, dk_acc, scale), (1, dv_acc, 1.0)):
            copy(low.at[w, at], pair.at[w, rows_at(i, tl)], ps.at[w, i], pr.at[w, i], s ^ 1).wait_recv()
            low[w, at, :] = (acc[at, :] * factor + pair[w, rows_at(i, tl), :].astype(F32)).astype(BF16)

            @pl.when(dest != s)
            def _():
                back_copy(w, i).start()

            @pl.when(dest == s)
            def _():
                land[w, slot, :, head_cols(mine)] = low[w, at, :]

    @pl.loop(0, heads)
    def _(h):
        for w in range(2):
            for k in range(r // 2):

                @pl.when(h * r + 2 * k + parity != s)
                def _():
                    copy(
                        low.at[w, rows_at(0, tl)], land.at[w, k, :, head_cols(h)], gs.at[w, 0], gr.at[w, h, k], s ^ 1
                    ).wait_recv()

    for w in range(2):
        outs[w][...] = functools.reduce(
            lambda a, b: a + b, [land[w, k].astype(F32) for k in range(r // 2)]
        ).astype(BF16)

    @pl.loop(0, heads)
    def _(h):
        @pl.when(h * r + to_sub != s)
        def _():
            do_copy(h).wait_send()
            copy(dq_low.at[rows_at(0, tl)], dq.at[:, head_cols(h)], qs.at[0], qr.at[h], s ^ 1).wait_recv()

    @pl.loop(0, blocks)
    def _(i):
        src = source_of(sub, i, ns, r)

        @pl.when(src != s)
        def _():
            dq_copy(i, src).wait_send()

    @pl.loop(0, half)
    def _(i):
        for w in range(2):
            pair_copy(w, i).wait_send()

            @pl.when(2 * i + parity != s)
            def _():
                back_copy(w, i).wait_send()

    for i in range(1, cube.stages):
        cube.step(i)
    grad_down[...] = jnp.transpose(held[0].astype(F32)).astype(BF16)
    cube.core_sent()
    cube.finish()


def run_attend_back(ns, heads, do, starts, q, k, v, o, lse, dy2, hidden):
    tl, lw = do.shape
    r = ns // heads
    nq = ns // r * tl
    nk = ns * tl
    dma = pltpu.SemaphoreType.DMA
    shape = jax.ShapeDtypeStruct
    return pl.pallas_call(
        functools.partial(attend_back_kernel, ns, heads),
        out_shape=(shape((tl, lw), BF16),) * 3 + (shape((hidden.shape[1], dy2.shape[1] // ns), BF16),),
        in_specs=[VMEM] * 9,
        out_specs=(VMEM,) * 4,
        scratch_shapes=[
            pltpu.VMEM((nq, HEAD_DIM), BF16),
            pltpu.VMEM((nq, HEAD_DIM), BF16),
            pltpu.VMEM((nk, HEAD_DIM), F32),
            pltpu.VMEM((nk, HEAD_DIM), F32),
            pltpu.VMEM((2, nk, HEAD_DIM), BF16),
            pltpu.VMEM((2, nk // 2, HEAD_DIM), BF16),
            pltpu.VMEM((2, r // 2, tl, lw), BF16),
            *CubeScatter.scratch(ns, dy2.shape[1] // ns, hidden.shape[1]),
            dma((heads,)), dma((ns // r,)),
            dma((2, ns // 2)), dma((2, ns // 2)),
            dma((2, ns // 2)), dma((2, heads, r // 2)),
            dma((ns // r,)), dma((heads,)),
        ],
        compiler_params=pltpu.CompilerParams(
            collective_id=4, has_side_effects=True, vmem_limit_bytes=VMEM_BYTES
        ),
        cost_estimate=pl.CostEstimate(flops=8 * 10**9, bytes_accessed=10 * 10**6, transcendentals=5 * 10**6),
        name="attend_back",
    )(do, starts, q, k, v, o, lse, dy2, hidden)


def cross_barrier(s, z, ns, n, between=None):
    bar = pltpu.get_barrier_semaphore()
    for axis, me, count in (("seq", s, ns), ("head", z, n)):
        for other in range(count):

            @pl.when(other != me)
            def _():
                pl.semaphore_signal(bar, inc=1, device_id={axis: other}, device_id_type=MESH)

    if between is not None:
        between()
    pl.semaphore_wait(bar, ns - 1 + n - 1)


def row_sums(left, right):
    ones = jnp.ones((8, left.shape[1]), F32)
    both = [
        lax.dot_general(ones, x, NT, precision=lax.Precision.HIGHEST, preferred_element_type=F32) for x in (left, right)
    ]
    return jnp.where(lax.broadcasted_iota(jnp.int32, both[0].shape, 0) < 4, both[0], both[1])


def as_column(sums, row):
    pick = (lax.broadcasted_iota(jnp.int32, (8, HEAD_DIM), 0) == row).astype(F32)
    return lax.dot_general(sums, pick, TN, precision=lax.Precision.HIGHEST, preferred_element_type=F32)


class SmallExchange:
    def __init__(self, axis, me, count, land, send_sem, recv_sem):
        self.axis, self.me, self.count, self.land = axis, me, count, land
        self.send_sem, self.recv_sem = send_sem, recv_sem

    def copy(self, slot, to):
        return remote(self.land.at[slot], self.land.at[slot], self.send_sem.at[to], self.recv_sem.at[slot], self.axis, to)

    def each(self, act):
        @pl.loop(0, self.count)
        def _(other):
            @pl.when(other != self.me)
            def _():
                act(other)

    def start(self):
        self.each(lambda other: self.copy(self.me, other).start())

    def receive(self):
        self.each(lambda other: self.copy(other, other).wait_recv())

    def finish(self):
        self.each(lambda other: self.copy(self.me, other).wait_send())


def turn(x, cos, sin):
    return x * cos + pltpu.roll(x, HEAD_DIM // 2, 1) * sin


def turn_back(x, cos, sin):
    return x * cos - pltpu.roll(x, HEAD_DIM // 2, 1) * sin


def project_kernel(
    n, ns, depth_full,
    tok, wq, wk, wv, wo, gq, gk, cos, sin,
    x_out, w_out, q_raw, k_raw, totals, q_rot, k_rot, v_low,
    x, w, land, lsem, ags, agr, cgs, cgr, ss, sr,
):
    s, z = lax.axis_index("seq"), lax.axis_index("head")
    rows, depth = tok.shape
    block, lw = wq.shape
    heads = lw // HEAD_DIM
    cross_barrier(s, z, ns, n)
    mine = rows_at(s, block)

    def head_gain(h):
        return head_cols(z * heads + h)

    loads = [pltpu.make_async_copy(tok, x.at[rows_at(z, rows)], lsem.at[0])] + [
        pltpu.make_async_copy(m, w.at[mine, pl.ds(i * lw, lw)], lsem.at[i + 1]) for i, m in enumerate((wq, wk, wv))
    ]
    for copy in loads:
        copy.start()
    loads[0].wait()
    cube = CubeGather(s, ns, w, block, cgs, cgr)
    levels = len(cube.orders[0])
    done = []

    def weights(k):
        todo = [0] if k == 0 and n > 2 else [i for i in range(levels) if i not in done]
        for i in todo:
            cube.level(i)
            done.append(i)

    def start_weights():
        w[mine, 3 * lw :] = jnp.transpose(wo[...].astype(F32)).astype(BF16)
        for copy in loads[1:]:
            copy.wait()
        cube.start()

    def multiply(src):
        at = rows_at(src, rows)
        for i, to in enumerate((q_raw, k_raw)):
            to[at, :] = mm(x[at, :], w[:, i * lw : (i + 1) * lw])
        v_low[at, :] = mm(x[at, :], w[:, 2 * lw : 3 * lw]).astype(BF16)

    part = rows // AG_CHUNKS

    def copy(src, c, up):
        at = pl.ds(pl.multiple_of(src * rows + c * part, part), part)
        return remote(x.at[at], x.at[at], ags.at[up, src, c], agr.at[src, c], "head", z + 1 if up else z - 1)

    more = (z > 0, z < n - 1)
    for c in range(AG_CHUNKS):
        for up in (0, 1):

            @pl.when(more[up])
            def _():
                copy(z, c, up).start()

    start_weights()

    def sides(k):
        return ((z + k, z + k < n, 0), (z - k, z - k >= 0, 1))

    for k in range(1, n):
        for c in range(AG_CHUNKS):
            for src, there, up in sides(k):

                @pl.when(there)
                def _():
                    copy(src, c, up).wait_recv()

                    @pl.when(more[up])
                    def _():
                        copy(src, c, up).start()

        if k <= 2:
            weights(k - 1)
        if k == min(2, n - 1):
            multiply(z)
            for src, there, _ in sides(1):
                pl.when(there)(functools.partial(multiply, src))
        if k > 1:
            for src, there, _ in sides(k):
                pl.when(there)(functools.partial(multiply, src))

    outs = [pltpu.make_async_copy(x, x_out, lsem.at[4]), pltpu.make_async_copy(w, w_out, lsem.at[5])]
    for out in outs:
        out.start()
    totals[...] = row_sums(q_raw[...] * q_raw[...], k_raw[...] * k_raw[...])
    land[z] = totals[...]
    small = SmallExchange("head", z, n, land, ss, sr)
    small.start()
    small.receive()
    total = land[0]
    for k in range(1, n):
        total = total + land[k]
    totals[...] = total
    for row, raw, gain, to in ((0, q_raw, gq, q_rot), (4, k_raw, gk, k_rot)):
        scale = lax.rsqrt(as_column(total, row) / depth_full + epsilon)
        for h in range(heads):
            cols = slice(h * HEAD_DIM, (h + 1) * HEAD_DIM)
            to[:, cols] = turn(raw[:, cols] * scale * gain[:, head_gain(h)], cos[...], sin[...]).astype(BF16)
    small.finish()
    cube.finish()
    for out in outs:
        out.wait()

    @pl.loop(0, n)
    def _(src):
        for c in range(AG_CHUNKS):

            @pl.when((src >= z) & (z > 0))
            def _():
                copy(src, c, 0).wait_send()

            @pl.when((src <= z) & (z < n - 1))
            def _():
                copy(src, c, 1).wait_send()


def run_project(n, ns, tok, wq, wk, wv, wo, gq, gk, cos, sin):
    rows, depth = tok.shape
    tl = rows * n
    lw = wq.shape[1]
    dma = pltpu.SemaphoreType.DMA
    shape = jax.ShapeDtypeStruct
    return pl.pallas_call(
        functools.partial(project_kernel, n, ns, depth),
        out_shape=(
            shape((tl, depth), BF16),
            shape((depth, 4 * lw), BF16),
            shape((tl, lw), F32),
            shape((tl, lw), F32),
            shape((8, tl), F32),
            shape((tl, lw), BF16),
            shape((tl, lw), BF16),
            shape((tl, lw), BF16),
        ),
        in_specs=[ANY] * 4 + [VMEM] * 5,
        out_specs=(ANY,) * 2 + (VMEM,) * 6,
        scratch_shapes=[
            pltpu.VMEM((tl, depth), BF16),
            pltpu.VMEM((depth, 4 * lw), BF16),
            pltpu.VMEM((n, 8, tl), F32),
            dma((6,)),
            dma((2, n, AG_CHUNKS)), dma((n, AG_CHUNKS)),
            *CubeGather.sems(ns),
            dma((n,)), dma((n,)),
        ],
        compiler_params=pltpu.CompilerParams(
            collective_id=5, has_side_effects=True, vmem_limit_bytes=VMEM_BYTES
        ),
        cost_estimate=pl.CostEstimate(flops=3 * 10**9, bytes_accessed=20 * 10**6, transcendentals=0),
        name="project",
    )(tok, wq, wk, wv, wo, gq, gk, cos, sin)


def input_kernel(
    n, ns, depth_full,
    dq, dk, dv, q_raw, k_raw, totals, gq, gk, cos, sin, x, w, att, dy1, attn_part, mlp_part,
    total, grad_q, grad_k, grad_v, grad_o, gains,
    dqkv, q_back, k_back, inner, land, message, message_z, gain_land,
    first, held, later, c0s, c0r, c1s, c1r,
    first_o, held_o, later_o, o0s, o0r, o1s, o1r,
    ss, sr, ms, mr, zs, zr, s1s, s1r,
):
    s, z = lax.axis_index("seq"), lax.axis_index("head")
    rows, depth = total.shape
    tl, lw = dq.shape
    block = depth // ns
    heads = lw // HEAD_DIM

    def head_gain(h):
        return head_cols(z * heads + h)

    sums = totals[...]
    scales = [lax.rsqrt(as_column(sums, row) / depth_full + epsilon) for row in (0, 4)]
    todo = ((dq, q_raw, gq, q_back), (dk, k_raw, gk, k_back))
    products = []

    def turn_all():
        message[...] = jnp.zeros_like(message)
        for i, (grad, raw, gain, back) in enumerate(todo):
            product = jnp.zeros((tl, HEAD_DIM), F32)
            for h in range(heads):
                cols = slice(h * HEAD_DIM, (h + 1) * HEAD_DIM)
                hat = raw[:, cols] * scales[i]
                turned = turn_back(grad[:, cols].astype(F32), cos[...], sin[...])
                message[0, pl.ds(i, 1), cols] = jnp.sum(turned * hat, axis=0, keepdims=True)
                turned = turned * gain[:, head_gain(h)]
                back[:, cols] = turned
                product = product + turned * hat
            products.append(product)
        inner[z] = row_sums(*products)
        for t in range(1, ns):
            message[t, pl.ds(0, 2), pl.ds(0, lw)] = message[0, pl.ds(0, 2), pl.ds(0, lw)]
        for t in range(ns):
            for i, part in enumerate((attn_part, mlp_part)):
                message[t, pl.ds(i, 1), pl.ds(lw, block)] = part[:, t * block : (t + 1) * block]

    cross_barrier(s, z, ns, n, turn_all)
    small = SmallExchange("head", z, n, inner, ss, sr)
    small.start()

    def message_copy(t, frm):
        return remote(message.at[t], message_z.at[frm], ms.at[t], mr.at[frm], "seq", t)

    def each_seq(act):
        @pl.loop(0, ns)
        def _(t):
            @pl.when(t != s)
            def _():
                act(t)

    message_z[s] = message[s]
    each_seq(lambda t: message_copy(t, s).start())
    dqkv[:, 2 * lw :] = dv[...]
    cube_o = CubeScatter(
        s, ns, lambda b: mm(dy1[:, rows_at(b, block)], att[...], TN), block, first_o, held_o, later_o, (o0s, o0r, o1s, o1r)
    )
    cube_o.send_core()
    cube_o.add_core()
    small.receive()
    sums = inner[0]
    for k in range(1, n):
        sums = sums + inner[k]
    for i, (grad, raw, gain, back) in enumerate(todo):
        mean = as_column(sums, 4 * i) / depth_full
        for h in range(heads):
            cols = slice(h * HEAD_DIM, (h + 1) * HEAD_DIM)
            to = slice(i * lw + h * HEAD_DIM, i * lw + (h + 1) * HEAD_DIM)
            dqkv[:, to] = (scales[i] * (back[:, cols] - raw[:, cols] * scales[i] * mean)).astype(BF16)

    width = depth // STEPS

    def weight_block(b):
        cols = rows_at(b, block)
        return mm(x[:, cols], dqkv[...], TN)

    def in_part(d, c):
        return mm(dqkv[rows_at(d, rows), :], w[rows_at(c, width), : 3 * lw], NT)

    cube = CubeScatter(s, ns, weight_block, block, first, held, later, (c0s, c0r, c1s, c1r))
    line = LineScatter(z, n, in_part, land, s1s, s1r, total)
    half = ns // 2

    def task(slot):
        for i, act in enumerate((cube.send_core, cube.add_core)):
            low = 1 + i * (half // 2)

            @pl.when((slot >= low) & (slot < low + half // 2))
            def _():
                for j in range(2):
                    act(2 * (slot - low) + j)

    done = 1 + half
    line.run(0, done, None, task)
    line.start_own()
    line.run(done, done + 3)
    for i in range(cube.stages - 1):
        cube_o.step(i)
    line.run(done + 3, line.slots)
    for i in range(cube.stages - 1):
        cube.step(i)

    each_seq(lambda t: message_copy(t, t).wait_recv())
    received = message_z[0]
    for t in range(1, ns):
        received = received + message_z[t]
    each_seq(lambda t: message_copy(t, s).wait_send())
    gain_land[z] = received
    rounds = SmallExchange("head", z, n, gain_land, zs, zr)
    rounds.start()
    line.own()
    cube_o.step(cube.stages - 1)
    grad_o[...] = jnp.transpose(held_o[0].astype(F32)).astype(BF16)
    cube.step(cube.stages - 1)
    for i, to in enumerate((grad_q, grad_k, grad_v)):
        to[...] = held[0, :, i * lw : (i + 1) * lw]
    rounds.receive()
    at = s * block
    gains[...] = jnp.zeros_like(gains)
    gains[0:2, :] = gain_land[at // lw, pl.ds(0, 2), pl.ds(pl.multiple_of(at % lw, block), block)]
    both = gain_land[0, pl.ds(0, 2), pl.ds(lw, block)]
    for k in range(1, n):
        both = both + gain_land[k, pl.ds(0, 2), pl.ds(lw, block)]
    gains[2:4, :] = both
    for one in (cube, cube_o):
        one.core_sent()
        one.finish()
    line.finish()
    small.finish()
    rounds.finish()


def run_input(n, ns, dq, dk, dv, q_raw, k_raw, totals, gq, gk, cos, sin, x, w, att, dy1, attn_part, mlp_part):
    tl, lw = dq.shape
    rows, depth = tl // n, x.shape[1]
    block = depth // ns
    dma = pltpu.SemaphoreType.DMA
    shape = jax.ShapeDtypeStruct
    return pl.pallas_call(
        functools.partial(input_kernel, n, ns, depth),
        out_shape=(shape((rows, depth), F32),)
        + (shape((block, lw), BF16),) * 3
        + (shape((lw, block), BF16), shape((8, block), F32)),
        in_specs=[VMEM] * 16,
        out_specs=(VMEM,) * 6,
        scratch_shapes=[
            pltpu.VMEM((tl, 3 * lw), BF16),
            pltpu.VMEM((tl, lw), F32),
            pltpu.VMEM((tl, lw), F32),
            pltpu.VMEM((n, 8, tl), F32),
            pltpu.VMEM((2, n, STEPS, rows, depth // STEPS), BF16),
            pltpu.VMEM((ns, 8, lw + block), F32),
            pltpu.VMEM((ns, 8, lw + block), F32),
            pltpu.VMEM((n, 8, lw + block), F32),
            *CubeScatter.scratch(ns, block, 3 * lw),
            *CubeScatter.scratch(ns, block, lw),
            dma((n,)), dma((n,)),
            dma((ns,)), dma((ns,)),
            dma((n,)), dma((n,)),
            *line_sems(n)["scatter"],
        ],
        compiler_params=pltpu.CompilerParams(
            collective_id=6, has_side_effects=True, vmem_limit_bytes=VMEM_BYTES
        ),
        cost_estimate=pl.CostEstimate(flops=8 * 10**9, bytes_accessed=30 * 10**6, transcendentals=0),
        name="into_input",
    )(dq, dk, dv, q_raw, k_raw, totals, gq, gk, cos, sin, x, w, att, dy1, attn_part, mlp_part)


def doc_starts(doc_lengths, token_index):
    ends = jnp.cumsum(doc_lengths)
    return jnp.sum(jnp.where(token_index[..., None] >= ends, doc_lengths, 0), axis=-1).astype(jnp.int32)


def turn_tables(positions):
    frequency = jnp.power(rope_base, -jnp.arange(HEAD_DIM // 2, dtype=F32) * (2.0 / HEAD_DIM))
    angles = positions.astype(F32)[:, None] * frequency[None, :]
    cos, sin = jnp.cos(angles), jnp.sin(angles)
    return jnp.concatenate([cos, cos], axis=1), jnp.concatenate([-sin, sin], axis=1)


def on_device(
    tokens,
    cotangent,
    doc_lengths,
    q_weight,
    k_weight,
    v_weight,
    o_weight,
    gate_weight,
    up_weight,
    down_weight,
    q_gain,
    k_gain,
    attn_gain,
    mlp_gain,
):
    ns, nz = lax.axis_size("seq"), lax.axis_size("head")
    seq_index, head_index = lax.axis_index("seq"), lax.axis_index("head")
    lw = q_weight.shape[1]
    heads = lw // HEAD_DIM
    tl = tokens.shape[0] * nz
    ff = gate_weight.shape[1]
    token_index = seq_index * tl + jnp.arange(tl, dtype=jnp.int32)
    cos, sin = turn_tables(token_index - doc_starts(doc_lengths, token_index))
    share = ns // heads
    sources = jnp.stack([source_of(seq_index % share, i, ns, share) for i in range(ns // share)])
    starts = doc_starts(doc_lengths, sources[:, None] * tl + jnp.arange(tl, dtype=jnp.int32)[None, :])
    gq, gk = q_gain[None], k_gain[None]

    x, w, q_raw, k_raw, totals, q_rot, k_rot, v_low = run_project(
        nz, ns, tokens, q_weight, k_weight, v_weight, o_weight, gq, gk, cos, sin
    )
    attended, q_held, k_held, v_held, o_held, lse, gate = run_attend(
        ns, heads, q_rot, k_rot, v_low, starts, gate_weight
    )
    output, h1r, branch, hidden, dy2, dg, du, mlp_part, up = run_forward(
        nz, ns, attended, tokens, cotangent, w, gate, up_weight, down_weight, attn_gain[None], mlp_gain[None]
    )
    middle, dy1, datt, attn_part, grad_gate, grad_up = run_backward(
        nz, ns, dg, du, h1r, cotangent, branch, w, gate, up, attn_gain[None]
    )
    dq, dk, dv, grad_down = run_attend_back(
        ns, heads, datt, starts, q_held, k_held, v_held, o_held, lse, dy2, hidden
    )
    last, grad_q, grad_k, grad_v, grad_o, gains = run_input(
        nz, ns, dq, dk, dv, q_raw, k_raw, totals, gq, gk, cos, sin, x, w, attended, dy1, attn_part, mlp_part
    )
    return (
        output,
        middle + last,
        grad_q.astype(F32),
        grad_k.astype(F32),
        grad_v.astype(F32),
        grad_o.astype(F32),
        grad_gate.astype(F32),
        grad_up.astype(F32),
        grad_down.astype(F32),
        gains[0],
        gains[1],
        gains[2],
        gains[3],
    )


def solution(mesh):
    in_specs = (
        P(("seq", "head"), None),
        P(("seq", "head"), None),
        P(),
        P("seq", "head"),
        P("seq", "head"),
        P("seq", "head"),
        P("head", "seq"),
        P("seq", "head"),
        P("seq", "head"),
        P("head", "seq"),
        P(),
        P(),
        P(),
        P(),
    )
    out_specs = (
        P(("seq", "head"), None),
        P(("seq", "head"), None),
        P("seq", "head"),
        P("seq", "head"),
        P("seq", "head"),
        P("head", "seq"),
        P("seq", "head"),
        P("seq", "head"),
        P("head", "seq"),
        P("seq"),
        P("seq"),
        P("seq"),
        P("seq"),
    )
    return jax.shard_map(
        on_device, mesh=mesh, in_specs=in_specs, out_specs=out_specs, check_vma=False
    )
```

```python
import functools

import jax
import jax.numpy as jnp
from jax import lax
from jax.experimental import pallas as pl
from jax.experimental.pallas import tpu as pltpu
from jax.sharding import PartitionSpec as P

HEAD_DIM = 128
epsilon = 1e-06
rope_base = 500000.0

MESH = pl.DeviceIdType.MESH
F32 = jnp.float32
BF16 = jnp.bfloat16
STEPS = 4
LAG = 1
EARLY = (7, 16)
AG_CHUNKS = 2
VMEM_BYTES = 62 * 1024 * 1024
ANY = pl.BlockSpec(memory_space=pl.ANY)
VMEM = pl.BlockSpec(memory_space=pltpu.VMEM)
SMEM = pl.BlockSpec(memory_space=pltpu.SMEM)
NN = (((1,), (0,)), ((), ()))
NT = (((1,), (1,)), ((), ()))
TN = (((0,), (0,)), ((), ()))


def first_of_document(docs, token):
    end, first = jnp.int32(0), jnp.zeros_like(token)
    for i in range(docs.shape[0]):
        end = end + docs[i]
        first = first + jnp.where(token >= end, docs[i], 0)
    return first


def mm(left, right, dims=NN):
    return lax.dot_general(left, right, dims, preferred_element_type=F32)


def early_part(ff):
    return ff * EARLY[0] // EARLY[1] // HEAD_DIM * HEAD_DIM


def rows_at(index, count):
    return pl.ds(pl.multiple_of(index * count, count), count)


def cube_barrier(s, z, ns, n, between=None):
    bar = pltpu.get_barrier_semaphore()
    bits = [1 << i for i in range(ns.bit_length() - 1)]
    for bit in bits:
        pl.semaphore_signal(bar, inc=1, device_id={"seq": s ^ bit}, device_id_type=MESH)
    for other, there in ((z - 1, z > 0), (z + 1, z < n - 1)):

        @pl.when(there)
        def _():
            pl.semaphore_signal(bar, inc=1, device_id={"head": other}, device_id_type=MESH)

    if between is not None:
        between()
    pl.semaphore_wait(bar, len(bits) + (z > 0).astype(jnp.int32) + (z < n - 1).astype(jnp.int32))


def line_gather(z, n, buf, rows, send_sem, recv_sem, use, hooks=(), ready=None):
    part = rows // AG_CHUNKS

    def copy(src, c, up):
        at = pl.ds(pl.multiple_of(src * rows + c * part, part), part)
        return pltpu.make_async_remote_copy(
            src_ref=buf.at[at],
            dst_ref=buf.at[at],
            send_sem=send_sem.at[up, src, c],
            recv_sem=recv_sem.at[src, c],
            device_id={"head": z + 1 if up else z - 1},
            device_id_type=MESH,
        )

    more = (z > 0, z < n - 1)
    for c in range(AG_CHUNKS):
        for up in (0, 1):

            @pl.when(more[up])
            def _():
                copy(z, c, up).start()

    if ready is not None:
        ready()
    use(z)

    @pl.loop(1, n)
    def _(k):
        sides = ((z + k, z + k < n, 0), (z - k, z - k >= 0, 1))
        for c in range(AG_CHUNKS):
            for src, there, up in sides:

                @pl.when(there)
                def _():
                    copy(src, c, up).wait_recv()

                    @pl.when(more[up])
                    def _():
                        copy(src, c, up).start()

        for src, there, up in sides:

            @pl.when(there)
            def _():
                use(src)

        for i, hook in enumerate(hooks):
            pl.when(k == i + 1)(hook)

    @pl.loop(0, n)
    def _(src):
        for c in range(AG_CHUNKS):

            @pl.when((src >= z) & (z > 0))
            def _():
                copy(src, c, 0).wait_send()

            @pl.when((src <= z) & (z < n - 1))
            def _():
                copy(src, c, 1).wait_send()


class LineScatter:
    def __init__(self, z, n, partial, land, send_sem, recv_sem, total):
        self.z, self.n, self.partial, self.land, self.total = z, n, partial, land, total
        self.send_sem, self.recv_sem = send_sem, recv_sem

    def copy(self, d, c, up):
        return pltpu.make_async_remote_copy(
            src_ref=self.land.at[up, d, c],
            dst_ref=self.land.at[up, d, c],
            send_sem=self.send_sem.at[up, d, c],
            recv_sem=self.recv_sem.at[up, d, c],
            device_id={"head": self.z + 1 if up else self.z - 1},
            device_id_type=MESH,
        )

    @property
    def slots(self):
        return (self.n - 1) * (STEPS + LAG)

    def run(self, low, high, before=None, after=None):
        z, n, land = self.z, self.n, self.land

        @pl.loop(low, high)
        def _(slot):
            if before is not None:
                before(slot)
            for up in (1, 0):
                t = slot - (z if up else n - 1 - z) * LAG
                j = t // STEPS
                c = t - j * STEPS
                d = n - 1 - j if up else j
                first = z == 0 if up else z == n - 1
                there = (t >= 0) & (j < n - 1) & ((d > z) if up else (d < z))

                @pl.when(there)
                def _():
                    mine = self.partial(d, c)

                    @pl.when(first)
                    def _():
                        land[up, d, c] = mine.astype(land.dtype)

                    @pl.when(jnp.logical_not(first))
                    def _():
                        self.copy(d, c, up).wait_recv()
                        land[up, d, c] = (land[up, d, c].astype(F32) + mine).astype(land.dtype)

                    self.copy(d, c, up).start()

            if after is not None:
                after(slot)

    def start_own(self):
        width = self.total.shape[1] // STEPS

        @pl.loop(0, STEPS)
        def _(c):
            self.total[:, rows_at(c, width)] = self.partial(self.z, c)

    def own(self):
        z, n, total = self.z, self.n, self.total
        width = total.shape[1] // STEPS

        @pl.loop(0, STEPS)
        def _(c):
            at = rows_at(c, width)
            for there, up in ((z > 0, 1), (z < n - 1, 0)):

                @pl.when(there)
                def _():
                    self.copy(z, c, up).wait_recv()
                    total[:, at] += self.land[up, z, c].astype(F32)

    def finish(self):
        @pl.loop(0, self.n * STEPS)
        def _(t):
            d, c = t // STEPS, t % STEPS
            for there, up in ((d > self.z, 1), (d < self.z, 0)):

                @pl.when(there)
                def _():
                    self.copy(d, c, up).wait_send()


def line_sems(n):
    dma = pltpu.SemaphoreType.DMA
    return {
        "gather": [dma((2, n, AG_CHUNKS)), dma((n, AG_CHUNKS))],
        "scatter": [dma((2, n, STEPS)), dma((2, n, STEPS))],
    }


BLOCK = 16


def row_scale(block):
    return lax.rsqrt(jnp.mean(block * block, axis=-1, keepdims=True) + epsilon)


def norm_back(e, normed, scale, gain):
    g = e * gain
    return scale * (g - normed * jnp.mean(g * normed, axis=-1, keepdims=True))


def sigmoid(x):
    return 1.0 / (1.0 + jnp.exp(-x))


def subsets(bits):
    found = [0]
    for bit in bits:
        found += [bit | other for other in found]
    return found


def orders_of(ns):
    chips = [1 << i for i in range(1, ns.bit_length() - 1)]
    return (chips, chips[::-1])


def remote(src, dst, send, recv, axis, to):
    return pltpu.make_async_remote_copy(
        src_ref=src, dst_ref=dst, send_sem=send, recv_sem=recv, device_id={axis: to}, device_id_type=MESH
    )


class CubeGather:
    def __init__(self, s, ns, buf, rows, send_sem, recv_sem, own=None):
        self.own = own
        self.s, self.buf, self.rows, self.send_sem, self.recv_sem = s, buf, rows, send_sem, recv_sem
        self.orders = [order + [1] for order in orders_of(ns)]

    def copy(self, half, bit, block):
        part = self.rows // 2
        at = pl.ds(pl.multiple_of(block * self.rows + half * part, part), part)
        source = self.buf.at[at]
        if block is self.s and self.own is not None:
            source = self.own.at[pl.ds(half * part, part)]
        return remote(
            source, self.buf.at[at],
            self.send_sem.at[bit.bit_length() - 1, block, half], self.recv_sem.at[block, half],
            "seq", self.s ^ bit,
        )

    @property
    def levels(self):
        return len(self.orders[0])

    def start(self):
        for i in range(self.levels):
            for half, order in enumerate(self.orders):
                self.copy(half, order[i], self.s).start()

    def level(self, i):
        for j in range(2**i):
            for half, order in enumerate(self.orders):
                block = self.s ^ order[i] ^ subsets(order[:i])[j]
                self.copy(half, order[i], block).wait_recv()
                for bit in order[i + 1 :]:
                    self.copy(half, bit, block).start()

    def finish(self):
        for half, order in enumerate(self.orders):
            for i, bit in enumerate(order):
                for other in subsets(order[:i]):
                    self.copy(half, bit, self.s ^ other if other else self.s).wait_send()

    @staticmethod
    def sems(ns):
        dma = pltpu.SemaphoreType.DMA
        return [dma((ns.bit_length() - 1, ns, 2)), dma((ns, 2))]


class CubeScatter:
    def __init__(self, s, ns, block, rows, first, held, later, sems):
        self.s, self.block, self.rows = s, block, rows
        self.first, self.held, self.later = first, held, later
        self.send0, self.recv0, self.send1, self.recv1 = sems
        self.orders = orders_of(ns)
        self.half = ns // 2

    def core_copy(self, j):
        return remote(self.first.at[j], self.held.at[j], self.send0.at[j], self.recv0.at[j], "seq", self.s ^ 1)

    def send_core(self, j=None):
        if j is None:
            pl.loop(0, self.half)(self.send_core)
            return
        j = self.half - 1 - j
        self.first[j] = self.block(self.s ^ (2 * j + 1)).astype(BF16)
        self.core_copy(j).start()

    def base(self, i):
        return sum(2 ** (self.stages - 1 - k) for k in range(i))

    def move(self, i, half, slot, other):
        part = self.rows // 2
        return remote(
            self.held.at[(self.orders[half][i] | other) >> 1, pl.ds(half * part, part)],
            self.later.at[half, slot], self.send1.at[half, slot], self.recv1.at[half, slot],
            "seq", self.s ^ self.orders[half][i],
        )

    def moves(self, i):
        part = self.rows // 2
        for half, order in enumerate(self.orders):
            for j, other in enumerate(subsets(order[i + 1 :])):
                slot = self.base(i) + j
                yield other >> 1, pl.ds(half * part, part), half, slot, self.move(i, half, slot, other)

    def add_core(self, j=None):
        if j is None:
            pl.loop(0, self.half)(self.add_core)
            return
        j = self.half - 1 - j
        mine = self.block(self.s ^ (2 * j))
        self.core_copy(j).wait_recv()
        self.held[j] = (self.held[j].astype(F32) + mine).astype(BF16)
        for half, order in enumerate(self.orders):
            for slot, other in enumerate(subsets(order[1:])):

                @pl.when(j == (order[0] | other) >> 1)
                def _():
                    self.move(0, half, slot, other).start()

    def send(self, i):
        for *_, copy in self.moves(i):
            copy.start()

    def take(self, i):
        for j, at, half, slot, copy in self.moves(i):
            copy.wait_recv()
            self.held[j, at] = (self.held[j, at].astype(F32) + self.later[half, slot].astype(F32)).astype(BF16)

    def step(self, i):
        self.take(i)
        if i + 1 < self.stages:
            self.send(i + 1)

    @property
    def stages(self):
        return len(self.orders[0])

    def core_sent(self):
        @pl.loop(0, self.half)
        def _(j):
            self.core_copy(j).wait_send()

    def finish(self):
        for i in range(self.stages):
            for *_, copy in self.moves(i):
                copy.wait_send()

    @staticmethod
    def scratch(ns, rows, width):
        dma = pltpu.SemaphoreType.DMA
        half = ns // 2
        return [
            pltpu.VMEM((half, rows, width), BF16),
            pltpu.VMEM((half, rows, width), BF16),
            pltpu.VMEM((2, half - 1, rows // 2, width), BF16),
            dma((half,)), dma((half,)), dma((2, half - 1)), dma((2, half - 1)),
        ]


def forward_kernel(
    n, ns,
    att, tok, cot, more, gate_b, up, down, attn_gain, mlp_gain,
    out, h1r_out, branch_out, hidden_out, dy2_out, dg_out, du_out, gain_part, up_out,
    h1r, hidden, dy2, dg, du,
    wo, wd, wg, wu, land, branch, h1, second, g_pre, u_pre,
    wsem, osem, bsem, g1s, g1r, s1s, s1r, g2s, g2r, s2s, s2r, us, ur, ds, dr,
):
    s, z = lax.axis_index("seq"), lax.axis_index("head")
    rows, depth = tok.shape
    lw, ff = att.shape[1], up.shape[1]
    block = depth // ns
    width = depth // STEPS
    mine = rows_at(s, block)
    l_o = pltpu.make_async_copy(more.at[:, pl.ds(0, lw)], wo, wsem.at[0])
    l_u = pltpu.make_async_copy(up, wu.at[mine], wsem.at[1])
    early = more.shape[1] - lw
    l_g = pltpu.make_async_copy(more.at[:, pl.ds(lw, early)], wg.at[:, pl.ds(0, early)], wsem.at[2])
    l_h = pltpu.make_async_copy(gate_b, wg.at[:, pl.ds(early, ff - early)], wsem.at[3])
    for copy in (l_o, l_u, l_g, l_h):
        copy.start()
    cube_barrier(s, z, ns, n)
    cube_u = CubeGather(s, ns, wu, block, us, ur)
    cube_d = CubeGather(s, ns, wd, block, ds, dr)
    levels = cube_u.levels
    l_u.wait()
    cube_u.start()
    l_o.wait()

    def out_part(d, c):
        return mm(att[rows_at(d, rows), :], wo[rows_at(c, width), :], NT)

    line = LineScatter(z, n, out_part, land, s1s, s1r, branch)
    line.run(0, STEPS)
    line.start_own()
    wd[mine, :] = jnp.transpose(down[...].astype(F32)).astype(BF16)
    cube_u.level(0)
    line.run(STEPS, 2 * STEPS)
    for i in range(1, levels - 1):
        cube_u.level(i)
    cube_d.start()
    line.run(2 * STEPS, line.slots)
    line.own()
    line.finish()
    o_branch = pltpu.make_async_copy(branch, branch_out, osem.at[0])
    o_branch.start()
    gain_part[...] = jnp.zeros_like(gain_part)

    @pl.loop(0, rows // BLOCK)
    def _(i):
        at = rows_at(i, BLOCK)
        y = branch[at, :]
        h = tok[at, :].astype(F32) + y * row_scale(y) * attn_gain[...]
        h1[at, :] = h
        h1r[pl.ds(pl.multiple_of(z * rows + i * BLOCK, BLOCK), BLOCK), :] = h.astype(BF16)

    fw = ff // STEPS
    o_up = pltpu.make_async_copy(wu, up_out, osem.at[1])
    o_h1r = pltpu.make_async_copy(h1r, h1r_out, osem.at[2])
    o_hidden = pltpu.make_async_copy(hidden, hidden_out, osem.at[3])
    o_dy2 = pltpu.make_async_copy(dy2, dy2_out, osem.at[4])

    def up_block(src):
        at = rows_at(src, rows)

        @pl.loop(0, STEPS)
        def _(c):
            cols = rows_at(c, fw)
            x = h1r[at, :]
            g = mm(x, wg[:, cols])
            u = mm(x, wu[:, cols])
            g_pre[at, cols] = g
            u_pre[at, cols] = u
            hidden[at, cols] = (g * sigmoid(g) * u).astype(BF16)

    def weights_there():
        l_g.wait()
        l_h.wait()
        cube_u.level(levels - 1)
        o_up.start()

    hooks = [functools.partial(cube_d.level, i) for i in range(levels)]
    line_gather(z, n, h1r, rows, g1s, g1r, up_block, hooks[: n - 1], weights_there)
    for hook in hooks[n - 1 :]:
        hook()
    o_h1r.start()
    o_hidden.start()

    def down_part(d, c):
        return mm(hidden[rows_at(d, rows), :], wd[rows_at(c, width), :], NT)

    line = LineScatter(z, n, down_part, land, s2s, s2r, second)
    line.run(0, STEPS)
    line.start_own()
    line.run(STEPS, line.slots)
    line.own()
    line.finish()

    @pl.loop(0, rows // BLOCK)
    def _(i):
        at = rows_at(i, BLOCK)
        y = second[at, :]
        scale = row_scale(y)
        normed = y * scale
        e = cot[at, :].astype(F32)
        out[at, :] = (h1[at, :] + normed * mlp_gain[...]).astype(BF16)
        gain_part[...] += jnp.sum(e * normed, axis=0, keepdims=True)
        dy2[pl.ds(pl.multiple_of(z * rows + i * BLOCK, BLOCK), BLOCK), :] = norm_back(
            e, normed, scale, mlp_gain[...]
        ).astype(BF16)

    def back_block(src):
        at = rows_at(src, rows)

        @pl.loop(0, STEPS)
        def _(c):
            cols = rows_at(c, fw)
            dh = mm(dy2[at, :], wd[:, cols])
            g = g_pre[at, cols]
            u = u_pre[at, cols]
            sig = sigmoid(g)
            du[at, cols] = (dh * g * sig).astype(BF16)
            dg[at, cols] = (dh * u * sig * (1.0 + g * (1.0 - sig))).astype(BF16)

        for copy in grads_out(src):
            copy.start()

    def grads_out(src):
        at = rows_at(src, rows)
        return [
            pltpu.make_async_copy(held.at[at], to.at[at], bsem.at[i, src])
            for i, (held, to) in enumerate(((dg, dg_out), (du, du_out)))
        ]

    line_gather(z, n, dy2, rows, g2s, g2r, back_block)
    o_dy2.start()
    for copy in (o_branch, o_up, o_h1r, o_hidden, o_dy2):
        copy.wait()

    @pl.loop(0, n)
    def _(src):
        for copy in grads_out(src):
            copy.wait()

    cube_u.finish()
    cube_d.finish()


def run_forward(n, ns, att, tok, cot, more, gate_b, up, down, attn_gain, mlp_gain):
    rows, depth = tok.shape
    tl, lw = att.shape
    ff = up.shape[1]
    dma = pltpu.SemaphoreType.DMA
    sems = line_sems(n)
    shape = jax.ShapeDtypeStruct
    return pl.pallas_call(
        functools.partial(forward_kernel, n, ns),
        out_shape=(
            shape((rows, depth), BF16),
            shape((tl, depth), BF16),
            shape((rows, depth), F32),
            shape((tl, ff), BF16),
            shape((tl, depth), BF16),
            shape((tl, ff), BF16),
            shape((tl, ff), BF16),
            shape((1, depth), F32),
            shape((depth, ff), BF16),
        ),
        in_specs=[VMEM, VMEM, VMEM, ANY, ANY, ANY, VMEM, VMEM, VMEM],
        out_specs=(VMEM, ANY, ANY, ANY, ANY, ANY, ANY, VMEM, ANY),
        scratch_shapes=[
            pltpu.VMEM((tl, depth), BF16),
            pltpu.VMEM((tl, ff), BF16),
            pltpu.VMEM((tl, depth), BF16),
            pltpu.VMEM((tl, ff), BF16),
            pltpu.VMEM((tl, ff), BF16),
            pltpu.VMEM((depth, lw), BF16),
            pltpu.VMEM((depth, ff), BF16),
            pltpu.VMEM((depth, ff), BF16),
            pltpu.VMEM((depth, ff), BF16),
            pltpu.VMEM((2, n, STEPS, rows, depth // STEPS), BF16),
            pltpu.VMEM((rows, depth), F32),
            pltpu.VMEM((rows, depth), F32),
            pltpu.VMEM((rows, depth), F32),
            pltpu.VMEM((tl, ff), F32),
            pltpu.VMEM((tl, ff), F32),
            dma((4,)),
            dma((5,)),
            dma((2, n)),
            *sems["gather"], *sems["scatter"], *sems["gather"], *sems["scatter"],
            *CubeGather.sems(ns), *CubeGather.sems(ns),
        ],
        compiler_params=pltpu.CompilerParams(
            collective_id=1, has_side_effects=True, vmem_limit_bytes=VMEM_BYTES
        ),
        cost_estimate=pl.CostEstimate(flops=18 * 10**9, bytes_accessed=40 * 10**6, transcendentals=2 * 10**6),
        name="feed_forward",
    )(att, tok, cot, more, gate_b, up, down, attn_gain, mlp_gain)


def backward_kernel(
    n, ns,
    dg, du, h1r_in, cot, branch, more, gate_b, up, attn_gain,
    middle, dy1, datt, gain_part, grad_gate, grad_up,
    h1r, wo, wg, wu, land, total,
    first, held_g, later_g, held_u, later_u,
    wsem, osem, s1s, s1r, g1s, g1r,
    ga, gb, gc, gd, ua, ub, uc, ud,
):
    s, z = lax.axis_index("seq"), lax.axis_index("head")
    rows, depth = cot.shape
    lw, ff = datt.shape[1], dg.shape[1]
    block = depth // ns
    width = depth // STEPS
    early = more.shape[1] - lw

    def weights_in(c):
        at = rows_at(c, width)
        return [
            pltpu.make_async_copy(more.at[at, pl.ds(lw, early)], wg.at[at, pl.ds(0, early)], wsem.at[0, c]),
            pltpu.make_async_copy(gate_b.at[at], wg.at[at, pl.ds(early, ff - early)], wsem.at[1, c]),
            pltpu.make_async_copy(up.at[at], wu.at[at], wsem.at[2, c]),
        ]

    l_h = pltpu.make_async_copy(h1r_in, h1r, osem.at[0])
    l_o = pltpu.make_async_copy(more.at[:, pl.ds(0, lw)], wo, osem.at[1])
    l_h.start()
    for c in range(STEPS):
        for copy in weights_in(c):
            copy.start()
    l_o.start()
    cube_barrier(s, z, ns, n)

    def weight_block(grad):
        return lambda b: mm(h1r[:, rows_at(b, block)], grad[...], TN)

    cube_g = CubeScatter(s, ns, weight_block(dg), block, first, held_g, later_g, (ga, gb, gc, gd))
    cube_u = CubeScatter(s, ns, weight_block(du), block, first, held_u, later_u, (ua, ub, uc, ud))

    def in_part(d, c):
        at, cols = rows_at(d, rows), rows_at(c, width)
        return mm(dg[at, :], wg[cols, :], NT) + mm(du[at, :], wu[cols, :], NT)

    line = LineScatter(z, n, in_part, land, s1s, s1r, total)
    half = ns // 2

    def there(slot):
        @pl.when(slot < STEPS)
        def _():
            for copy in weights_in(slot):
                copy.wait()

    def task(slot):
        def during(low, count, act):
            @pl.when((slot >= low) & (slot < low + half // count))
            def _():
                for i in range(count):
                    act(count * (slot - low) + i)

        def send_second(j):
            cube_g.core_copy(half - 1 - j).wait_send()
            cube_u.send_core(j)

        during(0, 2, cube_g.add_core)
        during(half // 2, 1, send_second)
        during(half // 2 + half, 1, cube_u.add_core)

    l_h.wait()
    cube_g.send_core()
    line.run(0, 2 * STEPS, there, task)
    line.start_own()
    line.run(2 * STEPS, line.slots, None, task)

    @pl.loop(line.slots, max(line.slots, half // 2 + 2 * half))
    def _(slot):
        task(slot)

    cube_g.step(0)
    line.own()
    line.finish()
    gain_part[...] = jnp.zeros_like(gain_part)

    @pl.loop(0, rows // BLOCK)
    def _(i):
        at = rows_at(i, BLOCK)
        y = branch[at, :]
        scale = row_scale(y)
        normed = y * scale
        e = cot[at, :].astype(F32) + total[at, :]
        middle[at, :] = e
        gain_part[...] += jnp.sum(e * normed, axis=0, keepdims=True)
        dy1[pl.ds(pl.multiple_of(z * rows + i * BLOCK, BLOCK), BLOCK), :] = norm_back(
            e, normed, scale, attn_gain[...]
        ).astype(BF16)

    l_o.wait()

    def att_block(src):
        at = rows_at(src, rows)
        datt[at, :] = mm(dy1[at, :], wo[...]).astype(BF16)

    todo = [functools.partial(cube.step, i) for i in range(1, cube_g.stages) for cube in (cube_g, cube_u)]
    line_gather(z, n, dy1, rows, g1s, g1r, att_block, todo[: n - 1], functools.partial(cube_u.step, 0))
    for step in todo[n - 1 :]:
        step()
    grad_gate[...] = held_g[0]
    grad_up[...] = held_u[0]
    cube_g.finish()
    cube_u.core_sent()
    cube_u.finish()


def run_backward(n, ns, dg, du, h1r, cot, branch, more, gate_b, up, attn_gain):
    rows, depth = cot.shape
    tl, ff = dg.shape
    lw = more.shape[1] + gate_b.shape[1] - ff
    block = depth // ns
    dma = pltpu.SemaphoreType.DMA
    sems = line_sems(n)
    shape = jax.ShapeDtypeStruct
    first, held, later, *cube_sems = CubeScatter.scratch(ns, block, ff)
    return pl.pallas_call(
        functools.partial(backward_kernel, n, ns),
        out_shape=(
            shape((rows, depth), F32),
            shape((tl, depth), BF16),
            shape((tl, lw), BF16),
            shape((1, depth), F32),
            shape((block, ff), BF16),
            shape((block, ff), BF16),
        ),
        in_specs=[VMEM, VMEM, ANY, VMEM, VMEM, ANY, ANY, ANY, VMEM],
        out_specs=(VMEM,) * 6,
        scratch_shapes=[
            pltpu.VMEM((tl, depth), BF16),
            pltpu.VMEM((depth, lw), BF16),
            pltpu.VMEM((depth, ff), BF16),
            pltpu.VMEM((depth, ff), BF16),
            pltpu.VMEM((2, n, STEPS, rows, depth // STEPS), BF16),
            pltpu.VMEM((rows, depth), F32),
            first, held, later, held, later,
            dma((3, STEPS)),
            dma((2,)),
            *sems["scatter"], *sems["gather"],
            *cube_sems, *cube_sems,
        ],
        compiler_params=pltpu.CompilerParams(
            collective_id=2, has_side_effects=True, vmem_limit_bytes=VMEM_BYTES
        ),
        cost_estimate=pl.CostEstimate(flops=18 * 10**9, bytes_accessed=30 * 10**6, transcendentals=0),
        name="into_attention",
    )(dg, du, h1r, cot, branch, more, gate_b, up, attn_gain)


LOG2E = 1.4426950408889634
NEG = -1e30


def seq_barrier(s, ns, between=None):
    bar = pltpu.get_barrier_semaphore()
    for other in range(ns):

        @pl.when(other != s)
        def _():
            pl.semaphore_signal(bar, inc=1, device_id={"seq": other}, device_id_type=MESH)

    if between is not None:
        between()
    pl.semaphore_wait(bar, ns - 1)


def share_of(s, ns, r):
    per = ns // (2 * r)
    chunk = s // per
    low = chunk < r
    sub = jnp.where(low, chunk, 2 * r - 1 - chunk)
    return sub, jnp.where(low, s - chunk * per, per + s - chunk * per)


def source_of(sub, i, ns, r):
    per = ns // (2 * r)
    return jnp.where(i < per, sub * per + i, (2 * r - 1 - sub) * per + i - per)


def head_cols(h):
    return pl.ds(pl.multiple_of(h * HEAD_DIM, HEAD_DIM), HEAD_DIM)


def attend_kernel(
    ns, heads, q_in, k_in, v_in, docs, gate,
    att, q_buf, k_buf, v_buf, o_buf, lse, gate_out,
    o_low, qs, qr, ks, kr, vs, vr, osend, orecv, local, cs, cr,
):
    s = lax.axis_index("seq")
    r = ns // heads
    blocks = ns // r
    tl = q_in.shape[0]
    mine, sub = s // r, s % r
    parity = s % 2
    to_sub, to_row = share_of(s, ns, r)

    def own_rows():
        for x, buf in ((k_in, k_buf), (v_in, v_buf)):
            buf[rows_at(s, tl), :] = x[:, head_cols(mine)]

        @pl.when(to_sub == sub)
        def _():
            q_buf[rows_at(to_row, tl), :] = q_in[:, head_cols(mine)]

    seq_barrier(s, ns, own_rows)

    def q_copy(h):
        return pltpu.make_async_remote_copy(
            src_ref=q_in.at[:, head_cols(h)],
            dst_ref=q_buf.at[rows_at(to_row, tl)],
            send_sem=qs.at[h],
            recv_sem=qr.at[to_row],
            device_id={"seq": h * r + to_sub},
            device_id_type=MESH,
        )

    def q_recv(i):
        return pltpu.make_async_remote_copy(
            src_ref=q_buf.at[rows_at(i, tl)],
            dst_ref=q_buf.at[rows_at(i, tl)],
            send_sem=qs.at[0],
            recv_sem=qr.at[i],
            device_id={"seq": s ^ 1},
            device_id_type=MESH,
        )

    def kv_copy(src, buf, send, recv, t, at):
        return pltpu.make_async_remote_copy(
            src_ref=src,
            dst_ref=buf.at[rows_at(at, tl)],
            send_sem=send,
            recv_sem=recv.at[at],
            device_id={"seq": t},
            device_id_type=MESH,
        )

    kv = ((k_in, k_buf, ks, kr), (v_in, v_buf, vs, vr))
    block = gate.shape[0]
    late = gate_out.shape[1]
    own = gate.at[:, pl.ds(gate.shape[1] - late, late)]
    own_gate = pltpu.make_async_copy(own, gate_out.at[rows_at(s, block)], local.at[0])
    cube = CubeGather(s, ns, gate_out, block, cs, cr, own)
    own_gate.start()

    def far(t):
        return (t != s) & (t % 2 == parity)

    @pl.loop(1, ns)
    def _(step):
        t = s ^ step

        @pl.when(far(t))
        def _():
            for x, buf, ss, rs in kv:
                kv_copy(x.at[:, head_cols(t // r)], buf, ss.at[0, t], rs, t, s).start()

    @pl.loop(0, heads)
    def _(h):
        @pl.when(h * r + to_sub != s)
        def _():
            q_copy(h).start()

    def pass_on(src, start):
        for _, buf, ss, rs in kv:
            copy = kv_copy(buf.at[rows_at(src, tl)], buf, ss.at[1, src], rs, s ^ 1, src)
            if start:
                copy.start()
            else:
                copy.wait_send()

    pass_on(s, True)

    @pl.loop(1, ns)
    def _(step):
        src = s ^ step

        @pl.when(far(src))
        def _():
            for x, buf, ss, rs in kv:
                kv_copy(buf.at[rows_at(src, tl)], buf, ss.at[0, 0], rs, s ^ 1, src).wait_recv()
            pass_on(src, True)

    @pl.loop(0, ns)
    def _(src):
        @pl.when(src % 2 != parity)
        def _():
            for x, buf, ss, rs in kv:
                kv_copy(buf.at[rows_at(src, tl)], buf, ss.at[0, 0], rs, s ^ 1, src).wait_recv()

    unit = HEAD_DIM ** (-0.5) * LOG2E

    def o_copy(i, t):
        return pltpu.make_async_remote_copy(
            src_ref=o_low.at[rows_at(i, tl)],
            dst_ref=att.at[:, head_cols(mine)],
            send_sem=osend.at[i],
            recv_sem=orecv.at[mine],
            device_id={"seq": t},
            device_id_type=MESH,
        )

    def attend_block(i):
        src = source_of(sub, i, ns, r)

        @pl.when(src != s)
        def _():
            q_recv(i).wait_recv()

        q = q_buf[rows_at(i, tl), :]
        start = first_of_document(docs, src * tl + lax.broadcasted_iota(jnp.int32, (1, tl), 1))
        key_at = lax.broadcasted_iota(jnp.int32, (tl, tl), 0)

        def step(j, carry, diagonal):
            top, total, acc = carry
            at = rows_at(j, tl)
            scores = mm(k_buf[at, :], q, NT) * unit
            allowed = key_at >= start - j * tl
            if diagonal:
                allowed = allowed & (key_at <= lax.broadcasted_iota(jnp.int32, (tl, tl), 1))
            scores = jnp.where(allowed, scores, NEG)
            new = jnp.maximum(top, jnp.max(scores, axis=0, keepdims=True))
            terms = jnp.exp2(scores - new)
            fade = jnp.exp2(top - new)
            return (
                new,
                total * fade + jnp.sum(terms, axis=0, keepdims=True),
                acc * fade + mm(v_buf[at, :], terms.astype(BF16), TN),
            )

        carry = (
            jnp.full((1, tl), NEG, F32),
            jnp.zeros((1, tl), F32),
            jnp.zeros((HEAD_DIM, tl), F32),
        )
        carry = lax.fori_loop(0, src, lambda j, c: step(j, c, False), carry)
        top, total, acc = step(src, carry, True)
        lse[pl.ds(i, 1), :] = top + jnp.log(total) * LOG2E
        o = jnp.transpose(acc / total)
        o_buf[rows_at(i, tl), :] = o
        o_low[rows_at(i, tl), :] = o.astype(BF16)

        @pl.when(src != s)
        def _():
            o_copy(i, src).start()

        @pl.when(src == s)
        def _():
            att[:, head_cols(mine)] = o.astype(BF16)

    cube.start()
    cuts = [0, blocks - 1, blocks, blocks]
    for i in range(3):
        pl.loop(cuts[i], cuts[i + 1])(attend_block)
        if i < 2:
            cube.level(i)
    for i in range(2, cube.levels):
        cube.level(i)

    own_gate.wait()

    @pl.loop(0, heads)
    def _(h):
        @pl.when(h * r + to_sub != s)
        def _():
            q_copy(h).wait_send()
            pltpu.make_async_remote_copy(
                src_ref=o_low.at[rows_at(0, tl)],
                dst_ref=att.at[:, head_cols(h)],
                send_sem=osend.at[0],
                recv_sem=orecv.at[h],
                device_id={"seq": s ^ 1},
                device_id_type=MESH,
            ).wait_recv()

    @pl.loop(0, blocks)
    def _(i):
        src = source_of(sub, i, ns, r)

        @pl.when(src != s)
        def _():
            o_copy(i, src).wait_send()

    pass_on(s, False)

    @pl.loop(1, ns)
    def _(step):
        t = s ^ step

        @pl.when(far(t))
        def _():
            for x, buf, ss, rs in kv:
                kv_copy(x.at[:, head_cols(t // r)], buf, ss.at[0, t], rs, t, s).wait_send()
            pass_on(t, False)

    cube.finish()


def run_attend(ns, heads, q, k, v, docs, gate):
    tl, lw = q.shape
    r = ns // heads
    nq = ns // r * tl
    nk = ns * tl
    dma = pltpu.SemaphoreType.DMA
    shape = jax.ShapeDtypeStruct
    return pl.pallas_call(
        functools.partial(attend_kernel, ns, heads),
        out_shape=(
            shape((tl, lw), BF16),
            shape((nq, HEAD_DIM), BF16),
            shape((nk, HEAD_DIM), BF16),
            shape((nk, HEAD_DIM), BF16),
            shape((nq, HEAD_DIM), F32),
            shape((ns // r, tl), F32),
            shape((gate.shape[0] * ns, gate.shape[1] - early_part(gate.shape[1])), BF16),
        ),
        in_specs=[VMEM] * 3 + [SMEM, VMEM],
        out_specs=(VMEM,) * 6 + (ANY,),
        scratch_shapes=[
            pltpu.VMEM((nq, HEAD_DIM), BF16),
            dma((heads,)), dma((ns // r,)),
            dma((2, ns)), dma((ns,)),
            dma((2, ns)), dma((ns,)),
            dma((ns // r,)), dma((heads,)),
            dma((1,)),
            *CubeGather.sems(ns),
        ],
        compiler_params=pltpu.CompilerParams(
            collective_id=3, has_side_effects=True, vmem_limit_bytes=VMEM_BYTES
        ),
        cost_estimate=pl.CostEstimate(flops=3 * 10**9, bytes_accessed=8 * 10**6, transcendentals=5 * 10**6),
        name="attend",
    )(q, k, v, docs, gate)


def attend_back_kernel(
    ns, heads, do_in, docs, q_buf, k_buf, v_buf, o_buf, lse, dy2, hidden,
    dq, dk, dv, grad_down,
    do_buf, dq_low, dk_acc, dv_acc, low, pair, land,
    first, held, later, ca, cb, cc, cd,
    ds_, dr_, ps, pr, gs, gr, qs, qr,
):
    s = lax.axis_index("seq")
    r = ns // heads
    blocks = ns // r
    tl = do_in.shape[0]
    mine, sub = s // r, s % r
    parity = s % 2

    def clear():
        dk_acc[...] = jnp.zeros_like(dk_acc)
        dv_acc[...] = jnp.zeros_like(dv_acc)

    seq_barrier(s, ns, clear)
    to_sub, to_row = share_of(s, ns, r)

    def copy(src, dst, send, recv, t):
        return pltpu.make_async_remote_copy(
            src_ref=src, dst_ref=dst, send_sem=send, recv_sem=recv, device_id={"seq": t}, device_id_type=MESH
        )

    def do_copy(h):
        return copy(
            do_in.at[:, head_cols(h)], do_buf.at[rows_at(to_row, tl)], ds_.at[h], dr_.at[to_row], h * r + to_sub
        )

    @pl.loop(0, heads)
    def _(h):
        @pl.when(h * r + to_sub != s)
        def _():
            do_copy(h).start()

    block = dy2.shape[1] // ns
    cube = CubeScatter(
        s, ns, lambda b: mm(dy2[:, rows_at(b, block)], hidden[:, : grad_down.shape[0]], TN), block, first, held, later, (ca, cb, cc, cd)
    )
    cube.send_core()
    cube.add_core()

    @pl.when(to_sub == sub)
    def _():
        do_buf[rows_at(to_row, tl), :] = do_in[:, head_cols(mine)]

    scale = HEAD_DIM ** (-0.5)
    unit = scale * LOG2E

    def dq_copy(i, t):
        return copy(dq_low.at[rows_at(i, tl)], dq.at[:, head_cols(mine)], qs.at[i], qr.at[mine], t)

    ones = jnp.ones((8, HEAD_DIM), F32)

    def back_block(i):
        src = source_of(sub, i, ns, r)
        rows = rows_at(i, tl)

        @pl.when(src != s)
        def _():
            copy(do_buf.at[rows], do_buf.at[rows], ds_.at[0], dr_.at[i], s ^ 1).wait_recv()

        q = q_buf[rows, :]
        do = do_buf[rows, :]
        start = first_of_document(docs, src * tl + lax.broadcasted_iota(jnp.int32, (1, tl), 1))
        norm = lse[pl.ds(i, 1), :]
        delta = lax.dot_general(
            ones, do.astype(F32) * o_buf[rows, :], NT,
            precision=lax.Precision.HIGHEST, preferred_element_type=F32,
        )[:1]
        key_at = lax.broadcasted_iota(jnp.int32, (tl, tl), 0)

        def step(j, dq_sum, diagonal):
            at = rows_at(j, tl)
            keys = k_buf[at, :]
            scores = mm(keys, q, NT) * unit
            allowed = key_at >= start - j * tl
            if diagonal:
                allowed = allowed & (key_at <= lax.broadcasted_iota(jnp.int32, (tl, tl), 1))
            p = jnp.where(allowed, jnp.exp2(scores - norm), 0.0)
            dp = mm(v_buf[at, :], do, NT)
            dscore = (p * (dp - delta)).astype(BF16)
            dv_acc[at, :] += mm(p.astype(BF16), do)
            dk_acc[at, :] += mm(dscore, q)
            return dq_sum + mm(dscore, keys, TN)

        dq_sum = lax.fori_loop(0, src, lambda j, c: step(j, c, False), jnp.zeros((tl, HEAD_DIM), F32))
        dq_sum = step(src, dq_sum, True)
        dq_low[rows, :] = (dq_sum * scale).astype(BF16)

        @pl.when(src != s)
        def _():
            dq_copy(i, src).start()

        @pl.when(src == s)
        def _():
            dq[:, head_cols(mine)] = dq_low[rows, :]

    pl.loop(0, blocks - 1)(back_block)
    cube.step(0)
    pl.loop(blocks - 1, blocks)(back_block)
    half = ns // 2

    def pair_copy(w, i):
        src = 2 * i + 1 - parity
        return copy(low.at[w, rows_at(src, tl)], pair.at[w, rows_at(i, tl)], ps.at[w, i], pr.at[w, i], s ^ 1)

    @pl.loop(0, half)
    def _(i):
        at = rows_at(2 * i + 1 - parity, tl)
        low[0, at, :] = (dk_acc[at, :] * scale).astype(BF16)
        pair_copy(0, i).start()
        low[1, at, :] = dv_acc[at, :].astype(BF16)
        pair_copy(1, i).start()

    slot = sub // 2
    outs = (dk, dv)

    def back_copy(w, i):
        dest = 2 * i + parity
        return copy(
            low.at[w, rows_at(dest, tl)], land.at[w, slot, :, head_cols(mine)], gs.at[w, i], gr.at[w, mine, slot], dest
        )

    @pl.loop(0, half)
    def _(i):
        dest = 2 * i + parity
        at = rows_at(dest, tl)
        for w, acc, factor in ((0, dk_acc, scale), (1, dv_acc, 1.0)):
            copy(low.at[w, at], pair.at[w, rows_at(i, tl)], ps.at[w, i], pr.at[w, i], s ^ 1).wait_recv()
            low[w, at, :] = (acc[at, :] * factor + pair[w, rows_at(i, tl), :].astype(F32)).astype(BF16)

            @pl.when(dest != s)
            def _():
                back_copy(w, i).start()

            @pl.when(dest == s)
            def _():
                land[w, slot, :, head_cols(mine)] = low[w, at, :]

    @pl.loop(0, heads)
    def _(h):
        for w in range(2):
            for k in range(r // 2):

                @pl.when(h * r + 2 * k + parity != s)
                def _():
                    copy(
                        low.at[w, rows_at(0, tl)], land.at[w, k, :, head_cols(h)], gs.at[w, 0], gr.at[w, h, k], s ^ 1
                    ).wait_recv()

    for w in range(2):
        outs[w][...] = functools.reduce(
            lambda a, b: a + b, [land[w, k].astype(F32) for k in range(r // 2)]
        ).astype(BF16)

    @pl.loop(0, heads)
    def _(h):
        @pl.when(h * r + to_sub != s)
        def _():
            do_copy(h).wait_send()
            copy(dq_low.at[rows_at(0, tl)], dq.at[:, head_cols(h)], qs.at[0], qr.at[h], s ^ 1).wait_recv()

    @pl.loop(0, blocks)
    def _(i):
        src = source_of(sub, i, ns, r)

        @pl.when(src != s)
        def _():
            dq_copy(i, src).wait_send()

    @pl.loop(0, half)
    def _(i):
        for w in range(2):
            pair_copy(w, i).wait_send()

            @pl.when(2 * i + parity != s)
            def _():
                back_copy(w, i).wait_send()

    for i in range(1, cube.stages):
        cube.step(i)
    grad_down[...] = jnp.transpose(held[0].astype(F32)).astype(BF16)
    cube.core_sent()
    cube.finish()


def run_attend_back(ns, heads, do, docs, q, k, v, o, lse, dy2, hidden):
    tl, lw = do.shape
    r = ns // heads
    nq = ns // r * tl
    nk = ns * tl
    dma = pltpu.SemaphoreType.DMA
    shape = jax.ShapeDtypeStruct
    return pl.pallas_call(
        functools.partial(attend_back_kernel, ns, heads),
        out_shape=(shape((tl, lw), BF16),) * 3 + (shape((hidden.shape[1] - lw, dy2.shape[1] // ns), BF16),),
        in_specs=[VMEM, SMEM] + [VMEM] * 7,
        out_specs=(VMEM,) * 4,
        scratch_shapes=[
            pltpu.VMEM((nq, HEAD_DIM), BF16),
            pltpu.VMEM((nq, HEAD_DIM), BF16),
            pltpu.VMEM((nk, HEAD_DIM), F32),
            pltpu.VMEM((nk, HEAD_DIM), F32),
            pltpu.VMEM((2, nk, HEAD_DIM), BF16),
            pltpu.VMEM((2, nk // 2, HEAD_DIM), BF16),
            pltpu.VMEM((2, r // 2, tl, lw), BF16),
            *CubeScatter.scratch(ns, dy2.shape[1] // ns, hidden.shape[1] - lw),
            dma((heads,)), dma((ns // r,)),
            dma((2, ns // 2)), dma((2, ns // 2)),
            dma((2, ns // 2)), dma((2, heads, r // 2)),
            dma((ns // r,)), dma((heads,)),
        ],
        compiler_params=pltpu.CompilerParams(
            collective_id=4, has_side_effects=True, vmem_limit_bytes=VMEM_BYTES
        ),
        cost_estimate=pl.CostEstimate(flops=8 * 10**9, bytes_accessed=10 * 10**6, transcendentals=5 * 10**6),
        name="attend_back",
    )(do, docs, q, k, v, o, lse, dy2, hidden)


def cross_barrier(s, z, ns, n, between=None):
    bar = pltpu.get_barrier_semaphore()
    for axis, me, count in (("seq", s, ns), ("head", z, n)):
        for other in range(count):

            @pl.when(other != me)
            def _():
                pl.semaphore_signal(bar, inc=1, device_id={axis: other}, device_id_type=MESH)

    if between is not None:
        between()
    pl.semaphore_wait(bar, ns - 1 + n - 1)


def row_sums(left, right):
    ones = jnp.ones((8, left.shape[1]), F32)
    both = [
        lax.dot_general(ones, x, NT, precision=lax.Precision.HIGHEST, preferred_element_type=F32) for x in (left, right)
    ]
    return jnp.where(lax.broadcasted_iota(jnp.int32, both[0].shape, 0) < 4, both[0], both[1])


def as_column(sums, row):
    pick = (lax.broadcasted_iota(jnp.int32, (8, HEAD_DIM), 0) == row).astype(F32)
    return lax.dot_general(sums, pick, TN, precision=lax.Precision.HIGHEST, preferred_element_type=F32)


class SmallExchange:
    def __init__(self, axis, me, count, land, send_sem, recv_sem):
        self.axis, self.me, self.count, self.land = axis, me, count, land
        self.send_sem, self.recv_sem = send_sem, recv_sem

    def copy(self, slot, to):
        return remote(self.land.at[slot], self.land.at[slot], self.send_sem.at[to], self.recv_sem.at[slot], self.axis, to)

    def each(self, act):
        @pl.loop(0, self.count)
        def _(other):
            @pl.when(other != self.me)
            def _():
                act(other)

    def start(self):
        self.each(lambda other: self.copy(self.me, other).start())

    def receive(self):
        self.each(lambda other: self.copy(other, other).wait_recv())

    def finish(self):
        self.each(lambda other: self.copy(self.me, other).wait_send())


def turn(x, cos, sin):
    return x * cos + pltpu.roll(x, HEAD_DIM // 2, 1) * sin


def turn_back(x, cos, sin):
    return x * cos - pltpu.roll(x, HEAD_DIM // 2, 1) * sin


def project_kernel(
    n, ns, depth_full,
    tok, wq, wk, wv, wo, gate, gq, gk, docs, turns,
    x_out, w_out, more_out, q_raw, k_raw, totals, q_rot, k_rot, v_low, cos, sin,
    x, w, own, land, lsem, ags, agr, cgs, cgr, egs, egr, ss, sr,
):
    s, z = lax.axis_index("seq"), lax.axis_index("head")
    rows, depth = tok.shape
    block, lw = wq.shape
    heads = lw // HEAD_DIM
    cross_barrier(s, z, ns, n)
    mine = rows_at(s, block)

    def head_gain(h):
        return head_cols(z * heads + h)

    loads = [pltpu.make_async_copy(tok, x.at[rows_at(z, rows)], lsem.at[0])] + [
        pltpu.make_async_copy(m, w.at[mine, pl.ds(i * lw, lw)], lsem.at[i + 1]) for i, m in enumerate((wq, wk, wv))
    ]
    for copy in loads:
        copy.start()
    loads[0].wait()
    cube = CubeGather(s, ns, w, block, cgs, cgr)
    own_more = pltpu.make_async_copy(own, more_out.at[mine], lsem.at[6])
    cube_e = CubeGather(s, ns, more_out, block, egs, egr, own)
    levels = cube.levels

    def weights(k):
        if k == 0:
            cube.level(0)
        else:
            for i in range(1, levels):
                cube.level(i)
                if i == levels - 2:
                    cube_e.start()

    def start_weights():
        for copy in loads[1:]:
            copy.wait()
        cube.start()

    def multiply(src):
        at = rows_at(src, rows)
        for i, to in enumerate((q_raw, k_raw)):
            to[at, :] = mm(x[at, :], w[:, i * lw : (i + 1) * lw])
        v_low[at, :] = mm(x[at, :], w[:, 2 * lw :]).astype(BF16)

    part = rows // AG_CHUNKS

    def copy(src, c, up):
        at = pl.ds(pl.multiple_of(src * rows + c * part, part), part)
        return remote(x.at[at], x.at[at], ags.at[up, src, c], agr.at[src, c], "head", z + 1 if up else z - 1)

    more = (z > 0, z < n - 1)
    for c in range(AG_CHUNKS):
        for up in (0, 1):

            @pl.when(more[up])
            def _():
                copy(z, c, up).start()

    start_weights()
    own[:, :lw] = jnp.transpose(wo[...].astype(F32)).astype(BF16)
    own[:, lw:] = gate[:, : own.shape[1] - lw]
    own_more.start()
    token = s * x.shape[0] + lax.broadcasted_iota(jnp.int32, cos.shape, 0)
    angle = (token - first_of_document(docs, token)).astype(F32) * turns[...]
    flip = jnp.where(lax.broadcasted_iota(jnp.int32, cos.shape, 1) < HEAD_DIM // 2, -1.0, 1.0)
    cos[...] = jnp.cos(angle)
    sin[...] = jnp.sin(angle) * flip

    def sides(k):
        return ((z + k, z + k < n, 0), (z - k, z - k >= 0, 1))

    for k in range(1, n):
        for c in range(AG_CHUNKS):
            for src, there, up in sides(k):

                @pl.when(there)
                def _():
                    copy(src, c, up).wait_recv()

                    @pl.when(more[up])
                    def _():
                        copy(src, c, up).start()

        if k <= 2:
            weights(k - 1)
        if k == min(2, n - 1):
            multiply(z)
            for src, there, _ in sides(1):
                pl.when(there)(functools.partial(multiply, src))
        if k > 1:
            for src, there, _ in sides(k):
                pl.when(there)(functools.partial(multiply, src))

    outs = [pltpu.make_async_copy(x, x_out, lsem.at[4]), pltpu.make_async_copy(w, w_out, lsem.at[5])]
    for out in outs:
        out.start()
    totals[...] = row_sums(q_raw[...] * q_raw[...], k_raw[...] * k_raw[...])
    land[z] = totals[...]
    small = SmallExchange("head", z, n, land, ss, sr)
    small.start()
    small.receive()
    total = land[0]
    for k in range(1, n):
        total = total + land[k]
    totals[...] = total
    for row, raw, gain, to in ((0, q_raw, gq, q_rot), (4, k_raw, gk, k_rot)):
        scale = lax.rsqrt(as_column(total, row) / depth_full + epsilon)
        for h in range(heads):
            cols = slice(h * HEAD_DIM, (h + 1) * HEAD_DIM)
            to[:, cols] = turn(raw[:, cols] * scale * gain[:, head_gain(h)], cos[...], sin[...]).astype(BF16)
        if row == 0:
            cube_e.level(0)
    for i in range(1, levels):
        cube_e.level(i)
    small.finish()
    cube.finish()
    cube_e.finish()
    for out in [*outs, own_more]:
        out.wait()

    @pl.loop(0, n)
    def _(src):
        for c in range(AG_CHUNKS):

            @pl.when((src >= z) & (z > 0))
            def _():
                copy(src, c, 0).wait_send()

            @pl.when((src <= z) & (z < n - 1))
            def _():
                copy(src, c, 1).wait_send()


def run_project(n, ns, tok, wq, wk, wv, wo, gate, gq, gk, docs, turns):
    rows, depth = tok.shape
    tl = rows * n
    lw = wq.shape[1]
    dma = pltpu.SemaphoreType.DMA
    shape = jax.ShapeDtypeStruct
    return pl.pallas_call(
        functools.partial(project_kernel, n, ns, depth),
        out_shape=(
            shape((tl, depth), BF16),
            shape((depth, 3 * lw), BF16),
            shape((depth, lw + early_part(gate.shape[1])), BF16),
            shape((tl, lw), F32),
            shape((tl, lw), F32),
            shape((8, tl), F32),
            shape((tl, lw), BF16),
            shape((tl, lw), BF16),
            shape((tl, lw), BF16),
            shape((tl, HEAD_DIM), F32),
            shape((tl, HEAD_DIM), F32),
        ),
        in_specs=[ANY] * 4 + [VMEM] * 4 + [SMEM, VMEM],
        out_specs=(ANY,) * 3 + (VMEM,) * 8,
        scratch_shapes=[
            pltpu.VMEM((tl, depth), BF16),
            pltpu.VMEM((depth, 3 * lw), BF16),
            pltpu.VMEM((wq.shape[0], lw + early_part(gate.shape[1])), BF16),
            pltpu.VMEM((n, 8, tl), F32),
            dma((7,)),
            dma((2, n, AG_CHUNKS)), dma((n, AG_CHUNKS)),
            *CubeGather.sems(ns), *CubeGather.sems(ns),
            dma((n,)), dma((n,)),
        ],
        compiler_params=pltpu.CompilerParams(
            collective_id=5, has_side_effects=True, vmem_limit_bytes=VMEM_BYTES
        ),
        cost_estimate=pl.CostEstimate(flops=3 * 10**9, bytes_accessed=20 * 10**6, transcendentals=0),
        name="project",
    )(tok, wq, wk, wv, wo, gate, gq, gk, docs, turns)


def input_kernel(
    n, ns, depth_full,
    dq, dk, dv, q_raw, k_raw, totals, gq, gk, cos, sin, x, w, att, dy1, attn_part, mlp_part, dy2_in, hidden_in,
    total, grad_q, grad_k, grad_v, grad_o, grad_down, gains,
    dy2, hidden, lsem, dqkv, q_back, k_back, inner, land, message, message_z, gain_land,
    first, held, later, c0s, c0r, c1s, c1r,
    first_o, held_o, later_o, o0s, o0r, o1s, o1r,
    ss, sr, ms, mr, zs, zr, s1s, s1r,
):
    s, z = lax.axis_index("seq"), lax.axis_index("head")
    rows, depth = total.shape
    tl, lw = dq.shape
    block = depth // ns
    heads = lw // HEAD_DIM

    def head_gain(h):
        return head_cols(z * heads + h)

    sums = totals[...]
    scales = [lax.rsqrt(as_column(sums, row) / depth_full + epsilon) for row in (0, 4)]
    todo = ((dq, q_raw, gq, q_back), (dk, k_raw, gk, k_back))
    products = []

    l_d = pltpu.make_async_copy(dy2_in, dy2, lsem.at[0])
    l_h = pltpu.make_async_copy(hidden_in.at[:, pl.ds(hidden_in.shape[1] - lw, lw)], hidden, lsem.at[1])
    l_d.start()
    l_h.start()

    def turn_all():
        message[...] = jnp.zeros_like(message)
        for i, (grad, raw, gain, back) in enumerate(todo):
            product = jnp.zeros((tl, HEAD_DIM), F32)
            for h in range(heads):
                cols = slice(h * HEAD_DIM, (h + 1) * HEAD_DIM)
                hat = raw[:, cols] * scales[i]
                turned = turn_back(grad[:, cols].astype(F32), cos[...], sin[...])
                message[0, pl.ds(i, 1), cols] = jnp.sum(turned * hat, axis=0, keepdims=True)
                turned = turned * gain[:, head_gain(h)]
                back[:, cols] = turned
                product = product + turned * hat
            products.append(product)
        inner[z] = row_sums(*products)
        for t in range(1, ns):
            message[t, pl.ds(0, 2), pl.ds(0, lw)] = message[0, pl.ds(0, 2), pl.ds(0, lw)]
        for t in range(ns):
            for i, part in enumerate((attn_part, mlp_part)):
                message[t, pl.ds(i, 1), pl.ds(lw, block)] = part[:, t * block : (t + 1) * block]

    cross_barrier(s, z, ns, n, turn_all)
    small = SmallExchange("head", z, n, inner, ss, sr)
    small.start()

    def message_copy(t, frm):
        return remote(message.at[t], message_z.at[frm], ms.at[t], mr.at[frm], "seq", t)

    def each_seq(act):
        @pl.loop(0, ns)
        def _(t):
            @pl.when(t != s)
            def _():
                act(t)

    message_z[s] = message[s]
    each_seq(lambda t: message_copy(t, s).start())
    dqkv[:, 2 * lw :] = dv[...]
    l_d.wait()
    l_h.wait()

    def early_block(b):
        cols = rows_at(b, block)
        return jnp.concatenate([mm(dy1[:, cols], att[...], TN), mm(dy2[:, cols], hidden[...], TN)], axis=1)

    cube_o = CubeScatter(
        s, ns, early_block, block, first_o, held_o, later_o, (o0s, o0r, o1s, o1r)
    )
    cube_o.send_core()
    cube_o.add_core()
    small.receive()
    sums = inner[0]
    for k in range(1, n):
        sums = sums + inner[k]
    for i, (grad, raw, gain, back) in enumerate(todo):
        mean = as_column(sums, 4 * i) / depth_full
        for h in range(heads):
            cols = slice(h * HEAD_DIM, (h + 1) * HEAD_DIM)
            to = slice(i * lw + h * HEAD_DIM, i * lw + (h + 1) * HEAD_DIM)
            dqkv[:, to] = (scales[i] * (back[:, cols] - raw[:, cols] * scales[i] * mean)).astype(BF16)

    width = depth // STEPS

    def weight_block(b):
        cols = rows_at(b, block)
        return mm(x[:, cols], dqkv[...], TN)

    def in_part(d, c):
        return mm(dqkv[rows_at(d, rows), :], w[rows_at(c, width), :], NT)

    cube = CubeScatter(s, ns, weight_block, block, first, held, later, (c0s, c0r, c1s, c1r))
    line = LineScatter(z, n, in_part, land, s1s, s1r, total)
    half = ns // 2

    def task(slot):
        for i, act in enumerate((cube.send_core, cube.add_core)):
            low = 1 + i * (half // 2)

            @pl.when((slot >= low) & (slot < low + half // 2))
            def _():
                for j in range(2):
                    act(2 * (slot - low) + j)

    done = 1 + half
    line.run(0, done, None, task)
    line.start_own()
    line.run(done, done + 3)
    for i in range(cube.stages - 1):
        cube_o.step(i)
    line.run(done + 3, line.slots)
    for i in range(cube.stages - 1):
        cube.step(i)

    each_seq(lambda t: message_copy(t, t).wait_recv())
    received = message_z[0]
    for t in range(1, ns):
        received = received + message_z[t]
    each_seq(lambda t: message_copy(t, s).wait_send())
    gain_land[z] = received
    rounds = SmallExchange("head", z, n, gain_land, zs, zr)
    rounds.start()
    line.own()
    cube_o.step(cube.stages - 1)
    grad_o[...] = jnp.transpose(held_o[0, :, :lw].astype(F32)).astype(BF16)
    grad_down[...] = jnp.transpose(held_o[0, :, lw:].astype(F32)).astype(BF16)
    cube.step(cube.stages - 1)
    for i, to in enumerate((grad_q, grad_k, grad_v)):
        to[...] = held[0, :, i * lw : (i + 1) * lw]
    rounds.receive()
    at = s * block
    gains[...] = jnp.zeros_like(gains)
    gains[0:2, :] = gain_land[at // lw, pl.ds(0, 2), pl.ds(pl.multiple_of(at % lw, block), block)]
    both = gain_land[0, pl.ds(0, 2), pl.ds(lw, block)]
    for k in range(1, n):
        both = both + gain_land[k, pl.ds(0, 2), pl.ds(lw, block)]
    gains[2:4, :] = both
    for one in (cube, cube_o):
        one.core_sent()
        one.finish()
    line.finish()
    small.finish()
    rounds.finish()


def run_input(n, ns, dq, dk, dv, q_raw, k_raw, totals, gq, gk, cos, sin, x, w, att, dy1, attn_part, mlp_part, dy2, hidden):
    tl, lw = dq.shape
    rows, depth = tl // n, x.shape[1]
    block = depth // ns
    dma = pltpu.SemaphoreType.DMA
    shape = jax.ShapeDtypeStruct
    return pl.pallas_call(
        functools.partial(input_kernel, n, ns, depth),
        out_shape=(shape((rows, depth), F32),)
        + (shape((block, lw), BF16),) * 3
        + (shape((lw, block), BF16), shape((lw, block), BF16), shape((8, block), F32)),
        in_specs=[VMEM] * 16 + [ANY] * 2,
        out_specs=(VMEM,) * 7,
        scratch_shapes=[
            pltpu.VMEM((tl, depth), BF16),
            pltpu.VMEM((tl, lw), BF16),
            dma((2,)),
            pltpu.VMEM((tl, 3 * lw), BF16),
            pltpu.VMEM((tl, lw), F32),
            pltpu.VMEM((tl, lw), F32),
            pltpu.VMEM((n, 8, tl), F32),
            pltpu.VMEM((2, n, STEPS, rows, depth // STEPS), BF16),
            pltpu.VMEM((ns, 8, lw + block), F32),
            pltpu.VMEM((ns, 8, lw + block), F32),
            pltpu.VMEM((n, 8, lw + block), F32),
            *CubeScatter.scratch(ns, block, 3 * lw),
            *CubeScatter.scratch(ns, block, 2 * lw),
            dma((n,)), dma((n,)),
            dma((ns,)), dma((ns,)),
            dma((n,)), dma((n,)),
            *line_sems(n)["scatter"],
        ],
        compiler_params=pltpu.CompilerParams(
            collective_id=6, has_side_effects=True, vmem_limit_bytes=VMEM_BYTES
        ),
        cost_estimate=pl.CostEstimate(flops=8 * 10**9, bytes_accessed=30 * 10**6, transcendentals=0),
        name="into_input",
    )(dq, dk, dv, q_raw, k_raw, totals, gq, gk, cos, sin, x, w, att, dy1, attn_part, mlp_part, dy2, hidden)


def widen_kernel(count, *refs):
    spec = WIDEN
    ins, rest = refs[:count], refs[count:]
    outs, rest = rest[: len(spec)], rest[len(spec) :]
    held, rest = rest[:count], rest[count:]
    wide, (load_sem, store_sem) = rest[: len(spec)], rest[len(spec) :]
    loads = [pltpu.make_async_copy(a, b, load_sem.at[i]) for i, (a, b) in enumerate(zip(ins, held))]
    stores = [pltpu.make_async_copy(a, b, store_sem.at[i]) for i, (a, b) in enumerate(zip(wide, outs))]
    for copy in loads:
        copy.start()
    at = 0
    for (parts, stacked), to, store in zip(spec, wide, stores):
        row = 0
        for i in range(at, at + parts):
            loads[i].wait()
            block = held[i][...].astype(to.dtype)
            if stacked:
                to[row : row + block.shape[0], :] = block
                row += block.shape[0]
            elif i == at:
                to[...] = block
            else:
                to[...] += block
        at += parts
        store.start()
    for copy in stores:
        copy.wait()


WIDEN = ((1, False), (1, False), (1, False), (2, True), (1, False), (1, False), (1, False), (1, False), (2, False))


def run_widen(arrays, outs):
    dma = pltpu.SemaphoreType.DMA
    return pl.pallas_call(
        functools.partial(widen_kernel, len(arrays)),
        out_shape=tuple(outs),
        in_specs=[ANY] * len(arrays),
        out_specs=(ANY,) * len(outs),
        scratch_shapes=[pltpu.VMEM(a.shape, a.dtype) for a in arrays]
        + [pltpu.VMEM(o.shape, o.dtype) for o in outs]
        + [dma((len(arrays),)), dma((len(outs),))],
        compiler_params=pltpu.CompilerParams(vmem_limit_bytes=VMEM_BYTES),
        name="widen",
    )(*arrays)


def on_device(
    tokens,
    cotangent,
    doc_lengths,
    q_weight,
    k_weight,
    v_weight,
    o_weight,
    gate_weight,
    up_weight,
    down_weight,
    q_gain,
    k_gain,
    attn_gain,
    mlp_gain,
):
    ns, nz = lax.axis_size("seq"), lax.axis_size("head")
    lw = q_weight.shape[1]
    heads = lw // HEAD_DIM
    block, ff = gate_weight.shape
    gq, gk = q_gain[None], k_gain[None]
    frequency = jnp.power(rope_base, -(jnp.arange(HEAD_DIM) % (HEAD_DIM // 2)).astype(F32) * (2.0 / HEAD_DIM))

    x, w, more, q_raw, k_raw, totals, q_rot, k_rot, v_low, cos, sin = run_project(
        nz, ns, tokens, q_weight, k_weight, v_weight, o_weight, gate_weight, gq, gk, doc_lengths, frequency[None]
    )
    attended, q_held, k_held, v_held, o_held, lse, gate_b = run_attend(
        ns, heads, q_rot, k_rot, v_low, doc_lengths, gate_weight
    )
    output, h1r, branch, hidden, dy2, dg, du, mlp_part, up = run_forward(
        nz, ns, attended, tokens, cotangent, more, gate_b, up_weight, down_weight, attn_gain[None], mlp_gain[None]
    )
    middle, dy1, datt, attn_part, grad_gate, grad_up = run_backward(
        nz, ns, dg, du, h1r, cotangent, branch, more, gate_b, up, attn_gain[None]
    )
    dq, dk, dv, down_a = run_attend_back(
        ns, heads, datt, doc_lengths, q_held, k_held, v_held, o_held, lse, dy2, hidden
    )
    last, grad_q, grad_k, grad_v, grad_o, down_b, gains = run_input(
        nz, ns, dq, dk, dv, q_raw, k_raw, totals, gq, gk, cos, sin, x, w, attended, dy1, attn_part, mlp_part, dy2, hidden
    )
    shape = jax.ShapeDtypeStruct
    small = shape((block, lw), F32)
    output, grad_gate, grad_up, grad_down, grad_q, grad_k, grad_v, grad_o, input_grad = run_widen(
        (output, grad_gate, grad_up, down_a, down_b, grad_q, grad_k, grad_v, grad_o, middle, last),
        (
            shape(output.shape, BF16),
            shape((block, ff), F32),
            shape((block, ff), F32),
            shape((ff, block), F32),
            small, small, small,
            shape((lw, block), F32),
            shape(middle.shape, F32),
        ),
    )
    return (
        output,
        input_grad,
        grad_q,
        grad_k,
        grad_v,
        grad_o,
        grad_gate,
        grad_up,
        grad_down,
        gains[0],
        gains[1],
        gains[2],
        gains[3],
    )


def solution(mesh):
    in_specs = (
        P(("seq", "head"), None),
        P(("seq", "head"), None),
        P(),
        P("seq", "head"),
        P("seq", "head"),
        P("seq", "head"),
        P("head", "seq"),
        P("seq", "head"),
        P("seq", "head"),
        P("head", "seq"),
        P(),
        P(),
        P(),
        P(),
    )
    out_specs = (
        P(("seq", "head"), None),
        P(("seq", "head"), None),
        P("seq", "head"),
        P("seq", "head"),
        P("seq", "head"),
        P("head", "seq"),
        P("seq", "head"),
        P("seq", "head"),
        P("head", "seq"),
        P("seq"),
        P("seq"),
        P("seq"),
        P("seq"),
    )
    return jax.shard_map(
        on_device, mesh=mesh, in_specs=in_specs, out_specs=out_specs, check_vma=False
    )
```

```python
import functools

import jax
import jax.numpy as jnp
from jax import lax
from jax.experimental import pallas as pl
from jax.experimental.pallas import tpu as pltpu
from jax.sharding import PartitionSpec as P

HEAD_DIM = 128
epsilon = 1e-06
rope_base = 500000.0

MESH = pl.DeviceIdType.MESH
F32 = jnp.float32
BF16 = jnp.bfloat16
STEPS = 4
LAG = 1
EARLY = (7, 16)
AG_CHUNKS = 2
VMEM_BYTES = 62 * 1024 * 1024
ANY = pl.BlockSpec(memory_space=pl.ANY)
VMEM = pl.BlockSpec(memory_space=pltpu.VMEM)
SMEM = pl.BlockSpec(memory_space=pltpu.SMEM)
NN = (((1,), (0,)), ((), ()))
NT = (((1,), (1,)), ((), ()))
TN = (((0,), (0,)), ((), ()))


def first_of_document(docs, token):
    end, first = jnp.int32(0), jnp.zeros_like(token)
    for i in range(docs.shape[0]):
        end = end + docs[i]
        first = first + jnp.where(token >= end, docs[i], 0)
    return first


def mm(left, right, dims=NN):
    return lax.dot_general(left, right, dims, preferred_element_type=F32)


def early_part(ff):
    return ff * EARLY[0] // EARLY[1] // HEAD_DIM * HEAD_DIM


def rows_at(index, count):
    return pl.ds(pl.multiple_of(index * count, count), count)


def cube_barrier(s, z, ns, n, between=None):
    bar = pltpu.get_barrier_semaphore()
    bits = [1 << i for i in range(ns.bit_length() - 1)]
    for bit in bits:
        pl.semaphore_signal(bar, inc=1, device_id={"seq": s ^ bit}, device_id_type=MESH)
    for other, there in ((z - 1, z > 0), (z + 1, z < n - 1)):

        @pl.when(there)
        def _():
            pl.semaphore_signal(bar, inc=1, device_id={"head": other}, device_id_type=MESH)

    if between is not None:
        between()
    pl.semaphore_wait(bar, len(bits) + (z > 0).astype(jnp.int32) + (z < n - 1).astype(jnp.int32))


def line_gather(z, n, buf, rows, send_sem, recv_sem, use, hooks=(), ready=None):
    part = rows // AG_CHUNKS

    def copy(src, c, up):
        at = pl.ds(pl.multiple_of(src * rows + c * part, part), part)
        return pltpu.make_async_remote_copy(
            src_ref=buf.at[at],
            dst_ref=buf.at[at],
            send_sem=send_sem.at[up, src, c],
            recv_sem=recv_sem.at[src, c],
            device_id={"head": z + 1 if up else z - 1},
            device_id_type=MESH,
        )

    more = (z > 0, z < n - 1)
    for c in range(AG_CHUNKS):
        for up in (0, 1):

            @pl.when(more[up])
            def _():
                copy(z, c, up).start()

    if ready is not None:
        ready()
    use(z)

    @pl.loop(1, n)
    def _(k):
        sides = ((z + k, z + k < n, 0), (z - k, z - k >= 0, 1))
        for c in range(AG_CHUNKS):
            for src, there, up in sides:

                @pl.when(there)
                def _():
                    copy(src, c, up).wait_recv()

                    @pl.when(more[up])
                    def _():
                        copy(src, c, up).start()

        for src, there, up in sides:

            @pl.when(there)
            def _():
                use(src)

        for i, hook in enumerate(hooks):
            pl.when(k == i + 1)(hook)

    @pl.loop(0, n)
    def _(src):
        for c in range(AG_CHUNKS):

            @pl.when((src >= z) & (z > 0))
            def _():
                copy(src, c, 0).wait_send()

            @pl.when((src <= z) & (z < n - 1))
            def _():
                copy(src, c, 1).wait_send()


class LineScatter:
    def __init__(self, z, n, partial, land, send_sem, recv_sem, total):
        self.z, self.n, self.partial, self.land, self.total = z, n, partial, land, total
        self.send_sem, self.recv_sem = send_sem, recv_sem

    def copy(self, d, c, up):
        return pltpu.make_async_remote_copy(
            src_ref=self.land.at[up, d, c],
            dst_ref=self.land.at[up, d, c],
            send_sem=self.send_sem.at[up, d, c],
            recv_sem=self.recv_sem.at[up, d, c],
            device_id={"head": self.z + 1 if up else self.z - 1},
            device_id_type=MESH,
        )

    @property
    def slots(self):
        return (self.n - 1) * (STEPS + LAG)

    def run(self, low, high, before=None, after=None):
        z, n, land = self.z, self.n, self.land

        @pl.loop(low, high)
        def _(slot):
            if before is not None:
                before(slot)
            for up in (1, 0):
                t = slot - (z if up else n - 1 - z) * LAG
                j = t // STEPS
                c = t - j * STEPS
                d = n - 1 - j if up else j
                first = z == 0 if up else z == n - 1
                there = (t >= 0) & (j < n - 1) & ((d > z) if up else (d < z))

                @pl.when(there)
                def _():
                    mine = self.partial(d, c)

                    @pl.when(first)
                    def _():
                        land[up, d, c] = mine.astype(land.dtype)

                    @pl.when(jnp.logical_not(first))
                    def _():
                        self.copy(d, c, up).wait_recv()
                        land[up, d, c] = (land[up, d, c].astype(F32) + mine).astype(land.dtype)

                    self.copy(d, c, up).start()

            if after is not None:
                after(slot)

    def start_own(self):
        width = self.total.shape[1] // STEPS

        @pl.loop(0, STEPS)
        def _(c):
            self.total[:, rows_at(c, width)] = self.partial(self.z, c)

    def own(self):
        z, n, total = self.z, self.n, self.total
        width = total.shape[1] // STEPS

        @pl.loop(0, STEPS)
        def _(c):
            at = rows_at(c, width)
            for there, up in ((z > 0, 1), (z < n - 1, 0)):

                @pl.when(there)
                def _():
                    self.copy(z, c, up).wait_recv()
                    total[:, at] += self.land[up, z, c].astype(F32)

    def finish(self):
        @pl.loop(0, self.n * STEPS)
        def _(t):
            d, c = t // STEPS, t % STEPS
            for there, up in ((d > self.z, 1), (d < self.z, 0)):

                @pl.when(there)
                def _():
                    self.copy(d, c, up).wait_send()


def line_sems(n):
    dma = pltpu.SemaphoreType.DMA
    return {
        "gather": [dma((2, n, AG_CHUNKS)), dma((n, AG_CHUNKS))],
        "scatter": [dma((2, n, STEPS)), dma((2, n, STEPS))],
    }


BLOCK = 16


def row_scale(block):
    return lax.rsqrt(jnp.mean(block * block, axis=-1, keepdims=True) + epsilon)


def norm_back(e, normed, scale, gain):
    g = e * gain
    return scale * (g - normed * jnp.mean(g * normed, axis=-1, keepdims=True))


def sigmoid(x):
    return 1.0 / (1.0 + jnp.exp(-x))


def subsets(bits):
    found = [0]
    for bit in bits:
        found += [bit | other for other in found]
    return found


def orders_of(ns):
    chips = [1 << i for i in range(1, ns.bit_length() - 1)]
    return (chips, chips[::-1])


def remote(src, dst, send, recv, axis, to):
    return pltpu.make_async_remote_copy(
        src_ref=src, dst_ref=dst, send_sem=send, recv_sem=recv, device_id={axis: to}, device_id_type=MESH
    )


class CubeGather:
    def __init__(self, s, ns, buf, rows, send_sem, recv_sem, own=None):
        self.own = own
        self.s, self.buf, self.rows, self.send_sem, self.recv_sem = s, buf, rows, send_sem, recv_sem
        self.orders = [order + [1] for order in orders_of(ns)]

    def copy(self, half, bit, block):
        part = self.rows // 2
        at = pl.ds(pl.multiple_of(block * self.rows + half * part, part), part)
        source = self.buf.at[at]
        if block is self.s and self.own is not None:
            source = self.own.at[pl.ds(half * part, part)]
        return remote(
            source, self.buf.at[at],
            self.send_sem.at[bit.bit_length() - 1, block, half], self.recv_sem.at[block, half],
            "seq", self.s ^ bit,
        )

    @property
    def levels(self):
        return len(self.orders[0])

    def start(self):
        for i in range(self.levels):
            for half, order in enumerate(self.orders):
                self.copy(half, order[i], self.s).start()

    def level(self, i):
        for j in range(2**i):
            for half, order in enumerate(self.orders):
                block = self.s ^ order[i] ^ subsets(order[:i])[j]
                self.copy(half, order[i], block).wait_recv()
                for bit in order[i + 1 :]:
                    self.copy(half, bit, block).start()

    def finish(self):
        for half, order in enumerate(self.orders):
            for i, bit in enumerate(order):
                for other in subsets(order[:i]):
                    self.copy(half, bit, self.s ^ other if other else self.s).wait_send()

    @staticmethod
    def sems(ns):
        dma = pltpu.SemaphoreType.DMA
        return [dma((ns.bit_length() - 1, ns, 2)), dma((ns, 2))]


class CubeScatter:
    def __init__(self, s, ns, block, rows, first, held, later, sems):
        self.s, self.block, self.rows = s, block, rows
        self.first, self.held, self.later = first, held, later
        self.send0, self.recv0, self.send1, self.recv1 = sems
        self.orders = orders_of(ns)
        self.half = ns // 2

    def core_copy(self, j):
        return remote(self.first.at[j], self.held.at[j], self.send0.at[j], self.recv0.at[j], "seq", self.s ^ 1)

    def send_core(self, j=None):
        if j is None:
            pl.loop(0, self.half)(self.send_core)
            return
        j = self.half - 1 - j
        self.first[j] = self.block(self.s ^ (2 * j + 1)).astype(BF16)
        self.core_copy(j).start()

    def base(self, i):
        return sum(2 ** (self.stages - 1 - k) for k in range(i))

    def move(self, i, half, slot, other):
        part = self.rows // 2
        return remote(
            self.held.at[(self.orders[half][i] | other) >> 1, pl.ds(half * part, part)],
            self.later.at[half, slot], self.send1.at[half, slot], self.recv1.at[half, slot],
            "seq", self.s ^ self.orders[half][i],
        )

    def moves(self, i):
        part = self.rows // 2
        for half, order in enumerate(self.orders):
            for j, other in enumerate(subsets(order[i + 1 :])):
                slot = self.base(i) + j
                yield other >> 1, pl.ds(half * part, part), half, slot, self.move(i, half, slot, other)

    def add_core(self, j=None):
        if j is None:
            pl.loop(0, self.half)(self.add_core)
            return
        j = self.half - 1 - j
        mine = self.block(self.s ^ (2 * j))
        self.core_copy(j).wait_recv()
        self.held[j] = (self.held[j].astype(F32) + mine).astype(BF16)
        for half, order in enumerate(self.orders):
            for slot, other in enumerate(subsets(order[1:])):

                @pl.when(j == (order[0] | other) >> 1)
                def _():
                    self.move(0, half, slot, other).start()

    def send(self, i):
        for *_, copy in self.moves(i):
            copy.start()

    def take(self, i):
        for j, at, half, slot, copy in self.moves(i):
            copy.wait_recv()
            self.held[j, at] = (self.held[j, at].astype(F32) + self.later[half, slot].astype(F32)).astype(BF16)

    def step(self, i):
        self.take(i)
        if i + 1 < self.stages:
            self.send(i + 1)

    @property
    def stages(self):
        return len(self.orders[0])

    def core_sent(self):
        @pl.loop(0, self.half)
        def _(j):
            self.core_copy(j).wait_send()

    def finish(self):
        for i in range(self.stages):
            for *_, copy in self.moves(i):
                copy.wait_send()

    @staticmethod
    def scratch(ns, rows, width):
        dma = pltpu.SemaphoreType.DMA
        half = ns // 2
        return [
            pltpu.VMEM((half, rows, width), BF16),
            pltpu.VMEM((half, rows, width), BF16),
            pltpu.VMEM((2, half - 1, rows // 2, width), BF16),
            dma((half,)), dma((half,)), dma((2, half - 1)), dma((2, half - 1)),
        ]


def forward_kernel(
    n, ns,
    att, tok, cot, more, gate_b, up, down, attn_gain, mlp_gain,
    out, h1r_out, branch_out, hidden_out, dy2_out, dg_out, du_out, gain_part, up_out,
    h1r, hidden, dy2, dg, du,
    wo, wd, wg, wu, land, branch, h1, second, g_pre, u_pre,
    wsem, osem, bsem, g1s, g1r, s1s, s1r, g2s, g2r, s2s, s2r, us, ur, ds, dr,
):
    s, z = lax.axis_index("seq"), lax.axis_index("head")
    rows, depth = tok.shape
    lw, ff = att.shape[1], up.shape[1]
    block = depth // ns
    width = depth // STEPS
    mine = rows_at(s, block)
    l_o = pltpu.make_async_copy(more.at[:, pl.ds(0, lw)], wo, wsem.at[0])
    l_u = pltpu.make_async_copy(up, wu.at[mine], wsem.at[1])
    early = more.shape[1] - lw
    l_g = pltpu.make_async_copy(more.at[:, pl.ds(lw, early)], wg.at[:, pl.ds(0, early)], wsem.at[2])
    l_h = pltpu.make_async_copy(gate_b, wg.at[:, pl.ds(early, ff - early)], wsem.at[3])
    for copy in (l_o, l_u, l_g, l_h):
        copy.start()
    cube_barrier(s, z, ns, n)
    cube_u = CubeGather(s, ns, wu, block, us, ur)
    cube_d = CubeGather(s, ns, wd, block, ds, dr)
    levels = cube_u.levels
    l_u.wait()
    cube_u.start()
    l_o.wait()

    def out_part(d, c):
        return mm(att[rows_at(d, rows), :], wo[rows_at(c, width), :], NT)

    line = LineScatter(z, n, out_part, land, s1s, s1r, branch)
    line.run(0, STEPS)
    line.start_own()
    wd[mine, :] = jnp.transpose(down[...].astype(F32)).astype(BF16)
    cube_u.level(0)
    line.run(STEPS, 2 * STEPS)
    for i in range(1, levels - 1):
        cube_u.level(i)
    cube_d.start()
    line.run(2 * STEPS, line.slots)
    line.own()
    line.finish()
    o_branch = pltpu.make_async_copy(branch, branch_out, osem.at[0])
    o_branch.start()
    gain_part[...] = jnp.zeros_like(gain_part)

    @pl.loop(0, rows // BLOCK)
    def _(i):
        at = rows_at(i, BLOCK)
        y = branch[at, :]
        h = tok[at, :].astype(F32) + y * row_scale(y) * attn_gain[...]
        h1[at, :] = h
        h1r[pl.ds(pl.multiple_of(z * rows + i * BLOCK, BLOCK), BLOCK), :] = h.astype(BF16)

    fw = ff // STEPS
    o_up = pltpu.make_async_copy(wu, up_out, osem.at[1])
    o_h1r = pltpu.make_async_copy(h1r, h1r_out, osem.at[2])
    o_hidden = pltpu.make_async_copy(hidden, hidden_out, osem.at[3])
    o_dy2 = pltpu.make_async_copy(dy2, dy2_out, osem.at[4])

    def up_block(src):
        at = rows_at(src, rows)

        @pl.loop(0, STEPS)
        def _(c):
            cols = rows_at(c, fw)
            x = h1r[at, :]
            g = mm(x, wg[:, cols])
            u = mm(x, wu[:, cols])
            g_pre[at, cols] = g
            u_pre[at, cols] = u
            hidden[at, cols] = (g * sigmoid(g) * u).astype(BF16)

    def weights_there():
        l_g.wait()
        l_h.wait()
        cube_u.level(levels - 1)
        o_up.start()

    hooks = [functools.partial(cube_d.level, i) for i in range(levels)]
    line_gather(z, n, h1r, rows, g1s, g1r, up_block, hooks[: n - 1], weights_there)
    for hook in hooks[n - 1 :]:
        hook()
    o_h1r.start()
    o_hidden.start()

    def down_part(d, c):
        return mm(hidden[rows_at(d, rows), :], wd[rows_at(c, width), :], NT)

    line = LineScatter(z, n, down_part, land, s2s, s2r, second)
    line.run(0, STEPS)
    line.start_own()
    line.run(STEPS, line.slots)
    line.own()
    line.finish()

    @pl.loop(0, rows // BLOCK)
    def _(i):
        at = rows_at(i, BLOCK)
        y = second[at, :]
        scale = row_scale(y)
        normed = y * scale
        e = cot[at, :].astype(F32)
        out[at, :] = (h1[at, :] + normed * mlp_gain[...]).astype(BF16)
        gain_part[...] += jnp.sum(e * normed, axis=0, keepdims=True)
        dy2[pl.ds(pl.multiple_of(z * rows + i * BLOCK, BLOCK), BLOCK), :] = norm_back(
            e, normed, scale, mlp_gain[...]
        ).astype(BF16)

    def back_block(src):
        at = rows_at(src, rows)

        @pl.loop(0, STEPS)
        def _(c):
            cols = rows_at(c, fw)
            dh = mm(dy2[at, :], wd[:, cols])
            g = g_pre[at, cols]
            u = u_pre[at, cols]
            sig = sigmoid(g)
            du[at, cols] = (dh * g * sig).astype(BF16)
            dg[at, cols] = (dh * u * sig * (1.0 + g * (1.0 - sig))).astype(BF16)

        for copy in grads_out(src):
            copy.start()

    def grads_out(src):
        at = rows_at(src, rows)
        return [
            pltpu.make_async_copy(held.at[at], to.at[at], bsem.at[i, src])
            for i, (held, to) in enumerate(((dg, dg_out), (du, du_out)))
        ]

    line_gather(z, n, dy2, rows, g2s, g2r, back_block)
    o_dy2.start()
    for copy in (o_branch, o_up, o_h1r, o_hidden, o_dy2):
        copy.wait()

    @pl.loop(0, n)
    def _(src):
        for copy in grads_out(src):
            copy.wait()

    cube_u.finish()
    cube_d.finish()


def run_forward(n, ns, att, tok, cot, more, gate_b, up, down, attn_gain, mlp_gain):
    rows, depth = tok.shape
    tl, lw = att.shape
    ff = up.shape[1]
    dma = pltpu.SemaphoreType.DMA
    sems = line_sems(n)
    shape = jax.ShapeDtypeStruct
    return pl.pallas_call(
        functools.partial(forward_kernel, n, ns),
        out_shape=(
            shape((rows, depth), BF16),
            shape((tl, depth), BF16),
            shape((rows, depth), F32),
            shape((tl, ff), BF16),
            shape((tl, depth), BF16),
            shape((tl, ff), BF16),
            shape((tl, ff), BF16),
            shape((1, depth), F32),
            shape((depth, ff), BF16),
        ),
        in_specs=[VMEM, VMEM, VMEM, ANY, ANY, ANY, VMEM, VMEM, VMEM],
        out_specs=(VMEM, ANY, ANY, ANY, ANY, ANY, ANY, VMEM, ANY),
        scratch_shapes=[
            pltpu.VMEM((tl, depth), BF16),
            pltpu.VMEM((tl, ff), BF16),
            pltpu.VMEM((tl, depth), BF16),
            pltpu.VMEM((tl, ff), BF16),
            pltpu.VMEM((tl, ff), BF16),
            pltpu.VMEM((depth, lw), BF16),
            pltpu.VMEM((depth, ff), BF16),
            pltpu.VMEM((depth, ff), BF16),
            pltpu.VMEM((depth, ff), BF16),
            pltpu.VMEM((2, n, STEPS, rows, depth // STEPS), BF16),
            pltpu.VMEM((rows, depth), F32),
            pltpu.VMEM((rows, depth), F32),
            pltpu.VMEM((rows, depth), F32),
            pltpu.VMEM((tl, ff), F32),
            pltpu.VMEM((tl, ff), F32),
            dma((4,)),
            dma((5,)),
            dma((2, n)),
            *sems["gather"], *sems["scatter"], *sems["gather"], *sems["scatter"],
            *CubeGather.sems(ns), *CubeGather.sems(ns),
        ],
        compiler_params=pltpu.CompilerParams(
            collective_id=1, has_side_effects=True, vmem_limit_bytes=VMEM_BYTES
        ),
        cost_estimate=pl.CostEstimate(flops=18 * 10**9, bytes_accessed=40 * 10**6, transcendentals=2 * 10**6),
        name="feed_forward",
    )(att, tok, cot, more, gate_b, up, down, attn_gain, mlp_gain)


def backward_kernel(
    n, ns,
    dg_in, du_in, h1r_in, cot, branch, more, gate_b, up, attn_gain,
    middle, dy1, datt, gain_part, grad_gate, grad_up,
    dg, du, h1r, wo, wg, wu, land, total,
    first, held_g, later_g, held_u, later_u,
    wsem, osem, s1s, s1r, g1s, g1r,
    ga, gb, gc, gd, ua, ub, uc, ud,
):
    s, z = lax.axis_index("seq"), lax.axis_index("head")
    rows, depth = cot.shape
    lw, ff = datt.shape[1], dg_in.shape[1]
    block = depth // ns
    width = depth // STEPS
    early = more.shape[1] - lw

    def weights_in(c):
        at = rows_at(c, width)
        return [
            pltpu.make_async_copy(more.at[at, pl.ds(lw, early)], wg.at[at, pl.ds(0, early)], wsem.at[0, c]),
            pltpu.make_async_copy(gate_b.at[at], wg.at[at, pl.ds(early, ff - early)], wsem.at[1, c]),
            pltpu.make_async_copy(up.at[at], wu.at[at], wsem.at[2, c]),
        ]

    l_h = pltpu.make_async_copy(h1r_in, h1r, osem.at[0])
    l_o = pltpu.make_async_copy(more.at[:, pl.ds(0, lw)], wo, osem.at[1])
    l_dg = pltpu.make_async_copy(dg_in, dg, osem.at[2])
    l_du = pltpu.make_async_copy(du_in, du, osem.at[3])
    for load in (l_dg, l_h, l_du):
        load.start()
    for c in range(STEPS):
        for copy in weights_in(c):
            copy.start()
    l_o.start()
    cube_barrier(s, z, ns, n)

    def weight_block(grad):
        return lambda b: mm(h1r[:, rows_at(b, block)], grad[...], TN)

    cube_g = CubeScatter(s, ns, weight_block(dg), block, first, held_g, later_g, (ga, gb, gc, gd))
    cube_u = CubeScatter(s, ns, weight_block(du), block, first, held_u, later_u, (ua, ub, uc, ud))

    def in_part(d, c):
        at, cols = rows_at(d, rows), rows_at(c, width)
        return mm(dg[at, :], wg[cols, :], NT) + mm(du[at, :], wu[cols, :], NT)

    line = LineScatter(z, n, in_part, land, s1s, s1r, total)
    half = ns // 2

    def there(slot):
        @pl.when(slot < STEPS)
        def _():
            for copy in weights_in(slot):
                copy.wait()

    def task(slot):
        def during(low, count, act):
            @pl.when((slot >= low) & (slot < low + half // count))
            def _():
                for i in range(count):
                    act(count * (slot - low) + i)

        def send_second(j):
            cube_g.core_copy(half - 1 - j).wait_send()
            cube_u.send_core(j)

        during(0, 2, cube_g.add_core)
        during(half // 2, 1, send_second)
        during(half // 2 + half, 1, cube_u.add_core)

    l_h.wait()
    l_dg.wait()
    cube_g.send_core()
    l_du.wait()
    line.run(0, 2 * STEPS, there, task)
    line.start_own()
    line.run(2 * STEPS, line.slots, None, task)

    @pl.loop(line.slots, max(line.slots, half // 2 + 2 * half))
    def _(slot):
        task(slot)

    cube_g.step(0)
    line.own()
    line.finish()
    gain_part[...] = jnp.zeros_like(gain_part)

    @pl.loop(0, rows // BLOCK)
    def _(i):
        at = rows_at(i, BLOCK)
        y = branch[at, :]
        scale = row_scale(y)
        normed = y * scale
        e = cot[at, :].astype(F32) + total[at, :]
        middle[at, :] = e
        gain_part[...] += jnp.sum(e * normed, axis=0, keepdims=True)
        dy1[pl.ds(pl.multiple_of(z * rows + i * BLOCK, BLOCK), BLOCK), :] = norm_back(
            e, normed, scale, attn_gain[...]
        ).astype(BF16)

    l_o.wait()

    def att_block(src):
        at = rows_at(src, rows)
        datt[at, :] = mm(dy1[at, :], wo[...]).astype(BF16)

    todo = [functools.partial(cube.step, i) for i in range(1, cube_g.stages) for cube in (cube_g, cube_u)]
    line_gather(z, n, dy1, rows, g1s, g1r, att_block, todo[: n - 1], functools.partial(cube_u.step, 0))
    for step in todo[n - 1 :]:
        step()
    grad_gate[...] = held_g[0]
    grad_up[...] = held_u[0]
    cube_g.finish()
    cube_u.core_sent()
    cube_u.finish()


def run_backward(n, ns, dg, du, h1r, cot, branch, more, gate_b, up, attn_gain):
    rows, depth = cot.shape
    tl, ff = dg.shape
    lw = more.shape[1] + gate_b.shape[1] - ff
    block = depth // ns
    dma = pltpu.SemaphoreType.DMA
    sems = line_sems(n)
    shape = jax.ShapeDtypeStruct
    first, held, later, *cube_sems = CubeScatter.scratch(ns, block, ff)
    return pl.pallas_call(
        functools.partial(backward_kernel, n, ns),
        out_shape=(
            shape((rows, depth), F32),
            shape((tl, depth), BF16),
            shape((tl, lw), BF16),
            shape((1, depth), F32),
            shape((block, ff), BF16),
            shape((block, ff), BF16),
        ),
        in_specs=[ANY, ANY, ANY, VMEM, VMEM, ANY, ANY, ANY, VMEM],
        out_specs=(VMEM,) * 6,
        scratch_shapes=[
            pltpu.VMEM((tl, ff), BF16),
            pltpu.VMEM((tl, ff), BF16),
            pltpu.VMEM((tl, depth), BF16),
            pltpu.VMEM((depth, lw), BF16),
            pltpu.VMEM((depth, ff), BF16),
            pltpu.VMEM((depth, ff), BF16),
            pltpu.VMEM((2, n, STEPS, rows, depth // STEPS), BF16),
            pltpu.VMEM((rows, depth), F32),
            first, held, later, held, later,
            dma((3, STEPS)),
            dma((4,)),
            *sems["scatter"], *sems["gather"],
            *cube_sems, *cube_sems,
        ],
        compiler_params=pltpu.CompilerParams(
            collective_id=2, has_side_effects=True, vmem_limit_bytes=VMEM_BYTES
        ),
        cost_estimate=pl.CostEstimate(flops=18 * 10**9, bytes_accessed=30 * 10**6, transcendentals=0),
        name="into_attention",
    )(dg, du, h1r, cot, branch, more, gate_b, up, attn_gain)


LOG2E = 1.4426950408889634
NEG = -1e30


def seq_barrier(s, ns, between=None):
    bar = pltpu.get_barrier_semaphore()
    for other in range(ns):

        @pl.when(other != s)
        def _():
            pl.semaphore_signal(bar, inc=1, device_id={"seq": other}, device_id_type=MESH)

    if between is not None:
        between()
    pl.semaphore_wait(bar, ns - 1)


def share_of(s, ns, r):
    per = ns // (2 * r)
    chunk = s // per
    low = chunk < r
    sub = jnp.where(low, chunk, 2 * r - 1 - chunk)
    return sub, jnp.where(low, s - chunk * per, per + s - chunk * per)


def source_of(sub, i, ns, r):
    per = ns // (2 * r)
    return jnp.where(i < per, sub * per + i, (2 * r - 1 - sub) * per + i - per)


def head_cols(h):
    return pl.ds(pl.multiple_of(h * HEAD_DIM, HEAD_DIM), HEAD_DIM)


def attend_part(
    ns, heads, q_in, k_in, v_in, docs, gate,
    att, q_out, k_out, v_out, o_buf, lse, gate_out,
    q_buf, k_buf, v_buf, o_low, qs, qr, ks, kr, vs, vr, osend, orecv, local, cs, cr, late,
):
    s = lax.axis_index("seq")
    r = ns // heads
    blocks = ns // r
    tl = q_in.shape[0]
    mine, sub = s // r, s % r
    parity = s % 2
    to_sub, to_row = share_of(s, ns, r)

    def own_rows():
        for x, buf in ((k_in, k_buf), (v_in, v_buf)):
            buf[rows_at(s, tl), :] = x[:, head_cols(mine)]

        @pl.when(to_sub == sub)
        def _():
            q_buf[rows_at(to_row, tl), :] = q_in[:, head_cols(mine)]

    own_rows()

    def q_copy(h):
        return pltpu.make_async_remote_copy(
            src_ref=q_in.at[:, head_cols(h)],
            dst_ref=q_buf.at[rows_at(to_row, tl)],
            send_sem=qs.at[h],
            recv_sem=qr.at[to_row],
            device_id={"seq": h * r + to_sub},
            device_id_type=MESH,
        )

    def q_recv(i):
        return pltpu.make_async_remote_copy(
            src_ref=q_buf.at[rows_at(i, tl)],
            dst_ref=q_buf.at[rows_at(i, tl)],
            send_sem=qs.at[0],
            recv_sem=qr.at[i],
            device_id={"seq": s ^ 1},
            device_id_type=MESH,
        )

    def kv_copy(src, buf, send, recv, t, at):
        return pltpu.make_async_remote_copy(
            src_ref=src,
            dst_ref=buf.at[rows_at(at, tl)],
            send_sem=send,
            recv_sem=recv.at[at],
            device_id={"seq": t},
            device_id_type=MESH,
        )

    kv = ((k_in, k_buf, ks, kr), (v_in, v_buf, vs, vr))
    block = gate.shape[0]
    cols = gate_out.shape[1]
    own = gate.at[:, pl.ds(gate.shape[1] - cols, cols)]
    own_gate = pltpu.make_async_copy(own, gate_out.at[rows_at(s, block)], local.at[0])
    cube = CubeGather(s, ns, gate_out, block, cs, cr, own)
    own_gate.start()

    def far(t):
        return (t != s) & (t % 2 == parity)

    @pl.loop(1, ns)
    def _(step):
        t = s ^ step

        @pl.when(far(t))
        def _():
            for x, buf, ss, rs in kv:
                kv_copy(x.at[:, head_cols(t // r)], buf, ss.at[0, t], rs, t, s).start()

    @pl.loop(0, heads)
    def _(h):
        @pl.when(h * r + to_sub != s)
        def _():
            q_copy(h).start()

    def pass_on(src, start):
        for _, buf, ss, rs in kv:
            copy = kv_copy(buf.at[rows_at(src, tl)], buf, ss.at[1, src], rs, s ^ 1, src)
            if start:
                copy.start()
            else:
                copy.wait_send()

    pass_on(s, True)

    @pl.loop(1, ns)
    def _(step):
        src = s ^ step

        @pl.when(far(src))
        def _():
            for x, buf, ss, rs in kv:
                kv_copy(buf.at[rows_at(src, tl)], buf, ss.at[0, 0], rs, s ^ 1, src).wait_recv()
            pass_on(src, True)

    @pl.loop(0, ns)
    def _(src):
        @pl.when(src % 2 != parity)
        def _():
            for x, buf, ss, rs in kv:
                kv_copy(buf.at[rows_at(src, tl)], buf, ss.at[0, 0], rs, s ^ 1, src).wait_recv()

    unit = HEAD_DIM ** (-0.5) * LOG2E

    def o_copy(i, t):
        return pltpu.make_async_remote_copy(
            src_ref=o_low.at[rows_at(i, tl)],
            dst_ref=att.at[:, head_cols(mine)],
            send_sem=osend.at[i],
            recv_sem=orecv.at[mine],
            device_id={"seq": t},
            device_id_type=MESH,
        )

    def attend_block(i):
        src = source_of(sub, i, ns, r)

        @pl.when(src != s)
        def _():
            q_recv(i).wait_recv()

        q = q_buf[rows_at(i, tl), :]
        start = first_of_document(docs, src * tl + lax.broadcasted_iota(jnp.int32, (1, tl), 1))
        key_at = lax.broadcasted_iota(jnp.int32, (tl, tl), 0)

        def step(j, carry, diagonal):
            top, total, acc = carry
            at = rows_at(j, tl)
            scores = mm(k_buf[at, :], q, NT) * unit
            allowed = key_at >= start - j * tl
            if diagonal:
                allowed = allowed & (key_at <= lax.broadcasted_iota(jnp.int32, (tl, tl), 1))
            scores = jnp.where(allowed, scores, NEG)
            new = jnp.maximum(top, jnp.max(scores, axis=0, keepdims=True))
            terms = jnp.exp2(scores - new)
            fade = jnp.exp2(top - new)
            return (
                new,
                total * fade + jnp.sum(terms, axis=0, keepdims=True),
                acc * fade + mm(v_buf[at, :], terms.astype(BF16), TN),
            )

        carry = (
            jnp.full((1, tl), NEG, F32),
            jnp.zeros((1, tl), F32),
            jnp.zeros((HEAD_DIM, tl), F32),
        )
        carry = lax.fori_loop(0, src, lambda j, c: step(j, c, False), carry)
        top, total, acc = step(src, carry, True)
        lse[pl.ds(i, 1), :] = top + jnp.log(total) * LOG2E
        o = jnp.transpose(acc / total)
        o_buf[rows_at(i, tl), :] = o
        o_low[rows_at(i, tl), :] = o.astype(BF16)

        @pl.when(src != s)
        def _():
            o_copy(i, src).start()

        @pl.when(src == s)
        def _():
            att[:, head_cols(mine)] = o.astype(BF16)

    late()
    cube.start()
    keep = [
        pltpu.make_async_copy(a, b, local.at[1 + i])
        for i, (a, b) in enumerate(((k_buf, k_out), (v_buf, v_out), (q_buf, q_out)))
    ]
    for copy in keep[:2]:
        copy.start()
    cuts = [0, blocks - 1, blocks, blocks]
    for i in range(3):
        pl.loop(cuts[i], cuts[i + 1])(attend_block)
        if i < 2:
            cube.level(i)
    for i in range(2, cube.levels):
        cube.level(i)

    keep[2].start()
    own_gate.wait()

    @pl.loop(0, heads)
    def _(h):
        @pl.when(h * r + to_sub != s)
        def _():
            q_copy(h).wait_send()
            pltpu.make_async_remote_copy(
                src_ref=o_low.at[rows_at(0, tl)],
                dst_ref=att.at[:, head_cols(h)],
                send_sem=osend.at[0],
                recv_sem=orecv.at[h],
                device_id={"seq": s ^ 1},
                device_id_type=MESH,
            ).wait_recv()

    @pl.loop(0, blocks)
    def _(i):
        src = source_of(sub, i, ns, r)

        @pl.when(src != s)
        def _():
            o_copy(i, src).wait_send()

    pass_on(s, False)

    @pl.loop(1, ns)
    def _(step):
        t = s ^ step

        @pl.when(far(t))
        def _():
            for x, buf, ss, rs in kv:
                kv_copy(x.at[:, head_cols(t // r)], buf, ss.at[0, t], rs, t, s).wait_send()
            pass_on(t, False)

    cube.finish()
    for copy in keep:
        copy.wait()


def attend_back_kernel(
    ns, heads, do_in, docs, q_in, k_in, v_in, o_in, lse, dy2_in, hidden_in,
    dq, dk, dv, grad_down,
    q_buf, k_buf, v_buf, o_buf, dy2, hidden, lsem,
    do_buf, dq_low, dk_acc, dv_acc, low, pair, land,
    first, held, later, ca, cb, cc, cd,
    ds_, dr_, ps, pr, gs, gr, qs, qr,
):
    s = lax.axis_index("seq")
    r = ns // heads
    blocks = ns // r
    tl = do_in.shape[0]
    mine, sub = s // r, s % r
    parity = s % 2

    loads = [
        pltpu.make_async_copy(a, b, lsem.at[i])
        for i, (a, b) in enumerate(
            ((dy2_in, dy2), (hidden_in, hidden), (q_in, q_buf), (k_in, k_buf), (v_in, v_buf), (o_in, o_buf))
        )
    ]
    for load in loads:
        load.start()

    def clear():
        dk_acc[...] = jnp.zeros_like(dk_acc)
        dv_acc[...] = jnp.zeros_like(dv_acc)

    seq_barrier(s, ns, clear)
    to_sub, to_row = share_of(s, ns, r)

    def copy(src, dst, send, recv, t):
        return pltpu.make_async_remote_copy(
            src_ref=src, dst_ref=dst, send_sem=send, recv_sem=recv, device_id={"seq": t}, device_id_type=MESH
        )

    def do_copy(h):
        return copy(
            do_in.at[:, head_cols(h)], do_buf.at[rows_at(to_row, tl)], ds_.at[h], dr_.at[to_row], h * r + to_sub
        )

    @pl.loop(0, heads)
    def _(h):
        @pl.when(h * r + to_sub != s)
        def _():
            do_copy(h).start()

    block = dy2.shape[1] // ns
    cube = CubeScatter(
        s, ns, lambda b: mm(dy2[:, rows_at(b, block)], hidden[:, : grad_down.shape[0]], TN), block, first, held, later, (ca, cb, cc, cd)
    )
    for load in loads:
        load.wait()
    cube.send_core()
    cube.add_core()

    @pl.when(to_sub == sub)
    def _():
        do_buf[rows_at(to_row, tl), :] = do_in[:, head_cols(mine)]

    scale = HEAD_DIM ** (-0.5)
    unit = scale * LOG2E

    def dq_copy(i, t):
        return copy(dq_low.at[rows_at(i, tl)], dq.at[:, head_cols(mine)], qs.at[i], qr.at[mine], t)

    ones = jnp.ones((8, HEAD_DIM), F32)

    def back_block(i):
        src = source_of(sub, i, ns, r)
        rows = rows_at(i, tl)

        @pl.when(src != s)
        def _():
            copy(do_buf.at[rows], do_buf.at[rows], ds_.at[0], dr_.at[i], s ^ 1).wait_recv()

        q = q_buf[rows, :]
        do = do_buf[rows, :]
        start = first_of_document(docs, src * tl + lax.broadcasted_iota(jnp.int32, (1, tl), 1))
        norm = lse[pl.ds(i, 1), :]
        delta = lax.dot_general(
            ones, do.astype(F32) * o_buf[rows, :], NT,
            precision=lax.Precision.HIGHEST, preferred_element_type=F32,
        )[:1]
        key_at = lax.broadcasted_iota(jnp.int32, (tl, tl), 0)

        def step(j, dq_sum, diagonal):
            at = rows_at(j, tl)
            keys = k_buf[at, :]
            scores = mm(keys, q, NT) * unit
            allowed = key_at >= start - j * tl
            if diagonal:
                allowed = allowed & (key_at <= lax.broadcasted_iota(jnp.int32, (tl, tl), 1))
            p = jnp.where(allowed, jnp.exp2(scores - norm), 0.0)
            dp = mm(v_buf[at, :], do, NT)
            dscore = (p * (dp - delta)).astype(BF16)
            dv_acc[at, :] += mm(p.astype(BF16), do)
            dk_acc[at, :] += mm(dscore, q)
            return dq_sum + mm(dscore, keys, TN)

        dq_sum = lax.fori_loop(0, src, lambda j, c: step(j, c, False), jnp.zeros((tl, HEAD_DIM), F32))
        dq_sum = step(src, dq_sum, True)
        dq_low[rows, :] = (dq_sum * scale).astype(BF16)

        @pl.when(src != s)
        def _():
            dq_copy(i, src).start()

        @pl.when(src == s)
        def _():
            dq[:, head_cols(mine)] = dq_low[rows, :]

    pl.loop(0, blocks - 1)(back_block)
    cube.step(0)
    pl.loop(blocks - 1, blocks)(back_block)
    half = ns // 2

    def pair_copy(w, i):
        src = 2 * i + 1 - parity
        return copy(low.at[w, rows_at(src, tl)], pair.at[w, rows_at(i, tl)], ps.at[w, i], pr.at[w, i], s ^ 1)

    @pl.loop(0, half)
    def _(i):
        at = rows_at(2 * i + 1 - parity, tl)
        low[0, at, :] = (dk_acc[at, :] * scale).astype(BF16)
        pair_copy(0, i).start()
        low[1, at, :] = dv_acc[at, :].astype(BF16)
        pair_copy(1, i).start()

    slot = sub // 2
    outs = (dk, dv)

    def back_copy(w, i):
        dest = 2 * i + parity
        return copy(
            low.at[w, rows_at(dest, tl)], land.at[w, slot, :, head_cols(mine)], gs.at[w, i], gr.at[w, mine, slot], dest
        )

    @pl.loop(0, half)
    def _(i):
        dest = 2 * i + parity
        at = rows_at(dest, tl)
        for w, acc, factor in ((0, dk_acc, scale), (1, dv_acc, 1.0)):
            copy(low.at[w, at], pair.at[w, rows_at(i, tl)], ps.at[w, i], pr.at[w, i], s ^ 1).wait_recv()
            low[w, at, :] = (acc[at, :] * factor + pair[w, rows_at(i, tl), :].astype(F32)).astype(BF16)

            @pl.when(dest != s)
            def _():
                back_copy(w, i).start()

            @pl.when(dest == s)
            def _():
                land[w, slot, :, head_cols(mine)] = low[w, at, :]

    @pl.loop(0, heads)
    def _(h):
        for w in range(2):
            for k in range(r // 2):

                @pl.when(h * r + 2 * k + parity != s)
                def _():
                    copy(
                        low.at[w, rows_at(0, tl)], land.at[w, k, :, head_cols(h)], gs.at[w, 0], gr.at[w, h, k], s ^ 1
                    ).wait_recv()

    for w in range(2):
        outs[w][...] = functools.reduce(
            lambda a, b: a + b, [land[w, k].astype(F32) for k in range(r // 2)]
        ).astype(BF16)

    @pl.loop(0, heads)
    def _(h):
        @pl.when(h * r + to_sub != s)
        def _():
            do_copy(h).wait_send()
            copy(dq_low.at[rows_at(0, tl)], dq.at[:, head_cols(h)], qs.at[0], qr.at[h], s ^ 1).wait_recv()

    @pl.loop(0, blocks)
    def _(i):
        src = source_of(sub, i, ns, r)

        @pl.when(src != s)
        def _():
            dq_copy(i, src).wait_send()

    @pl.loop(0, half)
    def _(i):
        for w in range(2):
            pair_copy(w, i).wait_send()

            @pl.when(2 * i + parity != s)
            def _():
                back_copy(w, i).wait_send()

    for i in range(1, cube.stages):
        cube.step(i)
    grad_down[...] = jnp.transpose(held[0].astype(F32)).astype(BF16)
    cube.core_sent()
    cube.finish()


def run_attend_back(ns, heads, do, docs, q, k, v, o, lse, dy2, hidden):
    tl, lw = do.shape
    r = ns // heads
    nq = ns // r * tl
    nk = ns * tl
    dma = pltpu.SemaphoreType.DMA
    shape = jax.ShapeDtypeStruct
    return pl.pallas_call(
        functools.partial(attend_back_kernel, ns, heads),
        out_shape=(shape((tl, lw), BF16),) * 3 + (shape((hidden.shape[1] - lw, dy2.shape[1] // ns), BF16),),
        in_specs=[VMEM, SMEM] + [ANY] * 4 + [VMEM] + [ANY] * 2,
        out_specs=(VMEM,) * 4,
        scratch_shapes=[
            pltpu.VMEM((nq, HEAD_DIM), BF16),
            pltpu.VMEM((nk, HEAD_DIM), BF16),
            pltpu.VMEM((nk, HEAD_DIM), BF16),
            pltpu.VMEM((nq, HEAD_DIM), F32),
            pltpu.VMEM(dy2.shape, BF16),
            pltpu.VMEM(hidden.shape, BF16),
            dma((6,)),
            pltpu.VMEM((nq, HEAD_DIM), BF16),
            pltpu.VMEM((nq, HEAD_DIM), BF16),
            pltpu.VMEM((nk, HEAD_DIM), F32),
            pltpu.VMEM((nk, HEAD_DIM), F32),
            pltpu.VMEM((2, nk, HEAD_DIM), BF16),
            pltpu.VMEM((2, nk // 2, HEAD_DIM), BF16),
            pltpu.VMEM((2, r // 2, tl, lw), BF16),
            *CubeScatter.scratch(ns, dy2.shape[1] // ns, hidden.shape[1] - lw),
            dma((heads,)), dma((ns // r,)),
            dma((2, ns // 2)), dma((2, ns // 2)),
            dma((2, ns // 2)), dma((2, heads, r // 2)),
            dma((ns // r,)), dma((heads,)),
        ],
        compiler_params=pltpu.CompilerParams(
            collective_id=4, has_side_effects=True, vmem_limit_bytes=VMEM_BYTES
        ),
        cost_estimate=pl.CostEstimate(flops=8 * 10**9, bytes_accessed=10 * 10**6, transcendentals=5 * 10**6),
        name="attend_back",
    )(do, docs, q, k, v, o, lse, dy2, hidden)


def cross_barrier(s, z, ns, n, between=None):
    bar = pltpu.get_barrier_semaphore()
    for axis, me, count in (("seq", s, ns), ("head", z, n)):
        for other in range(count):

            @pl.when(other != me)
            def _():
                pl.semaphore_signal(bar, inc=1, device_id={axis: other}, device_id_type=MESH)

    if between is not None:
        between()
    pl.semaphore_wait(bar, ns - 1 + n - 1)


def row_sums(left, right):
    ones = jnp.ones((8, left.shape[1]), F32)
    both = [
        lax.dot_general(ones, x, NT, precision=lax.Precision.HIGHEST, preferred_element_type=F32) for x in (left, right)
    ]
    return jnp.where(lax.broadcasted_iota(jnp.int32, both[0].shape, 0) < 4, both[0], both[1])


def as_column(sums, row):
    pick = (lax.broadcasted_iota(jnp.int32, (8, HEAD_DIM), 0) == row).astype(F32)
    return lax.dot_general(sums, pick, TN, precision=lax.Precision.HIGHEST, preferred_element_type=F32)


class SmallExchange:
    def __init__(self, axis, me, count, land, send_sem, recv_sem):
        self.axis, self.me, self.count, self.land = axis, me, count, land
        self.send_sem, self.recv_sem = send_sem, recv_sem

    def copy(self, slot, to):
        return remote(self.land.at[slot], self.land.at[slot], self.send_sem.at[to], self.recv_sem.at[slot], self.axis, to)

    def each(self, act):
        @pl.loop(0, self.count)
        def _(other):
            @pl.when(other != self.me)
            def _():
                act(other)

    def start(self):
        self.each(lambda other: self.copy(self.me, other).start())

    def receive(self):
        self.each(lambda other: self.copy(other, other).wait_recv())

    def finish(self):
        self.each(lambda other: self.copy(self.me, other).wait_send())


def turn(x, cos, sin):
    return x * cos + pltpu.roll(x, HEAD_DIM // 2, 1) * sin


def turn_back(x, cos, sin):
    return x * cos - pltpu.roll(x, HEAD_DIM // 2, 1) * sin


def project_part(
    n, ns, depth_full,
    tok, wq, wk, wv, wo, gate, gq, gk, docs, turns,
    x_out, w_out, more_out, q_out, k_out, totals, cos, sin,
    q_rot, k_rot, v_low, q_raw, k_raw, x, w, own, land, lsem, ags, agr, cgs, cgr, egs, egr, ss, sr,
):
    s, z = lax.axis_index("seq"), lax.axis_index("head")
    rows, depth = tok.shape
    block, lw = wq.shape
    heads = lw // HEAD_DIM
    cross_barrier(s, z, ns, n)
    mine = rows_at(s, block)

    def head_gain(h):
        return head_cols(z * heads + h)

    loads = [pltpu.make_async_copy(tok, x.at[rows_at(z, rows)], lsem.at[0])] + [
        pltpu.make_async_copy(m, w.at[mine, pl.ds(i * lw, lw)], lsem.at[i + 1]) for i, m in enumerate((wq, wk, wv))
    ]
    for copy in loads:
        copy.start()
    loads[0].wait()
    cube = CubeGather(s, ns, w, block, cgs, cgr)
    own_more = pltpu.make_async_copy(own, more_out.at[mine], lsem.at[8])
    cube_e = CubeGather(s, ns, more_out, block, egs, egr, own)
    levels = cube.levels

    def weights(k):
        if k == 0:
            cube.level(0)
        else:
            for i in range(1, levels):
                cube.level(i)
                if i == levels - 2:
                    cube_e.start()

    def start_weights():
        for copy in loads[1:]:
            copy.wait()
        cube.start()

    def multiply(src):
        at = rows_at(src, rows)
        for i, to in enumerate((q_raw, k_raw)):
            to[at, :] = mm(x[at, :], w[:, i * lw : (i + 1) * lw])
        v_low[at, :] = mm(x[at, :], w[:, 2 * lw :]).astype(BF16)

    part = rows // AG_CHUNKS

    def copy(src, c, up):
        at = pl.ds(pl.multiple_of(src * rows + c * part, part), part)
        return remote(x.at[at], x.at[at], ags.at[up, src, c], agr.at[src, c], "head", z + 1 if up else z - 1)

    more = (z > 0, z < n - 1)
    for c in range(AG_CHUNKS):
        for up in (0, 1):

            @pl.when(more[up])
            def _():
                copy(z, c, up).start()

    start_weights()
    own[:, :lw] = jnp.transpose(wo[...].astype(F32)).astype(BF16)
    own[:, lw:] = gate[:, : own.shape[1] - lw]
    own_more.start()
    token = s * x.shape[0] + lax.broadcasted_iota(jnp.int32, cos.shape, 0)
    angle = (token - first_of_document(docs, token)).astype(F32) * turns[...]
    flip = jnp.where(lax.broadcasted_iota(jnp.int32, cos.shape, 1) < HEAD_DIM // 2, -1.0, 1.0)
    cos[...] = jnp.cos(angle)
    sin[...] = jnp.sin(angle) * flip

    def sides(k):
        return ((z + k, z + k < n, 0), (z - k, z - k >= 0, 1))

    for k in range(1, n):
        for c in range(AG_CHUNKS):
            for src, there, up in sides(k):

                @pl.when(there)
                def _():
                    copy(src, c, up).wait_recv()

                    @pl.when(more[up])
                    def _():
                        copy(src, c, up).start()

        if k <= 2:
            weights(k - 1)
        if k == min(2, n - 1):
            multiply(z)
            for src, there, _ in sides(1):
                pl.when(there)(functools.partial(multiply, src))
        if k > 1:
            for src, there, _ in sides(k):
                pl.when(there)(functools.partial(multiply, src))

    outs = [
        pltpu.make_async_copy(a, b, lsem.at[4 + i])
        for i, (a, b) in enumerate(((x, x_out), (w, w_out), (q_raw, q_out), (k_raw, k_out)))
    ]
    for out in outs:
        out.start()
    totals[...] = row_sums(q_raw[...] * q_raw[...], k_raw[...] * k_raw[...])
    land[z] = totals[...]
    small = SmallExchange("head", z, n, land, ss, sr)
    small.start()
    small.receive()
    total = land[0]
    for k in range(1, n):
        total = total + land[k]
    totals[...] = total
    for row, raw, gain, to in ((0, q_raw, gq, q_rot), (4, k_raw, gk, k_rot)):
        scale = lax.rsqrt(as_column(total, row) / depth_full + epsilon)
        for h in range(heads):
            cols = slice(h * HEAD_DIM, (h + 1) * HEAD_DIM)
            to[:, cols] = turn(raw[:, cols] * scale * gain[:, head_gain(h)], cos[...], sin[...]).astype(BF16)
        if row == 0:
            cube_e.level(0)

    def late():
        for i in range(1, levels):
            cube_e.level(i)

    def finish():
        small.finish()
        cube.finish()
        cube_e.finish()
        for out in [*outs, own_more]:
            out.wait()

        @pl.loop(0, n)
        def _(src):
            for c in range(AG_CHUNKS):

                @pl.when((src >= z) & (z > 0))
                def _():
                    copy(src, c, 0).wait_send()

                @pl.when((src <= z) & (z < n - 1))
                def _():
                    copy(src, c, 1).wait_send()

    return late, finish


def front_kernel(n, ns, heads, depth_full, *refs):
    ins, refs = refs[:10], refs[10:]
    made, refs = refs[:8], refs[8:]
    attended, refs = refs[:7], refs[7:]
    first, second = refs[:18], refs[18:]
    late, finish = project_part(n, ns, depth_full, *ins, *made, *first)
    attend_part(ns, heads, *first[:3], ins[8], ins[5], *attended, *second, late=late)
    finish()


def run_front(n, ns, heads, tok, wq, wk, wv, wo, gate, gq, gk, docs, turns):
    rows, depth = tok.shape
    tl = rows * n
    block, lw = wq.shape
    r = ns // heads
    nq = ns // r * tl
    nk = ns * tl
    ff = gate.shape[1]
    early = early_part(ff)
    dma = pltpu.SemaphoreType.DMA
    shape = jax.ShapeDtypeStruct
    return pl.pallas_call(
        functools.partial(front_kernel, n, ns, heads, depth),
        out_shape=(
            shape((tl, depth), BF16),
            shape((depth, 3 * lw), BF16),
            shape((depth, lw + early), BF16),
            shape((tl, lw), F32),
            shape((tl, lw), F32),
            shape((8, tl), F32),
            shape((tl, HEAD_DIM), F32),
            shape((tl, HEAD_DIM), F32),
            shape((tl, lw), BF16),
            shape((nq, HEAD_DIM), BF16),
            shape((nk, HEAD_DIM), BF16),
            shape((nk, HEAD_DIM), BF16),
            shape((nq, HEAD_DIM), F32),
            shape((ns // r, tl), F32),
            shape((depth, ff - early), BF16),
        ),
        in_specs=[ANY] * 4 + [VMEM] * 4 + [SMEM, VMEM],
        out_specs=(ANY,) * 5 + (VMEM,) * 4 + (ANY,) * 3 + (VMEM,) * 2 + (ANY,),
        scratch_shapes=[
            pltpu.VMEM((tl, lw), BF16),
            pltpu.VMEM((tl, lw), BF16),
            pltpu.VMEM((tl, lw), BF16),
            pltpu.VMEM((tl, lw), F32),
            pltpu.VMEM((tl, lw), F32),
            pltpu.VMEM((tl, depth), BF16),
            pltpu.VMEM((depth, 3 * lw), BF16),
            pltpu.VMEM((block, lw + early), BF16),
            pltpu.VMEM((n, 8, tl), F32),
            dma((9,)),
            dma((2, n, AG_CHUNKS)), dma((n, AG_CHUNKS)),
            *CubeGather.sems(ns), *CubeGather.sems(ns),
            dma((n,)), dma((n,)),
            pltpu.VMEM((nq, HEAD_DIM), BF16),
            pltpu.VMEM((nk, HEAD_DIM), BF16),
            pltpu.VMEM((nk, HEAD_DIM), BF16),
            pltpu.VMEM((nq, HEAD_DIM), BF16),
            dma((heads,)), dma((ns // r,)),
            dma((2, ns)), dma((ns,)),
            dma((2, ns)), dma((ns,)),
            dma((ns // r,)), dma((heads,)),
            dma((4,)),
            *CubeGather.sems(ns),
        ],
        compiler_params=pltpu.CompilerParams(
            collective_id=5, has_side_effects=True, vmem_limit_bytes=VMEM_BYTES
        ),
        cost_estimate=pl.CostEstimate(flops=6 * 10**9, bytes_accessed=30 * 10**6, transcendentals=5 * 10**6),
        name="front",
    )(tok, wq, wk, wv, wo, gate, gq, gk, docs, turns)


def input_kernel(
    n, ns, depth_full,
    dq, dk, dv, q_raw, k_raw, totals, gq, gk, cos, sin, x_in, w_in, att, dy1_in, attn_part, mlp_part, dy2_in, hidden_in,
    total, grad_q, grad_k, grad_v, grad_o, grad_down, gains,
    x, w, dy1, dy2, hidden, lsem, dqkv, q_back, k_back, inner, land, message, message_z, gain_land,
    first, held, later, c0s, c0r, c1s, c1r,
    first_o, held_o, later_o, o0s, o0r, o1s, o1r,
    ss, sr, ms, mr, zs, zr, s1s, s1r,
):
    s, z = lax.axis_index("seq"), lax.axis_index("head")
    rows, depth = total.shape
    tl, lw = dq.shape
    block = depth // ns
    heads = lw // HEAD_DIM

    def head_gain(h):
        return head_cols(z * heads + h)

    sums = totals[...]
    scales = [lax.rsqrt(as_column(sums, row) / depth_full + epsilon) for row in (0, 4)]
    todo = ((dq, q_raw, gq, q_back), (dk, k_raw, gk, k_back))
    products = []

    l_d = pltpu.make_async_copy(dy2_in, dy2, lsem.at[0])
    l_h = pltpu.make_async_copy(hidden_in.at[:, pl.ds(hidden_in.shape[1] - lw, lw)], hidden, lsem.at[1])
    l_y = pltpu.make_async_copy(dy1_in, dy1, lsem.at[2])
    l_w = pltpu.make_async_copy(w_in, w, lsem.at[3])
    l_x = pltpu.make_async_copy(x_in, x, lsem.at[4])
    for load in (l_d, l_h, l_y, l_w, l_x):
        load.start()

    def turn_all():
        message[...] = jnp.zeros_like(message)
        for i, (grad, raw, gain, back) in enumerate(todo):
            product = jnp.zeros((tl, HEAD_DIM), F32)
            for h in range(heads):
                cols = slice(h * HEAD_DIM, (h + 1) * HEAD_DIM)
                hat = raw[:, cols] * scales[i]
                turned = turn_back(grad[:, cols].astype(F32), cos[...], sin[...])
                message[0, pl.ds(i, 1), cols] = jnp.sum(turned * hat, axis=0, keepdims=True)
                turned = turned * gain[:, head_gain(h)]
                back[:, cols] = turned
                product = product + turned * hat
            products.append(product)
        inner[z] = row_sums(*products)
        for t in range(1, ns):
            message[t, pl.ds(0, 2), pl.ds(0, lw)] = message[0, pl.ds(0, 2), pl.ds(0, lw)]
        for t in range(ns):
            for i, part in enumerate((attn_part, mlp_part)):
                message[t, pl.ds(i, 1), pl.ds(lw, block)] = part[:, t * block : (t + 1) * block]

    cross_barrier(s, z, ns, n, turn_all)
    small = SmallExchange("head", z, n, inner, ss, sr)
    small.start()

    def message_copy(t, frm):
        return remote(message.at[t], message_z.at[frm], ms.at[t], mr.at[frm], "seq", t)

    def each_seq(act):
        @pl.loop(0, ns)
        def _(t):
            @pl.when(t != s)
            def _():
                act(t)

    message_z[s] = message[s]
    each_seq(lambda t: message_copy(t, s).start())
    dqkv[:, 2 * lw :] = dv[...]
    for load in (l_d, l_h, l_y):
        load.wait()

    def early_block(b):
        cols = rows_at(b, block)
        return jnp.concatenate([mm(dy1[:, cols], att[...], TN), mm(dy2[:, cols], hidden[...], TN)], axis=1)

    cube_o = CubeScatter(
        s, ns, early_block, block, first_o, held_o, later_o, (o0s, o0r, o1s, o1r)
    )
    cube_o.send_core()
    cube_o.add_core()
    small.receive()
    sums = inner[0]
    for k in range(1, n):
        sums = sums + inner[k]
    for i, (grad, raw, gain, back) in enumerate(todo):
        mean = as_column(sums, 4 * i) / depth_full
        for h in range(heads):
            cols = slice(h * HEAD_DIM, (h + 1) * HEAD_DIM)
            to = slice(i * lw + h * HEAD_DIM, i * lw + (h + 1) * HEAD_DIM)
            dqkv[:, to] = (scales[i] * (back[:, cols] - raw[:, cols] * scales[i] * mean)).astype(BF16)

    width = depth // STEPS

    def weight_block(b):
        cols = rows_at(b, block)
        return mm(x[:, cols], dqkv[...], TN)

    def in_part(d, c):
        return mm(dqkv[rows_at(d, rows), :], w[rows_at(c, width), :], NT)

    cube = CubeScatter(s, ns, weight_block, block, first, held, later, (c0s, c0r, c1s, c1r))
    line = LineScatter(z, n, in_part, land, s1s, s1r, total)
    half = ns // 2

    def task(slot):
        for i, act in enumerate((cube.send_core, cube.add_core)):
            low = 1 + i * (half // 2)

            @pl.when((slot >= low) & (slot < low + half // 2))
            def _():
                for j in range(2):
                    act(2 * (slot - low) + j)

    done = 1 + half
    l_w.wait()
    l_x.wait()
    line.run(0, done, None, task)
    line.start_own()
    line.run(done, done + 3)
    for i in range(cube.stages - 1):
        cube_o.step(i)
    line.run(done + 3, line.slots)
    for i in range(cube.stages - 1):
        cube.step(i)

    each_seq(lambda t: message_copy(t, t).wait_recv())
    received = message_z[0]
    for t in range(1, ns):
        received = received + message_z[t]
    each_seq(lambda t: message_copy(t, s).wait_send())
    gain_land[z] = received
    rounds = SmallExchange("head", z, n, gain_land, zs, zr)
    rounds.start()
    line.own()
    cube_o.step(cube.stages - 1)
    grad_o[...] = jnp.transpose(held_o[0, :, :lw].astype(F32)).astype(BF16)
    grad_down[...] = jnp.transpose(held_o[0, :, lw:].astype(F32)).astype(BF16)
    cube.step(cube.stages - 1)
    for i, to in enumerate((grad_q, grad_k, grad_v)):
        to[...] = held[0, :, i * lw : (i + 1) * lw]
    rounds.receive()
    at = s * block
    gains[...] = jnp.zeros_like(gains)
    gains[0:2, :] = gain_land[at // lw, pl.ds(0, 2), pl.ds(pl.multiple_of(at % lw, block), block)]
    both = gain_land[0, pl.ds(0, 2), pl.ds(lw, block)]
    for k in range(1, n):
        both = both + gain_land[k, pl.ds(0, 2), pl.ds(lw, block)]
    gains[2:4, :] = both
    for one in (cube, cube_o):
        one.core_sent()
        one.finish()
    line.finish()
    small.finish()
    rounds.finish()


def run_input(n, ns, dq, dk, dv, q_raw, k_raw, totals, gq, gk, cos, sin, x, w, att, dy1, attn_part, mlp_part, dy2, hidden):
    tl, lw = dq.shape
    rows, depth = tl // n, x.shape[1]
    block = depth // ns
    dma = pltpu.SemaphoreType.DMA
    shape = jax.ShapeDtypeStruct
    return pl.pallas_call(
        functools.partial(input_kernel, n, ns, depth),
        out_shape=(shape((rows, depth), F32),)
        + (shape((block, lw), BF16),) * 3
        + (shape((lw, block), BF16), shape((lw, block), BF16), shape((8, block), F32)),
        in_specs=[VMEM] * 10 + [ANY] * 2 + [VMEM, ANY, VMEM, VMEM] + [ANY] * 2,
        out_specs=(VMEM,) * 7,
        scratch_shapes=[
            pltpu.VMEM(x.shape, BF16),
            pltpu.VMEM(w.shape, BF16),
            pltpu.VMEM((tl, depth), BF16),
            pltpu.VMEM((tl, depth), BF16),
            pltpu.VMEM((tl, lw), BF16),
            dma((5,)),
            pltpu.VMEM((tl, 3 * lw), BF16),
            pltpu.VMEM((tl, lw), F32),
            pltpu.VMEM((tl, lw), F32),
            pltpu.VMEM((n, 8, tl), F32),
            pltpu.VMEM((2, n, STEPS, rows, depth // STEPS), BF16),
            pltpu.VMEM((ns, 8, lw + block), F32),
            pltpu.VMEM((ns, 8, lw + block), F32),
            pltpu.VMEM((n, 8, lw + block), F32),
            *CubeScatter.scratch(ns, block, 3 * lw),
            *CubeScatter.scratch(ns, block, 2 * lw),
            dma((n,)), dma((n,)),
            dma((ns,)), dma((ns,)),
            dma((n,)), dma((n,)),
            *line_sems(n)["scatter"],
        ],
        compiler_params=pltpu.CompilerParams(
            collective_id=6, has_side_effects=True, vmem_limit_bytes=VMEM_BYTES
        ),
        cost_estimate=pl.CostEstimate(flops=8 * 10**9, bytes_accessed=30 * 10**6, transcendentals=0),
        name="into_input",
    )(dq, dk, dv, q_raw, k_raw, totals, gq, gk, cos, sin, x, w, att, dy1, attn_part, mlp_part, dy2, hidden)


def widen_kernel(count, *refs):
    spec = WIDEN
    ins, rest = refs[:count], refs[count:]
    outs, rest = rest[: len(spec)], rest[len(spec) :]
    held, rest = rest[:count], rest[count:]
    wide, (load_sem, store_sem) = rest[: len(spec)], rest[len(spec) :]
    loads = [pltpu.make_async_copy(a, b, load_sem.at[i]) for i, (a, b) in enumerate(zip(ins, held))]
    stores = [pltpu.make_async_copy(a, b, store_sem.at[i]) for i, (a, b) in enumerate(zip(wide, outs))]
    for copy in loads:
        copy.start()
    at = 0
    for (parts, stacked), to, store in zip(spec, wide, stores):
        row = 0
        for i in range(at, at + parts):
            loads[i].wait()
            block = held[i][...].astype(to.dtype)
            if stacked:
                to[row : row + block.shape[0], :] = block
                row += block.shape[0]
            elif i == at:
                to[...] = block
            else:
                to[...] += block
        at += parts
        store.start()
    for copy in stores:
        copy.wait()


WIDEN = ((1, False), (1, False), (1, False), (2, True), (1, False), (1, False), (1, False), (1, False), (2, False))


def run_widen(arrays, outs):
    dma = pltpu.SemaphoreType.DMA
    return pl.pallas_call(
        functools.partial(widen_kernel, len(arrays)),
        out_shape=tuple(outs),
        in_specs=[ANY] * len(arrays),
        out_specs=(ANY,) * len(outs),
        scratch_shapes=[pltpu.VMEM(a.shape, a.dtype) for a in arrays]
        + [pltpu.VMEM(o.shape, o.dtype) for o in outs]
        + [dma((len(arrays),)), dma((len(outs),))],
        compiler_params=pltpu.CompilerParams(vmem_limit_bytes=VMEM_BYTES),
        name="widen",
    )(*arrays)


def on_device(
    tokens,
    cotangent,
    doc_lengths,
    q_weight,
    k_weight,
    v_weight,
    o_weight,
    gate_weight,
    up_weight,
    down_weight,
    q_gain,
    k_gain,
    attn_gain,
    mlp_gain,
):
    ns, nz = lax.axis_size("seq"), lax.axis_size("head")
    lw = q_weight.shape[1]
    heads = lw // HEAD_DIM
    block, ff = gate_weight.shape
    gq, gk = q_gain[None], k_gain[None]
    frequency = jnp.power(rope_base, -(jnp.arange(HEAD_DIM) % (HEAD_DIM // 2)).astype(F32) * (2.0 / HEAD_DIM))

    x, w, more, q_raw, k_raw, totals, cos, sin, attended, q_held, k_held, v_held, o_held, lse, gate_b = run_front(
        nz, ns, heads, tokens, q_weight, k_weight, v_weight, o_weight, gate_weight, gq, gk, doc_lengths, frequency[None]
    )
    output, h1r, branch, hidden, dy2, dg, du, mlp_part, up = run_forward(
        nz, ns, attended, tokens, cotangent, more, gate_b, up_weight, down_weight, attn_gain[None], mlp_gain[None]
    )
    middle, dy1, datt, attn_part, grad_gate, grad_up = run_backward(
        nz, ns, dg, du, h1r, cotangent, branch, more, gate_b, up, attn_gain[None]
    )
    dq, dk, dv, down_a = run_attend_back(
        ns, heads, datt, doc_lengths, q_held, k_held, v_held, o_held, lse, dy2, hidden
    )
    last, grad_q, grad_k, grad_v, grad_o, down_b, gains = run_input(
        nz, ns, dq, dk, dv, q_raw, k_raw, totals, gq, gk, cos, sin, x, w, attended, dy1, attn_part, mlp_part, dy2, hidden
    )
    shape = jax.ShapeDtypeStruct
    small = shape((block, lw), F32)
    output, grad_gate, grad_up, grad_down, grad_q, grad_k, grad_v, grad_o, input_grad = run_widen(
        (output, grad_gate, grad_up, down_a, down_b, grad_q, grad_k, grad_v, grad_o, middle, last),
        (
            shape(output.shape, BF16),
            shape((block, ff), F32),
            shape((block, ff), F32),
            shape((ff, block), F32),
            small, small, small,
            shape((lw, block), F32),
            shape(middle.shape, F32),
        ),
    )
    return (
        output,
        input_grad,
        grad_q,
        grad_k,
        grad_v,
        grad_o,
        grad_gate,
        grad_up,
        grad_down,
        gains[0],
        gains[1],
        gains[2],
        gains[3],
    )


def solution(mesh):
    in_specs = (
        P(("seq", "head"), None),
        P(("seq", "head"), None),
        P(),
        P("seq", "head"),
        P("seq", "head"),
        P("seq", "head"),
        P("head", "seq"),
        P("seq", "head"),
        P("seq", "head"),
        P("head", "seq"),
        P(),
        P(),
        P(),
        P(),
    )
    out_specs = (
        P(("seq", "head"), None),
        P(("seq", "head"), None),
        P("seq", "head"),
        P("seq", "head"),
        P("seq", "head"),
        P("head", "seq"),
        P("seq", "head"),
        P("seq", "head"),
        P("head", "seq"),
        P("seq"),
        P("seq"),
        P("seq"),
        P("seq"),
    )
    return jax.shard_map(
        on_device, mesh=mesh, in_specs=in_specs, out_specs=out_specs, check_vma=False
    )
```

```python
import functools

import jax
import jax.numpy as jnp
from jax import lax
from jax.experimental import pallas as pl
from jax.experimental.pallas import tpu as pltpu
from jax.sharding import PartitionSpec as P

HEAD_DIM = 128
epsilon = 1e-06
rope_base = 500000.0

MESH = pl.DeviceIdType.MESH
F32 = jnp.float32
BF16 = jnp.bfloat16
STEPS = 4
LAG = 1
EARLY = (7, 16)
AG_CHUNKS = 2
VMEM_BYTES = 62 * 1024 * 1024
ANY = pl.BlockSpec(memory_space=pl.ANY)
VMEM = pl.BlockSpec(memory_space=pltpu.VMEM)
SMEM = pl.BlockSpec(memory_space=pltpu.SMEM)
NN = (((1,), (0,)), ((), ()))
NT = (((1,), (1,)), ((), ()))
TN = (((0,), (0,)), ((), ()))


def first_of_document(docs, token):
    end, first = jnp.int32(0), jnp.zeros_like(token)
    for i in range(docs.shape[0]):
        end = end + docs[i]
        first = first + jnp.where(token >= end, docs[i], 0)
    return first


def mm(left, right, dims=NN):
    return lax.dot_general(left, right, dims, preferred_element_type=F32)


def early_part(ff):
    return ff * EARLY[0] // EARLY[1] // HEAD_DIM * HEAD_DIM


def last_part(ff):
    return ff // STEPS


def rows_at(index, count):
    return pl.ds(pl.multiple_of(index * count, count), count)


def cube_barrier(s, z, ns, n, between=None):
    bar = pltpu.get_barrier_semaphore()
    bits = [1 << i for i in range(ns.bit_length() - 1)]
    for bit in bits:
        pl.semaphore_signal(bar, inc=1, device_id={"seq": s ^ bit}, device_id_type=MESH)
    for other, there in ((z - 1, z > 0), (z + 1, z < n - 1)):

        @pl.when(there)
        def _():
            pl.semaphore_signal(bar, inc=1, device_id={"head": other}, device_id_type=MESH)

    if between is not None:
        between()
    pl.semaphore_wait(bar, len(bits) + (z > 0).astype(jnp.int32) + (z < n - 1).astype(jnp.int32))


def line_gather(z, n, buf, rows, send_sem, recv_sem, use, hooks=(), ready=None):
    part = rows // AG_CHUNKS

    def copy(src, c, up):
        at = pl.ds(pl.multiple_of(src * rows + c * part, part), part)
        return pltpu.make_async_remote_copy(
            src_ref=buf.at[at],
            dst_ref=buf.at[at],
            send_sem=send_sem.at[up, src, c],
            recv_sem=recv_sem.at[src, c],
            device_id={"head": z + 1 if up else z - 1},
            device_id_type=MESH,
        )

    more = (z > 0, z < n - 1)
    for c in range(AG_CHUNKS):
        for up in (0, 1):

            @pl.when(more[up])
            def _():
                copy(z, c, up).start()

    if ready is not None:
        ready()
    use(z)

    @pl.loop(1, n)
    def _(k):
        sides = ((z + k, z + k < n, 0), (z - k, z - k >= 0, 1))
        for c in range(AG_CHUNKS):
            for src, there, up in sides:

                @pl.when(there)
                def _():
                    copy(src, c, up).wait_recv()

                    @pl.when(more[up])
                    def _():
                        copy(src, c, up).start()

        for src, there, up in sides:

            @pl.when(there)
            def _():
                use(src)

        for i, hook in enumerate(hooks):
            pl.when(k == i + 1)(hook)

    @pl.loop(0, n)
    def _(src):
        for c in range(AG_CHUNKS):

            @pl.when((src >= z) & (z > 0))
            def _():
                copy(src, c, 0).wait_send()

            @pl.when((src <= z) & (z < n - 1))
            def _():
                copy(src, c, 1).wait_send()


class LineScatter:
    def __init__(self, z, n, partial, land, send_sem, recv_sem, total):
        self.z, self.n, self.partial, self.land, self.total = z, n, partial, land, total
        self.send_sem, self.recv_sem = send_sem, recv_sem

    def copy(self, d, c, up):
        return pltpu.make_async_remote_copy(
            src_ref=self.land.at[up, d, c],
            dst_ref=self.land.at[up, d, c],
            send_sem=self.send_sem.at[up, d, c],
            recv_sem=self.recv_sem.at[up, d, c],
            device_id={"head": self.z + 1 if up else self.z - 1},
            device_id_type=MESH,
        )

    @property
    def slots(self):
        return (self.n - 1) * (STEPS + LAG)

    def run(self, low, high, before=None, after=None):
        z, n, land = self.z, self.n, self.land

        @pl.loop(low, high)
        def _(slot):
            if before is not None:
                before(slot)
            for up in (1, 0):
                t = slot - (z if up else n - 1 - z) * LAG
                j = t // STEPS
                c = t - j * STEPS
                d = n - 1 - j if up else j
                first = z == 0 if up else z == n - 1
                there = (t >= 0) & (j < n - 1) & ((d > z) if up else (d < z))

                @pl.when(there)
                def _():
                    mine = self.partial(d, c)

                    @pl.when(first)
                    def _():
                        land[up, d, c] = mine.astype(land.dtype)

                    @pl.when(jnp.logical_not(first))
                    def _():
                        self.copy(d, c, up).wait_recv()
                        land[up, d, c] = (land[up, d, c].astype(F32) + mine).astype(land.dtype)

                    self.copy(d, c, up).start()

            if after is not None:
                after(slot)

    def start_own(self):
        width = self.total.shape[1] // STEPS

        @pl.loop(0, STEPS)
        def _(c):
            self.total[:, rows_at(c, width)] = self.partial(self.z, c)

    def own(self):
        z, n, total = self.z, self.n, self.total
        width = total.shape[1] // STEPS

        @pl.loop(0, STEPS)
        def _(c):
            at = rows_at(c, width)
            for there, up in ((z > 0, 1), (z < n - 1, 0)):

                @pl.when(there)
                def _():
                    self.copy(z, c, up).wait_recv()
                    total[:, at] += self.land[up, z, c].astype(F32)

    def finish(self):
        @pl.loop(0, self.n * STEPS)
        def _(t):
            d, c = t // STEPS, t % STEPS
            for there, up in ((d > self.z, 1), (d < self.z, 0)):

                @pl.when(there)
                def _():
                    self.copy(d, c, up).wait_send()


def line_sems(n):
    dma = pltpu.SemaphoreType.DMA
    return {
        "gather": [dma((2, n, AG_CHUNKS)), dma((n, AG_CHUNKS))],
        "scatter": [dma((2, n, STEPS)), dma((2, n, STEPS))],
    }


BLOCK = 64


def row_scale(block):
    return lax.rsqrt(jnp.mean(block * block, axis=-1, keepdims=True) + epsilon)


def norm_back(e, normed, scale, gain):
    g = e * gain
    return scale * (g - normed * jnp.mean(g * normed, axis=-1, keepdims=True))


def sigmoid(x):
    return 1.0 / (1.0 + jnp.exp(-x))


def subsets(bits):
    found = [0]
    for bit in bits:
        found += [bit | other for other in found]
    return found


def orders_of(ns):
    chips = [1 << i for i in range(1, ns.bit_length() - 1)]
    return (chips, chips[::-1])


def remote(src, dst, send, recv, axis, to):
    return pltpu.make_async_remote_copy(
        src_ref=src, dst_ref=dst, send_sem=send, recv_sem=recv, device_id={axis: to}, device_id_type=MESH
    )


class CubeGather:
    def __init__(self, s, ns, buf, rows, send_sem, recv_sem, own=None):
        self.own = own
        self.s, self.buf, self.rows, self.send_sem, self.recv_sem = s, buf, rows, send_sem, recv_sem
        self.orders = [order + [1] for order in orders_of(ns)]

    def copy(self, half, bit, block):
        part = self.rows // 2
        at = pl.ds(pl.multiple_of(block * self.rows + half * part, part), part)
        source = self.buf.at[at]
        if block is self.s and self.own is not None:
            source = self.own.at[pl.ds(half * part, part)]
        return remote(
            source, self.buf.at[at],
            self.send_sem.at[bit.bit_length() - 1, block, half], self.recv_sem.at[block, half],
            "seq", self.s ^ bit,
        )

    @property
    def levels(self):
        return len(self.orders[0])

    def start(self):
        for i in range(self.levels):
            for half, order in enumerate(self.orders):
                self.copy(half, order[i], self.s).start()

    def level(self, i):
        for j in range(2**i):
            for half, order in enumerate(self.orders):
                block = self.s ^ order[i] ^ subsets(order[:i])[j]
                self.copy(half, order[i], block).wait_recv()
                for bit in order[i + 1 :]:
                    self.copy(half, bit, block).start()

    def finish(self):
        for half, order in enumerate(self.orders):
            for i, bit in enumerate(order):
                for other in subsets(order[:i]):
                    self.copy(half, bit, self.s ^ other if other else self.s).wait_send()

    @staticmethod
    def sems(ns):
        dma = pltpu.SemaphoreType.DMA
        return [dma((ns.bit_length() - 1, ns, 2)), dma((ns, 2))]


class CubeScatter:
    def __init__(self, s, ns, block, rows, first, held, later, sems):
        self.s, self.block, self.rows = s, block, rows
        self.first, self.held, self.later = first, held, later
        self.send0, self.recv0, self.send1, self.recv1 = sems
        self.orders = orders_of(ns)
        self.half = ns // 2

    def core_copy(self, j):
        return remote(self.first.at[j], self.held.at[j], self.send0.at[j], self.recv0.at[j], "seq", self.s ^ 1)

    def send_core(self, j=None):
        if j is None:
            pl.loop(0, self.half)(self.send_core)
            return
        j = self.half - 1 - j
        self.first[j] = self.block(self.s ^ (2 * j + 1)).astype(BF16)
        self.core_copy(j).start()

    def base(self, i):
        return sum(2 ** (self.stages - 1 - k) for k in range(i))

    def move(self, i, half, slot, other):
        part = self.rows // 2
        return remote(
            self.held.at[(self.orders[half][i] | other) >> 1, pl.ds(half * part, part)],
            self.later.at[half, slot], self.send1.at[half, slot], self.recv1.at[half, slot],
            "seq", self.s ^ self.orders[half][i],
        )

    def moves(self, i):
        part = self.rows // 2
        for half, order in enumerate(self.orders):
            for j, other in enumerate(subsets(order[i + 1 :])):
                slot = self.base(i) + j
                yield other >> 1, pl.ds(half * part, part), half, slot, self.move(i, half, slot, other)

    def add_core(self, j=None):
        if j is None:
            pl.loop(0, self.half)(self.add_core)
            return
        j = self.half - 1 - j
        mine = self.block(self.s ^ (2 * j))
        self.core_copy(j).wait_recv()
        self.held[j] = (self.held[j].astype(F32) + mine).astype(BF16)
        for half, order in enumerate(self.orders):
            for slot, other in enumerate(subsets(order[1:])):

                @pl.when(j == (order[0] | other) >> 1)
                def _():
                    self.move(0, half, slot, other).start()

    def send(self, i):
        for *_, copy in self.moves(i):
            copy.start()

    def take(self, i):
        for j, at, half, slot, copy in self.moves(i):
            copy.wait_recv()
            self.held[j, at] = (self.held[j, at].astype(F32) + self.later[half, slot].astype(F32)).astype(BF16)

    def step(self, i):
        self.take(i)
        if i + 1 < self.stages:
            self.send(i + 1)

    @property
    def stages(self):
        return len(self.orders[0])

    def core_sent(self):
        @pl.loop(0, self.half)
        def _(j):
            self.core_copy(j).wait_send()

    def finish(self):
        for i in range(self.stages):
            for *_, copy in self.moves(i):
                copy.wait_send()

    @staticmethod
    def scratch(ns, rows, width):
        dma = pltpu.SemaphoreType.DMA
        half = ns // 2
        return [
            pltpu.VMEM((half, rows, width), BF16),
            pltpu.VMEM((half, rows, width), BF16),
            pltpu.VMEM((2, half - 1, rows // 2, width), BF16),
            dma((half,)), dma((half,)), dma((2, half - 1)), dma((2, half - 1)),
        ]


def forward_kernel(
    n, ns,
    att, tok, cot, more, gate_b, gate_own, up, down, attn_gain, mlp_gain,
    out, h1r_out, branch_out, hidden_out, dy2_out, dg_out, du_out, gain_part, up_out,
    h1r, hidden, dy2, dg, du,
    wo, wd, wg, wu, land, branch, h1, second, g_pre, u_pre,
    wsem, osem, bsem, g1s, g1r, s1s, s1r, g2s, g2r, s2s, s2r, us, ur, ds, dr,
):
    s, z = lax.axis_index("seq"), lax.axis_index("head")
    rows, depth = tok.shape
    lw, ff = att.shape[1], up.shape[1]
    block = depth // ns
    width = depth // STEPS
    mine = rows_at(s, block)
    l_o = pltpu.make_async_copy(more.at[:, pl.ds(0, lw)], wo, wsem.at[0])
    last = last_part(ff)
    l_u = pltpu.make_async_copy(up, wu.at[mine, pl.ds(last, ff)], wsem.at[1])
    l_c = pltpu.make_async_copy(gate_own.at[:, pl.ds(ff - last, last)], wu.at[mine, pl.ds(0, last)], wsem.at[4])
    early = more.shape[1] - lw
    l_g = pltpu.make_async_copy(more.at[:, pl.ds(lw, early)], wg.at[:, pl.ds(0, early)], wsem.at[2])
    l_h = pltpu.make_async_copy(gate_b, wg.at[:, pl.ds(early, ff - early - last)], wsem.at[3])
    for copy in (l_o, l_u, l_c, l_g, l_h):
        copy.start()
    cube_barrier(s, z, ns, n)
    cube_u = CubeGather(s, ns, wu, block, us, ur)
    cube_d = CubeGather(s, ns, wd, block, ds, dr)
    levels = cube_u.levels
    l_u.wait()
    l_c.wait()
    cube_u.start()
    l_o.wait()

    def out_part(d, c):
        return mm(att[rows_at(d, rows), :], wo[rows_at(c, width), :], NT)

    line = LineScatter(z, n, out_part, land, s1s, s1r, branch)
    line.run(0, STEPS)
    line.start_own()
    wd[mine, :] = jnp.transpose(down[...].astype(F32)).astype(BF16)
    line.run(STEPS, 2 * STEPS)
    cube_u.level(0)
    line.run(2 * STEPS, 3 * STEPS)
    for i in range(1, levels - 1):
        cube_u.level(i)
    cube_d.start()
    line.run(3 * STEPS, line.slots)
    line.own()
    line.finish()
    o_branch = pltpu.make_async_copy(branch, branch_out, osem.at[0])
    o_branch.start()
    gain_part[...] = jnp.zeros_like(gain_part)

    @pl.loop(0, rows // BLOCK)
    def _(i):
        at = rows_at(i, BLOCK)
        y = branch[at, :]
        h = tok[at, :].astype(F32) + y * row_scale(y) * attn_gain[...]
        h1[at, :] = h
        h1r[pl.ds(pl.multiple_of(z * rows + i * BLOCK, BLOCK), BLOCK), :] = h.astype(BF16)

    fw = ff // STEPS
    o_up = pltpu.make_async_copy(wu, up_out, osem.at[1])
    o_h1r = pltpu.make_async_copy(h1r, h1r_out, osem.at[2])
    o_hidden = pltpu.make_async_copy(hidden, hidden_out, osem.at[3])
    o_dy2 = pltpu.make_async_copy(dy2, dy2_out, osem.at[4])

    def up_block(src):
        at = rows_at(src, rows)

        def columns(c, gate):
            cols = rows_at(c, fw)
            x = h1r[at, :]
            g = mm(x, gate)
            u = mm(x, wu[:, pl.ds(pl.multiple_of(last + c * fw, HEAD_DIM), fw)])
            g_pre[at, cols] = g
            u_pre[at, cols] = u
            hidden[at, cols] = (g * sigmoid(g) * u).astype(BF16)

        pl.loop(0, STEPS - 1)(lambda c: columns(c, wg[:, rows_at(c, fw)]))
        columns(STEPS - 1, wu[:, :last])

    def weights_there():
        l_g.wait()
        l_h.wait()
        cube_u.level(levels - 1)
        o_up.start()

    hooks = [functools.partial(cube_d.level, i) for i in range(levels)]
    line_gather(z, n, h1r, rows, g1s, g1r, up_block, hooks[: n - 1], weights_there)
    for hook in hooks[n - 1 :]:
        hook()
    o_h1r.start()
    o_hidden.start()

    def down_part(d, c):
        return mm(hidden[rows_at(d, rows), :], wd[rows_at(c, width), :], NT)

    line = LineScatter(z, n, down_part, land, s2s, s2r, second)
    line.run(0, STEPS)
    line.start_own()
    line.run(STEPS, line.slots)
    line.own()
    line.finish()

    @pl.loop(0, rows // BLOCK)
    def _(i):
        at = rows_at(i, BLOCK)
        y = second[at, :]
        scale = row_scale(y)
        normed = y * scale
        e = cot[at, :].astype(F32)
        out[at, :] = (h1[at, :] + normed * mlp_gain[...]).astype(BF16)
        gain_part[...] += jnp.sum(e * normed, axis=0, keepdims=True)
        dy2[pl.ds(pl.multiple_of(z * rows + i * BLOCK, BLOCK), BLOCK), :] = norm_back(
            e, normed, scale, mlp_gain[...]
        ).astype(BF16)

    def back_block(src):
        at = rows_at(src, rows)

        @pl.loop(0, STEPS)
        def _(c):
            cols = rows_at(c, fw)
            dh = mm(dy2[at, :], wd[:, cols])
            g = g_pre[at, cols]
            u = u_pre[at, cols]
            sig = sigmoid(g)
            du[at, cols] = (dh * g * sig).astype(BF16)
            dg[at, cols] = (dh * u * sig * (1.0 + g * (1.0 - sig))).astype(BF16)

        for copy in grads_out(src):
            copy.start()

    def grads_out(src):
        at = rows_at(src, rows)
        return [
            pltpu.make_async_copy(held.at[at], to.at[at], bsem.at[i, src])
            for i, (held, to) in enumerate(((dg, dg_out), (du, du_out)))
        ]

    line_gather(z, n, dy2, rows, g2s, g2r, back_block)
    o_dy2.start()
    for copy in (o_branch, o_up, o_h1r, o_hidden, o_dy2):
        copy.wait()

    @pl.loop(0, n)
    def _(src):
        for copy in grads_out(src):
            copy.wait()

    cube_u.finish()
    cube_d.finish()


def run_forward(n, ns, att, tok, cot, more, gate_b, gate_own, up, down, attn_gain, mlp_gain):
    rows, depth = tok.shape
    tl, lw = att.shape
    ff = up.shape[1]
    dma = pltpu.SemaphoreType.DMA
    sems = line_sems(n)
    shape = jax.ShapeDtypeStruct
    return pl.pallas_call(
        functools.partial(forward_kernel, n, ns),
        out_shape=(
            shape((rows, depth), BF16),
            shape((tl, depth), BF16),
            shape((rows, depth), F32),
            shape((tl, ff), BF16),
            shape((tl, depth), BF16),
            shape((tl, ff), BF16),
            shape((tl, ff), BF16),
            shape((1, depth), F32),
            shape((depth, ff + last_part(ff)), BF16),
        ),
        in_specs=[VMEM, VMEM, VMEM, ANY, ANY, ANY, ANY, VMEM, VMEM, VMEM],
        out_specs=(VMEM, ANY, ANY, ANY, ANY, ANY, ANY, VMEM, ANY),
        scratch_shapes=[
            pltpu.VMEM((tl, depth), BF16),
            pltpu.VMEM((tl, ff), BF16),
            pltpu.VMEM((tl, depth), BF16),
            pltpu.VMEM((tl, ff), BF16),
            pltpu.VMEM((tl, ff), BF16),
            pltpu.VMEM((depth, lw), BF16),
            pltpu.VMEM((depth, ff), BF16),
            pltpu.VMEM((depth, ff - last_part(ff)), BF16),
            pltpu.VMEM((depth, ff + last_part(ff)), BF16),
            pltpu.VMEM((2, n, STEPS, rows, depth // STEPS), BF16),
            pltpu.VMEM((rows, depth), F32),
            pltpu.VMEM((rows, depth), F32),
            pltpu.VMEM((rows, depth), F32),
            pltpu.VMEM((tl, ff), F32),
            pltpu.VMEM((tl, ff), F32),
            dma((5,)),
            dma((5,)),
            dma((2, n)),
            *sems["gather"], *sems["scatter"], *sems["gather"], *sems["scatter"],
            *CubeGather.sems(ns), *CubeGather.sems(ns),
        ],
        compiler_params=pltpu.CompilerParams(
            collective_id=1, has_side_effects=True, vmem_limit_bytes=VMEM_BYTES
        ),
        cost_estimate=pl.CostEstimate(flops=18 * 10**9, bytes_accessed=40 * 10**6, transcendentals=2 * 10**6),
        name="feed_forward",
    )(att, tok, cot, more, gate_b, gate_own, up, down, attn_gain, mlp_gain)


def backward_kernel(
    n, ns,
    dg_in, du_in, h1r_in, cot, branch, more, gate_b, up, attn_gain,
    middle, dy1, datt, gain_part, grad_gate, grad_up,
    dg, du, h1r, wo, wg, wu, land, total,
    first, held_g, later_g, held_u, later_u,
    wsem, osem, s1s, s1r, g1s, g1r,
    ga, gb, gc, gd, ua, ub, uc, ud,
):
    s, z = lax.axis_index("seq"), lax.axis_index("head")
    rows, depth = cot.shape
    lw, ff = datt.shape[1], dg_in.shape[1]
    block = depth // ns
    width = depth // STEPS
    early = more.shape[1] - lw
    last = last_part(ff)

    def weights_in(c):
        at = rows_at(c, width)
        return [
            pltpu.make_async_copy(more.at[at, pl.ds(lw, early)], wg.at[at, pl.ds(0, early)], wsem.at[0, c]),
            pltpu.make_async_copy(gate_b.at[at], wg.at[at, pl.ds(early, ff - early - last)], wsem.at[1, c]),
            pltpu.make_async_copy(up.at[at, pl.ds(0, last)], wg.at[at, pl.ds(ff - last, last)], wsem.at[3, c]),
            pltpu.make_async_copy(up.at[at, pl.ds(last, ff)], wu.at[at], wsem.at[2, c]),
        ]

    l_h = pltpu.make_async_copy(h1r_in, h1r, osem.at[0])
    l_o = pltpu.make_async_copy(more.at[:, pl.ds(0, lw)], wo, osem.at[1])
    l_dg = pltpu.make_async_copy(dg_in, dg, osem.at[2])
    l_du = pltpu.make_async_copy(du_in, du, osem.at[3])
    for load in (l_dg, l_h, l_du):
        load.start()
    for c in range(STEPS):
        for copy in weights_in(c):
            copy.start()
    l_o.start()
    cube_barrier(s, z, ns, n)

    def weight_block(grad):
        return lambda b: mm(h1r[:, rows_at(b, block)], grad[...], TN)

    cube_g = CubeScatter(s, ns, weight_block(dg), block, first, held_g, later_g, (ga, gb, gc, gd))
    cube_u = CubeScatter(s, ns, weight_block(du), block, first, held_u, later_u, (ua, ub, uc, ud))

    def in_part(d, c):
        at, cols = rows_at(d, rows), rows_at(c, width)
        return mm(dg[at, :], wg[cols, :], NT) + mm(du[at, :], wu[cols, :], NT)

    line = LineScatter(z, n, in_part, land, s1s, s1r, total)
    half = ns // 2

    def there(slot):
        @pl.when(slot < STEPS)
        def _():
            for copy in weights_in(slot):
                copy.wait()

    def task(slot):
        def during(low, count, act):
            @pl.when((slot >= low) & (slot < low + half // count))
            def _():
                for i in range(count):
                    act(count * (slot - low) + i)

        def send_second(j):
            cube_g.core_copy(half - 1 - j).wait_send()
            cube_u.send_core(j)

        during(0, 2, cube_g.add_core)
        during(half // 2, 1, send_second)
        during(half // 2 + half, 1, cube_u.add_core)

    l_h.wait()
    l_dg.wait()
    cube_g.send_core()
    l_du.wait()
    line.run(0, 2 * STEPS, there, task)
    line.start_own()
    line.run(2 * STEPS, line.slots, None, task)

    @pl.loop(line.slots, max(line.slots, half // 2 + 2 * half))
    def _(slot):
        task(slot)

    cube_g.step(0)
    line.own()
    line.finish()
    gain_part[...] = jnp.zeros_like(gain_part)

    @pl.loop(0, rows // BLOCK)
    def _(i):
        at = rows_at(i, BLOCK)
        y = branch[at, :]
        scale = row_scale(y)
        normed = y * scale
        e = cot[at, :].astype(F32) + total[at, :]
        middle[at, :] = e
        gain_part[...] += jnp.sum(e * normed, axis=0, keepdims=True)
        dy1[pl.ds(pl.multiple_of(z * rows + i * BLOCK, BLOCK), BLOCK), :] = norm_back(
            e, normed, scale, attn_gain[...]
        ).astype(BF16)

    l_o.wait()

    def att_block(src):
        at = rows_at(src, rows)
        datt[at, :] = mm(dy1[at, :], wo[...]).astype(BF16)

    todo = [functools.partial(cube.step, i) for i in range(1, cube_g.stages) for cube in (cube_g, cube_u)]
    line_gather(z, n, dy1, rows, g1s, g1r, att_block, todo[: n - 1], functools.partial(cube_u.step, 0))
    for step in todo[n - 1 :]:
        step()
    grad_gate[...] = held_g[0]
    grad_up[...] = held_u[0]
    cube_g.finish()
    cube_u.core_sent()
    cube_u.finish()


def run_backward(n, ns, dg, du, h1r, cot, branch, more, gate_b, up, attn_gain):
    rows, depth = cot.shape
    tl, ff = dg.shape
    lw = more.shape[1] + gate_b.shape[1] + last_part(ff) - ff
    block = depth // ns
    dma = pltpu.SemaphoreType.DMA
    sems = line_sems(n)
    shape = jax.ShapeDtypeStruct
    first, held, later, *cube_sems = CubeScatter.scratch(ns, block, ff)
    return pl.pallas_call(
        functools.partial(backward_kernel, n, ns),
        out_shape=(
            shape((rows, depth), F32),
            shape((tl, depth), BF16),
            shape((tl, lw), BF16),
            shape((1, depth), F32),
            shape((block, ff), BF16),
            shape((block, ff), BF16),
        ),
        in_specs=[ANY, ANY, ANY, VMEM, VMEM, ANY, ANY, ANY, VMEM],
        out_specs=(VMEM,) * 6,
        scratch_shapes=[
            pltpu.VMEM((tl, ff), BF16),
            pltpu.VMEM((tl, ff), BF16),
            pltpu.VMEM((tl, depth), BF16),
            pltpu.VMEM((depth, lw), BF16),
            pltpu.VMEM((depth, ff), BF16),
            pltpu.VMEM((depth, ff), BF16),
            pltpu.VMEM((2, n, STEPS, rows, depth // STEPS), BF16),
            pltpu.VMEM((rows, depth), F32),
            first, held, later, held, later,
            dma((4, STEPS)),
            dma((4,)),
            *sems["scatter"], *sems["gather"],
            *cube_sems, *cube_sems,
        ],
        compiler_params=pltpu.CompilerParams(
            collective_id=2, has_side_effects=True, vmem_limit_bytes=VMEM_BYTES
        ),
        cost_estimate=pl.CostEstimate(flops=18 * 10**9, bytes_accessed=30 * 10**6, transcendentals=0),
        name="into_attention",
    )(dg, du, h1r, cot, branch, more, gate_b, up, attn_gain)


LOG2E = 1.4426950408889634
NEG = -1e30


def seq_barrier(s, ns, between=None):
    bar = pltpu.get_barrier_semaphore()
    for other in range(ns):

        @pl.when(other != s)
        def _():
            pl.semaphore_signal(bar, inc=1, device_id={"seq": other}, device_id_type=MESH)

    if between is not None:
        between()
    pl.semaphore_wait(bar, ns - 1)


def share_of(s, ns, r):
    per = ns // (2 * r)
    chunk = s // per
    low = chunk < r
    sub = jnp.where(low, chunk, 2 * r - 1 - chunk)
    return sub, jnp.where(low, s - chunk * per, per + s - chunk * per)


def source_of(sub, i, ns, r):
    per = ns // (2 * r)
    return jnp.where(i < per, sub * per + i, (2 * r - 1 - sub) * per + i - per)


def head_cols(h):
    return pl.ds(pl.multiple_of(h * HEAD_DIM, HEAD_DIM), HEAD_DIM)


def attend_part(
    ns, heads, q_in, k_in, v_in, docs, gate,
    att, q_out, k_out, v_out, o_buf, lse, gate_out,
    q_buf, k_buf, v_buf, o_low, qs, qr, ks, kr, vs, vr, osend, orecv, local, cs, cr, late,
):
    s = lax.axis_index("seq")
    r = ns // heads
    blocks = ns // r
    tl = q_in.shape[0]
    mine, sub = s // r, s % r
    parity = s % 2
    to_sub, to_row = share_of(s, ns, r)

    def own_rows():
        for x, buf in ((k_in, k_buf), (v_in, v_buf)):
            buf[rows_at(s, tl), :] = x[:, head_cols(mine)]

        @pl.when(to_sub == sub)
        def _():
            q_buf[rows_at(to_row, tl), :] = q_in[:, head_cols(mine)]

    own_rows()

    def q_copy(h):
        return pltpu.make_async_remote_copy(
            src_ref=q_in.at[:, head_cols(h)],
            dst_ref=q_buf.at[rows_at(to_row, tl)],
            send_sem=qs.at[h],
            recv_sem=qr.at[to_row],
            device_id={"seq": h * r + to_sub},
            device_id_type=MESH,
        )

    def q_recv(i):
        return pltpu.make_async_remote_copy(
            src_ref=q_buf.at[rows_at(i, tl)],
            dst_ref=q_buf.at[rows_at(i, tl)],
            send_sem=qs.at[0],
            recv_sem=qr.at[i],
            device_id={"seq": s ^ 1},
            device_id_type=MESH,
        )

    def kv_copy(src, buf, send, recv, t, at):
        return pltpu.make_async_remote_copy(
            src_ref=src,
            dst_ref=buf.at[rows_at(at, tl)],
            send_sem=send,
            recv_sem=recv.at[at],
            device_id={"seq": t},
            device_id_type=MESH,
        )

    kv = ((k_in, k_buf, ks, kr), (v_in, v_buf, vs, vr))
    block = gate.shape[0]
    cols = gate_out.shape[1]
    own = gate.at[:, pl.ds(early_part(gate.shape[1]), cols)]
    own_gate = pltpu.make_async_copy(own, gate_out.at[rows_at(s, block)], local.at[0])
    cube = CubeGather(s, ns, gate_out, block, cs, cr, own)
    own_gate.start()

    def far(t):
        return (t != s) & (t % 2 == parity)

    @pl.loop(1, ns)
    def _(step):
        t = s ^ step

        @pl.when(far(t))
        def _():
            for x, buf, ss, rs in kv:
                kv_copy(x.at[:, head_cols(t // r)], buf, ss.at[0, t], rs, t, s).start()

    @pl.loop(0, heads)
    def _(h):
        @pl.when(h * r + to_sub != s)
        def _():
            q_copy(h).start()

    def pass_on(src, start):
        for _, buf, ss, rs in kv:
            copy = kv_copy(buf.at[rows_at(src, tl)], buf, ss.at[1, src], rs, s ^ 1, src)
            if start:
                copy.start()
            else:
                copy.wait_send()

    pass_on(s, True)

    @pl.loop(1, ns)
    def _(step):
        src = s ^ step

        @pl.when(far(src))
        def _():
            for x, buf, ss, rs in kv:
                kv_copy(buf.at[rows_at(src, tl)], buf, ss.at[0, 0], rs, s ^ 1, src).wait_recv()
            pass_on(src, True)

    @pl.loop(0, ns)
    def _(src):
        @pl.when(src % 2 != parity)
        def _():
            for x, buf, ss, rs in kv:
                kv_copy(buf.at[rows_at(src, tl)], buf, ss.at[0, 0], rs, s ^ 1, src).wait_recv()

    unit = HEAD_DIM ** (-0.5) * LOG2E

    def o_copy(i, t):
        return pltpu.make_async_remote_copy(
            src_ref=o_low.at[rows_at(i, tl)],
            dst_ref=att.at[:, head_cols(mine)],
            send_sem=osend.at[i],
            recv_sem=orecv.at[mine],
            device_id={"seq": t},
            device_id_type=MESH,
        )

    def attend_block(i):
        src = source_of(sub, i, ns, r)

        @pl.when(src != s)
        def _():
            q_recv(i).wait_recv()

        q = q_buf[rows_at(i, tl), :]
        start = first_of_document(docs, src * tl + lax.broadcasted_iota(jnp.int32, (1, tl), 1))
        key_at = lax.broadcasted_iota(jnp.int32, (tl, tl), 0)

        def step(j, carry, diagonal):
            top, total, acc = carry
            at = rows_at(j, tl)
            scores = mm(k_buf[at, :], q, NT) * unit
            allowed = key_at >= start - j * tl
            if diagonal:
                allowed = allowed & (key_at <= lax.broadcasted_iota(jnp.int32, (tl, tl), 1))
            scores = jnp.where(allowed, scores, NEG)
            new = jnp.maximum(top, jnp.max(scores, axis=0, keepdims=True))
            terms = jnp.exp2(scores - new)
            fade = jnp.exp2(top - new)
            return (
                new,
                total * fade + jnp.sum(terms, axis=0, keepdims=True),
                acc * fade + mm(v_buf[at, :], terms.astype(BF16), TN),
            )

        carry = (
            jnp.full((1, tl), NEG, F32),
            jnp.zeros((1, tl), F32),
            jnp.zeros((HEAD_DIM, tl), F32),
        )
        carry = lax.fori_loop(0, src, lambda j, c: step(j, c, False), carry)
        top, total, acc = step(src, carry, True)
        lse[pl.ds(i, 1), :] = top + jnp.log(total) * LOG2E
        o = jnp.transpose(acc / total)
        o_buf[rows_at(i, tl), :] = o
        o_low[rows_at(i, tl), :] = o.astype(BF16)

        @pl.when(src != s)
        def _():
            o_copy(i, src).start()

        @pl.when(src == s)
        def _():
            att[:, head_cols(mine)] = o.astype(BF16)

    late()
    cube.start()
    keep = [
        pltpu.make_async_copy(a, b, local.at[1 + i])
        for i, (a, b) in enumerate(((k_buf, k_out), (v_buf, v_out), (q_buf, q_out)))
    ]
    for copy in keep[:2]:
        copy.start()
    cuts = [0, blocks - 1, blocks, blocks]
    for i in range(3):
        pl.loop(cuts[i], cuts[i + 1])(attend_block)
        if i < 2:
            cube.level(i)
    for i in range(2, cube.levels):
        cube.level(i)

    keep[2].start()
    own_gate.wait()

    @pl.loop(0, heads)
    def _(h):
        @pl.when(h * r + to_sub != s)
        def _():
            q_copy(h).wait_send()
            pltpu.make_async_remote_copy(
                src_ref=o_low.at[rows_at(0, tl)],
                dst_ref=att.at[:, head_cols(h)],
                send_sem=osend.at[0],
                recv_sem=orecv.at[h],
                device_id={"seq": s ^ 1},
                device_id_type=MESH,
            ).wait_recv()

    @pl.loop(0, blocks)
    def _(i):
        src = source_of(sub, i, ns, r)

        @pl.when(src != s)
        def _():
            o_copy(i, src).wait_send()

    pass_on(s, False)

    @pl.loop(1, ns)
    def _(step):
        t = s ^ step

        @pl.when(far(t))
        def _():
            for x, buf, ss, rs in kv:
                kv_copy(x.at[:, head_cols(t // r)], buf, ss.at[0, t], rs, t, s).wait_send()
            pass_on(t, False)

    cube.finish()
    for copy in keep:
        copy.wait()


def attend_back_kernel(
    ns, heads, do_in, docs, q_in, k_in, v_in, o_in, lse, dy2_in, hidden_in,
    dq, dk, dv, grad_down,
    q_buf, k_buf, v_buf, o_buf, dy2, hidden, lsem,
    do_buf, dq_low, dk_acc, dv_acc, low, pair, land,
    first, held, later, ca, cb, cc, cd,
    ds_, dr_, ps, pr, gs, gr, qs, qr,
):
    s = lax.axis_index("seq")
    r = ns // heads
    blocks = ns // r
    tl = do_in.shape[0]
    mine, sub = s // r, s % r
    parity = s % 2

    loads = [
        pltpu.make_async_copy(a, b, lsem.at[i])
        for i, (a, b) in enumerate(
            ((dy2_in, dy2), (hidden_in, hidden), (q_in, q_buf), (k_in, k_buf), (v_in, v_buf), (o_in, o_buf))
        )
    ]
    for load in loads:
        load.start()

    def clear():
        dk_acc[...] = jnp.zeros_like(dk_acc)
        dv_acc[...] = jnp.zeros_like(dv_acc)

    seq_barrier(s, ns, clear)
    to_sub, to_row = share_of(s, ns, r)

    def copy(src, dst, send, recv, t):
        return pltpu.make_async_remote_copy(
            src_ref=src, dst_ref=dst, send_sem=send, recv_sem=recv, device_id={"seq": t}, device_id_type=MESH
        )

    def do_copy(h):
        return copy(
            do_in.at[:, head_cols(h)], do_buf.at[rows_at(to_row, tl)], ds_.at[h], dr_.at[to_row], h * r + to_sub
        )

    @pl.loop(0, heads)
    def _(h):
        @pl.when(h * r + to_sub != s)
        def _():
            do_copy(h).start()

    block = dy2.shape[1] // ns
    cube = CubeScatter(
        s, ns, lambda b: mm(dy2[:, rows_at(b, block)], hidden[:, : grad_down.shape[0]], TN), block, first, held, later, (ca, cb, cc, cd)
    )
    for load in loads:
        load.wait()
    cube.send_core()
    cube.add_core()

    @pl.when(to_sub == sub)
    def _():
        do_buf[rows_at(to_row, tl), :] = do_in[:, head_cols(mine)]

    scale = HEAD_DIM ** (-0.5)
    unit = scale * LOG2E

    def dq_copy(i, t):
        return copy(dq_low.at[rows_at(i, tl)], dq.at[:, head_cols(mine)], qs.at[i], qr.at[mine], t)

    ones = jnp.ones((8, HEAD_DIM), F32)

    def back_block(i):
        src = source_of(sub, i, ns, r)
        rows = rows_at(i, tl)

        @pl.when(src != s)
        def _():
            copy(do_buf.at[rows], do_buf.at[rows], ds_.at[0], dr_.at[i], s ^ 1).wait_recv()

        q = q_buf[rows, :]
        do = do_buf[rows, :]
        start = first_of_document(docs, src * tl + lax.broadcasted_iota(jnp.int32, (1, tl), 1))
        norm = lse[pl.ds(i, 1), :]
        delta = lax.dot_general(
            ones, do.astype(F32) * o_buf[rows, :], NT,
            precision=lax.Precision.HIGHEST, preferred_element_type=F32,
        )[:1]
        key_at = lax.broadcasted_iota(jnp.int32, (tl, tl), 0)

        def step(j, dq_sum, diagonal):
            at = rows_at(j, tl)
            keys = k_buf[at, :]
            scores = mm(keys, q, NT) * unit
            allowed = key_at >= start - j * tl
            if diagonal:
                allowed = allowed & (key_at <= lax.broadcasted_iota(jnp.int32, (tl, tl), 1))
            p = jnp.where(allowed, jnp.exp2(scores - norm), 0.0)
            dp = mm(v_buf[at, :], do, NT)
            dscore = (p * (dp - delta)).astype(BF16)
            dv_acc[at, :] += mm(p.astype(BF16), do)
            dk_acc[at, :] += mm(dscore, q)
            return dq_sum + mm(dscore, keys, TN)

        dq_sum = lax.fori_loop(0, src, lambda j, c: step(j, c, False), jnp.zeros((tl, HEAD_DIM), F32))
        dq_sum = step(src, dq_sum, True)
        dq_low[rows, :] = (dq_sum * scale).astype(BF16)

        @pl.when(src != s)
        def _():
            dq_copy(i, src).start()

        @pl.when(src == s)
        def _():
            dq[:, head_cols(mine)] = dq_low[rows, :]

    pl.loop(0, blocks - 1)(back_block)
    cube.step(0)
    pl.loop(blocks - 1, blocks)(back_block)
    half = ns // 2

    def pair_copy(w, i):
        src = 2 * i + 1 - parity
        return copy(low.at[w, rows_at(src, tl)], pair.at[w, rows_at(i, tl)], ps.at[w, i], pr.at[w, i], s ^ 1)

    @pl.loop(0, half)
    def _(i):
        at = rows_at(2 * i + 1 - parity, tl)
        low[0, at, :] = (dk_acc[at, :] * scale).astype(BF16)
        pair_copy(0, i).start()
        low[1, at, :] = dv_acc[at, :].astype(BF16)
        pair_copy(1, i).start()

    slot = sub // 2
    outs = (dk, dv)

    def back_copy(w, i):
        dest = 2 * i + parity
        return copy(
            low.at[w, rows_at(dest, tl)], land.at[w, slot, :, head_cols(mine)], gs.at[w, i], gr.at[w, mine, slot], dest
        )

    @pl.loop(0, half)
    def _(i):
        dest = 2 * i + parity
        at = rows_at(dest, tl)
        for w, acc, factor in ((0, dk_acc, scale), (1, dv_acc, 1.0)):
            copy(low.at[w, at], pair.at[w, rows_at(i, tl)], ps.at[w, i], pr.at[w, i], s ^ 1).wait_recv()
            low[w, at, :] = (acc[at, :] * factor + pair[w, rows_at(i, tl), :].astype(F32)).astype(BF16)

            @pl.when(dest != s)
            def _():
                back_copy(w, i).start()

            @pl.when(dest == s)
            def _():
                land[w, slot, :, head_cols(mine)] = low[w, at, :]

    @pl.loop(0, heads)
    def _(h):
        for w in range(2):
            for k in range(r // 2):

                @pl.when(h * r + 2 * k + parity != s)
                def _():
                    copy(
                        low.at[w, rows_at(0, tl)], land.at[w, k, :, head_cols(h)], gs.at[w, 0], gr.at[w, h, k], s ^ 1
                    ).wait_recv()

    for w in range(2):
        outs[w][...] = functools.reduce(
            lambda a, b: a + b, [land[w, k].astype(F32) for k in range(r // 2)]
        ).astype(BF16)

    @pl.loop(0, heads)
    def _(h):
        @pl.when(h * r + to_sub != s)
        def _():
            do_copy(h).wait_send()
            copy(dq_low.at[rows_at(0, tl)], dq.at[:, head_cols(h)], qs.at[0], qr.at[h], s ^ 1).wait_recv()

    @pl.loop(0, blocks)
    def _(i):
        src = source_of(sub, i, ns, r)

        @pl.when(src != s)
        def _():
            dq_copy(i, src).wait_send()

    @pl.loop(0, half)
    def _(i):
        for w in range(2):
            pair_copy(w, i).wait_send()

            @pl.when(2 * i + parity != s)
            def _():
                back_copy(w, i).wait_send()

    for i in range(1, cube.stages):
        cube.step(i)
    grad_down[...] = jnp.transpose(held[0].astype(F32)).astype(BF16)
    cube.core_sent()
    cube.finish()


def run_attend_back(ns, heads, do, docs, q, k, v, o, lse, dy2, hidden):
    tl, lw = do.shape
    r = ns // heads
    nq = ns // r * tl
    nk = ns * tl
    dma = pltpu.SemaphoreType.DMA
    shape = jax.ShapeDtypeStruct
    return pl.pallas_call(
        functools.partial(attend_back_kernel, ns, heads),
        out_shape=(shape((tl, lw), BF16),) * 3 + (shape((hidden.shape[1] - lw, dy2.shape[1] // ns), BF16),),
        in_specs=[VMEM, SMEM] + [ANY] * 4 + [VMEM] + [ANY] * 2,
        out_specs=(VMEM,) * 4,
        scratch_shapes=[
            pltpu.VMEM((nq, HEAD_DIM), BF16),
            pltpu.VMEM((nk, HEAD_DIM), BF16),
            pltpu.VMEM((nk, HEAD_DIM), BF16),
            pltpu.VMEM((nq, HEAD_DIM), F32),
            pltpu.VMEM(dy2.shape, BF16),
            pltpu.VMEM(hidden.shape, BF16),
            dma((6,)),
            pltpu.VMEM((nq, HEAD_DIM), BF16),
            pltpu.VMEM((nq, HEAD_DIM), BF16),
            pltpu.VMEM((nk, HEAD_DIM), F32),
            pltpu.VMEM((nk, HEAD_DIM), F32),
            pltpu.VMEM((2, nk, HEAD_DIM), BF16),
            pltpu.VMEM((2, nk // 2, HEAD_DIM), BF16),
            pltpu.VMEM((2, r // 2, tl, lw), BF16),
            *CubeScatter.scratch(ns, dy2.shape[1] // ns, hidden.shape[1] - lw),
            dma((heads,)), dma((ns // r,)),
            dma((2, ns // 2)), dma((2, ns // 2)),
            dma((2, ns // 2)), dma((2, heads, r // 2)),
            dma((ns // r,)), dma((heads,)),
        ],
        compiler_params=pltpu.CompilerParams(
            collective_id=4, has_side_effects=True, vmem_limit_bytes=VMEM_BYTES
        ),
        cost_estimate=pl.CostEstimate(flops=8 * 10**9, bytes_accessed=10 * 10**6, transcendentals=5 * 10**6),
        name="attend_back",
    )(do, docs, q, k, v, o, lse, dy2, hidden)


def cross_barrier(s, z, ns, n, between=None):
    bar = pltpu.get_barrier_semaphore()
    for axis, me, count in (("seq", s, ns), ("head", z, n)):
        for other in range(count):

            @pl.when(other != me)
            def _():
                pl.semaphore_signal(bar, inc=1, device_id={axis: other}, device_id_type=MESH)

    if between is not None:
        between()
    pl.semaphore_wait(bar, ns - 1 + n - 1)


def row_sums(left, right):
    ones = jnp.ones((8, left.shape[1]), F32)
    both = [
        lax.dot_general(ones, x, NT, precision=lax.Precision.HIGHEST, preferred_element_type=F32) for x in (left, right)
    ]
    return jnp.where(lax.broadcasted_iota(jnp.int32, both[0].shape, 0) < 4, both[0], both[1])


def as_column(sums, row):
    pick = (lax.broadcasted_iota(jnp.int32, (8, HEAD_DIM), 0) == row).astype(F32)
    return lax.dot_general(sums, pick, TN, precision=lax.Precision.HIGHEST, preferred_element_type=F32)


class SmallExchange:
    def __init__(self, axis, me, count, land, send_sem, recv_sem):
        self.axis, self.me, self.count, self.land = axis, me, count, land
        self.send_sem, self.recv_sem = send_sem, recv_sem

    def copy(self, slot, to):
        return remote(self.land.at[slot], self.land.at[slot], self.send_sem.at[to], self.recv_sem.at[slot], self.axis, to)

    def each(self, act):
        @pl.loop(0, self.count)
        def _(other):
            @pl.when(other != self.me)
            def _():
                act(other)

    def start(self):
        self.each(lambda other: self.copy(self.me, other).start())

    def receive(self):
        self.each(lambda other: self.copy(other, other).wait_recv())

    def finish(self):
        self.each(lambda other: self.copy(self.me, other).wait_send())


def turn(x, cos, sin):
    return x * cos + pltpu.roll(x, HEAD_DIM // 2, 1) * sin


def turn_back(x, cos, sin):
    return x * cos - pltpu.roll(x, HEAD_DIM // 2, 1) * sin


def project_part(
    n, ns, depth_full,
    tok, wq, wk, wv, wo, gate, gq, gk, docs, turns,
    x_out, w_out, more_out, q_out, k_out, totals, cos, sin,
    q_rot, k_rot, v_low, q_raw, k_raw, x, w, own, land, lsem, ags, agr, cgs, cgr, egs, egr, ss, sr,
):
    s, z = lax.axis_index("seq"), lax.axis_index("head")
    rows, depth = tok.shape
    block, lw = wq.shape
    heads = lw // HEAD_DIM
    cross_barrier(s, z, ns, n)
    mine = rows_at(s, block)

    def head_gain(h):
        return head_cols(z * heads + h)

    loads = [pltpu.make_async_copy(tok, x.at[rows_at(z, rows)], lsem.at[0])] + [
        pltpu.make_async_copy(m, w.at[mine, pl.ds(i * lw, lw)], lsem.at[i + 1]) for i, m in enumerate((wq, wk, wv))
    ]
    for copy in loads:
        copy.start()
    loads[0].wait()
    cube = CubeGather(s, ns, w, block, cgs, cgr)
    own_more = pltpu.make_async_copy(own, more_out.at[mine], lsem.at[8])
    cube_e = CubeGather(s, ns, more_out, block, egs, egr, own)
    levels = cube.levels

    def weights(k):
        if k == 0:
            cube.level(0)
        else:
            for i in range(1, levels):
                cube.level(i)
                if i == levels - 2:
                    cube_e.start()

    def start_weights():
        for copy in loads[1:]:
            copy.wait()
        cube.start()

    def multiply(src):
        at = rows_at(src, rows)
        for i, to in enumerate((q_raw, k_raw)):
            to[at, :] = mm(x[at, :], w[:, i * lw : (i + 1) * lw])
        v_low[at, :] = mm(x[at, :], w[:, 2 * lw :]).astype(BF16)

    part = rows // AG_CHUNKS

    def copy(src, c, up):
        at = pl.ds(pl.multiple_of(src * rows + c * part, part), part)
        return remote(x.at[at], x.at[at], ags.at[up, src, c], agr.at[src, c], "head", z + 1 if up else z - 1)

    more = (z > 0, z < n - 1)
    for c in range(AG_CHUNKS):
        for up in (0, 1):

            @pl.when(more[up])
            def _():
                copy(z, c, up).start()

    start_weights()
    own[:, :lw] = jnp.transpose(wo[...].astype(F32)).astype(BF16)
    own[:, lw:] = gate[:, : own.shape[1] - lw]
    own_more.start()
    token = s * x.shape[0] + lax.broadcasted_iota(jnp.int32, cos.shape, 0)
    angle = (token - first_of_document(docs, token)).astype(F32) * turns[...]
    flip = jnp.where(lax.broadcasted_iota(jnp.int32, cos.shape, 1) < HEAD_DIM // 2, -1.0, 1.0)
    cos[...] = jnp.cos(angle)
    sin[...] = jnp.sin(angle) * flip

    def sides(k):
        return ((z + k, z + k < n, 0), (z - k, z - k >= 0, 1))

    for k in range(1, n):
        for c in range(AG_CHUNKS):
            for src, there, up in sides(k):

                @pl.when(there)
                def _():
                    copy(src, c, up).wait_recv()

                    @pl.when(more[up])
                    def _():
                        copy(src, c, up).start()

        if k <= 2:
            weights(k - 1)
        if k == min(2, n - 1):
            multiply(z)
            for src, there, _ in sides(1):
                pl.when(there)(functools.partial(multiply, src))
        if k > 1:
            for src, there, _ in sides(k):
                pl.when(there)(functools.partial(multiply, src))

    outs = [
        pltpu.make_async_copy(a, b, lsem.at[4 + i])
        for i, (a, b) in enumerate(((x, x_out), (w, w_out), (q_raw, q_out), (k_raw, k_out)))
    ]
    for out in outs:
        out.start()
    totals[...] = row_sums(q_raw[...] * q_raw[...], k_raw[...] * k_raw[...])
    land[z] = totals[...]
    small = SmallExchange("head", z, n, land, ss, sr)
    small.start()
    small.receive()
    total = land[0]
    for k in range(1, n):
        total = total + land[k]
    totals[...] = total
    for row, raw, gain, to in ((0, q_raw, gq, q_rot), (4, k_raw, gk, k_rot)):
        scale = lax.rsqrt(as_column(total, row) / depth_full + epsilon)
        for h in range(heads):
            cols = slice(h * HEAD_DIM, (h + 1) * HEAD_DIM)
            to[:, cols] = turn(raw[:, cols] * scale * gain[:, head_gain(h)], cos[...], sin[...]).astype(BF16)
        if row == 0:
            cube_e.level(0)

    def late():
        for i in range(1, levels):
            cube_e.level(i)

    def finish():
        small.finish()
        cube.finish()
        cube_e.finish()
        for out in [*outs, own_more]:
            out.wait()

        @pl.loop(0, n)
        def _(src):
            for c in range(AG_CHUNKS):

                @pl.when((src >= z) & (z > 0))
                def _():
                    copy(src, c, 0).wait_send()

                @pl.when((src <= z) & (z < n - 1))
                def _():
                    copy(src, c, 1).wait_send()

    return late, finish


def front_kernel(n, ns, heads, depth_full, *refs):
    ins, refs = refs[:10], refs[10:]
    made, refs = refs[:8], refs[8:]
    attended, refs = refs[:7], refs[7:]
    first, second = refs[:18], refs[18:]
    late, finish = project_part(n, ns, depth_full, *ins, *made, *first)
    attend_part(ns, heads, *first[:3], ins[8], ins[5], *attended, *second, late=late)
    finish()


def run_front(n, ns, heads, tok, wq, wk, wv, wo, gate, gq, gk, docs, turns):
    rows, depth = tok.shape
    tl = rows * n
    block, lw = wq.shape
    r = ns // heads
    nq = ns // r * tl
    nk = ns * tl
    ff = gate.shape[1]
    early = early_part(ff)
    dma = pltpu.SemaphoreType.DMA
    shape = jax.ShapeDtypeStruct
    return pl.pallas_call(
        functools.partial(front_kernel, n, ns, heads, depth),
        out_shape=(
            shape((tl, depth), BF16),
            shape((depth, 3 * lw), BF16),
            shape((depth, lw + early), BF16),
            shape((tl, lw), F32),
            shape((tl, lw), F32),
            shape((8, tl), F32),
            shape((tl, HEAD_DIM), F32),
            shape((tl, HEAD_DIM), F32),
            shape((tl, lw), BF16),
            shape((nq, HEAD_DIM), BF16),
            shape((nk, HEAD_DIM), BF16),
            shape((nk, HEAD_DIM), BF16),
            shape((nq, HEAD_DIM), F32),
            shape((ns // r, tl), F32),
            shape((depth, ff - early - last_part(ff)), BF16),
        ),
        in_specs=[ANY] * 4 + [VMEM] * 4 + [SMEM, VMEM],
        out_specs=(ANY,) * 5 + (VMEM,) * 4 + (ANY,) * 3 + (VMEM,) * 2 + (ANY,),
        scratch_shapes=[
            pltpu.VMEM((tl, lw), BF16),
            pltpu.VMEM((tl, lw), BF16),
            pltpu.VMEM((tl, lw), BF16),
            pltpu.VMEM((tl, lw), F32),
            pltpu.VMEM((tl, lw), F32),
            pltpu.VMEM((tl, depth), BF16),
            pltpu.VMEM((depth, 3 * lw), BF16),
            pltpu.VMEM((block, lw + early), BF16),
            pltpu.VMEM((n, 8, tl), F32),
            dma((9,)),
            dma((2, n, AG_CHUNKS)), dma((n, AG_CHUNKS)),
            *CubeGather.sems(ns), *CubeGather.sems(ns),
            dma((n,)), dma((n,)),
            pltpu.VMEM((nq, HEAD_DIM), BF16),
            pltpu.VMEM((nk, HEAD_DIM), BF16),
            pltpu.VMEM((nk, HEAD_DIM), BF16),
            pltpu.VMEM((nq, HEAD_DIM), BF16),
            dma((heads,)), dma((ns // r,)),
            dma((2, ns)), dma((ns,)),
            dma((2, ns)), dma((ns,)),
            dma((ns // r,)), dma((heads,)),
            dma((4,)),
            *CubeGather.sems(ns),
        ],
        compiler_params=pltpu.CompilerParams(
            collective_id=5, has_side_effects=True, vmem_limit_bytes=VMEM_BYTES
        ),
        cost_estimate=pl.CostEstimate(flops=6 * 10**9, bytes_accessed=30 * 10**6, transcendentals=5 * 10**6),
        name="front",
    )(tok, wq, wk, wv, wo, gate, gq, gk, docs, turns)


def input_kernel(
    n, ns, depth_full,
    dq, dk, dv, q_raw, k_raw, totals, gq, gk, cos, sin, x_in, w_in, att, dy1_in, attn_part, mlp_part, dy2_in, hidden_in,
    total, grad_q, grad_k, grad_v, grad_o, grad_down, gains,
    x, w, dy1, dy2, hidden, lsem, dqkv, q_back, k_back, inner, land, message, message_z, gain_land,
    first, held, later, c0s, c0r, c1s, c1r,
    first_o, held_o, later_o, o0s, o0r, o1s, o1r,
    ss, sr, ms, mr, zs, zr, s1s, s1r,
):
    s, z = lax.axis_index("seq"), lax.axis_index("head")
    rows, depth = total.shape
    tl, lw = dq.shape
    block = depth // ns
    heads = lw // HEAD_DIM

    def head_gain(h):
        return head_cols(z * heads + h)

    sums = totals[...]
    scales = [lax.rsqrt(as_column(sums, row) / depth_full + epsilon) for row in (0, 4)]
    todo = ((dq, q_raw, gq, q_back), (dk, k_raw, gk, k_back))
    products = []

    l_d = pltpu.make_async_copy(dy2_in, dy2, lsem.at[0])
    l_h = pltpu.make_async_copy(hidden_in.at[:, pl.ds(hidden_in.shape[1] - lw, lw)], hidden, lsem.at[1])
    l_y = pltpu.make_async_copy(dy1_in, dy1, lsem.at[2])
    l_w = pltpu.make_async_copy(w_in, w, lsem.at[3])
    l_x = pltpu.make_async_copy(x_in, x, lsem.at[4])
    for load in (l_d, l_h, l_y, l_w, l_x):
        load.start()

    def turn_all():
        message[...] = jnp.zeros_like(message)
        for i, (grad, raw, gain, back) in enumerate(todo):
            product = jnp.zeros((tl, HEAD_DIM), F32)
            for h in range(heads):
                cols = slice(h * HEAD_DIM, (h + 1) * HEAD_DIM)
                hat = raw[:, cols] * scales[i]
                turned = turn_back(grad[:, cols].astype(F32), cos[...], sin[...])
                message[0, pl.ds(i, 1), cols] = jnp.sum(turned * hat, axis=0, keepdims=True)
                turned = turned * gain[:, head_gain(h)]
                back[:, cols] = turned
                product = product + turned * hat
            products.append(product)
        inner[z] = row_sums(*products)
        for t in range(1, ns):
            message[t, pl.ds(0, 2), pl.ds(0, lw)] = message[0, pl.ds(0, 2), pl.ds(0, lw)]
        for t in range(ns):
            for i, part in enumerate((attn_part, mlp_part)):
                message[t, pl.ds(i, 1), pl.ds(lw, block)] = part[:, t * block : (t + 1) * block]

    cross_barrier(s, z, ns, n, turn_all)
    small = SmallExchange("head", z, n, inner, ss, sr)
    small.start()

    def message_copy(t, frm):
        return remote(message.at[t], message_z.at[frm], ms.at[t], mr.at[frm], "seq", t)

    def each_seq(act):
        @pl.loop(0, ns)
        def _(t):
            @pl.when(t != s)
            def _():
                act(t)

    message_z[s] = message[s]
    each_seq(lambda t: message_copy(t, s).start())
    dqkv[:, 2 * lw :] = dv[...]
    for load in (l_d, l_h, l_y):
        load.wait()

    def early_block(b):
        cols = rows_at(b, block)
        return jnp.concatenate([mm(dy1[:, cols], att[...], TN), mm(dy2[:, cols], hidden[...], TN)], axis=1)

    cube_o = CubeScatter(
        s, ns, early_block, block, first_o, held_o, later_o, (o0s, o0r, o1s, o1r)
    )
    cube_o.send_core()
    cube_o.add_core()
    small.receive()
    sums = inner[0]
    for k in range(1, n):
        sums = sums + inner[k]
    for i, (grad, raw, gain, back) in enumerate(todo):
        mean = as_column(sums, 4 * i) / depth_full
        for h in range(heads):
            cols = slice(h * HEAD_DIM, (h + 1) * HEAD_DIM)
            to = slice(i * lw + h * HEAD_DIM, i * lw + (h + 1) * HEAD_DIM)
            dqkv[:, to] = (scales[i] * (back[:, cols] - raw[:, cols] * scales[i] * mean)).astype(BF16)

    width = depth // STEPS

    def weight_block(b):
        cols = rows_at(b, block)
        return mm(x[:, cols], dqkv[...], TN)

    def in_part(d, c):
        return mm(dqkv[rows_at(d, rows), :], w[rows_at(c, width), :], NT)

    cube = CubeScatter(s, ns, weight_block, block, first, held, later, (c0s, c0r, c1s, c1r))
    line = LineScatter(z, n, in_part, land, s1s, s1r, total)
    half = ns // 2

    def task(slot):
        for i, act in enumerate((cube.send_core, cube.add_core)):
            low = 1 + i * (half // 2)

            @pl.when((slot >= low) & (slot < low + half // 2))
            def _():
                for j in range(2):
                    act(2 * (slot - low) + j)

    done = 1 + half
    l_w.wait()
    l_x.wait()
    line.run(0, done, None, task)
    line.start_own()
    line.run(done, done + 3)
    for i in range(cube.stages - 1):
        cube_o.step(i)
    line.run(done + 3, line.slots)
    for i in range(cube.stages - 1):
        cube.step(i)

    each_seq(lambda t: message_copy(t, t).wait_recv())
    received = message_z[0]
    for t in range(1, ns):
        received = received + message_z[t]
    each_seq(lambda t: message_copy(t, s).wait_send())
    gain_land[z] = received
    rounds = SmallExchange("head", z, n, gain_land, zs, zr)
    rounds.start()
    line.own()
    cube_o.step(cube.stages - 1)
    grad_o[...] = jnp.transpose(held_o[0, :, :lw].astype(F32)).astype(BF16)
    grad_down[...] = jnp.transpose(held_o[0, :, lw:].astype(F32)).astype(BF16)
    cube.step(cube.stages - 1)
    for i, to in enumerate((grad_q, grad_k, grad_v)):
        to[...] = held[0, :, i * lw : (i + 1) * lw]
    rounds.receive()
    at = s * block
    gains[...] = jnp.zeros_like(gains)
    gains[0:2, :] = gain_land[at // lw, pl.ds(0, 2), pl.ds(pl.multiple_of(at % lw, block), block)]
    both = gain_land[0, pl.ds(0, 2), pl.ds(lw, block)]
    for k in range(1, n):
        both = both + gain_land[k, pl.ds(0, 2), pl.ds(lw, block)]
    gains[2:4, :] = both
    for one in (cube, cube_o):
        one.core_sent()
        one.finish()
    line.finish()
    small.finish()
    rounds.finish()


def run_input(n, ns, dq, dk, dv, q_raw, k_raw, totals, gq, gk, cos, sin, x, w, att, dy1, attn_part, mlp_part, dy2, hidden):
    tl, lw = dq.shape
    rows, depth = tl // n, x.shape[1]
    block = depth // ns
    dma = pltpu.SemaphoreType.DMA
    shape = jax.ShapeDtypeStruct
    return pl.pallas_call(
        functools.partial(input_kernel, n, ns, depth),
        out_shape=(shape((rows, depth), F32),)
        + (shape((block, lw), BF16),) * 3
        + (shape((lw, block), BF16), shape((lw, block), BF16), shape((8, block), F32)),
        in_specs=[VMEM] * 10 + [ANY] * 2 + [VMEM, ANY, VMEM, VMEM] + [ANY] * 2,
        out_specs=(VMEM,) * 7,
        scratch_shapes=[
            pltpu.VMEM(x.shape, BF16),
            pltpu.VMEM(w.shape, BF16),
            pltpu.VMEM((tl, depth), BF16),
            pltpu.VMEM((tl, depth), BF16),
            pltpu.VMEM((tl, lw), BF16),
            dma((5,)),
            pltpu.VMEM((tl, 3 * lw), BF16),
            pltpu.VMEM((tl, lw), F32),
            pltpu.VMEM((tl, lw), F32),
            pltpu.VMEM((n, 8, tl), F32),
            pltpu.VMEM((2, n, STEPS, rows, depth // STEPS), BF16),
            pltpu.VMEM((ns, 8, lw + block), F32),
            pltpu.VMEM((ns, 8, lw + block), F32),
            pltpu.VMEM((n, 8, lw + block), F32),
            *CubeScatter.scratch(ns, block, 3 * lw),
            *CubeScatter.scratch(ns, block, 2 * lw),
            dma((n,)), dma((n,)),
            dma((ns,)), dma((ns,)),
            dma((n,)), dma((n,)),
            *line_sems(n)["scatter"],
        ],
        compiler_params=pltpu.CompilerParams(
            collective_id=6, has_side_effects=True, vmem_limit_bytes=VMEM_BYTES
        ),
        cost_estimate=pl.CostEstimate(flops=8 * 10**9, bytes_accessed=30 * 10**6, transcendentals=0),
        name="into_input",
    )(dq, dk, dv, q_raw, k_raw, totals, gq, gk, cos, sin, x, w, att, dy1, attn_part, mlp_part, dy2, hidden)


def widen_kernel(count, *refs):
    spec = WIDEN
    ins, rest = refs[:count], refs[count:]
    outs, rest = rest[: len(spec)], rest[len(spec) :]
    held, rest = rest[:count], rest[count:]
    wide, (load_sem, store_sem) = rest[: len(spec)], rest[len(spec) :]
    loads = [pltpu.make_async_copy(a, b, load_sem.at[i]) for i, (a, b) in enumerate(zip(ins, held))]
    stores = [pltpu.make_async_copy(a, b, store_sem.at[i]) for i, (a, b) in enumerate(zip(wide, outs))]
    for copy in loads:
        copy.start()
    at = 0
    for (parts, stacked), to, store in zip(spec, wide, stores):
        row = 0
        for i in range(at, at + parts):
            loads[i].wait()
            block = held[i][...].astype(to.dtype)
            if stacked:
                to[row : row + block.shape[0], :] = block
                row += block.shape[0]
            elif i == at:
                to[...] = block
            else:
                to[...] += block
        at += parts
        store.start()
    for copy in stores:
        copy.wait()


WIDEN = ((1, False), (1, False), (1, False), (2, True), (1, False), (1, False), (1, False), (1, False), (2, False))


def run_widen(arrays, outs):
    dma = pltpu.SemaphoreType.DMA
    return pl.pallas_call(
        functools.partial(widen_kernel, len(arrays)),
        out_shape=tuple(outs),
        in_specs=[ANY] * len(arrays),
        out_specs=(ANY,) * len(outs),
        scratch_shapes=[pltpu.VMEM(a.shape, a.dtype) for a in arrays]
        + [pltpu.VMEM(o.shape, o.dtype) for o in outs]
        + [dma((len(arrays),)), dma((len(outs),))],
        compiler_params=pltpu.CompilerParams(vmem_limit_bytes=VMEM_BYTES),
        name="widen",
    )(*arrays)


def on_device(
    tokens,
    cotangent,
    doc_lengths,
    q_weight,
    k_weight,
    v_weight,
    o_weight,
    gate_weight,
    up_weight,
    down_weight,
    q_gain,
    k_gain,
    attn_gain,
    mlp_gain,
):
    ns, nz = lax.axis_size("seq"), lax.axis_size("head")
    lw = q_weight.shape[1]
    heads = lw // HEAD_DIM
    block, ff = gate_weight.shape
    gq, gk = q_gain[None], k_gain[None]
    frequency = jnp.power(rope_base, -(jnp.arange(HEAD_DIM) % (HEAD_DIM // 2)).astype(F32) * (2.0 / HEAD_DIM))

    x, w, more, q_raw, k_raw, totals, cos, sin, attended, q_held, k_held, v_held, o_held, lse, gate_b = run_front(
        nz, ns, heads, tokens, q_weight, k_weight, v_weight, o_weight, gate_weight, gq, gk, doc_lengths, frequency[None]
    )
    output, h1r, branch, hidden, dy2, dg, du, mlp_part, up = run_forward(
        nz, ns, attended, tokens, cotangent, more, gate_b, gate_weight, up_weight, down_weight, attn_gain[None], mlp_gain[None]
    )
    middle, dy1, datt, attn_part, grad_gate, grad_up = run_backward(
        nz, ns, dg, du, h1r, cotangent, branch, more, gate_b, up, attn_gain[None]
    )
    dq, dk, dv, down_a = run_attend_back(
        ns, heads, datt, doc_lengths, q_held, k_held, v_held, o_held, lse, dy2, hidden
    )
    last, grad_q, grad_k, grad_v, grad_o, down_b, gains = run_input(
        nz, ns, dq, dk, dv, q_raw, k_raw, totals, gq, gk, cos, sin, x, w, attended, dy1, attn_part, mlp_part, dy2, hidden
    )
    shape = jax.ShapeDtypeStruct
    small = shape((block, lw), F32)
    output, grad_gate, grad_up, grad_down, grad_q, grad_k, grad_v, grad_o, input_grad = run_widen(
        (output, grad_gate, grad_up, down_a, down_b, grad_q, grad_k, grad_v, grad_o, middle, last),
        (
            shape(output.shape, BF16),
            shape((block, ff), F32),
            shape((block, ff), F32),
            shape((ff, block), F32),
            small, small, small,
            shape((lw, block), F32),
            shape(middle.shape, F32),
        ),
    )
    return (
        output,
        input_grad,
        grad_q,
        grad_k,
        grad_v,
        grad_o,
        grad_gate,
        grad_up,
        grad_down,
        gains[0],
        gains[1],
        gains[2],
        gains[3],
    )


def solution(mesh):
    in_specs = (
        P(("seq", "head"), None),
        P(("seq", "head"), None),
        P(),
        P("seq", "head"),
        P("seq", "head"),
        P("seq", "head"),
        P("head", "seq"),
        P("seq", "head"),
        P("seq", "head"),
        P("head", "seq"),
        P(),
        P(),
        P(),
        P(),
    )
    out_specs = (
        P(("seq", "head"), None),
        P(("seq", "head"), None),
        P("seq", "head"),
        P("seq", "head"),
        P("seq", "head"),
        P("head", "seq"),
        P("seq", "head"),
        P("seq", "head"),
        P("head", "seq"),
        P("seq"),
        P("seq"),
        P("seq"),
        P("seq"),
    )
    return jax.shard_map(
        on_device, mesh=mesh, in_specs=in_specs, out_specs=out_specs, check_vma=False
    )
```

```python
import functools

import jax
import jax.numpy as jnp
from jax import lax
from jax.experimental import pallas as pl
from jax.experimental.pallas import tpu as pltpu
from jax.sharding import PartitionSpec as P

HEAD_DIM = 128
epsilon = 1e-06
rope_base = 500000.0

MESH = pl.DeviceIdType.MESH
F32 = jnp.float32
BF16 = jnp.bfloat16
STEPS = 4
LAG = 1
EARLY = (7, 16)
AG_CHUNKS = 2
VMEM_BYTES = 62 * 1024 * 1024
ANY = pl.BlockSpec(memory_space=pl.ANY)
VMEM = pl.BlockSpec(memory_space=pltpu.VMEM)
SMEM = pl.BlockSpec(memory_space=pltpu.SMEM)
NN = (((1,), (0,)), ((), ()))
NT = (((1,), (1,)), ((), ()))
TN = (((0,), (0,)), ((), ()))


def first_of_document(docs, token):
    end, first = jnp.int32(0), jnp.zeros_like(token)
    for i in range(docs.shape[0]):
        end = end + docs[i]
        first = first + jnp.where(token >= end, docs[i], 0)
    return first


def mm(left, right, dims=NN):
    return lax.dot_general(left, right, dims, preferred_element_type=F32)


def early_part(ff):
    return ff * EARLY[0] // EARLY[1] // HEAD_DIM * HEAD_DIM


def last_part(ff):
    return ff // STEPS


def rows_at(index, count):
    return pl.ds(pl.multiple_of(index * count, count), count)


def cube_barrier(s, z, ns, n, between=None):
    bar = pltpu.get_barrier_semaphore()
    bits = [1 << i for i in range(ns.bit_length() - 1)]
    for bit in bits:
        pl.semaphore_signal(bar, inc=1, device_id={"seq": s ^ bit}, device_id_type=MESH)
    for other, there in ((z - 1, z > 0), (z + 1, z < n - 1)):

        @pl.when(there)
        def _():
            pl.semaphore_signal(bar, inc=1, device_id={"head": other}, device_id_type=MESH)

    if between is not None:
        between()
    pl.semaphore_wait(bar, len(bits) + (z > 0).astype(jnp.int32) + (z < n - 1).astype(jnp.int32))


def line_gather(z, n, buf, rows, send_sem, recv_sem, use, hooks=(), ready=None):
    part = rows // AG_CHUNKS

    def copy(src, c, up):
        at = pl.ds(pl.multiple_of(src * rows + c * part, part), part)
        return pltpu.make_async_remote_copy(
            src_ref=buf.at[at],
            dst_ref=buf.at[at],
            send_sem=send_sem.at[up, src, c],
            recv_sem=recv_sem.at[src, c],
            device_id={"head": z + 1 if up else z - 1},
            device_id_type=MESH,
        )

    more = (z > 0, z < n - 1)
    for c in range(AG_CHUNKS):
        for up in (0, 1):

            @pl.when(more[up])
            def _():
                copy(z, c, up).start()

    if ready is not None:
        ready()
    use(z)

    @pl.loop(1, n)
    def _(k):
        sides = ((z + k, z + k < n, 0), (z - k, z - k >= 0, 1))
        for c in range(AG_CHUNKS):
            for src, there, up in sides:

                @pl.when(there)
                def _():
                    copy(src, c, up).wait_recv()

                    @pl.when(more[up])
                    def _():
                        copy(src, c, up).start()

        for src, there, up in sides:

            @pl.when(there)
            def _():
                use(src)

        for i, hook in enumerate(hooks):
            pl.when(k == i + 1)(hook)

    @pl.loop(0, n)
    def _(src):
        for c in range(AG_CHUNKS):

            @pl.when((src >= z) & (z > 0))
            def _():
                copy(src, c, 0).wait_send()

            @pl.when((src <= z) & (z < n - 1))
            def _():
                copy(src, c, 1).wait_send()


class LineScatter:
    def __init__(self, z, n, partial, land, send_sem, recv_sem, total, own_late=False):
        self.own_late = own_late
        self.z, self.n, self.partial, self.land, self.total = z, n, partial, land, total
        self.send_sem, self.recv_sem = send_sem, recv_sem

    def copy(self, d, c, up):
        return pltpu.make_async_remote_copy(
            src_ref=self.land.at[up, d, c],
            dst_ref=self.land.at[up, d, c],
            send_sem=self.send_sem.at[up, d, c],
            recv_sem=self.recv_sem.at[up, d, c],
            device_id={"head": self.z + 1 if up else self.z - 1},
            device_id_type=MESH,
        )

    @property
    def slots(self):
        return (self.n - 1) * (STEPS + LAG)

    def run(self, low, high, before=None, after=None):
        z, n, land = self.z, self.n, self.land

        @pl.loop(low, high)
        def _(slot):
            if before is not None:
                before(slot)
            for up in (1, 0):
                t = slot - (z if up else n - 1 - z) * LAG
                j = t // STEPS
                c = t - j * STEPS
                d = n - 1 - j if up else j
                first = z == 0 if up else z == n - 1
                there = (t >= 0) & (j < n - 1) & ((d > z) if up else (d < z))

                @pl.when(there)
                def _():
                    mine = self.partial(d, c)

                    @pl.when(first)
                    def _():
                        land[up, d, c] = mine.astype(land.dtype)

                    @pl.when(jnp.logical_not(first))
                    def _():
                        self.copy(d, c, up).wait_recv()
                        land[up, d, c] = (land[up, d, c].astype(F32) + mine).astype(land.dtype)

                    self.copy(d, c, up).start()

            if self.own_late:
                @pl.when(slot >= self.slots - STEPS)
                def _():
                    self.own_chunk(slot - (self.slots - STEPS))

            if after is not None:
                after(slot)

    def own_chunk(self, c):
        width = self.total.shape[1] // STEPS
        self.total[:, rows_at(c, width)] = self.partial(self.z, c)

    def start_own(self):
        pl.loop(0, STEPS)(self.own_chunk)

    def own(self):
        z, n, total = self.z, self.n, self.total
        width = total.shape[1] // STEPS

        @pl.loop(0, STEPS)
        def _(c):
            at = rows_at(c, width)
            for there, up in ((z > 0, 1), (z < n - 1, 0)):

                @pl.when(there)
                def _():
                    self.copy(z, c, up).wait_recv()
                    total[:, at] += self.land[up, z, c].astype(F32)

    def finish(self):
        @pl.loop(0, self.n * STEPS)
        def _(t):
            d, c = t // STEPS, t % STEPS
            for there, up in ((d > self.z, 1), (d < self.z, 0)):

                @pl.when(there)
                def _():
                    self.copy(d, c, up).wait_send()


def line_sems(n):
    dma = pltpu.SemaphoreType.DMA
    return {
        "gather": [dma((2, n, AG_CHUNKS)), dma((n, AG_CHUNKS))],
        "scatter": [dma((2, n, STEPS)), dma((2, n, STEPS))],
    }


BLOCK = 64


def row_scale(block):
    return lax.rsqrt(jnp.mean(block * block, axis=-1, keepdims=True) + epsilon)


def norm_back(e, normed, scale, gain):
    g = e * gain
    return scale * (g - normed * jnp.mean(g * normed, axis=-1, keepdims=True))


def sigmoid(x):
    return 1.0 / (1.0 + jnp.exp(-x))


def subsets(bits):
    found = [0]
    for bit in bits:
        found += [bit | other for other in found]
    return found


def orders_of(ns):
    chips = [1 << i for i in range(1, ns.bit_length() - 1)]
    return (chips, chips[::-1])


def remote(src, dst, send, recv, axis, to):
    return pltpu.make_async_remote_copy(
        src_ref=src, dst_ref=dst, send_sem=send, recv_sem=recv, device_id={axis: to}, device_id_type=MESH
    )


class CubeGather:
    def __init__(self, s, ns, buf, rows, send_sem, recv_sem, own=None):
        self.own = own
        self.s, self.buf, self.rows, self.send_sem, self.recv_sem = s, buf, rows, send_sem, recv_sem
        self.orders = [order + [1] for order in orders_of(ns)]

    def copy(self, half, bit, block):
        part = self.rows // 2
        at = pl.ds(pl.multiple_of(block * self.rows + half * part, part), part)
        source = self.buf.at[at]
        if block is self.s and self.own is not None:
            source = self.own.at[pl.ds(half * part, part)]
        return remote(
            source, self.buf.at[at],
            self.send_sem.at[bit.bit_length() - 1, block, half], self.recv_sem.at[block, half],
            "seq", self.s ^ bit,
        )

    @property
    def levels(self):
        return len(self.orders[0])

    def start(self):
        for i in range(self.levels):
            for half, order in enumerate(self.orders):
                self.copy(half, order[i], self.s).start()

    def level(self, i):
        for j in range(2**i):
            for half, order in enumerate(self.orders):
                block = self.s ^ order[i] ^ subsets(order[:i])[j]
                self.copy(half, order[i], block).wait_recv()
                for bit in order[i + 1 :]:
                    self.copy(half, bit, block).start()

    def finish(self):
        for half, order in enumerate(self.orders):
            for i, bit in enumerate(order):
                for other in subsets(order[:i]):
                    self.copy(half, bit, self.s ^ other if other else self.s).wait_send()

    @staticmethod
    def sems(ns):
        dma = pltpu.SemaphoreType.DMA
        return [dma((ns.bit_length() - 1, ns, 2)), dma((ns, 2))]


class CubeScatter:
    def __init__(self, s, ns, block, rows, first, held, later, sems):
        self.s, self.block, self.rows = s, block, rows
        self.first, self.held, self.later = first, held, later
        self.send0, self.recv0, self.send1, self.recv1 = sems
        self.orders = orders_of(ns)
        self.half = ns // 2

    def core_copy(self, j):
        return remote(self.first.at[j], self.held.at[j], self.send0.at[j], self.recv0.at[j], "seq", self.s ^ 1)

    def send_core(self, j=None):
        if j is None:
            pl.loop(0, self.half)(self.send_core)
            return
        j = self.half - 1 - j
        self.first[j] = self.block(self.s ^ (2 * j + 1)).astype(BF16)
        self.core_copy(j).start()

    def base(self, i):
        return sum(2 ** (self.stages - 1 - k) for k in range(i))

    def move(self, i, half, slot, other):
        part = self.rows // 2
        return remote(
            self.held.at[(self.orders[half][i] | other) >> 1, pl.ds(half * part, part)],
            self.later.at[half, slot], self.send1.at[half, slot], self.recv1.at[half, slot],
            "seq", self.s ^ self.orders[half][i],
        )

    def moves(self, i):
        part = self.rows // 2
        for half, order in enumerate(self.orders):
            for j, other in enumerate(subsets(order[i + 1 :])):
                slot = self.base(i) + j
                yield other >> 1, pl.ds(half * part, part), half, slot, self.move(i, half, slot, other)

    def add_core(self, j=None):
        if j is None:
            pl.loop(0, self.half)(self.add_core)
            return
        j = self.half - 1 - j
        mine = self.block(self.s ^ (2 * j))
        self.core_copy(j).wait_recv()
        self.held[j] = (self.held[j].astype(F32) + mine).astype(BF16)
        for half, order in enumerate(self.orders):
            for slot, other in enumerate(subsets(order[1:])):

                @pl.when(j == (order[0] | other) >> 1)
                def _():
                    self.move(0, half, slot, other).start()

    def send(self, i):
        for *_, copy in self.moves(i):
            copy.start()

    def take(self, i):
        for j, at, half, slot, copy in self.moves(i):
            copy.wait_recv()
            self.held[j, at] = (self.held[j, at].astype(F32) + self.later[half, slot].astype(F32)).astype(BF16)

    def step(self, i):
        self.take(i)
        if i + 1 < self.stages:
            self.send(i + 1)

    @property
    def stages(self):
        return len(self.orders[0])

    def core_sent(self):
        @pl.loop(0, self.half)
        def _(j):
            self.core_copy(j).wait_send()

    def finish(self):
        for i in range(self.stages):
            for *_, copy in self.moves(i):
                copy.wait_send()

    @staticmethod
    def scratch(ns, rows, width):
        dma = pltpu.SemaphoreType.DMA
        half = ns // 2
        return [
            pltpu.VMEM((half, rows, width), BF16),
            pltpu.VMEM((half, rows, width), BF16),
            pltpu.VMEM((2, half - 1, rows // 2, width), BF16),
            dma((half,)), dma((half,)), dma((2, half - 1)), dma((2, half - 1)),
        ]


def forward_kernel(
    n, ns,
    att, tok, cot, more, gate_b, gate_own, up, down, attn_gain, mlp_gain,
    out, h1r_out, branch_out, hidden_out, dy2_out, dg_out, du_out, gain_part, up_out,
    h1r, hidden, dy2, dg, du,
    wo, wd, wg, wu, land, branch, h1, second, g_pre, u_pre,
    wsem, osem, bsem, g1s, g1r, s1s, s1r, g2s, g2r, s2s, s2r, us, ur, ds, dr,
):
    s, z = lax.axis_index("seq"), lax.axis_index("head")
    rows, depth = tok.shape
    lw, ff = att.shape[1], up.shape[1]
    block = depth // ns
    width = depth // STEPS
    mine = rows_at(s, block)
    l_o = pltpu.make_async_copy(more.at[:, pl.ds(0, lw)], wo, wsem.at[0])
    last = last_part(ff)
    l_u = pltpu.make_async_copy(up, wu.at[mine, pl.ds(last, ff)], wsem.at[1])
    l_c = pltpu.make_async_copy(gate_own.at[:, pl.ds(ff - last, last)], wu.at[mine, pl.ds(0, last)], wsem.at[4])
    early = more.shape[1] - lw
    l_g = pltpu.make_async_copy(more.at[:, pl.ds(lw, early)], wg.at[:, pl.ds(0, early)], wsem.at[2])
    l_h = pltpu.make_async_copy(gate_b, wg.at[:, pl.ds(early, ff - early - last)], wsem.at[3])
    for copy in (l_o, l_u, l_c, l_g, l_h):
        copy.start()
    cube_barrier(s, z, ns, n)
    cube_u = CubeGather(s, ns, wu, block, us, ur)
    cube_d = CubeGather(s, ns, wd, block, ds, dr)
    levels = cube_u.levels
    l_u.wait()
    l_c.wait()
    cube_u.start()
    l_o.wait()

    def out_part(d, c):
        return mm(att[rows_at(d, rows), :], wo[rows_at(c, width), :], NT)

    line = LineScatter(z, n, out_part, land, s1s, s1r, branch)
    line.run(0, STEPS)
    line.start_own()
    wd[mine, :] = jnp.transpose(down[...].astype(F32)).astype(BF16)
    line.run(STEPS, 2 * STEPS)
    cube_u.level(0)
    line.run(2 * STEPS, 3 * STEPS)
    for i in range(1, levels - 1):
        cube_u.level(i)
    cube_d.start()
    line.run(3 * STEPS, line.slots)
    line.own()
    line.finish()
    o_branch = pltpu.make_async_copy(branch, branch_out, osem.at[0])
    o_branch.start()
    gain_part[...] = jnp.zeros_like(gain_part)

    @pl.loop(0, rows // BLOCK)
    def _(i):
        at = rows_at(i, BLOCK)
        y = branch[at, :]
        h = tok[at, :].astype(F32) + y * row_scale(y) * attn_gain[...]
        h1[at, :] = h
        h1r[pl.ds(pl.multiple_of(z * rows + i * BLOCK, BLOCK), BLOCK), :] = h.astype(BF16)

    fw = ff // STEPS
    o_up = pltpu.make_async_copy(wu, up_out, osem.at[1])
    o_h1r = pltpu.make_async_copy(h1r, h1r_out, osem.at[2])
    o_hidden = pltpu.make_async_copy(hidden, hidden_out, osem.at[3])
    o_dy2 = pltpu.make_async_copy(dy2, dy2_out, osem.at[4])

    def up_block(src):
        at = rows_at(src, rows)

        def columns(c, gate):
            cols = rows_at(c, fw)
            x = h1r[at, :]
            g = mm(x, gate)
            u = mm(x, wu[:, pl.ds(pl.multiple_of(last + c * fw, HEAD_DIM), fw)])
            g_pre[at, cols] = g
            u_pre[at, cols] = u
            hidden[at, cols] = (g * sigmoid(g) * u).astype(BF16)

        pl.loop(0, STEPS - 1)(lambda c: columns(c, wg[:, rows_at(c, fw)]))
        columns(STEPS - 1, wu[:, :last])

    def weights_there():
        l_g.wait()
        l_h.wait()
        cube_u.level(levels - 1)
        o_up.start()

    hooks = [functools.partial(cube_d.level, i) for i in range(levels)]
    line_gather(z, n, h1r, rows, g1s, g1r, up_block, hooks[: n - 1], weights_there)
    for hook in hooks[n - 1 :]:
        hook()
    o_h1r.start()
    o_hidden.start()

    def down_part(d, c):
        return mm(hidden[rows_at(d, rows), :], wd[rows_at(c, width), :], NT)

    line = LineScatter(z, n, down_part, land, s2s, s2r, second)
    line.run(0, STEPS)
    line.start_own()
    line.run(STEPS, line.slots)
    line.own()
    line.finish()

    @pl.loop(0, rows // BLOCK)
    def _(i):
        at = rows_at(i, BLOCK)
        y = second[at, :]
        scale = row_scale(y)
        normed = y * scale
        e = cot[at, :].astype(F32)
        out[at, :] = (h1[at, :] + normed * mlp_gain[...]).astype(BF16)
        gain_part[...] += jnp.sum(e * normed, axis=0, keepdims=True)
        dy2[pl.ds(pl.multiple_of(z * rows + i * BLOCK, BLOCK), BLOCK), :] = norm_back(
            e, normed, scale, mlp_gain[...]
        ).astype(BF16)

    def back_block(src):
        at = rows_at(src, rows)

        @pl.loop(0, STEPS)
        def _(c):
            cols = rows_at(c, fw)
            dh = mm(dy2[at, :], wd[:, cols])
            g = g_pre[at, cols]
            u = u_pre[at, cols]
            sig = sigmoid(g)
            du[at, cols] = (dh * g * sig).astype(BF16)
            dg[at, cols] = (dh * u * sig * (1.0 + g * (1.0 - sig))).astype(BF16)

        for copy in grads_out(src):
            copy.start()

    def grads_out(src):
        at = rows_at(src, rows)
        return [
            pltpu.make_async_copy(held.at[at], to.at[at], bsem.at[i, src])
            for i, (held, to) in enumerate(((dg, dg_out), (du, du_out)))
        ]

    line_gather(z, n, dy2, rows, g2s, g2r, back_block)
    o_dy2.start()
    for copy in (o_branch, o_up, o_h1r, o_hidden, o_dy2):
        copy.wait()

    @pl.loop(0, n)
    def _(src):
        for copy in grads_out(src):
            copy.wait()

    cube_u.finish()
    cube_d.finish()


def run_forward(n, ns, att, tok, cot, more, gate_b, gate_own, up, down, attn_gain, mlp_gain):
    rows, depth = tok.shape
    tl, lw = att.shape
    ff = up.shape[1]
    dma = pltpu.SemaphoreType.DMA
    sems = line_sems(n)
    shape = jax.ShapeDtypeStruct
    return pl.pallas_call(
        functools.partial(forward_kernel, n, ns),
        out_shape=(
            shape((rows, depth), BF16),
            shape((tl, depth), BF16),
            shape((rows, depth), F32),
            shape((tl, ff), BF16),
            shape((tl, depth), BF16),
            shape((tl, ff), BF16),
            shape((tl, ff), BF16),
            shape((1, depth), F32),
            shape((depth, ff + last_part(ff)), BF16),
        ),
        in_specs=[VMEM, VMEM, VMEM, ANY, ANY, ANY, ANY, VMEM, VMEM, VMEM],
        out_specs=(VMEM, ANY, ANY, ANY, ANY, ANY, ANY, VMEM, ANY),
        scratch_shapes=[
            pltpu.VMEM((tl, depth), BF16),
            pltpu.VMEM((tl, ff), BF16),
            pltpu.VMEM((tl, depth), BF16),
            pltpu.VMEM((tl, ff), BF16),
            pltpu.VMEM((tl, ff), BF16),
            pltpu.VMEM((depth, lw), BF16),
            pltpu.VMEM((depth, ff), BF16),
            pltpu.VMEM((depth, ff - last_part(ff)), BF16),
            pltpu.VMEM((depth, ff + last_part(ff)), BF16),
            pltpu.VMEM((2, n, STEPS, rows, depth // STEPS), BF16),
            pltpu.VMEM((rows, depth), F32),
            pltpu.VMEM((rows, depth), F32),
            pltpu.VMEM((rows, depth), F32),
            pltpu.VMEM((tl, ff), F32),
            pltpu.VMEM((tl, ff), F32),
            dma((5,)),
            dma((5,)),
            dma((2, n)),
            *sems["gather"], *sems["scatter"], *sems["gather"], *sems["scatter"],
            *CubeGather.sems(ns), *CubeGather.sems(ns),
        ],
        compiler_params=pltpu.CompilerParams(
            collective_id=1, has_side_effects=True, vmem_limit_bytes=VMEM_BYTES
        ),
        cost_estimate=pl.CostEstimate(flops=18 * 10**9, bytes_accessed=40 * 10**6, transcendentals=2 * 10**6),
        name="feed_forward",
    )(att, tok, cot, more, gate_b, gate_own, up, down, attn_gain, mlp_gain)


def backward_kernel(
    n, ns,
    dg_in, du_in, h1r_in, cot, branch, more, gate_b, up, attn_gain,
    middle, dy1, datt, gain_part, grad_gate, grad_up,
    dg, du, h1r, wo, wg, wu, land, total,
    first, held_g, later_g, held_u, later_u,
    wsem, osem, s1s, s1r, g1s, g1r,
    ga, gb, gc, gd, ua, ub, uc, ud,
):
    s, z = lax.axis_index("seq"), lax.axis_index("head")
    rows, depth = cot.shape
    lw, ff = datt.shape[1], dg_in.shape[1]
    block = depth // ns
    width = depth // STEPS
    early = more.shape[1] - lw
    last = last_part(ff)

    def weights_in(c):
        at = rows_at(c, width)
        return [
            pltpu.make_async_copy(more.at[at, pl.ds(lw, early)], wg.at[at, pl.ds(0, early)], wsem.at[0, c]),
            pltpu.make_async_copy(gate_b.at[at], wg.at[at, pl.ds(early, ff - early - last)], wsem.at[1, c]),
            pltpu.make_async_copy(up.at[at, pl.ds(0, last)], wg.at[at, pl.ds(ff - last, last)], wsem.at[3, c]),
            pltpu.make_async_copy(up.at[at, pl.ds(last, ff)], wu.at[at], wsem.at[2, c]),
        ]

    l_h = pltpu.make_async_copy(h1r_in, h1r, osem.at[0])
    l_o = pltpu.make_async_copy(more.at[:, pl.ds(0, lw)], wo, osem.at[1])
    l_dg = pltpu.make_async_copy(dg_in, dg, osem.at[2])
    l_du = pltpu.make_async_copy(du_in, du, osem.at[3])
    for load in (l_dg, l_h, l_du):
        load.start()
    for c in range(STEPS):
        for copy in weights_in(c):
            copy.start()
    l_o.start()
    cube_barrier(s, z, ns, n)

    def weight_block(grad):
        return lambda b: mm(h1r[:, rows_at(b, block)], grad[...], TN)

    cube_g = CubeScatter(s, ns, weight_block(dg), block, first, held_g, later_g, (ga, gb, gc, gd))
    cube_u = CubeScatter(s, ns, weight_block(du), block, first, held_u, later_u, (ua, ub, uc, ud))

    def in_part(d, c):
        at, cols = rows_at(d, rows), rows_at(c, width)
        return mm(dg[at, :], wg[cols, :], NT) + mm(du[at, :], wu[cols, :], NT)

    line = LineScatter(z, n, in_part, land, s1s, s1r, total, True)
    half = ns // 2

    def there(slot):
        @pl.when(slot < STEPS)
        def _():
            for copy in weights_in(slot):
                copy.wait()

    def task(slot):
        def during(low, count, act):
            @pl.when((slot >= low) & (slot < low + half // count))
            def _():
                for i in range(count):
                    act(count * (slot - low) + i)

        def send_second(j):
            cube_g.core_copy(half - 1 - j).wait_send()
            cube_u.send_core(j)

        during(0, 2, cube_g.add_core)
        during(half // 2, 1, send_second)
        during(half // 2 + half, 1, cube_u.add_core)

    l_h.wait()
    l_dg.wait()
    cube_g.send_core()
    l_du.wait()
    line.run(0, 2 * STEPS, there, task)
    line.run(2 * STEPS, line.slots, None, task)

    @pl.loop(line.slots, max(line.slots, half // 2 + 2 * half))
    def _(slot):
        task(slot)

    cube_g.step(0)
    line.own()
    line.finish()
    gain_part[...] = jnp.zeros_like(gain_part)

    @pl.loop(0, rows // BLOCK)
    def _(i):
        at = rows_at(i, BLOCK)
        y = branch[at, :]
        scale = row_scale(y)
        normed = y * scale
        e = cot[at, :].astype(F32) + total[at, :]
        middle[at, :] = e
        gain_part[...] += jnp.sum(e * normed, axis=0, keepdims=True)
        dy1[pl.ds(pl.multiple_of(z * rows + i * BLOCK, BLOCK), BLOCK), :] = norm_back(
            e, normed, scale, attn_gain[...]
        ).astype(BF16)

    l_o.wait()

    def att_block(src):
        at = rows_at(src, rows)
        datt[at, :] = mm(dy1[at, :], wo[...]).astype(BF16)

    todo = [functools.partial(cube.step, i) for i in range(1, cube_g.stages) for cube in (cube_g, cube_u)]
    line_gather(z, n, dy1, rows, g1s, g1r, att_block, todo[: n - 1], functools.partial(cube_u.step, 0))
    for step in todo[n - 1 :]:
        step()
    grad_gate[...] = held_g[0]
    grad_up[...] = held_u[0]
    cube_g.finish()
    cube_u.core_sent()
    cube_u.finish()


def run_backward(n, ns, dg, du, h1r, cot, branch, more, gate_b, up, attn_gain):
    rows, depth = cot.shape
    tl, ff = dg.shape
    lw = more.shape[1] + gate_b.shape[1] + last_part(ff) - ff
    block = depth // ns
    dma = pltpu.SemaphoreType.DMA
    sems = line_sems(n)
    shape = jax.ShapeDtypeStruct
    first, held, later, *cube_sems = CubeScatter.scratch(ns, block, ff)
    return pl.pallas_call(
        functools.partial(backward_kernel, n, ns),
        out_shape=(
            shape((rows, depth), F32),
            shape((tl, depth), BF16),
            shape((tl, lw), BF16),
            shape((1, depth), F32),
            shape((block, ff), BF16),
            shape((block, ff), BF16),
        ),
        in_specs=[ANY, ANY, ANY, VMEM, VMEM, ANY, ANY, ANY, VMEM],
        out_specs=(VMEM,) * 6,
        scratch_shapes=[
            pltpu.VMEM((tl, ff), BF16),
            pltpu.VMEM((tl, ff), BF16),
            pltpu.VMEM((tl, depth), BF16),
            pltpu.VMEM((depth, lw), BF16),
            pltpu.VMEM((depth, ff), BF16),
            pltpu.VMEM((depth, ff), BF16),
            pltpu.VMEM((2, n, STEPS, rows, depth // STEPS), BF16),
            pltpu.VMEM((rows, depth), F32),
            first, held, later, held, later,
            dma((4, STEPS)),
            dma((4,)),
            *sems["scatter"], *sems["gather"],
            *cube_sems, *cube_sems,
        ],
        compiler_params=pltpu.CompilerParams(
            collective_id=2, has_side_effects=True, vmem_limit_bytes=VMEM_BYTES
        ),
        cost_estimate=pl.CostEstimate(flops=18 * 10**9, bytes_accessed=30 * 10**6, transcendentals=0),
        name="into_attention",
    )(dg, du, h1r, cot, branch, more, gate_b, up, attn_gain)


LOG2E = 1.4426950408889634
NEG = -1e30


def seq_barrier(s, ns, between=None):
    bar = pltpu.get_barrier_semaphore()
    for other in range(ns):

        @pl.when(other != s)
        def _():
            pl.semaphore_signal(bar, inc=1, device_id={"seq": other}, device_id_type=MESH)

    if between is not None:
        between()
    pl.semaphore_wait(bar, ns - 1)


def share_of(s, ns, r):
    per = ns // (2 * r)
    chunk = s // per
    low = chunk < r
    sub = jnp.where(low, chunk, 2 * r - 1 - chunk)
    return sub, jnp.where(low, s - chunk * per, per + s - chunk * per)


def source_of(sub, i, ns, r):
    per = ns // (2 * r)
    return jnp.where(i < per, sub * per + i, (2 * r - 1 - sub) * per + i - per)


def head_cols(h):
    return pl.ds(pl.multiple_of(h * HEAD_DIM, HEAD_DIM), HEAD_DIM)


def attend_part(
    ns, heads, q_in, k_in, v_in, docs, gate,
    att, q_out, k_out, v_out, o_buf, lse, gate_out,
    q_buf, k_buf, v_buf, o_low, qs, qr, ks, kr, vs, vr, osend, orecv, local, cs, cr, late,
):
    s = lax.axis_index("seq")
    r = ns // heads
    blocks = ns // r
    tl = q_in.shape[0]
    mine, sub = s // r, s % r
    parity = s % 2
    to_sub, to_row = share_of(s, ns, r)

    def own_rows():
        for x, buf in ((k_in, k_buf), (v_in, v_buf)):
            buf[rows_at(s, tl), :] = x[:, head_cols(mine)]

        @pl.when(to_sub == sub)
        def _():
            q_buf[rows_at(to_row, tl), :] = q_in[:, head_cols(mine)]

    own_rows()

    def q_copy(h):
        return pltpu.make_async_remote_copy(
            src_ref=q_in.at[:, head_cols(h)],
            dst_ref=q_buf.at[rows_at(to_row, tl)],
            send_sem=qs.at[h],
            recv_sem=qr.at[to_row],
            device_id={"seq": h * r + to_sub},
            device_id_type=MESH,
        )

    def q_recv(i):
        return pltpu.make_async_remote_copy(
            src_ref=q_buf.at[rows_at(i, tl)],
            dst_ref=q_buf.at[rows_at(i, tl)],
            send_sem=qs.at[0],
            recv_sem=qr.at[i],
            device_id={"seq": s ^ 1},
            device_id_type=MESH,
        )

    def kv_copy(src, buf, send, recv, t, at):
        return pltpu.make_async_remote_copy(
            src_ref=src,
            dst_ref=buf.at[rows_at(at, tl)],
            send_sem=send,
            recv_sem=recv.at[at],
            device_id={"seq": t},
            device_id_type=MESH,
        )

    kv = ((k_in, k_buf, ks, kr), (v_in, v_buf, vs, vr))
    block = gate.shape[0]
    cols = gate_out.shape[1]
    own = gate.at[:, pl.ds(early_part(gate.shape[1]), cols)]
    own_gate = pltpu.make_async_copy(own, gate_out.at[rows_at(s, block)], local.at[0])
    cube = CubeGather(s, ns, gate_out, block, cs, cr, own)
    own_gate.start()

    def far(t):
        return (t != s) & (t % 2 == parity)

    @pl.loop(1, ns)
    def _(step):
        t = s ^ step

        @pl.when(far(t))
        def _():
            for x, buf, ss, rs in kv:
                kv_copy(x.at[:, head_cols(t // r)], buf, ss.at[0, t], rs, t, s).start()

    @pl.loop(0, heads)
    def _(h):
        @pl.when(h * r + to_sub != s)
        def _():
            q_copy(h).start()

    def pass_on(src, start):
        for _, buf, ss, rs in kv:
            copy = kv_copy(buf.at[rows_at(src, tl)], buf, ss.at[1, src], rs, s ^ 1, src)
            if start:
                copy.start()
            else:
                copy.wait_send()

    pass_on(s, True)

    @pl.loop(1, ns)
    def _(step):
        src = s ^ step

        @pl.when(far(src))
        def _():
            for x, buf, ss, rs in kv:
                kv_copy(buf.at[rows_at(src, tl)], buf, ss.at[0, 0], rs, s ^ 1, src).wait_recv()
            pass_on(src, True)

    @pl.loop(0, ns)
    def _(src):
        @pl.when(src % 2 != parity)
        def _():
            for x, buf, ss, rs in kv:
                kv_copy(buf.at[rows_at(src, tl)], buf, ss.at[0, 0], rs, s ^ 1, src).wait_recv()

    unit = HEAD_DIM ** (-0.5) * LOG2E

    def o_copy(i, t):
        return pltpu.make_async_remote_copy(
            src_ref=o_low.at[rows_at(i, tl)],
            dst_ref=att.at[:, head_cols(mine)],
            send_sem=osend.at[i],
            recv_sem=orecv.at[mine],
            device_id={"seq": t},
            device_id_type=MESH,
        )

    def attend_block(i):
        src = source_of(sub, i, ns, r)

        @pl.when(src != s)
        def _():
            q_recv(i).wait_recv()

        q = q_buf[rows_at(i, tl), :]
        start = first_of_document(docs, src * tl + lax.broadcasted_iota(jnp.int32, (1, tl), 1))
        key_at = lax.broadcasted_iota(jnp.int32, (tl, tl), 0)

        def step(j, carry, diagonal):
            top, total, acc = carry
            at = rows_at(j, tl)
            scores = mm(k_buf[at, :], q, NT) * unit
            allowed = key_at >= start - j * tl
            if diagonal:
                allowed = allowed & (key_at <= lax.broadcasted_iota(jnp.int32, (tl, tl), 1))
            scores = jnp.where(allowed, scores, NEG)
            new = jnp.maximum(top, jnp.max(scores, axis=0, keepdims=True))
            terms = jnp.exp2(scores - new)
            fade = jnp.exp2(top - new)
            return (
                new,
                total * fade + jnp.sum(terms, axis=0, keepdims=True),
                acc * fade + mm(v_buf[at, :], terms.astype(BF16), TN),
            )

        carry = (
            jnp.full((1, tl), NEG, F32),
            jnp.zeros((1, tl), F32),
            jnp.zeros((HEAD_DIM, tl), F32),
        )
        carry = lax.fori_loop(0, src, lambda j, c: step(j, c, False), carry)
        top, total, acc = step(src, carry, True)
        lse[pl.ds(i, 1), :] = top + jnp.log(total) * LOG2E
        o = jnp.transpose(acc / total)
        o_buf[rows_at(i, tl), :] = o
        o_low[rows_at(i, tl), :] = o.astype(BF16)

        @pl.when(src != s)
        def _():
            o_copy(i, src).start()

        @pl.when(src == s)
        def _():
            att[:, head_cols(mine)] = o.astype(BF16)

    late()
    cube.start()
    keep = [
        pltpu.make_async_copy(a, b, local.at[1 + i])
        for i, (a, b) in enumerate(((k_buf, k_out), (v_buf, v_out), (q_buf, q_out)))
    ]
    for copy in keep[:2]:
        copy.start()
    cuts = [0, blocks - 1, blocks, blocks]
    for i in range(3):
        pl.loop(cuts[i], cuts[i + 1])(attend_block)
        if i < 2:
            cube.level(i)
    for i in range(2, cube.levels):
        cube.level(i)

    keep[2].start()
    own_gate.wait()

    @pl.loop(0, heads)
    def _(h):
        @pl.when(h * r + to_sub != s)
        def _():
            q_copy(h).wait_send()
            pltpu.make_async_remote_copy(
                src_ref=o_low.at[rows_at(0, tl)],
                dst_ref=att.at[:, head_cols(h)],
                send_sem=osend.at[0],
                recv_sem=orecv.at[h],
                device_id={"seq": s ^ 1},
                device_id_type=MESH,
            ).wait_recv()

    @pl.loop(0, blocks)
    def _(i):
        src = source_of(sub, i, ns, r)

        @pl.when(src != s)
        def _():
            o_copy(i, src).wait_send()

    pass_on(s, False)

    @pl.loop(1, ns)
    def _(step):
        t = s ^ step

        @pl.when(far(t))
        def _():
            for x, buf, ss, rs in kv:
                kv_copy(x.at[:, head_cols(t // r)], buf, ss.at[0, t], rs, t, s).wait_send()
            pass_on(t, False)

    cube.finish()
    for copy in keep:
        copy.wait()


def attend_back_part(
    n, ns, heads, free, do_in, docs, q_in, k_in, v_in, o_in, lse, dy2_in, hidden_in,
    grad_down,
    q_buf, k_buf, v_buf, o_buf, dy2, hidden, lsem, dq, dk, dv,
    do_buf, dq_low, dk_acc, dv_acc, low, pair, land,
    first, held, later, ca, cb, cc, cd,
    ds_, dr_, ps, pr, gs, gr, qs, qr,
):
    s = lax.axis_index("seq")
    r = ns // heads
    blocks = ns // r
    tl = do_in.shape[0]
    mine, sub = s // r, s % r
    parity = s % 2

    loads = [
        pltpu.make_async_copy(a, b, lsem.at[i])
        for i, (a, b) in enumerate(
            ((dy2_in, dy2), (hidden_in, hidden), (q_in, q_buf), (k_in, k_buf), (v_in, v_buf), (o_in, o_buf))
        )
    ]
    for load in loads:
        load.start()

    def clear():
        dk_acc[...] = jnp.zeros_like(dk_acc)
        dv_acc[...] = jnp.zeros_like(dv_acc)

    cross_barrier(s, lax.axis_index("head"), ns, n, clear)
    to_sub, to_row = share_of(s, ns, r)

    def copy(src, dst, send, recv, t):
        return pltpu.make_async_remote_copy(
            src_ref=src, dst_ref=dst, send_sem=send, recv_sem=recv, device_id={"seq": t}, device_id_type=MESH
        )

    def do_copy(h):
        return copy(
            do_in.at[:, head_cols(h)], do_buf.at[rows_at(to_row, tl)], ds_.at[h], dr_.at[to_row], h * r + to_sub
        )

    @pl.loop(0, heads)
    def _(h):
        @pl.when(h * r + to_sub != s)
        def _():
            do_copy(h).start()

    block = dy2.shape[1] // ns
    cube = CubeScatter(
        s, ns, lambda b: mm(dy2[:, rows_at(b, block)], hidden[:, : grad_down.shape[0]], TN), block, first, held, later, (ca, cb, cc, cd)
    )
    for load in loads:
        load.wait()
    cube.send_core()
    cube.add_core()

    @pl.when(to_sub == sub)
    def _():
        do_buf[rows_at(to_row, tl), :] = do_in[:, head_cols(mine)]

    scale = HEAD_DIM ** (-0.5)
    unit = scale * LOG2E

    def dq_copy(i, t):
        return copy(dq_low.at[rows_at(i, tl)], dq.at[:, head_cols(mine)], qs.at[i], qr.at[mine], t)

    ones = jnp.ones((8, HEAD_DIM), F32)

    def back_block(i):
        src = source_of(sub, i, ns, r)
        rows = rows_at(i, tl)

        @pl.when(src != s)
        def _():
            copy(do_buf.at[rows], do_buf.at[rows], ds_.at[0], dr_.at[i], s ^ 1).wait_recv()

        q = q_buf[rows, :]
        do = do_buf[rows, :]
        start = first_of_document(docs, src * tl + lax.broadcasted_iota(jnp.int32, (1, tl), 1))
        norm = lse[pl.ds(i, 1), :]
        delta = lax.dot_general(
            ones, do.astype(F32) * o_buf[rows, :], NT,
            precision=lax.Precision.HIGHEST, preferred_element_type=F32,
        )[:1]
        key_at = lax.broadcasted_iota(jnp.int32, (tl, tl), 0)

        def step(j, dq_sum, diagonal):
            at = rows_at(j, tl)
            keys = k_buf[at, :]
            scores = mm(keys, q, NT) * unit
            allowed = key_at >= start - j * tl
            if diagonal:
                allowed = allowed & (key_at <= lax.broadcasted_iota(jnp.int32, (tl, tl), 1))
            p = jnp.where(allowed, jnp.exp2(scores - norm), 0.0)
            dp = mm(v_buf[at, :], do, NT)
            dscore = (p * (dp - delta)).astype(BF16)
            dv_acc[at, :] += mm(p.astype(BF16), do)
            dk_acc[at, :] += mm(dscore, q)
            return dq_sum + mm(dscore, keys, TN)

        dq_sum = lax.fori_loop(0, src, lambda j, c: step(j, c, False), jnp.zeros((tl, HEAD_DIM), F32))
        dq_sum = step(src, dq_sum, True)
        dq_low[rows, :] = (dq_sum * scale).astype(BF16)

        @pl.when(src != s)
        def _():
            dq_copy(i, src).start()

        @pl.when(src == s)
        def _():
            dq[:, head_cols(mine)] = dq_low[rows, :]

    pl.loop(0, blocks - 1)(back_block)
    cube.step(0)
    pl.loop(blocks - 1, blocks)(back_block)
    half = ns // 2

    def pair_copy(w, i):
        src = 2 * i + 1 - parity
        return copy(low.at[w, rows_at(src, tl)], pair.at[w, rows_at(i, tl)], ps.at[w, i], pr.at[w, i], s ^ 1)

    @pl.loop(0, half)
    def _(i):
        at = rows_at(2 * i + 1 - parity, tl)
        low[0, at, :] = (dk_acc[at, :] * scale).astype(BF16)
        pair_copy(0, i).start()
        low[1, at, :] = dv_acc[at, :].astype(BF16)
        pair_copy(1, i).start()

    slot = sub // 2
    outs = (dk, dv)

    def back_copy(w, i):
        dest = 2 * i + parity
        return copy(
            low.at[w, rows_at(dest, tl)], land.at[w, slot, :, head_cols(mine)], gs.at[w, i], gr.at[w, mine, slot], dest
        )

    @pl.loop(0, half)
    def _(i):
        dest = 2 * i + parity
        at = rows_at(dest, tl)
        for w, acc, factor in ((0, dk_acc, scale), (1, dv_acc, 1.0)):
            copy(low.at[w, at], pair.at[w, rows_at(i, tl)], ps.at[w, i], pr.at[w, i], s ^ 1).wait_recv()
            low[w, at, :] = (acc[at, :] * factor + pair[w, rows_at(i, tl), :].astype(F32)).astype(BF16)

            @pl.when(dest != s)
            def _():
                back_copy(w, i).start()

            @pl.when(dest == s)
            def _():
                land[w, slot, :, head_cols(mine)] = low[w, at, :]

    free()

    @pl.loop(0, heads)
    def _(h):
        for w in range(2):
            for k in range(r // 2):

                @pl.when(h * r + 2 * k + parity != s)
                def _():
                    copy(
                        low.at[w, rows_at(0, tl)], land.at[w, k, :, head_cols(h)], gs.at[w, 0], gr.at[w, h, k], s ^ 1
                    ).wait_recv()

    for w in range(2):
        outs[w][...] = functools.reduce(
            lambda a, b: a + b, [land[w, k].astype(F32) for k in range(r // 2)]
        ).astype(BF16)

    @pl.loop(0, heads)
    def _(h):
        @pl.when(h * r + to_sub != s)
        def _():
            do_copy(h).wait_send()
            copy(dq_low.at[rows_at(0, tl)], dq.at[:, head_cols(h)], qs.at[0], qr.at[h], s ^ 1).wait_recv()

    def late():
        for i in range(1, cube.stages):
            cube.step(i)
        grad_down[...] = jnp.transpose(held[0].astype(F32)).astype(BF16)

    def finish():
        @pl.loop(0, blocks)
        def _(i):
            src = source_of(sub, i, ns, r)

            @pl.when(src != s)
            def _():
                dq_copy(i, src).wait_send()

        @pl.loop(0, half)
        def _(i):
            for w in range(2):
                pair_copy(w, i).wait_send()

                @pl.when(2 * i + parity != s)
                def _():
                    back_copy(w, i).wait_send()

        cube.finish()

    return cube.core_sent, late, finish


def cross_barrier(s, z, ns, n, between=None):
    bar = pltpu.get_barrier_semaphore()
    for axis, me, count in (("seq", s, ns), ("head", z, n)):
        for other in range(count):

            @pl.when(other != me)
            def _():
                pl.semaphore_signal(bar, inc=1, device_id={axis: other}, device_id_type=MESH)

    if between is not None:
        between()
    pl.semaphore_wait(bar, ns - 1 + n - 1)


def row_sums(left, right):
    ones = jnp.ones((8, left.shape[1]), F32)
    both = [
        lax.dot_general(ones, x, NT, precision=lax.Precision.HIGHEST, preferred_element_type=F32) for x in (left, right)
    ]
    return jnp.where(lax.broadcasted_iota(jnp.int32, both[0].shape, 0) < 4, both[0], both[1])


def as_column(sums, row):
    pick = (lax.broadcasted_iota(jnp.int32, (8, HEAD_DIM), 0) == row).astype(F32)
    return lax.dot_general(sums, pick, TN, precision=lax.Precision.HIGHEST, preferred_element_type=F32)


class SmallExchange:
    def __init__(self, axis, me, count, land, send_sem, recv_sem):
        self.axis, self.me, self.count, self.land = axis, me, count, land
        self.send_sem, self.recv_sem = send_sem, recv_sem

    def copy(self, slot, to):
        return remote(self.land.at[slot], self.land.at[slot], self.send_sem.at[to], self.recv_sem.at[slot], self.axis, to)

    def each(self, act):
        @pl.loop(0, self.count)
        def _(other):
            @pl.when(other != self.me)
            def _():
                act(other)

    def start(self):
        self.each(lambda other: self.copy(self.me, other).start())

    def receive(self):
        self.each(lambda other: self.copy(other, other).wait_recv())

    def finish(self):
        self.each(lambda other: self.copy(self.me, other).wait_send())


def turn(x, cos, sin):
    return x * cos + pltpu.roll(x, HEAD_DIM // 2, 1) * sin


def turn_back(x, cos, sin):
    return x * cos - pltpu.roll(x, HEAD_DIM // 2, 1) * sin


def project_part(
    n, ns, depth_full,
    tok, wq, wk, wv, wo, gate, gq, gk, docs, turns,
    x_out, w_out, more_out, q_out, k_out, totals, cos, sin,
    q_rot, k_rot, v_low, q_raw, k_raw, x, w, own, land, lsem, ags, agr, cgs, cgr, egs, egr, ss, sr,
):
    s, z = lax.axis_index("seq"), lax.axis_index("head")
    rows, depth = tok.shape
    block, lw = wq.shape
    heads = lw // HEAD_DIM
    cross_barrier(s, z, ns, n)
    mine = rows_at(s, block)

    def head_gain(h):
        return head_cols(z * heads + h)

    loads = [pltpu.make_async_copy(tok, x.at[rows_at(z, rows)], lsem.at[0])] + [
        pltpu.make_async_copy(m, w.at[mine, pl.ds(i * lw, lw)], lsem.at[i + 1]) for i, m in enumerate((wq, wk, wv))
    ]
    for copy in loads:
        copy.start()
    loads[0].wait()
    cube = CubeGather(s, ns, w, block, cgs, cgr)
    own_more = pltpu.make_async_copy(own, more_out.at[mine], lsem.at[8])
    cube_e = CubeGather(s, ns, more_out, block, egs, egr, own)
    levels = cube.levels

    def weights(k):
        if k == 0:
            cube.level(0)
        else:
            for i in range(1, levels):
                cube.level(i)
                if i == levels - 2:
                    cube_e.start()

    def start_weights():
        for copy in loads[1:]:
            copy.wait()
        cube.start()

    def multiply(src):
        at = rows_at(src, rows)
        for i, to in enumerate((q_raw, k_raw)):
            to[at, :] = mm(x[at, :], w[:, i * lw : (i + 1) * lw])
        v_low[at, :] = mm(x[at, :], w[:, 2 * lw :]).astype(BF16)

    part = rows // AG_CHUNKS

    def copy(src, c, up):
        at = pl.ds(pl.multiple_of(src * rows + c * part, part), part)
        return remote(x.at[at], x.at[at], ags.at[up, src, c], agr.at[src, c], "head", z + 1 if up else z - 1)

    more = (z > 0, z < n - 1)
    for c in range(AG_CHUNKS):
        for up in (0, 1):

            @pl.when(more[up])
            def _():
                copy(z, c, up).start()

    start_weights()
    own[:, :lw] = jnp.transpose(wo[...].astype(F32)).astype(BF16)
    own[:, lw:] = gate[:, : own.shape[1] - lw]
    own_more.start()
    token = s * x.shape[0] + lax.broadcasted_iota(jnp.int32, cos.shape, 0)
    angle = (token - first_of_document(docs, token)).astype(F32) * turns[...]
    flip = jnp.where(lax.broadcasted_iota(jnp.int32, cos.shape, 1) < HEAD_DIM // 2, -1.0, 1.0)
    cos[...] = jnp.cos(angle)
    sin[...] = jnp.sin(angle) * flip

    def sides(k):
        return ((z + k, z + k < n, 0), (z - k, z - k >= 0, 1))

    for k in range(1, n):
        for c in range(AG_CHUNKS):
            for src, there, up in sides(k):

                @pl.when(there)
                def _():
                    copy(src, c, up).wait_recv()

                    @pl.when(more[up])
                    def _():
                        copy(src, c, up).start()

        if k <= 2:
            weights(k - 1)
        if k == min(2, n - 1):
            multiply(z)
            for src, there, _ in sides(1):
                pl.when(there)(functools.partial(multiply, src))
        if k > 1:
            for src, there, _ in sides(k):
                pl.when(there)(functools.partial(multiply, src))

    outs = [
        pltpu.make_async_copy(a, b, lsem.at[4 + i])
        for i, (a, b) in enumerate(((x, x_out), (w, w_out), (q_raw, q_out), (k_raw, k_out)))
    ]
    for out in outs:
        out.start()
    totals[...] = row_sums(q_raw[...] * q_raw[...], k_raw[...] * k_raw[...])
    land[z] = totals[...]
    small = SmallExchange("head", z, n, land, ss, sr)
    small.start()
    small.receive()
    total = land[0]
    for k in range(1, n):
        total = total + land[k]
    totals[...] = total
    for row, raw, gain, to in ((0, q_raw, gq, q_rot), (4, k_raw, gk, k_rot)):
        scale = lax.rsqrt(as_column(total, row) / depth_full + epsilon)
        for h in range(heads):
            cols = slice(h * HEAD_DIM, (h + 1) * HEAD_DIM)
            to[:, cols] = turn(raw[:, cols] * scale * gain[:, head_gain(h)], cos[...], sin[...]).astype(BF16)
        if row == 0:
            cube_e.level(0)

    def late():
        for i in range(1, levels):
            cube_e.level(i)

    def finish():
        small.finish()
        cube.finish()
        cube_e.finish()
        for out in [*outs, own_more]:
            out.wait()

        @pl.loop(0, n)
        def _(src):
            for c in range(AG_CHUNKS):

                @pl.when((src >= z) & (z > 0))
                def _():
                    copy(src, c, 0).wait_send()

                @pl.when((src <= z) & (z < n - 1))
                def _():
                    copy(src, c, 1).wait_send()

    return late, finish


def front_kernel(n, ns, heads, depth_full, *refs):
    ins, refs = refs[:10], refs[10:]
    made, refs = refs[:8], refs[8:]
    attended, refs = refs[:7], refs[7:]
    first, second = refs[:18], refs[18:]
    late, finish = project_part(n, ns, depth_full, *ins, *made, *first)
    attend_part(ns, heads, *first[:3], ins[8], ins[5], *attended, *second, late=late)
    finish()


def run_front(n, ns, heads, tok, wq, wk, wv, wo, gate, gq, gk, docs, turns):
    rows, depth = tok.shape
    tl = rows * n
    block, lw = wq.shape
    r = ns // heads
    nq = ns // r * tl
    nk = ns * tl
    ff = gate.shape[1]
    early = early_part(ff)
    dma = pltpu.SemaphoreType.DMA
    shape = jax.ShapeDtypeStruct
    return pl.pallas_call(
        functools.partial(front_kernel, n, ns, heads, depth),
        out_shape=(
            shape((tl, depth), BF16),
            shape((depth, 3 * lw), BF16),
            shape((depth, lw + early), BF16),
            shape((tl, lw), F32),
            shape((tl, lw), F32),
            shape((8, tl), F32),
            shape((tl, HEAD_DIM), F32),
            shape((tl, HEAD_DIM), F32),
            shape((tl, lw), BF16),
            shape((nq, HEAD_DIM), BF16),
            shape((nk, HEAD_DIM), BF16),
            shape((nk, HEAD_DIM), BF16),
            shape((nq, HEAD_DIM), F32),
            shape((ns // r, tl), F32),
            shape((depth, ff - early - last_part(ff)), BF16),
        ),
        in_specs=[ANY] * 4 + [VMEM] * 4 + [SMEM, VMEM],
        out_specs=(ANY,) * 5 + (VMEM,) * 4 + (ANY,) * 3 + (VMEM,) * 2 + (ANY,),
        scratch_shapes=[
            pltpu.VMEM((tl, lw), BF16),
            pltpu.VMEM((tl, lw), BF16),
            pltpu.VMEM((tl, lw), BF16),
            pltpu.VMEM((tl, lw), F32),
            pltpu.VMEM((tl, lw), F32),
            pltpu.VMEM((tl, depth), BF16),
            pltpu.VMEM((depth, 3 * lw), BF16),
            pltpu.VMEM((block, lw + early), BF16),
            pltpu.VMEM((n, 8, tl), F32),
            dma((9,)),
            dma((2, n, AG_CHUNKS)), dma((n, AG_CHUNKS)),
            *CubeGather.sems(ns), *CubeGather.sems(ns),
            dma((n,)), dma((n,)),
            pltpu.VMEM((nq, HEAD_DIM), BF16),
            pltpu.VMEM((nk, HEAD_DIM), BF16),
            pltpu.VMEM((nk, HEAD_DIM), BF16),
            pltpu.VMEM((nq, HEAD_DIM), BF16),
            dma((heads,)), dma((ns // r,)),
            dma((2, ns)), dma((ns,)),
            dma((2, ns)), dma((ns,)),
            dma((ns // r,)), dma((heads,)),
            dma((4,)),
            *CubeGather.sems(ns),
        ],
        compiler_params=pltpu.CompilerParams(
            collective_id=5, has_side_effects=True, vmem_limit_bytes=VMEM_BYTES
        ),
        cost_estimate=pl.CostEstimate(flops=6 * 10**9, bytes_accessed=30 * 10**6, transcendentals=5 * 10**6),
        name="front",
    )(tok, wq, wk, wv, wo, gate, gq, gk, docs, turns)


def input_part(
    n, ns, depth_full, sent, late,
    dq, dk, dv, q_raw, k_raw, totals, gq, gk, cos, sin, x_in, w_in, att, dy1_in, attn_part, mlp_part,
    total, grad_q, grad_k, grad_v, grad_o, grad_down, gains,
    dy2, hidden, first, q_back, k_back,
    w, dy1, lsem, dqkv, inner, land, message, message_z, gain_land,
    held, later, c0s, c0r, c1s, c1r,
    held_o, later_o, o0s, o0r, o1s, o1r,
    ss, sr, ms, mr, zs, zr, s1s, s1r,
):
    s, z = lax.axis_index("seq"), lax.axis_index("head")
    rows, depth = total.shape
    tl, lw = dq.shape
    block = depth // ns
    heads = lw // HEAD_DIM

    def head_gain(h):
        return head_cols(z * heads + h)

    sums = totals[...]
    scales = [lax.rsqrt(as_column(sums, row) / depth_full + epsilon) for row in (0, 4)]
    todo = ((dq, q_raw, gq, q_back), (dk, k_raw, gk, k_back))
    products = []

    x = dy2
    l_y = pltpu.make_async_copy(dy1_in, dy1, lsem.at[0])
    l_w = pltpu.make_async_copy(w_in, w, lsem.at[1])
    l_x = pltpu.make_async_copy(x_in, x, lsem.at[2])

    def turn_all():
        message[...] = jnp.zeros_like(message)
        for i, (grad, raw, gain, back) in enumerate(todo):
            product = jnp.zeros((tl, HEAD_DIM), F32)
            for h in range(heads):
                cols = slice(h * HEAD_DIM, (h + 1) * HEAD_DIM)
                hat = raw[h * tl : (h + 1) * tl, :] * scales[i]
                turned = turn_back(grad[:, cols].astype(F32), cos[...], sin[...])
                message[0, pl.ds(i, 1), cols] = jnp.sum(turned * hat, axis=0, keepdims=True)
                turned = turned * gain[:, head_gain(h)]
                back[h * tl : (h + 1) * tl, :] = turned
                product = product + turned * hat
            products.append(product)
        inner[z] = row_sums(*products)
        for t in range(1, ns):
            message[t, pl.ds(0, 2), pl.ds(0, lw)] = message[0, pl.ds(0, 2), pl.ds(0, lw)]
        for t in range(ns):
            for i, part in enumerate((attn_part, mlp_part)):
                message[t, pl.ds(i, 1), pl.ds(lw, block)] = part[:, t * block : (t + 1) * block]

    turn_all()
    small = SmallExchange("head", z, n, inner, ss, sr)
    small.start()

    def message_copy(t, frm):
        return remote(message.at[t], message_z.at[frm], ms.at[t], mr.at[frm], "seq", t)

    def each_seq(act):
        @pl.loop(0, ns)
        def _(t):
            @pl.when(t != s)
            def _():
                act(t)

    message_z[s] = message[s]
    each_seq(lambda t: message_copy(t, s).start())
    dqkv[:, 2 * lw :] = dv[...]
    l_y.wait()
    ff = hidden.shape[1]

    def early_block(b):
        cols = rows_at(b, block)
        return jnp.concatenate([mm(dy1[:, cols], att[...], TN), mm(dy2[:, cols], hidden[:, ff - lw :], TN)], axis=1)

    cube_o = CubeScatter(
        s, ns, early_block, block, first.at[:, :, pl.ds(0, 2 * lw)], held_o, later_o, (o0s, o0r, o1s, o1r)
    )
    sent()
    cube_o.send_core()
    cube_o.add_core()
    l_x.start()
    late()
    small.receive()
    sums = inner[0]
    for k in range(1, n):
        sums = sums + inner[k]
    for i, (grad, raw, gain, back) in enumerate(todo):
        mean = as_column(sums, 4 * i) / depth_full
        for h in range(heads):
            cols = slice(h * HEAD_DIM, (h + 1) * HEAD_DIM)
            to = slice(i * lw + h * HEAD_DIM, i * lw + (h + 1) * HEAD_DIM)
            dqkv[:, to] = (scales[i] * (back[h * tl : (h + 1) * tl, :] - raw[h * tl : (h + 1) * tl, :] * scales[i] * mean)).astype(BF16)

    width = depth // STEPS

    def weight_block(b):
        cols = rows_at(b, block)
        return mm(x[:, cols], dqkv[...], TN)

    def in_part(d, c):
        return mm(dqkv[rows_at(d, rows), :], w[rows_at(c, width), :], NT)

    cube = CubeScatter(s, ns, weight_block, block, first, held, later, (c0s, c0r, c1s, c1r))
    line = LineScatter(z, n, in_part, land, s1s, s1r, total, True)
    half = ns // 2

    def task(slot):
        for i, act in enumerate((cube.send_core, cube.add_core)):
            low = 1 + i * (half // 2)

            @pl.when((slot >= low) & (slot < low + half // 2))
            def _():
                for j in range(2):
                    act(2 * (slot - low) + j)

    done = 1 + half
    l_w.wait()
    l_x.wait()
    cube_o.core_sent()
    line.run(0, done, None, task)
    line.run(done, done + 3)
    for i in range(cube.stages - 1):
        cube_o.step(i)
    line.run(done + 3, line.slots)
    for i in range(cube.stages - 1):
        cube.step(i)

    each_seq(lambda t: message_copy(t, t).wait_recv())
    received = message_z[0]
    for t in range(1, ns):
        received = received + message_z[t]
    each_seq(lambda t: message_copy(t, s).wait_send())
    gain_land[z] = received
    rounds = SmallExchange("head", z, n, gain_land, zs, zr)
    rounds.start()
    line.own()
    cube_o.step(cube.stages - 1)
    grad_o[...] = jnp.transpose(held_o[0, :, :lw].astype(F32)).astype(BF16)
    grad_down[...] = jnp.transpose(held_o[0, :, lw:].astype(F32)).astype(BF16)
    cube.step(cube.stages - 1)
    for i, to in enumerate((grad_q, grad_k, grad_v)):
        to[...] = held[0, :, i * lw : (i + 1) * lw]
    rounds.receive()
    at = s * block
    gains[...] = jnp.zeros_like(gains)
    gains[0:2, :] = gain_land[at // lw, pl.ds(0, 2), pl.ds(pl.multiple_of(at % lw, block), block)]
    both = gain_land[0, pl.ds(0, 2), pl.ds(lw, block)]
    for k in range(1, n):
        both = both + gain_land[k, pl.ds(0, 2), pl.ds(lw, block)]
    gains[2:4, :] = both
    cube.core_sent()
    cube.finish()
    cube_o.finish()
    line.finish()
    small.finish()
    rounds.finish()


def back_kernel(n, ns, heads, depth_full, *refs):
    ins, more, refs = refs[:9], refs[9:22], refs[22:]
    down, outs, refs = refs[0], refs[1:8], refs[8:]
    held, rest, raw_sem = refs[:32], refs[32:-1], refs[-1]
    dy2, hidden, dq, dk, dv, dk_acc, first = held[4], held[5], *held[7:10], held[12], held[17]
    half, tl = dk_acc.shape[0] // 2, dq.shape[0]
    back, raws = ([acc.at[pl.ds(i * half, tl * heads)] for i in range(2)] for acc in (dk_acc, held[13]))
    raw_loads = [
        pltpu.make_async_copy(m.at[:, pl.ds(h * HEAD_DIM, HEAD_DIM)], to.at[pl.ds(h * tl, tl)], raw_sem.at[i, h])
        for i, (m, to) in enumerate(zip(more[:2], raws))
        for h in range(heads)
    ]

    def free():
        for load in raw_loads:
            load.start()

    starts = [
        pltpu.make_async_copy(more[10], rest[1], rest[2].at[0]), pltpu.make_async_copy(more[8], rest[0], rest[2].at[1])
    ]
    for load in starts:
        load.start()
    sent, late, finish = attend_back_part(n, ns, heads, free, *ins, down, *held)
    for load in raw_loads:
        load.wait()
    input_part(n, ns, depth_full, sent, late, dq, dk, dv, *raws, *more[2:], *outs, dy2, hidden, first, *back, *rest)
    finish()


def run_back(n, ns, heads, do, docs, q, k, v, o, lse, dy2, hidden, *more):
    q_raw, k_raw, totals, gq, gk, cos, sin, x, w, att, dy1, attn_part, mlp_part = more
    tl, lw = do.shape
    rows, depth = tl // n, x.shape[1]
    block = depth // ns
    ff = hidden.shape[1]
    r = ns // heads
    nq = ns // r * tl
    nk = ns * tl
    dma = pltpu.SemaphoreType.DMA
    shape = jax.ShapeDtypeStruct
    first, held, later, *cube_sems = CubeScatter.scratch(ns, block, 3 * lw)
    return pl.pallas_call(
        functools.partial(back_kernel, n, ns, heads, depth),
        out_shape=(shape((ff - lw, block), BF16), shape((rows, depth), F32))
        + (shape((block, lw), BF16),) * 3
        + (shape((lw, block), BF16), shape((lw, block), BF16), shape((8, block), F32)),
        in_specs=[VMEM, SMEM] + [ANY] * 4 + [VMEM] + [ANY] * 4 + [VMEM] * 5 + [ANY] * 2 + [VMEM, ANY, VMEM, VMEM],
        out_specs=(VMEM,) * 8,
        scratch_shapes=[
            pltpu.VMEM((nq, HEAD_DIM), BF16),
            pltpu.VMEM((nk, HEAD_DIM), BF16),
            pltpu.VMEM((nk, HEAD_DIM), BF16),
            pltpu.VMEM((nq, HEAD_DIM), F32),
            pltpu.VMEM(dy2.shape, BF16),
            pltpu.VMEM(hidden.shape, BF16),
            dma((6,)),
            pltpu.VMEM((tl, lw), BF16),
            pltpu.VMEM((tl, lw), BF16),
            pltpu.VMEM((tl, lw), BF16),
            pltpu.VMEM((nq, HEAD_DIM), BF16),
            pltpu.VMEM((nq, HEAD_DIM), BF16),
            pltpu.VMEM((nk, HEAD_DIM), F32),
            pltpu.VMEM((nk, HEAD_DIM), F32),
            pltpu.VMEM((2, nk, HEAD_DIM), BF16),
            pltpu.VMEM((2, nk // 2, HEAD_DIM), BF16),
            pltpu.VMEM((2, r // 2, tl, lw), BF16),
            *CubeScatter.scratch(ns, block, ff - lw),
            dma((heads,)), dma((ns // r,)),
            dma((2, ns // 2)), dma((2, ns // 2)),
            dma((2, ns // 2)), dma((2, heads, r // 2)),
            dma((ns // r,)), dma((heads,)),
            pltpu.VMEM(w.shape, BF16),
            pltpu.VMEM((tl, depth), BF16),
            dma((3,)),
            pltpu.VMEM((tl, 3 * lw), BF16),
            pltpu.VMEM((n, 8, tl), F32),
            pltpu.VMEM((2, n, STEPS, rows, depth // STEPS), BF16),
            pltpu.VMEM((ns, 8, lw + block), F32),
            pltpu.VMEM((ns, 8, lw + block), F32),
            pltpu.VMEM((n, 8, lw + block), F32),
            held, later, *cube_sems,
            *CubeScatter.scratch(ns, block, 2 * lw)[1:],
            dma((n,)), dma((n,)),
            dma((ns,)), dma((ns,)),
            dma((n,)), dma((n,)),
            *line_sems(n)["scatter"],
            dma((2, heads)),
        ],
        compiler_params=pltpu.CompilerParams(
            collective_id=6, has_side_effects=True, vmem_limit_bytes=VMEM_BYTES
        ),
        cost_estimate=pl.CostEstimate(flops=16 * 10**9, bytes_accessed=40 * 10**6, transcendentals=5 * 10**6),
        name="back",
    )(do, docs, q, k, v, o, lse, dy2, hidden, *more)


def widen_kernel(count, *refs):
    spec = WIDEN
    ins, rest = refs[:count], refs[count:]
    outs, rest = rest[: len(spec)], rest[len(spec) :]
    held, rest = rest[:count], rest[count:]
    wide, (load_sem, store_sem) = rest[: len(spec)], rest[len(spec) :]
    loads = [pltpu.make_async_copy(a, b, load_sem.at[i]) for i, (a, b) in enumerate(zip(ins, held))]
    stores = [pltpu.make_async_copy(a, b, store_sem.at[i]) for i, (a, b) in enumerate(zip(wide, outs))]
    for copy in loads:
        copy.start()
    at = 0
    for (parts, stacked), to, store in zip(spec, wide, stores):
        row = 0
        for i in range(at, at + parts):
            loads[i].wait()
            block = held[i][...].astype(to.dtype)
            if stacked:
                to[row : row + block.shape[0], :] = block
                row += block.shape[0]
            elif i == at:
                to[...] = block
            else:
                to[...] += block
        at += parts
        store.start()
    for copy in stores:
        copy.wait()


WIDEN = ((1, False), (1, False), (1, False), (2, True), (1, False), (1, False), (1, False), (1, False), (2, False))


def run_widen(arrays, outs):
    dma = pltpu.SemaphoreType.DMA
    return pl.pallas_call(
        functools.partial(widen_kernel, len(arrays)),
        out_shape=tuple(outs),
        in_specs=[ANY] * len(arrays),
        out_specs=(ANY,) * len(outs),
        scratch_shapes=[pltpu.VMEM(a.shape, a.dtype) for a in arrays]
        + [pltpu.VMEM(o.shape, o.dtype) for o in outs]
        + [dma((len(arrays),)), dma((len(outs),))],
        compiler_params=pltpu.CompilerParams(vmem_limit_bytes=VMEM_BYTES),
        name="widen",
    )(*arrays)


def on_device(
    tokens,
    cotangent,
    doc_lengths,
    q_weight,
    k_weight,
    v_weight,
    o_weight,
    gate_weight,
    up_weight,
    down_weight,
    q_gain,
    k_gain,
    attn_gain,
    mlp_gain,
):
    ns, nz = lax.axis_size("seq"), lax.axis_size("head")
    lw = q_weight.shape[1]
    heads = lw // HEAD_DIM
    block, ff = gate_weight.shape
    gq, gk = q_gain[None], k_gain[None]
    frequency = jnp.power(rope_base, -(jnp.arange(HEAD_DIM) % (HEAD_DIM // 2)).astype(F32) * (2.0 / HEAD_DIM))

    x, w, more, q_raw, k_raw, totals, cos, sin, attended, q_held, k_held, v_held, o_held, lse, gate_b = run_front(
        nz, ns, heads, tokens, q_weight, k_weight, v_weight, o_weight, gate_weight, gq, gk, doc_lengths, frequency[None]
    )
    output, h1r, branch, hidden, dy2, dg, du, mlp_part, up = run_forward(
        nz, ns, attended, tokens, cotangent, more, gate_b, gate_weight, up_weight, down_weight, attn_gain[None], mlp_gain[None]
    )
    middle, dy1, datt, attn_part, grad_gate, grad_up = run_backward(
        nz, ns, dg, du, h1r, cotangent, branch, more, gate_b, up, attn_gain[None]
    )
    down_a, last, grad_q, grad_k, grad_v, grad_o, down_b, gains = run_back(
        nz, ns, heads, datt, doc_lengths, q_held, k_held, v_held, o_held, lse, dy2, hidden,
        q_raw, k_raw, totals, gq, gk, cos, sin, x, w, attended, dy1, attn_part, mlp_part,
    )
    shape = jax.ShapeDtypeStruct
    small = shape((block, lw), F32)
    output, grad_gate, grad_up, grad_down, grad_q, grad_k, grad_v, grad_o, input_grad = run_widen(
        (output, grad_gate, grad_up, down_a, down_b, grad_q, grad_k, grad_v, grad_o, middle, last),
        (
            shape(output.shape, BF16),
            shape((block, ff), F32),
            shape((block, ff), F32),
            shape((ff, block), F32),
            small, small, small,
            shape((lw, block), F32),
            shape(middle.shape, F32),
        ),
    )
    return (
        output,
        input_grad,
        grad_q,
        grad_k,
        grad_v,
        grad_o,
        grad_gate,
        grad_up,
        grad_down,
        gains[0],
        gains[1],
        gains[2],
        gains[3],
    )


def solution(mesh):
    in_specs = (
        P(("seq", "head"), None),
        P(("seq", "head"), None),
        P(),
        P("seq", "head"),
        P("seq", "head"),
        P("seq", "head"),
        P("head", "seq"),
        P("seq", "head"),
        P("seq", "head"),
        P("head", "seq"),
        P(),
        P(),
        P(),
        P(),
    )
    out_specs = (
        P(("seq", "head"), None),
        P(("seq", "head"), None),
        P("seq", "head"),
        P("seq", "head"),
        P("seq", "head"),
        P("head", "seq"),
        P("seq", "head"),
        P("seq", "head"),
        P("head", "seq"),
        P("seq"),
        P("seq"),
        P("seq"),
        P("seq"),
    )
    return jax.shard_map(
        on_device, mesh=mesh, in_specs=in_specs, out_specs=out_specs, check_vma=False
    )
```

```python
import functools

import jax
import jax.numpy as jnp
from jax import lax
from jax.experimental import pallas as pl
from jax.experimental.pallas import tpu as pltpu
from jax.sharding import PartitionSpec as P

HEAD_DIM = 128
epsilon = 1e-06
rope_base = 500000.0

MESH = pl.DeviceIdType.MESH
F32 = jnp.float32
BF16 = jnp.bfloat16
STEPS = 4
LAG = 1
EARLY = (10, 16)
AG_CHUNKS = 2
VMEM_BYTES = 62 * 1024 * 1024
ANY = pl.BlockSpec(memory_space=pl.ANY)
VMEM = pl.BlockSpec(memory_space=pltpu.VMEM)
SMEM = pl.BlockSpec(memory_space=pltpu.SMEM)
NN = (((1,), (0,)), ((), ()))
NT = (((1,), (1,)), ((), ()))
TN = (((0,), (0,)), ((), ()))


def first_of_document(docs, token):
    end, first = jnp.int32(0), jnp.zeros_like(token)
    for i in range(docs.shape[0]):
        end = end + docs[i]
        first = first + jnp.where(token >= end, docs[i], 0)
    return first


def mm(left, right, dims=NN):
    return lax.dot_general(left, right, dims, preferred_element_type=F32)


def early_part(ff):
    return ff * EARLY[0] // EARLY[1] // HEAD_DIM * HEAD_DIM


def last_part(ff):
    return ff // STEPS


def rows_at(index, count):
    return pl.ds(pl.multiple_of(index * count, count), count)


def cube_barrier(s, z, ns, n, between=None):
    bar = pltpu.get_barrier_semaphore()
    bits = [1 << i for i in range(ns.bit_length() - 1)]
    for bit in bits:
        pl.semaphore_signal(bar, inc=1, device_id={"seq": s ^ bit}, device_id_type=MESH)
    for other, there in ((z - 1, z > 0), (z + 1, z < n - 1)):

        @pl.when(there)
        def _():
            pl.semaphore_signal(bar, inc=1, device_id={"head": other}, device_id_type=MESH)

    if between is not None:
        between()
    pl.semaphore_wait(bar, len(bits) + (z > 0).astype(jnp.int32) + (z < n - 1).astype(jnp.int32))


def line_gather(z, n, buf, rows, send_sem, recv_sem, use, hooks=(), ready=None):
    part = rows // AG_CHUNKS

    def copy(src, c, up):
        at = pl.ds(pl.multiple_of(src * rows + c * part, part), part)
        return pltpu.make_async_remote_copy(
            src_ref=buf.at[at],
            dst_ref=buf.at[at],
            send_sem=send_sem.at[up, src, c],
            recv_sem=recv_sem.at[src, c],
            device_id={"head": z + 1 if up else z - 1},
            device_id_type=MESH,
        )

    more = (z > 0, z < n - 1)
    for c in range(AG_CHUNKS):
        for up in (0, 1):

            @pl.when(more[up])
            def _():
                copy(z, c, up).start()

    if ready is not None:
        ready()
    use(z)

    @pl.loop(1, n)
    def _(k):
        sides = ((z + k, z + k < n, 0), (z - k, z - k >= 0, 1))
        for c in range(AG_CHUNKS):
            for src, there, up in sides:

                @pl.when(there)
                def _():
                    copy(src, c, up).wait_recv()

                    @pl.when(more[up])
                    def _():
                        copy(src, c, up).start()

        for src, there, up in sides:

            @pl.when(there)
            def _():
                use(src)

        for i, hook in enumerate(hooks):
            pl.when(k == i + 1)(hook)

    @pl.loop(0, n)
    def _(src):
        for c in range(AG_CHUNKS):

            @pl.when((src >= z) & (z > 0))
            def _():
                copy(src, c, 0).wait_send()

            @pl.when((src <= z) & (z < n - 1))
            def _():
                copy(src, c, 1).wait_send()


class LineScatter:
    def __init__(self, z, n, partial, land, send_sem, recv_sem, total, own_late=False):
        self.own_late = own_late
        self.z, self.n, self.partial, self.land, self.total = z, n, partial, land, total
        self.send_sem, self.recv_sem = send_sem, recv_sem

    def copy(self, d, c, up):
        return pltpu.make_async_remote_copy(
            src_ref=self.land.at[up, d, c],
            dst_ref=self.land.at[up, d, c],
            send_sem=self.send_sem.at[up, d, c],
            recv_sem=self.recv_sem.at[up, d, c],
            device_id={"head": self.z + 1 if up else self.z - 1},
            device_id_type=MESH,
        )

    @property
    def slots(self):
        return (self.n - 1) * (STEPS + LAG)

    def run(self, low, high, before=None, after=None):
        z, n, land = self.z, self.n, self.land

        @pl.loop(low, high)
        def _(slot):
            if before is not None:
                before(slot)
            for up in (1, 0):
                t = slot - (z if up else n - 1 - z) * LAG
                j = t // STEPS
                c = t - j * STEPS
                d = n - 1 - j if up else j
                first = z == 0 if up else z == n - 1
                there = (t >= 0) & (j < n - 1) & ((d > z) if up else (d < z))

                @pl.when(there)
                def _():
                    mine = self.partial(d, c)

                    @pl.when(first)
                    def _():
                        land[up, d, c] = mine.astype(land.dtype)

                    @pl.when(jnp.logical_not(first))
                    def _():
                        self.copy(d, c, up).wait_recv()
                        land[up, d, c] = (land[up, d, c].astype(F32) + mine).astype(land.dtype)

                    self.copy(d, c, up).start()

            if self.own_late:
                @pl.when(slot >= self.slots - STEPS)
                def _():
                    self.own_chunk(slot - (self.slots - STEPS))

            if after is not None:
                after(slot)

    def own_chunk(self, c):
        width = self.total.shape[1] // STEPS
        self.total[:, rows_at(c, width)] = self.partial(self.z, c)

    def start_own(self):
        pl.loop(0, STEPS)(self.own_chunk)

    def own(self):
        z, n, total = self.z, self.n, self.total
        width = total.shape[1] // STEPS

        @pl.loop(0, STEPS)
        def _(c):
            at = rows_at(c, width)
            for there, up in ((z > 0, 1), (z < n - 1, 0)):

                @pl.when(there)
                def _():
                    self.copy(z, c, up).wait_recv()
                    total[:, at] += self.land[up, z, c].astype(F32)

    def finish(self):
        @pl.loop(0, self.n * STEPS)
        def _(t):
            d, c = t // STEPS, t % STEPS
            for there, up in ((d > self.z, 1), (d < self.z, 0)):

                @pl.when(there)
                def _():
                    self.copy(d, c, up).wait_send()


def line_sems(n):
    dma = pltpu.SemaphoreType.DMA
    return {
        "gather": [dma((2, n, AG_CHUNKS)), dma((n, AG_CHUNKS))],
        "scatter": [dma((2, n, STEPS)), dma((2, n, STEPS))],
    }


BLOCK = 64


def row_scale(block):
    return lax.rsqrt(jnp.mean(block * block, axis=-1, keepdims=True) + epsilon)


def norm_back(e, normed, scale, gain):
    g = e * gain
    return scale * (g - normed * jnp.mean(g * normed, axis=-1, keepdims=True))


def sigmoid(x):
    return 1.0 / (1.0 + jnp.exp(-x))


def subsets(bits):
    found = [0]
    for bit in bits:
        found += [bit | other for other in found]
    return found


def orders_of(ns):
    chips = [1 << i for i in range(1, ns.bit_length() - 1)]
    return (chips, chips[::-1])


def remote(src, dst, send, recv, axis, to):
    return pltpu.make_async_remote_copy(
        src_ref=src, dst_ref=dst, send_sem=send, recv_sem=recv, device_id={axis: to}, device_id_type=MESH
    )


class CubeGather:
    def __init__(self, s, ns, buf, rows, send_sem, recv_sem, own=None):
        self.own = own
        self.s, self.buf, self.rows, self.send_sem, self.recv_sem = s, buf, rows, send_sem, recv_sem
        self.orders = [order + [1] for order in orders_of(ns)]

    def copy(self, half, bit, block):
        part = self.rows // 2
        at = pl.ds(pl.multiple_of(block * self.rows + half * part, part), part)
        source = self.buf.at[at]
        if block is self.s and self.own is not None:
            source = self.own.at[pl.ds(half * part, part)]
        return remote(
            source, self.buf.at[at],
            self.send_sem.at[bit.bit_length() - 1, block, half], self.recv_sem.at[block, half],
            "seq", self.s ^ bit,
        )

    @property
    def levels(self):
        return len(self.orders[0])

    def start(self):
        for i in range(self.levels):
            for half, order in enumerate(self.orders):
                self.copy(half, order[i], self.s).start()

    def level(self, i):
        for j in range(2**i):
            for half, order in enumerate(self.orders):
                block = self.s ^ order[i] ^ subsets(order[:i])[j]
                self.copy(half, order[i], block).wait_recv()
                for bit in order[i + 1 :]:
                    self.copy(half, bit, block).start()

    def finish(self):
        for half, order in enumerate(self.orders):
            for i, bit in enumerate(order):
                for other in subsets(order[:i]):
                    self.copy(half, bit, self.s ^ other if other else self.s).wait_send()

    @staticmethod
    def sems(ns):
        dma = pltpu.SemaphoreType.DMA
        return [dma((ns.bit_length() - 1, ns, 2)), dma((ns, 2))]


class CubeScatter:
    def __init__(self, s, ns, block, rows, first, held, later, sems):
        self.s, self.block, self.rows = s, block, rows
        self.first, self.held, self.later = first, held, later
        self.send0, self.recv0, self.send1, self.recv1 = sems
        self.orders = orders_of(ns)
        self.half = ns // 2

    def core_copy(self, j):
        return remote(self.first.at[j], self.held.at[j], self.send0.at[j], self.recv0.at[j], "seq", self.s ^ 1)

    def send_core(self, j=None):
        if j is None:
            pl.loop(0, self.half)(self.send_core)
            return
        j = self.half - 1 - j
        self.first[j] = self.block(self.s ^ (2 * j + 1)).astype(BF16)
        self.core_copy(j).start()

    def base(self, i):
        return sum(2 ** (self.stages - 1 - k) for k in range(i))

    def move(self, i, half, slot, other):
        part = self.rows // 2
        return remote(
            self.held.at[(self.orders[half][i] | other) >> 1, pl.ds(half * part, part)],
            self.later.at[half, slot], self.send1.at[half, slot], self.recv1.at[half, slot],
            "seq", self.s ^ self.orders[half][i],
        )

    def moves(self, i):
        part = self.rows // 2
        for half, order in enumerate(self.orders):
            for j, other in enumerate(subsets(order[i + 1 :])):
                slot = self.base(i) + j
                yield other >> 1, pl.ds(half * part, part), half, slot, self.move(i, half, slot, other)

    def add_core(self, j=None):
        if j is None:
            pl.loop(0, self.half)(self.add_core)
            return
        j = self.half - 1 - j
        mine = self.block(self.s ^ (2 * j))
        self.core_copy(j).wait_recv()
        self.held[j] = (self.held[j].astype(F32) + mine).astype(BF16)
        for half, order in enumerate(self.orders):
            for slot, other in enumerate(subsets(order[1:])):

                @pl.when(j == (order[0] | other) >> 1)
                def _():
                    self.move(0, half, slot, other).start()

    def send(self, i):
        for *_, copy in self.moves(i):
            copy.start()

    def take(self, i):
        for j, at, half, slot, copy in self.moves(i):
            copy.wait_recv()
            self.held[j, at] = (self.held[j, at].astype(F32) + self.later[half, slot].astype(F32)).astype(BF16)

    def step(self, i):
        self.take(i)
        if i + 1 < self.stages:
            self.send(i + 1)

    @property
    def stages(self):
        return len(self.orders[0])

    def core_sent(self):
        @pl.loop(0, self.half)
        def _(j):
            self.core_copy(j).wait_send()

    def finish(self):
        for i in range(self.stages):
            for *_, copy in self.moves(i):
                copy.wait_send()

    @staticmethod
    def scratch(ns, rows, width):
        dma = pltpu.SemaphoreType.DMA
        half = ns // 2
        return [
            pltpu.VMEM((half, rows, width), BF16),
            pltpu.VMEM((half, rows, width), BF16),
            pltpu.VMEM((2, half - 1, rows // 2, width), BF16),
            dma((half,)), dma((half,)), dma((2, half - 1)), dma((2, half - 1)),
        ]


def forward_kernel(
    n, ns,
    att, tok, cot, more, gate_b, gate_own, up, down, attn_gain, mlp_gain,
    out, h1r_out, branch_out, hidden_out, dy2_out, dg_out, du_out, gain_part, up_out,
    h1r, hidden, dy2, dg, du,
    wo, wd, wg, wu, land, branch, h1, second, g_pre, u_pre,
    wsem, osem, bsem, g1s, g1r, s1s, s1r, g2s, g2r, s2s, s2r, us, ur, ds, dr,
):
    s, z = lax.axis_index("seq"), lax.axis_index("head")
    rows, depth = tok.shape
    lw, ff = att.shape[1], up.shape[1]
    block = depth // ns
    width = depth // STEPS
    mine = rows_at(s, block)
    l_o = pltpu.make_async_copy(more.at[:, pl.ds(0, lw)], wo, wsem.at[0])
    last = last_part(ff)
    l_u = pltpu.make_async_copy(up, wu.at[mine, pl.ds(last, ff)], wsem.at[1])
    l_c = pltpu.make_async_copy(gate_own.at[:, pl.ds(ff - last, last)], wu.at[mine, pl.ds(0, last)], wsem.at[4])
    early = more.shape[1] - lw
    l_g = pltpu.make_async_copy(more.at[:, pl.ds(lw, early)], wg.at[:, pl.ds(0, early)], wsem.at[2])
    l_h = pltpu.make_async_copy(gate_b, wg.at[:, pl.ds(early, ff - early - last)], wsem.at[3])
    for copy in (l_o, l_u, l_c, l_g, l_h):
        copy.start()
    cube_barrier(s, z, ns, n)
    cube_u = CubeGather(s, ns, wu, block, us, ur)
    cube_d = CubeGather(s, ns, wd, block, ds, dr)
    levels = cube_u.levels
    l_u.wait()
    l_c.wait()
    cube_u.start()
    l_o.wait()

    def out_part(d, c):
        return mm(att[rows_at(d, rows), :], wo[rows_at(c, width), :], NT)

    line = LineScatter(z, n, out_part, land, s1s, s1r, branch)
    line.run(0, STEPS)
    line.start_own()
    wd[mine, :] = jnp.transpose(down[...].astype(F32)).astype(BF16)
    line.run(STEPS, 2 * STEPS)
    cube_u.level(0)
    line.run(2 * STEPS, 3 * STEPS)
    for i in range(1, levels - 1):
        cube_u.level(i)
    cube_d.start()
    line.run(3 * STEPS, line.slots)
    line.own()
    line.finish()
    o_branch = pltpu.make_async_copy(branch, branch_out, osem.at[0])
    o_branch.start()
    gain_part[...] = jnp.zeros_like(gain_part)

    @pl.loop(0, rows // BLOCK)
    def _(i):
        at = rows_at(i, BLOCK)
        y = branch[at, :]
        h = tok[at, :].astype(F32) + y * row_scale(y) * attn_gain[...]
        h1[at, :] = h
        h1r[pl.ds(pl.multiple_of(z * rows + i * BLOCK, BLOCK), BLOCK), :] = h.astype(BF16)

    fw = ff // STEPS
    o_up = pltpu.make_async_copy(wu, up_out, osem.at[1])
    o_h1r = pltpu.make_async_copy(h1r, h1r_out, osem.at[2])
    o_hidden = pltpu.make_async_copy(hidden, hidden_out, osem.at[3])
    o_dy2 = pltpu.make_async_copy(dy2, dy2_out, osem.at[4])

    def up_block(src):
        at = rows_at(src, rows)

        def columns(c, gate):
            cols = rows_at(c, fw)
            x = h1r[at, :]
            g = mm(x, gate)
            u = mm(x, wu[:, pl.ds(pl.multiple_of(last + c * fw, HEAD_DIM), fw)])
            g_pre[at, cols] = g
            u_pre[at, cols] = u
            hidden[at, cols] = (g * sigmoid(g) * u).astype(BF16)

        pl.loop(0, STEPS - 1)(lambda c: columns(c, wg[:, rows_at(c, fw)]))
        columns(STEPS - 1, wu[:, :last])

    def weights_there():
        l_g.wait()
        l_h.wait()
        cube_u.level(levels - 1)
        o_up.start()

    hooks = [functools.partial(cube_d.level, i) for i in range(levels)]
    line_gather(z, n, h1r, rows, g1s, g1r, up_block, hooks[: n - 1], weights_there)
    for hook in hooks[n - 1 :]:
        hook()
    o_h1r.start()
    o_hidden.start()

    def down_part(d, c):
        return mm(hidden[rows_at(d, rows), :], wd[rows_at(c, width), :], NT)

    line = LineScatter(z, n, down_part, land, s2s, s2r, second)
    line.run(0, STEPS)
    line.start_own()
    line.run(STEPS, line.slots)
    line.own()
    line.finish()

    @pl.loop(0, rows // BLOCK)
    def _(i):
        at = rows_at(i, BLOCK)
        y = second[at, :]
        scale = row_scale(y)
        normed = y * scale
        e = cot[at, :].astype(F32)
        out[at, :] = (h1[at, :] + normed * mlp_gain[...]).astype(BF16)
        gain_part[...] += jnp.sum(e * normed, axis=0, keepdims=True)
        dy2[pl.ds(pl.multiple_of(z * rows + i * BLOCK, BLOCK), BLOCK), :] = norm_back(
            e, normed, scale, mlp_gain[...]
        ).astype(BF16)

    def back_block(src):
        at = rows_at(src, rows)

        @pl.loop(0, STEPS)
        def _(c):
            cols = rows_at(c, fw)
            dh = mm(dy2[at, :], wd[:, cols])
            g = g_pre[at, cols]
            u = u_pre[at, cols]
            sig = sigmoid(g)
            du[at, cols] = (dh * g * sig).astype(BF16)
            dg[at, cols] = (dh * u * sig * (1.0 + g * (1.0 - sig))).astype(BF16)

        for copy in grads_out(src):
            copy.start()

    def grads_out(src):
        at = rows_at(src, rows)
        return [
            pltpu.make_async_copy(held.at[at], to.at[at], bsem.at[i, src])
            for i, (held, to) in enumerate(((dg, dg_out), (du, du_out)))
        ]

    line_gather(z, n, dy2, rows, g2s, g2r, back_block)
    o_dy2.start()
    for copy in (o_branch, o_up, o_h1r, o_hidden, o_dy2):
        copy.wait()

    @pl.loop(0, n)
    def _(src):
        for copy in grads_out(src):
            copy.wait()

    cube_u.finish()
    cube_d.finish()


def run_forward(n, ns, att, tok, cot, more, gate_b, gate_own, up, down, attn_gain, mlp_gain):
    rows, depth = tok.shape
    tl, lw = att.shape
    ff = up.shape[1]
    dma = pltpu.SemaphoreType.DMA
    sems = line_sems(n)
    shape = jax.ShapeDtypeStruct
    return pl.pallas_call(
        functools.partial(forward_kernel, n, ns),
        out_shape=(
            shape((rows, depth), BF16),
            shape((tl, depth), BF16),
            shape((rows, depth), F32),
            shape((tl, ff), BF16),
            shape((tl, depth), BF16),
            shape((tl, ff), BF16),
            shape((tl, ff), BF16),
            shape((1, depth), F32),
            shape((depth, ff + last_part(ff)), BF16),
        ),
        in_specs=[VMEM, VMEM, VMEM, ANY, ANY, ANY, ANY, VMEM, VMEM, VMEM],
        out_specs=(VMEM, ANY, ANY, ANY, ANY, ANY, ANY, VMEM, ANY),
        scratch_shapes=[
            pltpu.VMEM((tl, depth), BF16),
            pltpu.VMEM((tl, ff), BF16),
            pltpu.VMEM((tl, depth), BF16),
            pltpu.VMEM((tl, ff), BF16),
            pltpu.VMEM((tl, ff), BF16),
            pltpu.VMEM((depth, lw), BF16),
            pltpu.VMEM((depth, ff), BF16),
            pltpu.VMEM((depth, ff - last_part(ff)), BF16),
            pltpu.VMEM((depth, ff + last_part(ff)), BF16),
            pltpu.VMEM((2, n, STEPS, rows, depth // STEPS), BF16),
            pltpu.VMEM((rows, depth), F32),
            pltpu.VMEM((rows, depth), F32),
            pltpu.VMEM((rows, depth), F32),
            pltpu.VMEM((tl, ff), F32),
            pltpu.VMEM((tl, ff), F32),
            dma((5,)),
            dma((5,)),
            dma((2, n)),
            *sems["gather"], *sems["scatter"], *sems["gather"], *sems["scatter"],
            *CubeGather.sems(ns), *CubeGather.sems(ns),
        ],
        compiler_params=pltpu.CompilerParams(
            collective_id=1, has_side_effects=True, vmem_limit_bytes=VMEM_BYTES
        ),
        cost_estimate=pl.CostEstimate(flops=18 * 10**9, bytes_accessed=40 * 10**6, transcendentals=2 * 10**6),
        name="feed_forward",
    )(att, tok, cot, more, gate_b, gate_own, up, down, attn_gain, mlp_gain)


def backward_kernel(
    n, ns,
    dg_in, du_in, h1r_in, cot, branch, more, gate_b, up, attn_gain,
    middle, dy1, datt, gain_part, grad_gate, grad_up,
    dg, du, h1r, wo, wg, wu, land, total,
    first, held_g, later_g, held_u, later_u,
    wsem, osem, s1s, s1r, g1s, g1r,
    ga, gb, gc, gd, ua, ub, uc, ud,
):
    s, z = lax.axis_index("seq"), lax.axis_index("head")
    rows, depth = cot.shape
    lw, ff = datt.shape[1], dg_in.shape[1]
    block = depth // ns
    width = depth // STEPS
    early = more.shape[1] - lw
    last = last_part(ff)

    def weights_in(c):
        at = rows_at(c, width)
        return [
            pltpu.make_async_copy(more.at[at, pl.ds(lw, early)], wg.at[at, pl.ds(0, early)], wsem.at[0, c]),
            pltpu.make_async_copy(gate_b.at[at], wg.at[at, pl.ds(early, ff - early - last)], wsem.at[1, c]),
            pltpu.make_async_copy(up.at[at, pl.ds(0, last)], wg.at[at, pl.ds(ff - last, last)], wsem.at[3, c]),
            pltpu.make_async_copy(up.at[at, pl.ds(last, ff)], wu.at[at], wsem.at[2, c]),
        ]

    l_h = pltpu.make_async_copy(h1r_in, h1r, osem.at[0])
    l_o = pltpu.make_async_copy(more.at[:, pl.ds(0, lw)], wo, osem.at[1])
    l_dg = pltpu.make_async_copy(dg_in, dg, osem.at[2])
    l_du = pltpu.make_async_copy(du_in, du, osem.at[3])
    for load in (l_dg, l_h, l_du):
        load.start()
    for c in range(STEPS):
        for copy in weights_in(c):
            copy.start()
    l_o.start()
    cube_barrier(s, z, ns, n)

    def weight_block(grad):
        return lambda b: mm(h1r[:, rows_at(b, block)], grad[...], TN)

    cube_g = CubeScatter(s, ns, weight_block(dg), block, first, held_g, later_g, (ga, gb, gc, gd))
    cube_u = CubeScatter(s, ns, weight_block(du), block, first, held_u, later_u, (ua, ub, uc, ud))

    def in_part(d, c):
        at, cols = rows_at(d, rows), rows_at(c, width)
        return mm(dg[at, :], wg[cols, :], NT) + mm(du[at, :], wu[cols, :], NT)

    line = LineScatter(z, n, in_part, land, s1s, s1r, total, True)
    half = ns // 2

    def there(slot):
        @pl.when(slot < STEPS)
        def _():
            for copy in weights_in(slot):
                copy.wait()

    def task(slot):
        def during(low, count, act):
            @pl.when((slot >= low) & (slot < low + half // count))
            def _():
                for i in range(count):
                    act(count * (slot - low) + i)

        def send_second(j):
            cube_g.core_copy(half - 1 - j).wait_send()
            cube_u.send_core(j)

        during(0, 2, cube_g.add_core)
        during(half // 2, 1, send_second)
        during(half // 2 + half, 1, cube_u.add_core)

    l_h.wait()
    l_dg.wait()
    cube_g.send_core()
    l_du.wait()
    line.run(0, 2 * STEPS, there, task)
    line.run(2 * STEPS, line.slots, None, task)

    @pl.loop(line.slots, max(line.slots, half // 2 + 2 * half))
    def _(slot):
        task(slot)

    cube_g.step(0)
    line.own()
    line.finish()
    gain_part[...] = jnp.zeros_like(gain_part)

    @pl.loop(0, rows // BLOCK)
    def _(i):
        at = rows_at(i, BLOCK)
        y = branch[at, :]
        scale = row_scale(y)
        normed = y * scale
        e = cot[at, :].astype(F32) + total[at, :]
        middle[at, :] = e
        gain_part[...] += jnp.sum(e * normed, axis=0, keepdims=True)
        dy1[pl.ds(pl.multiple_of(z * rows + i * BLOCK, BLOCK), BLOCK), :] = norm_back(
            e, normed, scale, attn_gain[...]
        ).astype(BF16)

    l_o.wait()

    def att_block(src):
        at = rows_at(src, rows)
        datt[at, :] = mm(dy1[at, :], wo[...]).astype(BF16)

    todo = [functools.partial(cube.step, i) for i in range(1, cube_g.stages) for cube in (cube_g, cube_u)]
    line_gather(z, n, dy1, rows, g1s, g1r, att_block, todo[: n - 1], functools.partial(cube_u.step, 0))
    for step in todo[n - 1 :]:
        step()
    grad_gate[...] = held_g[0]
    grad_up[...] = held_u[0]
    cube_g.finish()
    cube_u.core_sent()
    cube_u.finish()


def run_backward(n, ns, dg, du, h1r, cot, branch, more, gate_b, up, attn_gain):
    rows, depth = cot.shape
    tl, ff = dg.shape
    lw = more.shape[1] + gate_b.shape[1] + last_part(ff) - ff
    block = depth // ns
    dma = pltpu.SemaphoreType.DMA
    sems = line_sems(n)
    shape = jax.ShapeDtypeStruct
    first, held, later, *cube_sems = CubeScatter.scratch(ns, block, ff)
    return pl.pallas_call(
        functools.partial(backward_kernel, n, ns),
        out_shape=(
            shape((rows, depth), F32),
            shape((tl, depth), BF16),
            shape((tl, lw), BF16),
            shape((1, depth), F32),
            shape((block, ff), BF16),
            shape((block, ff), BF16),
        ),
        in_specs=[ANY, ANY, ANY, VMEM, VMEM, ANY, ANY, ANY, VMEM],
        out_specs=(VMEM,) * 6,
        scratch_shapes=[
            pltpu.VMEM((tl, ff), BF16),
            pltpu.VMEM((tl, ff), BF16),
            pltpu.VMEM((tl, depth), BF16),
            pltpu.VMEM((depth, lw), BF16),
            pltpu.VMEM((depth, ff), BF16),
            pltpu.VMEM((depth, ff), BF16),
            pltpu.VMEM((2, n, STEPS, rows, depth // STEPS), BF16),
            pltpu.VMEM((rows, depth), F32),
            first, held, later, held, later,
            dma((4, STEPS)),
            dma((4,)),
            *sems["scatter"], *sems["gather"],
            *cube_sems, *cube_sems,
        ],
        compiler_params=pltpu.CompilerParams(
            collective_id=2, has_side_effects=True, vmem_limit_bytes=VMEM_BYTES
        ),
        cost_estimate=pl.CostEstimate(flops=18 * 10**9, bytes_accessed=30 * 10**6, transcendentals=0),
        name="into_attention",
    )(dg, du, h1r, cot, branch, more, gate_b, up, attn_gain)


LOG2E = 1.4426950408889634
NEG = -1e30


def seq_barrier(s, ns, between=None):
    bar = pltpu.get_barrier_semaphore()
    for other in range(ns):

        @pl.when(other != s)
        def _():
            pl.semaphore_signal(bar, inc=1, device_id={"seq": other}, device_id_type=MESH)

    if between is not None:
        between()
    pl.semaphore_wait(bar, ns - 1)


def share_of(s, ns, r):
    per = ns // (2 * r)
    chunk = s // per
    low = chunk < r
    sub = jnp.where(low, chunk, 2 * r - 1 - chunk)
    return sub, jnp.where(low, s - chunk * per, per + s - chunk * per)


def source_of(sub, i, ns, r):
    per = ns // (2 * r)
    return jnp.where(i < per, sub * per + i, (2 * r - 1 - sub) * per + i - per)


def head_cols(h):
    return pl.ds(pl.multiple_of(h * HEAD_DIM, HEAD_DIM), HEAD_DIM)


def attend_part(
    ns, heads, q_in, k_in, v_in, docs, gate,
    att, q_out, k_out, v_out, o_buf, lse, gate_out,
    q_buf, k_buf, v_buf, o_low, qs, qr, ks, kr, vs, vr, osend, orecv, local, cs, cr, late,
):
    s = lax.axis_index("seq")
    r = ns // heads
    blocks = ns // r
    tl = q_in.shape[0]
    mine, sub = s // r, s % r
    parity = s % 2
    to_sub, to_row = share_of(s, ns, r)

    def own_rows():
        for x, buf in ((k_in, k_buf), (v_in, v_buf)):
            buf[rows_at(s, tl), :] = x[:, head_cols(mine)]

        @pl.when(to_sub == sub)
        def _():
            q_buf[rows_at(to_row, tl), :] = q_in[:, head_cols(mine)]

    own_rows()

    def q_copy(h):
        return pltpu.make_async_remote_copy(
            src_ref=q_in.at[:, head_cols(h)],
            dst_ref=q_buf.at[rows_at(to_row, tl)],
            send_sem=qs.at[h],
            recv_sem=qr.at[to_row],
            device_id={"seq": h * r + to_sub},
            device_id_type=MESH,
        )

    def q_recv(i):
        return pltpu.make_async_remote_copy(
            src_ref=q_buf.at[rows_at(i, tl)],
            dst_ref=q_buf.at[rows_at(i, tl)],
            send_sem=qs.at[0],
            recv_sem=qr.at[i],
            device_id={"seq": s ^ 1},
            device_id_type=MESH,
        )

    def kv_copy(src, buf, send, recv, t, at):
        return pltpu.make_async_remote_copy(
            src_ref=src,
            dst_ref=buf.at[rows_at(at, tl)],
            send_sem=send,
            recv_sem=recv.at[at],
            device_id={"seq": t},
            device_id_type=MESH,
        )

    kv = ((k_in, k_buf, ks, kr), (v_in, v_buf, vs, vr))
    block = gate.shape[0]
    cols = gate_out.shape[1]
    own = gate.at[:, pl.ds(early_part(gate.shape[1]), cols)]
    own_gate = pltpu.make_async_copy(own, gate_out.at[rows_at(s, block)], local.at[0])
    cube = CubeGather(s, ns, gate_out, block, cs, cr, own)
    own_gate.start()

    def far(t):
        return (t != s) & (t % 2 == parity)

    @pl.loop(1, ns)
    def _(step):
        t = s ^ step

        @pl.when(far(t))
        def _():
            for x, buf, ss, rs in kv:
                kv_copy(x.at[:, head_cols(t // r)], buf, ss.at[0, t], rs, t, s).start()

    @pl.loop(0, heads)
    def _(h):
        @pl.when(h * r + to_sub != s)
        def _():
            q_copy(h).start()

    def pass_on(src, start):
        for _, buf, ss, rs in kv:
            copy = kv_copy(buf.at[rows_at(src, tl)], buf, ss.at[1, src], rs, s ^ 1, src)
            if start:
                copy.start()
            else:
                copy.wait_send()

    pass_on(s, True)

    @pl.loop(1, ns)
    def _(step):
        src = s ^ step

        @pl.when(far(src))
        def _():
            for x, buf, ss, rs in kv:
                kv_copy(buf.at[rows_at(src, tl)], buf, ss.at[0, 0], rs, s ^ 1, src).wait_recv()
            pass_on(src, True)

    @pl.loop(0, ns)
    def _(src):
        @pl.when(src % 2 != parity)
        def _():
            for x, buf, ss, rs in kv:
                kv_copy(buf.at[rows_at(src, tl)], buf, ss.at[0, 0], rs, s ^ 1, src).wait_recv()

    unit = HEAD_DIM ** (-0.5) * LOG2E

    def o_copy(i, t):
        return pltpu.make_async_remote_copy(
            src_ref=o_low.at[rows_at(i, tl)],
            dst_ref=att.at[:, head_cols(mine)],
            send_sem=osend.at[i],
            recv_sem=orecv.at[mine],
            device_id={"seq": t},
            device_id_type=MESH,
        )

    def attend_block(i):
        src = source_of(sub, i, ns, r)

        @pl.when(src != s)
        def _():
            q_recv(i).wait_recv()

        q = q_buf[rows_at(i, tl), :]
        start = first_of_document(docs, src * tl + lax.broadcasted_iota(jnp.int32, (1, tl), 1))
        key_at = lax.broadcasted_iota(jnp.int32, (tl, tl), 0)

        def step(j, carry, diagonal):
            top, total, acc = carry
            at = rows_at(j, tl)
            scores = mm(k_buf[at, :], q, NT) * unit
            allowed = key_at >= start - j * tl
            if diagonal:
                allowed = allowed & (key_at <= lax.broadcasted_iota(jnp.int32, (tl, tl), 1))
            scores = jnp.where(allowed, scores, NEG)
            new = jnp.maximum(top, jnp.max(scores, axis=0, keepdims=True))
            terms = jnp.exp2(scores - new)
            fade = jnp.exp2(top - new)
            return (
                new,
                total * fade + jnp.sum(terms, axis=0, keepdims=True),
                acc * fade + mm(v_buf[at, :], terms.astype(BF16), TN),
            )

        carry = (
            jnp.full((1, tl), NEG, F32),
            jnp.zeros((1, tl), F32),
            jnp.zeros((HEAD_DIM, tl), F32),
        )
        carry = lax.fori_loop(0, src, lambda j, c: step(j, c, False), carry)
        top, total, acc = step(src, carry, True)
        lse[pl.ds(i, 1), :] = top + jnp.log(total) * LOG2E
        o = jnp.transpose(acc / total)
        o_buf[rows_at(i, tl), :] = o
        o_low[rows_at(i, tl), :] = o.astype(BF16)

        @pl.when(src != s)
        def _():
            o_copy(i, src).start()

        @pl.when(src == s)
        def _():
            att[:, head_cols(mine)] = o.astype(BF16)

    late()
    cube.start()
    keep = [
        pltpu.make_async_copy(a, b, local.at[1 + i])
        for i, (a, b) in enumerate(((k_buf, k_out), (v_buf, v_out), (q_buf, q_out)))
    ]
    for copy in keep[:2]:
        copy.start()
    cuts = [0, blocks - 1, blocks, blocks]
    for i in range(3):
        pl.loop(cuts[i], cuts[i + 1])(attend_block)
        if i < 2:
            cube.level(i)
    for i in range(2, cube.levels):
        cube.level(i)

    keep[2].start()
    own_gate.wait()

    @pl.loop(0, heads)
    def _(h):
        @pl.when(h * r + to_sub != s)
        def _():
            q_copy(h).wait_send()
            pltpu.make_async_remote_copy(
                src_ref=o_low.at[rows_at(0, tl)],
                dst_ref=att.at[:, head_cols(h)],
                send_sem=osend.at[0],
                recv_sem=orecv.at[h],
                device_id={"seq": s ^ 1},
                device_id_type=MESH,
            ).wait_recv()

    @pl.loop(0, blocks)
    def _(i):
        src = source_of(sub, i, ns, r)

        @pl.when(src != s)
        def _():
            o_copy(i, src).wait_send()

    pass_on(s, False)

    @pl.loop(1, ns)
    def _(step):
        t = s ^ step

        @pl.when(far(t))
        def _():
            for x, buf, ss, rs in kv:
                kv_copy(x.at[:, head_cols(t // r)], buf, ss.at[0, t], rs, t, s).wait_send()
            pass_on(t, False)

    cube.finish()
    for copy in keep:
        copy.wait()


def attend_back_part(
    n, ns, heads, free, do_in, docs, q_in, k_in, v_in, o_in, lse, dy2_in, hidden_in,
    grad_down,
    q_buf, k_buf, v_buf, o_buf, dy2, hidden, lsem, dq, dk, dv,
    do_buf, dq_low, dk_acc, dv_acc, low, pair, land,
    first, held, later, ca, cb, cc, cd,
    ds_, dr_, ps, pr, gs, gr, qs, qr,
):
    s = lax.axis_index("seq")
    r = ns // heads
    blocks = ns // r
    tl = do_in.shape[0]
    mine, sub = s // r, s % r
    parity = s % 2

    loads = [
        pltpu.make_async_copy(a, b, lsem.at[i])
        for i, (a, b) in enumerate(
            ((dy2_in, dy2), (hidden_in, hidden), (q_in, q_buf), (k_in, k_buf), (v_in, v_buf), (o_in, o_buf))
        )
    ]
    for load in loads:
        load.start()

    def clear():
        dk_acc[...] = jnp.zeros_like(dk_acc)
        dv_acc[...] = jnp.zeros_like(dv_acc)

    cross_barrier(s, lax.axis_index("head"), ns, n, clear)
    to_sub, to_row = share_of(s, ns, r)

    def copy(src, dst, send, recv, t):
        return pltpu.make_async_remote_copy(
            src_ref=src, dst_ref=dst, send_sem=send, recv_sem=recv, device_id={"seq": t}, device_id_type=MESH
        )

    def do_copy(h):
        return copy(
            do_in.at[:, head_cols(h)], do_buf.at[rows_at(to_row, tl)], ds_.at[h], dr_.at[to_row], h * r + to_sub
        )

    @pl.loop(0, heads)
    def _(h):
        @pl.when(h * r + to_sub != s)
        def _():
            do_copy(h).start()

    block = dy2.shape[1] // ns
    cube = CubeScatter(
        s, ns, lambda b: mm(dy2[:, rows_at(b, block)], hidden[:, : grad_down.shape[0]], TN), block, first, held, later, (ca, cb, cc, cd)
    )
    for load in loads:
        load.wait()
    cube.send_core()
    cube.add_core()

    @pl.when(to_sub == sub)
    def _():
        do_buf[rows_at(to_row, tl), :] = do_in[:, head_cols(mine)]

    scale = HEAD_DIM ** (-0.5)
    unit = scale * LOG2E

    def dq_copy(i, t):
        return copy(dq_low.at[rows_at(i, tl)], dq.at[:, head_cols(mine)], qs.at[i], qr.at[mine], t)

    ones = jnp.ones((8, HEAD_DIM), F32)

    def back_block(i):
        src = source_of(sub, i, ns, r)
        rows = rows_at(i, tl)

        @pl.when(src != s)
        def _():
            copy(do_buf.at[rows], do_buf.at[rows], ds_.at[0], dr_.at[i], s ^ 1).wait_recv()

        q = q_buf[rows, :]
        do = do_buf[rows, :]
        start = first_of_document(docs, src * tl + lax.broadcasted_iota(jnp.int32, (1, tl), 1))
        norm = lse[pl.ds(i, 1), :]
        delta = lax.dot_general(
            ones, do.astype(F32) * o_buf[rows, :], NT,
            precision=lax.Precision.HIGHEST, preferred_element_type=F32,
        )[:1]
        key_at = lax.broadcasted_iota(jnp.int32, (tl, tl), 0)

        def step(j, dq_sum, diagonal):
            at = rows_at(j, tl)
            keys = k_buf[at, :]
            scores = mm(keys, q, NT) * unit
            allowed = key_at >= start - j * tl
            if diagonal:
                allowed = allowed & (key_at <= lax.broadcasted_iota(jnp.int32, (tl, tl), 1))
            p = jnp.where(allowed, jnp.exp2(scores - norm), 0.0)
            dp = mm(v_buf[at, :], do, NT)
            dscore = (p * (dp - delta)).astype(BF16)
            dv_acc[at, :] += mm(p.astype(BF16), do)
            dk_acc[at, :] += mm(dscore, q)
            return dq_sum + mm(dscore, keys, TN)

        dq_sum = lax.fori_loop(0, src, lambda j, c: step(j, c, False), jnp.zeros((tl, HEAD_DIM), F32))
        dq_sum = step(src, dq_sum, True)
        dq_low[rows, :] = (dq_sum * scale).astype(BF16)

        @pl.when(src != s)
        def _():
            dq_copy(i, src).start()

        @pl.when(src == s)
        def _():
            dq[:, head_cols(mine)] = dq_low[rows, :]

    pl.loop(0, blocks - 1)(back_block)
    cube.step(0)
    pl.loop(blocks - 1, blocks)(back_block)
    half = ns // 2

    def pair_copy(w, i):
        src = 2 * i + 1 - parity
        return copy(low.at[w, rows_at(src, tl)], pair.at[w, rows_at(i, tl)], ps.at[w, i], pr.at[w, i], s ^ 1)

    @pl.loop(0, half)
    def _(i):
        at = rows_at(2 * i + 1 - parity, tl)
        low[0, at, :] = (dk_acc[at, :] * scale).astype(BF16)
        pair_copy(0, i).start()
        low[1, at, :] = dv_acc[at, :].astype(BF16)
        pair_copy(1, i).start()

    slot = sub // 2
    outs = (dk, dv)

    def back_copy(w, i):
        dest = 2 * i + parity
        return copy(
            low.at[w, rows_at(dest, tl)], land.at[w, slot, :, head_cols(mine)], gs.at[w, i], gr.at[w, mine, slot], dest
        )

    @pl.loop(0, half)
    def _(i):
        dest = 2 * i + parity
        at = rows_at(dest, tl)
        for w, acc, factor in ((0, dk_acc, scale), (1, dv_acc, 1.0)):
            copy(low.at[w, at], pair.at[w, rows_at(i, tl)], ps.at[w, i], pr.at[w, i], s ^ 1).wait_recv()
            low[w, at, :] = (acc[at, :] * factor + pair[w, rows_at(i, tl), :].astype(F32)).astype(BF16)

            @pl.when(dest != s)
            def _():
                back_copy(w, i).start()

            @pl.when(dest == s)
            def _():
                land[w, slot, :, head_cols(mine)] = low[w, at, :]

    free()

    @pl.loop(0, heads)
    def _(h):
        for w in range(2):
            for k in range(r // 2):

                @pl.when(h * r + 2 * k + parity != s)
                def _():
                    copy(
                        low.at[w, rows_at(0, tl)], land.at[w, k, :, head_cols(h)], gs.at[w, 0], gr.at[w, h, k], s ^ 1
                    ).wait_recv()

    for w in range(2):
        outs[w][...] = functools.reduce(
            lambda a, b: a + b, [land[w, k].astype(F32) for k in range(r // 2)]
        ).astype(BF16)

    @pl.loop(0, heads)
    def _(h):
        @pl.when(h * r + to_sub != s)
        def _():
            do_copy(h).wait_send()
            copy(dq_low.at[rows_at(0, tl)], dq.at[:, head_cols(h)], qs.at[0], qr.at[h], s ^ 1).wait_recv()

    def late():
        for i in range(1, cube.stages):
            cube.step(i)
        grad_down[...] = jnp.transpose(held[0].astype(F32)).astype(BF16)

    def finish():
        @pl.loop(0, blocks)
        def _(i):
            src = source_of(sub, i, ns, r)

            @pl.when(src != s)
            def _():
                dq_copy(i, src).wait_send()

        @pl.loop(0, half)
        def _(i):
            for w in range(2):
                pair_copy(w, i).wait_send()

                @pl.when(2 * i + parity != s)
                def _():
                    back_copy(w, i).wait_send()

        cube.finish()

    return cube.core_sent, late, finish


def cross_barrier(s, z, ns, n, between=None):
    bar = pltpu.get_barrier_semaphore()
    for axis, me, count in (("seq", s, ns), ("head", z, n)):
        for other in range(count):

            @pl.when(other != me)
            def _():
                pl.semaphore_signal(bar, inc=1, device_id={axis: other}, device_id_type=MESH)

    if between is not None:
        between()
    pl.semaphore_wait(bar, ns - 1 + n - 1)


def row_sums(left, right):
    ones = jnp.ones((8, left.shape[1]), F32)
    both = [
        lax.dot_general(ones, x, NT, precision=lax.Precision.HIGHEST, preferred_element_type=F32) for x in (left, right)
    ]
    return jnp.where(lax.broadcasted_iota(jnp.int32, both[0].shape, 0) < 4, both[0], both[1])


def as_column(sums, row):
    pick = (lax.broadcasted_iota(jnp.int32, (8, HEAD_DIM), 0) == row).astype(F32)
    return lax.dot_general(sums, pick, TN, precision=lax.Precision.HIGHEST, preferred_element_type=F32)


class SmallExchange:
    def __init__(self, axis, me, count, land, send_sem, recv_sem):
        self.axis, self.me, self.count, self.land = axis, me, count, land
        self.send_sem, self.recv_sem = send_sem, recv_sem

    def copy(self, slot, to):
        return remote(self.land.at[slot], self.land.at[slot], self.send_sem.at[to], self.recv_sem.at[slot], self.axis, to)

    def each(self, act):
        @pl.loop(0, self.count)
        def _(other):
            @pl.when(other != self.me)
            def _():
                act(other)

    def start(self):
        self.each(lambda other: self.copy(self.me, other).start())

    def receive(self):
        self.each(lambda other: self.copy(other, other).wait_recv())

    def finish(self):
        self.each(lambda other: self.copy(self.me, other).wait_send())


def turn(x, cos, sin):
    return x * cos + pltpu.roll(x, HEAD_DIM // 2, 1) * sin


def turn_back(x, cos, sin):
    return x * cos - pltpu.roll(x, HEAD_DIM // 2, 1) * sin


def project_part(
    n, ns, depth_full,
    tok, wq, wk, wv, wo, gate, gq, gk, docs, turns,
    x_out, w_out, more_out, q_out, k_out, totals, cos, sin,
    q_rot, k_rot, v_low, q_raw, k_raw, x, w, own, land, lsem, ags, agr, cgs, cgr, egs, egr, ss, sr,
):
    s, z = lax.axis_index("seq"), lax.axis_index("head")
    rows, depth = tok.shape
    block, lw = wq.shape
    heads = lw // HEAD_DIM
    cross_barrier(s, z, ns, n)
    mine = rows_at(s, block)

    def head_gain(h):
        return head_cols(z * heads + h)

    loads = [pltpu.make_async_copy(tok, x.at[rows_at(z, rows)], lsem.at[0])] + [
        pltpu.make_async_copy(m, w.at[mine, pl.ds(i * lw, lw)], lsem.at[i + 1]) for i, m in enumerate((wq, wk, wv))
    ]
    for copy in loads:
        copy.start()
    loads[0].wait()
    cube = CubeGather(s, ns, w, block, cgs, cgr)
    own_more = pltpu.make_async_copy(own, more_out.at[mine], lsem.at[8])
    cube_e = CubeGather(s, ns, more_out, block, egs, egr, own)
    levels = cube.levels

    def weights(k):
        if k == 0:
            cube.level(0)
        else:
            for i in range(1, levels):
                cube.level(i)
                if i == levels - 2:
                    cube_e.start()

    def start_weights():
        for copy in loads[1:]:
            copy.wait()
        cube.start()

    def multiply(src):
        at = rows_at(src, rows)
        for i, to in enumerate((q_raw, k_raw)):
            to[at, :] = mm(x[at, :], w[:, i * lw : (i + 1) * lw])
        v_low[at, :] = mm(x[at, :], w[:, 2 * lw :]).astype(BF16)

    part = rows // AG_CHUNKS

    def copy(src, c, up):
        at = pl.ds(pl.multiple_of(src * rows + c * part, part), part)
        return remote(x.at[at], x.at[at], ags.at[up, src, c], agr.at[src, c], "head", z + 1 if up else z - 1)

    more = (z > 0, z < n - 1)
    for c in range(AG_CHUNKS):
        for up in (0, 1):

            @pl.when(more[up])
            def _():
                copy(z, c, up).start()

    start_weights()
    own[:, :lw] = jnp.transpose(wo[...].astype(F32)).astype(BF16)
    own[:, lw:] = gate[:, : own.shape[1] - lw]
    own_more.start()
    token = s * x.shape[0] + lax.broadcasted_iota(jnp.int32, cos.shape, 0)
    angle = (token - first_of_document(docs, token)).astype(F32) * turns[...]
    flip = jnp.where(lax.broadcasted_iota(jnp.int32, cos.shape, 1) < HEAD_DIM // 2, -1.0, 1.0)
    cos[...] = jnp.cos(angle)
    sin[...] = jnp.sin(angle) * flip

    def sides(k):
        return ((z + k, z + k < n, 0), (z - k, z - k >= 0, 1))

    for k in range(1, n):
        for c in range(AG_CHUNKS):
            for src, there, up in sides(k):

                @pl.when(there)
                def _():
                    copy(src, c, up).wait_recv()

                    @pl.when(more[up])
                    def _():
                        copy(src, c, up).start()

        if k <= 2:
            weights(k - 1)
        if k == min(2, n - 1):
            multiply(z)
            for src, there, _ in sides(1):
                pl.when(there)(functools.partial(multiply, src))
        if k > 1:
            for src, there, _ in sides(k):
                pl.when(there)(functools.partial(multiply, src))

    outs = [
        pltpu.make_async_copy(a, b, lsem.at[4 + i])
        for i, (a, b) in enumerate(((x, x_out), (w, w_out), (q_raw, q_out), (k_raw, k_out)))
    ]
    for out in outs:
        out.start()
    totals[...] = row_sums(q_raw[...] * q_raw[...], k_raw[...] * k_raw[...])
    land[z] = totals[...]
    small = SmallExchange("head", z, n, land, ss, sr)
    small.start()
    small.receive()
    total = land[0]
    for k in range(1, n):
        total = total + land[k]
    totals[...] = total
    for row, raw, gain, to in ((0, q_raw, gq, q_rot), (4, k_raw, gk, k_rot)):
        scale = lax.rsqrt(as_column(total, row) / depth_full + epsilon)
        for h in range(heads):
            cols = slice(h * HEAD_DIM, (h + 1) * HEAD_DIM)
            to[:, cols] = turn(raw[:, cols] * scale * gain[:, head_gain(h)], cos[...], sin[...]).astype(BF16)
        if row == 0:
            cube_e.level(0)

    def late():
        for i in range(1, levels):
            cube_e.level(i)

    def finish():
        small.finish()
        cube.finish()
        cube_e.finish()
        for out in [*outs, own_more]:
            out.wait()

        @pl.loop(0, n)
        def _(src):
            for c in range(AG_CHUNKS):

                @pl.when((src >= z) & (z > 0))
                def _():
                    copy(src, c, 0).wait_send()

                @pl.when((src <= z) & (z < n - 1))
                def _():
                    copy(src, c, 1).wait_send()

    return late, finish


def front_kernel(n, ns, heads, depth_full, *refs):
    ins, refs = refs[:10], refs[10:]
    made, refs = refs[:8], refs[8:]
    attended, refs = refs[:7], refs[7:]
    first, second = refs[:18], refs[18:]
    late, finish = project_part(n, ns, depth_full, *ins, *made, *first)
    attend_part(ns, heads, *first[:3], ins[8], ins[5], *attended, *second, late=late)
    finish()


def run_front(n, ns, heads, tok, wq, wk, wv, wo, gate, gq, gk, docs, turns):
    rows, depth = tok.shape
    tl = rows * n
    block, lw = wq.shape
    r = ns // heads
    nq = ns // r * tl
    nk = ns * tl
    ff = gate.shape[1]
    early = early_part(ff)
    dma = pltpu.SemaphoreType.DMA
    shape = jax.ShapeDtypeStruct
    return pl.pallas_call(
        functools.partial(front_kernel, n, ns, heads, depth),
        out_shape=(
            shape((tl, depth), BF16),
            shape((depth, 3 * lw), BF16),
            shape((depth, lw + early), BF16),
            shape((tl, lw), F32),
            shape((tl, lw), F32),
            shape((8, tl), F32),
            shape((tl, HEAD_DIM), F32),
            shape((tl, HEAD_DIM), F32),
            shape((tl, lw), BF16),
            shape((nq, HEAD_DIM), BF16),
            shape((nk, HEAD_DIM), BF16),
            shape((nk, HEAD_DIM), BF16),
            shape((nq, HEAD_DIM), F32),
            shape((ns // r, tl), F32),
            shape((depth, ff - early - last_part(ff)), BF16),
        ),
        in_specs=[ANY] * 4 + [VMEM] * 4 + [SMEM, VMEM],
        out_specs=(ANY,) * 5 + (VMEM,) * 4 + (ANY,) * 3 + (VMEM,) * 2 + (ANY,),
        scratch_shapes=[
            pltpu.VMEM((tl, lw), BF16),
            pltpu.VMEM((tl, lw), BF16),
            pltpu.VMEM((tl, lw), BF16),
            pltpu.VMEM((tl, lw), F32),
            pltpu.VMEM((tl, lw), F32),
            pltpu.VMEM((tl, depth), BF16),
            pltpu.VMEM((depth, 3 * lw), BF16),
            pltpu.VMEM((block, lw + early), BF16),
            pltpu.VMEM((n, 8, tl), F32),
            dma((9,)),
            dma((2, n, AG_CHUNKS)), dma((n, AG_CHUNKS)),
            *CubeGather.sems(ns), *CubeGather.sems(ns),
            dma((n,)), dma((n,)),
            pltpu.VMEM((nq, HEAD_DIM), BF16),
            pltpu.VMEM((nk, HEAD_DIM), BF16),
            pltpu.VMEM((nk, HEAD_DIM), BF16),
            pltpu.VMEM((nq, HEAD_DIM), BF16),
            dma((heads,)), dma((ns // r,)),
            dma((2, ns)), dma((ns,)),
            dma((2, ns)), dma((ns,)),
            dma((ns // r,)), dma((heads,)),
            dma((4,)),
            *CubeGather.sems(ns),
        ],
        compiler_params=pltpu.CompilerParams(
            collective_id=5, has_side_effects=True, vmem_limit_bytes=VMEM_BYTES
        ),
        cost_estimate=pl.CostEstimate(flops=6 * 10**9, bytes_accessed=30 * 10**6, transcendentals=5 * 10**6),
        name="front",
    )(tok, wq, wk, wv, wo, gate, gq, gk, docs, turns)


def input_part(
    n, ns, depth_full, sent, late,
    dq, dk, dv, q_raw, k_raw, totals, gq, gk, cos, sin, x_in, w_in, att, dy1_in, attn_part, mlp_part,
    total, grad_q, grad_k, grad_v, grad_o, grad_down, gains,
    dy2, hidden, first, q_back, k_back,
    w, dy1, lsem, dqkv, inner, land, message, message_z, gain_land,
    held, later, c0s, c0r, c1s, c1r,
    held_o, later_o, o0s, o0r, o1s, o1r,
    ss, sr, ms, mr, zs, zr, s1s, s1r,
):
    s, z = lax.axis_index("seq"), lax.axis_index("head")
    rows, depth = total.shape
    tl, lw = dq.shape
    block = depth // ns
    heads = lw // HEAD_DIM

    def head_gain(h):
        return head_cols(z * heads + h)

    sums = totals[...]
    scales = [lax.rsqrt(as_column(sums, row) / depth_full + epsilon) for row in (0, 4)]
    todo = ((dq, q_raw, gq, q_back), (dk, k_raw, gk, k_back))
    products = []

    x = dy2
    l_y = pltpu.make_async_copy(dy1_in, dy1, lsem.at[0])
    l_w = pltpu.make_async_copy(w_in, w, lsem.at[1])
    l_x = pltpu.make_async_copy(x_in, x, lsem.at[2])

    def turn_all():
        message[...] = jnp.zeros_like(message)
        for i, (grad, raw, gain, back) in enumerate(todo):
            product = jnp.zeros((tl, HEAD_DIM), F32)
            for h in range(heads):
                cols = slice(h * HEAD_DIM, (h + 1) * HEAD_DIM)
                hat = raw[h * tl : (h + 1) * tl, :] * scales[i]
                turned = turn_back(grad[:, cols].astype(F32), cos[...], sin[...])
                message[0, pl.ds(i, 1), cols] = jnp.sum(turned * hat, axis=0, keepdims=True)
                turned = turned * gain[:, head_gain(h)]
                back[h * tl : (h + 1) * tl, :] = turned
                product = product + turned * hat
            products.append(product)
        inner[z] = row_sums(*products)
        for t in range(1, ns):
            message[t, pl.ds(0, 2), pl.ds(0, lw)] = message[0, pl.ds(0, 2), pl.ds(0, lw)]
        for t in range(ns):
            for i, part in enumerate((attn_part, mlp_part)):
                message[t, pl.ds(i, 1), pl.ds(lw, block)] = part[:, t * block : (t + 1) * block]

    turn_all()
    small = SmallExchange("head", z, n, inner, ss, sr)
    small.start()

    def message_copy(t, frm):
        return remote(message.at[t], message_z.at[frm], ms.at[t], mr.at[frm], "seq", t)

    def each_seq(act):
        @pl.loop(0, ns)
        def _(t):
            @pl.when(t != s)
            def _():
                act(t)

    message_z[s] = message[s]
    each_seq(lambda t: message_copy(t, s).start())
    dqkv[:, 2 * lw :] = dv[...]
    l_y.wait()
    ff = hidden.shape[1]

    def early_block(b):
        cols = rows_at(b, block)
        return jnp.concatenate([mm(dy1[:, cols], att[...], TN), mm(dy2[:, cols], hidden[:, ff - lw :], TN)], axis=1)

    cube_o = CubeScatter(
        s, ns, early_block, block, first.at[:, :, pl.ds(0, 2 * lw)], held_o, later_o, (o0s, o0r, o1s, o1r)
    )
    sent()
    cube_o.send_core()
    cube_o.add_core()
    l_x.start()
    late()
    small.receive()
    sums = inner[0]
    for k in range(1, n):
        sums = sums + inner[k]
    for i, (grad, raw, gain, back) in enumerate(todo):
        mean = as_column(sums, 4 * i) / depth_full
        for h in range(heads):
            cols = slice(h * HEAD_DIM, (h + 1) * HEAD_DIM)
            to = slice(i * lw + h * HEAD_DIM, i * lw + (h + 1) * HEAD_DIM)
            dqkv[:, to] = (scales[i] * (back[h * tl : (h + 1) * tl, :] - raw[h * tl : (h + 1) * tl, :] * scales[i] * mean)).astype(BF16)

    width = depth // STEPS

    def weight_block(b):
        cols = rows_at(b, block)
        return mm(x[:, cols], dqkv[...], TN)

    def in_part(d, c):
        return mm(dqkv[rows_at(d, rows), :], w[rows_at(c, width), :], NT)

    cube = CubeScatter(s, ns, weight_block, block, first, held, later, (c0s, c0r, c1s, c1r))
    line = LineScatter(z, n, in_part, land, s1s, s1r, total, True)
    half = ns // 2

    def task(slot):
        for i, act in enumerate((cube.send_core, cube.add_core)):
            low = 1 + i * (half // 2)

            @pl.when((slot >= low) & (slot < low + half // 2))
            def _():
                for j in range(2):
                    act(2 * (slot - low) + j)

    done = 1 + half
    l_w.wait()
    l_x.wait()
    cube_o.core_sent()
    line.run(0, done, None, task)
    line.run(done, done + 3)
    for i in range(cube.stages - 1):
        cube_o.step(i)
    line.run(done + 3, line.slots)
    for i in range(cube.stages - 1):
        cube.step(i)

    each_seq(lambda t: message_copy(t, t).wait_recv())
    received = message_z[0]
    for t in range(1, ns):
        received = received + message_z[t]
    each_seq(lambda t: message_copy(t, s).wait_send())
    gain_land[z] = received
    rounds = SmallExchange("head", z, n, gain_land, zs, zr)
    rounds.start()
    line.own()
    cube_o.step(cube.stages - 1)
    grad_o[...] = jnp.transpose(held_o[0, :, :lw].astype(F32)).astype(BF16)
    grad_down[...] = jnp.transpose(held_o[0, :, lw:].astype(F32)).astype(BF16)
    cube.step(cube.stages - 1)
    for i, to in enumerate((grad_q, grad_k, grad_v)):
        to[...] = held[0, :, i * lw : (i + 1) * lw]
    rounds.receive()
    at = s * block
    gains[...] = jnp.zeros_like(gains)
    gains[0:2, :] = gain_land[at // lw, pl.ds(0, 2), pl.ds(pl.multiple_of(at % lw, block), block)]
    both = gain_land[0, pl.ds(0, 2), pl.ds(lw, block)]
    for k in range(1, n):
        both = both + gain_land[k, pl.ds(0, 2), pl.ds(lw, block)]
    gains[2:4, :] = both
    cube.core_sent()
    cube.finish()
    cube_o.finish()
    line.finish()
    small.finish()
    rounds.finish()


def back_kernel(n, ns, heads, depth_full, *refs):
    ins, more, refs = refs[:9], refs[9:22], refs[22:]
    down, outs, refs = refs[0], refs[1:8], refs[8:]
    held, rest, raw_sem = refs[:32], refs[32:-1], refs[-1]
    dy2, hidden, dq, dk, dv, dk_acc, first = held[4], held[5], *held[7:10], held[12], held[17]
    half, tl = dk_acc.shape[0] // 2, dq.shape[0]
    back, raws = ([acc.at[pl.ds(i * half, tl * heads)] for i in range(2)] for acc in (dk_acc, held[13]))
    raw_loads = [
        pltpu.make_async_copy(m.at[:, pl.ds(h * HEAD_DIM, HEAD_DIM)], to.at[pl.ds(h * tl, tl)], raw_sem.at[i, h])
        for i, (m, to) in enumerate(zip(more[:2], raws))
        for h in range(heads)
    ]

    def free():
        for load in raw_loads:
            load.start()

    starts = [
        pltpu.make_async_copy(more[10], rest[1], rest[2].at[0]), pltpu.make_async_copy(more[8], rest[0], rest[2].at[1])
    ]
    for load in starts:
        load.start()
    sent, late, finish = attend_back_part(n, ns, heads, free, *ins, down, *held)
    for load in raw_loads:
        load.wait()
    input_part(n, ns, depth_full, sent, late, dq, dk, dv, *raws, *more[2:], *outs, dy2, hidden, first, *back, *rest)
    finish()


def run_back(n, ns, heads, do, docs, q, k, v, o, lse, dy2, hidden, *more):
    q_raw, k_raw, totals, gq, gk, cos, sin, x, w, att, dy1, attn_part, mlp_part = more
    tl, lw = do.shape
    rows, depth = tl // n, x.shape[1]
    block = depth // ns
    ff = hidden.shape[1]
    r = ns // heads
    nq = ns // r * tl
    nk = ns * tl
    dma = pltpu.SemaphoreType.DMA
    shape = jax.ShapeDtypeStruct
    first, held, later, *cube_sems = CubeScatter.scratch(ns, block, 3 * lw)
    return pl.pallas_call(
        functools.partial(back_kernel, n, ns, heads, depth),
        out_shape=(shape((ff - lw, block), BF16), shape((rows, depth), F32))
        + (shape((block, lw), BF16),) * 3
        + (shape((lw, block), BF16), shape((lw, block), BF16), shape((8, block), F32)),
        in_specs=[VMEM, SMEM] + [ANY] * 4 + [VMEM] + [ANY] * 4 + [VMEM] * 5 + [ANY] * 2 + [VMEM, ANY, VMEM, VMEM],
        out_specs=(VMEM,) * 8,
        scratch_shapes=[
            pltpu.VMEM((nq, HEAD_DIM), BF16),
            pltpu.VMEM((nk, HEAD_DIM), BF16),
            pltpu.VMEM((nk, HEAD_DIM), BF16),
            pltpu.VMEM((nq, HEAD_DIM), F32),
            pltpu.VMEM(dy2.shape, BF16),
            pltpu.VMEM(hidden.shape, BF16),
            dma((6,)),
            pltpu.VMEM((tl, lw), BF16),
            pltpu.VMEM((tl, lw), BF16),
            pltpu.VMEM((tl, lw), BF16),
            pltpu.VMEM((nq, HEAD_DIM), BF16),
            pltpu.VMEM((nq, HEAD_DIM), BF16),
            pltpu.VMEM((nk, HEAD_DIM), F32),
            pltpu.VMEM((nk, HEAD_DIM), F32),
            pltpu.VMEM((2, nk, HEAD_DIM), BF16),
            pltpu.VMEM((2, nk // 2, HEAD_DIM), BF16),
            pltpu.VMEM((2, r // 2, tl, lw), BF16),
            *CubeScatter.scratch(ns, block, ff - lw),
            dma((heads,)), dma((ns // r,)),
            dma((2, ns // 2)), dma((2, ns // 2)),
            dma((2, ns // 2)), dma((2, heads, r // 2)),
            dma((ns // r,)), dma((heads,)),
            pltpu.VMEM(w.shape, BF16),
            pltpu.VMEM((tl, depth), BF16),
            dma((3,)),
            pltpu.VMEM((tl, 3 * lw), BF16),
            pltpu.VMEM((n, 8, tl), F32),
            pltpu.VMEM((2, n, STEPS, rows, depth // STEPS), BF16),
            pltpu.VMEM((ns, 8, lw + block), F32),
            pltpu.VMEM((ns, 8, lw + block), F32),
            pltpu.VMEM((n, 8, lw + block), F32),
            held, later, *cube_sems,
            *CubeScatter.scratch(ns, block, 2 * lw)[1:],
            dma((n,)), dma((n,)),
            dma((ns,)), dma((ns,)),
            dma((n,)), dma((n,)),
            *line_sems(n)["scatter"],
            dma((2, heads)),
        ],
        compiler_params=pltpu.CompilerParams(
            collective_id=6, has_side_effects=True, vmem_limit_bytes=VMEM_BYTES
        ),
        cost_estimate=pl.CostEstimate(flops=16 * 10**9, bytes_accessed=40 * 10**6, transcendentals=5 * 10**6),
        name="back",
    )(do, docs, q, k, v, o, lse, dy2, hidden, *more)


def widen_kernel(count, *refs):
    spec = WIDEN
    ins, rest = refs[:count], refs[count:]
    outs, rest = rest[: len(spec)], rest[len(spec) :]
    held, rest = rest[:count], rest[count:]
    wide, (load_sem, store_sem) = rest[: len(spec)], rest[len(spec) :]
    loads = [pltpu.make_async_copy(a, b, load_sem.at[i]) for i, (a, b) in enumerate(zip(ins, held))]
    stores = [pltpu.make_async_copy(a, b, store_sem.at[i]) for i, (a, b) in enumerate(zip(wide, outs))]
    for copy in loads:
        copy.start()
    at = 0
    for (parts, stacked), to, store in zip(spec, wide, stores):
        row = 0
        for i in range(at, at + parts):
            loads[i].wait()
            block = held[i][...].astype(to.dtype)
            if stacked:
                to[row : row + block.shape[0], :] = block
                row += block.shape[0]
            elif i == at:
                to[...] = block
            else:
                to[...] += block
        at += parts
        store.start()
    for copy in stores:
        copy.wait()


WIDEN = ((1, False), (1, False), (1, False), (2, True), (1, False), (1, False), (1, False), (1, False), (2, False))


def run_widen(arrays, outs):
    dma = pltpu.SemaphoreType.DMA
    return pl.pallas_call(
        functools.partial(widen_kernel, len(arrays)),
        out_shape=tuple(outs),
        in_specs=[ANY] * len(arrays),
        out_specs=(ANY,) * len(outs),
        scratch_shapes=[pltpu.VMEM(a.shape, a.dtype) for a in arrays]
        + [pltpu.VMEM(o.shape, o.dtype) for o in outs]
        + [dma((len(arrays),)), dma((len(outs),))],
        compiler_params=pltpu.CompilerParams(vmem_limit_bytes=VMEM_BYTES),
        name="widen",
    )(*arrays)


def on_device(
    tokens,
    cotangent,
    doc_lengths,
    q_weight,
    k_weight,
    v_weight,
    o_weight,
    gate_weight,
    up_weight,
    down_weight,
    q_gain,
    k_gain,
    attn_gain,
    mlp_gain,
):
    ns, nz = lax.axis_size("seq"), lax.axis_size("head")
    lw = q_weight.shape[1]
    heads = lw // HEAD_DIM
    block, ff = gate_weight.shape
    gq, gk = q_gain[None], k_gain[None]
    frequency = jnp.power(rope_base, -(jnp.arange(HEAD_DIM) % (HEAD_DIM // 2)).astype(F32) * (2.0 / HEAD_DIM))

    x, w, more, q_raw, k_raw, totals, cos, sin, attended, q_held, k_held, v_held, o_held, lse, gate_b = run_front(
        nz, ns, heads, tokens, q_weight, k_weight, v_weight, o_weight, gate_weight, gq, gk, doc_lengths, frequency[None]
    )
    output, h1r, branch, hidden, dy2, dg, du, mlp_part, up = run_forward(
        nz, ns, attended, tokens, cotangent, more, gate_b, gate_weight, up_weight, down_weight, attn_gain[None], mlp_gain[None]
    )
    middle, dy1, datt, attn_part, grad_gate, grad_up = run_backward(
        nz, ns, dg, du, h1r, cotangent, branch, more, gate_b, up, attn_gain[None]
    )
    down_a, last, grad_q, grad_k, grad_v, grad_o, down_b, gains = run_back(
        nz, ns, heads, datt, doc_lengths, q_held, k_held, v_held, o_held, lse, dy2, hidden,
        q_raw, k_raw, totals, gq, gk, cos, sin, x, w, attended, dy1, attn_part, mlp_part,
    )
    shape = jax.ShapeDtypeStruct
    small = shape((block, lw), F32)
    output, grad_gate, grad_up, grad_down, grad_q, grad_k, grad_v, grad_o, input_grad = run_widen(
        (output, grad_gate, grad_up, down_a, down_b, grad_q, grad_k, grad_v, grad_o, middle, last),
        (
            shape(output.shape, BF16),
            shape((block, ff), F32),
            shape((block, ff), F32),
            shape((ff, block), F32),
            small, small, small,
            shape((lw, block), F32),
            shape(middle.shape, F32),
        ),
    )
    return (
        output,
        input_grad,
        grad_q,
        grad_k,
        grad_v,
        grad_o,
        grad_gate,
        grad_up,
        grad_down,
        gains[0],
        gains[1],
        gains[2],
        gains[3],
    )


def solution(mesh):
    in_specs = (
        P(("seq", "head"), None),
        P(("seq", "head"), None),
        P(),
        P("seq", "head"),
        P("seq", "head"),
        P("seq", "head"),
        P("head", "seq"),
        P("seq", "head"),
        P("seq", "head"),
        P("head", "seq"),
        P(),
        P(),
        P(),
        P(),
    )
    out_specs = (
        P(("seq", "head"), None),
        P(("seq", "head"), None),
        P("seq", "head"),
        P("seq", "head"),
        P("seq", "head"),
        P("head", "seq"),
        P("seq", "head"),
        P("seq", "head"),
        P("head", "seq"),
        P("seq"),
        P("seq"),
        P("seq"),
        P("seq"),
    )
    return jax.shard_map(
        on_device, mesh=mesh, in_specs=in_specs, out_specs=out_specs, check_vma=False
    )
```
